32 devices in a mesh: stream: 2 (over x), dp: 16 (over z, y, core).
Axes of the slice: x: 2, y: 2, z: 4, core: 2. Of those that a mesh axis runs over, the one named last changes fastest.
Arguments:
- text_states: bfloat16 [8192, 768], P(('stream', 'dp')), may hold values from -6 to 6
- image_states: bfloat16 [2304, 1024], P(('stream', 'dp')), may hold values from -6 to 6
- caption_lengths: int32 [64], P(('stream', 'dp')), may hold values from 8 to 128, as said below
- text_query: bfloat16 [768, 1024], replicated, may hold values from -0.21875 to 0.21875
- text_keyval: bfloat16 [768, 2048], replicated, may hold values from -0.21875 to 0.21875
- text_attend: bfloat16 [1024, 768], replicated, may hold values from -0.75 to 0.75
- text_up: bfloat16 [768, 3072], replicated, may hold values from -0.21875 to 0.21875
- text_down: bfloat16 [3072, 768], replicated, may hold values from -0.109375 to 0.109375
- text_qkv: bfloat16 [768, 2304], replicated, may hold values from -0.21875 to 0.21875
- text_output: bfloat16 [768, 768], replicated, may hold values from -0.875 to 0.875
- text_gains: float32 [3, 768], replicated, may hold values from 0.5 to 1.5
- image_query: bfloat16 [1024, 1024], replicated, may hold values from -0.1875 to 0.1875
- image_keyval: bfloat16 [1024, 2048], replicated, may hold values from -0.1875 to 0.1875
- image_attend: bfloat16 [1024, 1024], replicated, may hold values from -0.75 to 0.75
- image_up: bfloat16 [1024, 1024], replicated, may hold values from -0.1875 to 0.1875
- image_down: bfloat16 [1024, 1024], replicated, may hold values from -0.1875 to 0.1875
- image_qkv: bfloat16 [1024, 3072], replicated, may hold values from -0.1875 to 0.1875
- image_output: bfloat16 [1024, 1024], replicated, may hold values from -0.75 to 0.75
- image_gains: float32 [3, 1024], replicated, may hold values from 0.5 to 1.5
- text_cotangent: bfloat16 [8192, 768], P(('stream', 'dp')), may hold values from -6 to 6
- image_cotangent: bfloat16 [2304, 1024], P(('stream', 'dp')), may hold values from -6 to 6
Outputs:
- text_result: bfloat16 [8192, 768], P(('stream', 'dp'))
- image_result: bfloat16 [2304, 1024], P(('stream', 'dp'))
- text_grad: bfloat16 [8192, 768], P(('stream', 'dp'))
- image_grad: bfloat16 [2304, 1024], P(('stream', 'dp'))
- text_weight_grads: float32 [10223616], P(('stream', 'dp'))
- image_weight_grads: float32 [10485760], P(('stream', 'dp'))
- text_gain_grads: float32 [3, 768], replicated
- image_gain_grads: float32 [3, 1024], replicated
The draws below stay inside these ranges and needn't reach their ends.
Inputs may be any that keep to these rules, and one draw needn't show every extreme that they name: `caption_lengths`: on every device the first of its pairs has a caption of 128 tokens.
All inputs are finite; a program needn't handle non-finite values.
Results may differ from the reference program's by a relative error of at most 0.02.
Values may be sent and summed in bfloat16 or wider, within the bound.
No kernel may reach another device: no remote copies, remote signals or barrier semaphores. Data moves between devices by JAX's collectives and lax.ppermute only.
A program may use at most 448 MiB of HBM per device.

```python
import jax
import jax.numpy as jnp
from jax import lax

D_T = 768
H_T = 12
FF_T = 3072
D_I = 1024
H_I = 8
FF_I = 1024
D_C = 1024
H_C = 8
LMAX = 128
REGIONS = 36
PAIRS_DEV = 2
PAIRS = 64


def draw_caption_lengths(key, part):
    key = jax.random.fold_in(key, 11)
    lengths_drawn = jax.random.randint(key, (PAIRS,), 8, LMAX + 1)
    longest = jnp.arange(PAIRS, dtype=jnp.int32) % PAIRS_DEV == 0
    return jnp.where(longest, LMAX, lengths_drawn).astype(jnp.int32)


def strengthened(entries, key, source, target, blocks, factor):
    owner, partner = [(jnp.arange(entries.shape[axis_at]) // (entries.shape[axis_at] // blocks)).reshape([-1 if axis == axis_at else 1 for axis in range(entries.ndim)]) for axis_at in (source, target)]
    chosen = jax.random.permutation(key, blocks)[partner]
    strong = (owner == chosen) | (owner == (partner + blocks // 2) % blocks)
    return jnp.where(strong, factor * entries, entries)


def block_levels(stream_key, dims, cuts, smallest, top_value):
    gain = 1.0
    for dim, shards_of in cuts:
        heights = jax.random.uniform(jax.random.fold_in(jax.random.fold_in(stream_key, 6), dim), (shards_of,), jnp.float32, smallest / len(cuts), top_value / len(cuts))
        gain = gain * jnp.repeat(jnp.exp(heights), dims[dim] // shards_of).reshape((-1,) + (1,) * (len(dims) - 1 - dim))
    return gain


def normal_values(key, shape, spread, reach, shards=(), held_as=jnp.bfloat16):
    result = jax.random.normal(key, shape, jnp.float32) * spread
    if len(shards) > 0:
        result = block_levels(key, shape, shards, -0.22, 0.18) * result
    return jnp.clip(result, min=-reach, max=reach).astype(held_as)


def bell_draw_with(key, shape, spread, limit, split, heavy, held_as=jnp.bfloat16):
    drawn = spread * jax.random.normal(key, shape, jnp.float32)
    if split:
        drawn = drawn * block_levels(key, shape, split, -0.22, 0.18)
    return jnp.clip(strengthened(drawn, jax.random.fold_in(key, 3), *heavy), -limit, limit).astype(held_as)


def setup_inputs(seed: int = 0) -> dict:
    streams_of = jax.random.split(jax.random.key(seed), 22)
    return {
        "text_states": bell_draw_with(streams_of[0], (PAIRS * LMAX, D_T), 1.0, 6.0, ((0, 32),), (0, 1, 32, 2.75)),
        "image_states": bell_draw_with(streams_of[1], (PAIRS * REGIONS, D_I), 1.0, 6.0, ((0, 32),), (0, 1, 32, 2.75)),
        "caption_lengths": draw_caption_lengths(jax.random.fold_in(streams_of[21], 71), 0),
        "text_query": normal_values(streams_of[3], (D_T, D_C), D_T ** -0.5, 0.21875),
        "text_keyval": normal_values(streams_of[4], (D_T, 2 * D_C), D_T ** -0.5, 0.21875),
        "text_attend": normal_values(streams_of[5], (D_C, D_T), (D_C // 16) ** -0.5, 0.75),
        "text_up": normal_values(streams_of[6], (D_T, FF_T), D_T ** -0.5, 0.21875),
        "text_down": normal_values(streams_of[7], (FF_T, D_T), FF_T ** -0.5, 0.109375),
        "text_qkv": normal_values(streams_of[8], (D_T, 3 * D_T), D_T ** -0.5, 0.21875),
        "text_output": normal_values(streams_of[9], (D_T, D_T), (D_T // 16) ** -0.5, 0.875),
        "text_gains": jnp.clip(1.0 + 0.1 * jax.random.normal(streams_of[10], (3, D_T), jnp.float32), 0.5, 1.5),
        "image_query": normal_values(streams_of[11], (D_I, D_C), D_I ** -0.5, 0.1875),
        "image_keyval": normal_values(streams_of[12], (D_I, 2 * D_C), D_I ** -0.5, 0.1875),
        "image_attend": normal_values(streams_of[13], (D_C, D_I), (D_C // 16) ** -0.5, 0.75),
        "image_up": normal_values(streams_of[14], (D_I, FF_I), D_I ** -0.5, 0.1875),
        "image_down": normal_values(streams_of[15], (FF_I, D_I), FF_I ** -0.5, 0.1875),
        "image_qkv": normal_values(streams_of[16], (D_I, 3 * D_I), D_I ** -0.5, 0.1875),
        "image_output": normal_values(streams_of[17], (D_I, D_I), (D_I // 16) ** -0.5, 0.75),
        "image_gains": jnp.clip(1.0 + 0.1 * jax.random.normal(streams_of[18], (3, D_I), jnp.float32), 0.5, 1.5),
        "text_cotangent": normal_values(streams_of[19], (PAIRS * LMAX, D_T), 1.0, 6.0, ((0, 32),)),
        "image_cotangent": normal_values(streams_of[20], (PAIRS * REGIONS, D_I), 1.0, 6.0, ((0, 32),)),
    }


@jax.custom_vjp
def low(v):
    return lax.optimization_barrier(v.astype(jnp.bfloat16)).astype(jnp.float32)

@jax.custom_vjp
def low_back(v):
    return v

def low_keep(v):
    return (low(v), None)

def low_pass(kept, grad):
    return (grad,)

def back_keep(v):
    return (v, None)

def back_low(kept, grad):
    return (low(grad),)
low.defvjp(low_keep, low_pass)
low_back.defvjp(back_keep, back_low)
masked_score = -1e+30

def layer_norm(tensor, gain_row):
    centred = tensor - lax.optimization_barrier(jnp.mean(tensor, axis=-1, keepdims=True))
    inverse = lax.rsqrt(lax.optimization_barrier(jnp.mean(centred * centred, axis=-1, keepdims=True)) + 1e-05)
    return centred * inverse * gain_row

def gelu_exact(tensor):
    return jax.nn.gelu(tensor, approximate=False)

def product(left_side, right_side):
    return jnp.dot(left_side, right_side, precision=lax.Precision.HIGHEST)

def attend(queries, keyvalues, keymask, scaling):
    scores = low_back(scaling * jnp.einsum('bqhd,bkhd->bhqk', queries, keyvalues[:, :, 0], precision=lax.Precision.HIGHEST))
    if keymask is not None:
        scores = jnp.where(keymask[:, None, None, :], scores, masked_score)
    weights = low(jax.nn.softmax(scores, axis=-1))
    context = jnp.einsum('bhqk,bkhd->bqhd', weights, keyvalues[:, :, 1], precision=lax.Precision.HIGHEST)
    return low(low_back(context.reshape(context.shape[0] * context.shape[1], -1)))

def stream_rest(states, context, weights, gain_rows, head_count, seq_len, keymask):
    attend_proj, up_proj, down_proj, qkv_proj, output_proj = weights
    num_rows, model_width = states.shape
    head_size = model_width // head_count
    before = states + low_back(product(context, attend_proj))
    first_norm = layer_norm(before, gain_rows[0])
    hidden_pre = low_back(product(low(first_norm), up_proj))
    middle = first_norm + low_back(product(low(gelu_exact(hidden_pre)), down_proj))
    second_norm = layer_norm(middle, gain_rows[1])
    packed = low(low_back(product(low(second_norm), qkv_proj)))
    packed = packed.reshape(num_rows // seq_len, seq_len, 3, head_count, head_size)
    attended = attend(packed[:, :, 0], packed[:, :, 1:], keymask, head_size ** (-0.5))
    closing = second_norm + low_back(product(attended, output_proj))
    return layer_norm(closing, gain_rows[2])

def layer(weights, text_rows, image_rows, lengths):
    tq, tkv, tat, tup, tdn, tqkv, tout, tgain, iq, ikv, iat, iup, idn, iqkv, iout, igain = weights
    pair_count = lengths.shape[0]
    text_len = text_rows.shape[0] // pair_count
    region_count = image_rows.shape[0] // pair_count
    co_size = D_C // H_C
    valid = jnp.arange(text_len, dtype=jnp.int32)[None, :] < lengths[:, None]
    text_queries = low(low_back(product(text_rows, tq))).reshape(pair_count, text_len, H_C, co_size)
    text_kv = low(low_back(product(text_rows, tkv))).reshape(pair_count, text_len, 2, H_C, co_size)
    image_queries = low(low_back(product(image_rows, iq))).reshape(pair_count, region_count, H_C, co_size)
    image_kv = low(low_back(product(image_rows, ikv))).reshape(pair_count, region_count, 2, H_C, co_size)
    text_context = attend(text_queries, image_kv, None, co_size ** (-0.5))
    image_context = attend(image_queries, text_kv, valid, co_size ** (-0.5))
    text_out = stream_rest(text_rows, text_context, (tat, tup, tdn, tqkv, tout), tgain, H_T, text_len, valid)
    text_out = text_out * valid.reshape(-1, 1)
    image_out = stream_rest(image_rows, image_context, (iat, iup, idn, iqkv, iout), igain, H_I, region_count, None)
    return (text_out, image_out)

def reference(text_states, image_states, caption_lengths, text_query, text_keyval, text_attend, text_up, text_down, text_qkv, text_output, text_gains, image_query, image_keyval, image_attend, image_up, image_down, image_qkv, image_output, image_gains, text_cotangent, image_cotangent):
    weights = tuple((member.astype(jnp.float32) for member in (text_query, text_keyval, text_attend, text_up, text_down, text_qkv, text_output, text_gains, image_query, image_keyval, image_attend, image_up, image_down, image_qkv, image_output, image_gains)))
    offset = PAIRS // 2 * REGIONS
    text_full = text_states.astype(jnp.float32)
    image_full = jnp.roll(image_states.astype(jnp.float32), offset, axis=0)
    per_group = 32
    groups = PAIRS // per_group

    def forward(weight_set, text_in, image_in):

        def one_group(member):
            return layer(weight_set, member[0], member[1], member[2])
        outs = lax.map(jax.checkpoint(one_group), (text_in.reshape(groups, per_group * LMAX, D_T), image_in.reshape(groups, per_group * REGIONS, D_I), caption_lengths.reshape(groups, per_group)))
        return (outs[0].reshape(PAIRS * LMAX, D_T), outs[1].reshape(PAIRS * REGIONS, D_I))
    (text_out, image_out), pull_back = jax.vjp(forward, weights, text_full, image_full)
    grad_weights, grad_text, grad_image = pull_back((text_cotangent.astype(jnp.float32), jnp.roll(image_cotangent.astype(jnp.float32), offset, axis=0)))
    text_flat = jnp.concatenate([grad_weights[member].reshape(-1) for member in range(7)])
    image_flat = jnp.concatenate([grad_weights[member].reshape(-1) for member in range(8, 15)])
    return (text_out.astype(jnp.bfloat16), jnp.roll(image_out, offset, axis=0).astype(jnp.bfloat16), grad_text.astype(jnp.bfloat16), jnp.roll(grad_image, offset, axis=0).astype(jnp.bfloat16), text_flat, image_flat, grad_weights[7], grad_weights[15])
```

```python
import functools

import jax
import jax.numpy as jnp
from jax import lax
from jax.experimental import pallas as pl
from jax.experimental.pallas import tpu as pltpu
from jax.sharding import PartitionSpec as P

H_T = 12
H_I = 8
H_C = 8
D_C = 1024
LANES = 128
UNIT = 256
masked_score = -1e30
F32 = jnp.float32
BF16 = jnp.bfloat16


def mm(a, b):
    return jnp.dot(a, b, preferred_element_type=F32)


def mm_nt(a, b):
    return lax.dot_general(a, b, (((1,), (1,)), ((), ())), preferred_element_type=F32)


def mm_tn(a, b):
    return lax.dot_general(a, b, (((0,), (0,)), ((), ())), preferred_element_type=F32)


def cost(flops, nbytes, trans=0):
    return pl.CostEstimate(
        flops=int(flops), bytes_accessed=int(nbytes), transcendentals=int(trans)
    )


def key_masks(lens_ref, pairs, rows, keys, fixed):
    columns = lax.broadcasted_iota(jnp.int32, (rows, keys), 1)
    if fixed is not None:
        same = columns < fixed
        return [same] * pairs
    return [columns < lens_ref[p] for p in range(pairs)]


def lane_masks(rows, heads_in):
    if heads_in == 1:
        return [None]
    lanes = lax.broadcasted_iota(jnp.int32, (rows, LANES), 1)
    return [lanes < LANES // 2, lanes >= LANES // 2]


def only(block, mask):
    if mask is None:
        return block
    return jnp.where(mask, block, jnp.zeros_like(block))


def joined(blocks, masks):
    if len(blocks) == 1:
        return blocks[0]
    return jnp.where(masks[0], blocks[0], blocks[1])


def softmax_rows(scores):
    highest = jnp.max(scores, axis=-1, keepdims=True)
    raised = jnp.exp(scores - highest)
    return raised * (1.0 / jnp.sum(raised, axis=-1, keepdims=True))


def attend_kernel(lens_ref, q_ref, k_ref, v_ref, o_ref, *, pairs, heads_in, fixed, scaling):
    ql = q_ref.shape[0] // pairs
    kl = k_ref.shape[0] // pairs
    masks = key_masks(lens_ref, pairs, ql, kl, fixed)
    lanes = lane_masks(ql, heads_in)
    for p in range(pairs):
        q = q_ref[p * ql : (p + 1) * ql, :]
        k = k_ref[p * kl : (p + 1) * kl, :]
        v = v_ref[p * kl : (p + 1) * kl, :]
        parts = []
        for lane in lanes:
            s = jnp.where(masks[p], mm_nt(only(q, lane), k) * scaling, masked_score)
            parts.append(mm(softmax_rows(s).astype(BF16), v))
        o_ref[p * ql : (p + 1) * ql, :] = joined(parts, lanes).astype(BF16)


def attend(lens, q, k, v, cols, pairs, blocks, heads_in, fixed, scaling):
    rows = q.shape[0]
    krows = k.shape[0]

    def spec(count, start):
        return pl.BlockSpec((count, LANES), lambda j, start=start: (0, start + j))

    return pl.pallas_call(
        functools.partial(
            attend_kernel, pairs=pairs, heads_in=heads_in, fixed=fixed, scaling=scaling
        ),
        grid=(blocks,),
        in_specs=[
            pl.BlockSpec(memory_space=pltpu.SMEM),
            spec(rows, cols[0]),
            spec(krows, cols[1]),
            spec(krows, cols[2]),
        ],
        out_specs=spec(rows, 0),
        out_shape=jax.ShapeDtypeStruct((rows, blocks * LANES), BF16),
        cost_estimate=cost(
            4 * blocks * heads_in * rows * krows // pairs * LANES,
            4 * blocks * LANES * (rows + krows),
            blocks * heads_in * rows * krows // pairs,
        ),
        name="attend",
    )(lens, q, k, v)


def attend_back_kernel(
    lens_ref, q_ref, k_ref, v_ref, g_ref, *rest, pairs, heads_in, fixed, scaling, packed
):
    if packed:
        out_ref, dk_ref, dv_ref = rest
        dq_ref, dk_out = out_ref, dk_ref
    else:
        dq_ref, out_ref, dv_ref = rest
        dk_out = out_ref
    step = pl.program_id(1)
    ql = q_ref.shape[0] // pairs
    kl = k_ref.shape[0] // pairs

    @pl.when(step == 0)
    def _():
        masks = key_masks(lens_ref, pairs, ql, kl, fixed)
        qlanes = lane_masks(ql, heads_in)
        klanes = lane_masks(kl, heads_in)
        for p in range(pairs):
            qs = slice(p * ql, (p + 1) * ql)
            ks = slice(p * kl, (p + 1) * kl)
            q, g = q_ref[qs, :], g_ref[qs, :]
            k, v = k_ref[ks, :], v_ref[ks, :]
            dq, dk, dv = [], [], []
            for lane in qlanes:
                s = jnp.where(masks[p], mm_nt(only(q, lane), k) * scaling, masked_score)
                w = softmax_rows(s)
                dv.append(mm_tn(w.astype(BF16), g))
                dp = mm_nt(only(g, lane), v)
                inner = jnp.sum(w * dp, axis=-1, keepdims=True)
                ds = (w * (dp - inner)).astype(BF16)
                dq.append(mm(ds, k))
                dk.append(mm_tn(ds, q))
            dq_ref[qs, :] = (joined(dq, qlanes) * scaling).astype(BF16)
            dk_out[ks, :] = (joined(dk, klanes) * scaling).astype(BF16)
            dv_ref[ks, :] = joined(dv, klanes).astype(BF16)

    if packed:

        @pl.when(step == 1)
        def _():
            out_ref[...] = dk_ref[...]

        @pl.when(step == 2)
        def _():
            out_ref[...] = dv_ref[...]
    else:

        @pl.when(step == 1)
        def _():
            out_ref[...] = dv_ref[...]


def attend_back(lens, q, k, v, g, cols, pairs, blocks, heads_in, fixed, scaling, packed):
    rows = q.shape[0]
    krows = k.shape[0]

    def spec(count, start):
        return pl.BlockSpec((count, LANES), lambda j, t, start=start: (0, start + j))

    if packed:
        steps = 3
        out_specs = pl.BlockSpec((rows, LANES), lambda j, t: (0, t * blocks + j))
        out_shape = jax.ShapeDtypeStruct((rows, 3 * blocks * LANES), BF16)
        scratch = [pltpu.VMEM((krows, LANES), BF16)] * 2
    else:
        steps = 2
        out_specs = [
            spec(rows, 0),
            pl.BlockSpec((krows, LANES), lambda j, t: (0, t * blocks + j)),
        ]
        out_shape = [
            jax.ShapeDtypeStruct((rows, blocks * LANES), BF16),
            jax.ShapeDtypeStruct((krows, 2 * blocks * LANES), BF16),
        ]
        scratch = [pltpu.VMEM((krows, LANES), BF16)]
    return pl.pallas_call(
        functools.partial(
            attend_back_kernel,
            pairs=pairs,
            heads_in=heads_in,
            fixed=fixed,
            scaling=scaling,
            packed=packed,
        ),
        grid=(blocks, steps),
        in_specs=[
            pl.BlockSpec(memory_space=pltpu.SMEM),
            spec(rows, cols[0]),
            spec(krows, cols[1]),
            spec(krows, cols[2]),
            spec(rows, 0),
        ],
        out_specs=out_specs,
        out_shape=out_shape,
        scratch_shapes=scratch,
        cost_estimate=cost(
            10 * blocks * heads_in * rows * krows // pairs * LANES,
            8 * blocks * LANES * (rows + krows),
            blocks * heads_in * rows * krows // pairs,
        ),
        name="attend_back",
    )(lens, q, k, v, g)


def flat_kernel(core_ref, a0_ref, a1_ref, b0_ref, b1_ref, *rest, columns):
    out_ref, stage_ref = rest[-2:]
    core = core_ref[0]
    count = columns // UNIT
    bm = a0_ref.shape[1]
    a0 = a0_ref[...].T
    a1 = a1_ref[...].T
    u = 0
    while u < count:
        width = 2 if u + 1 < count else 1
        picks = [
            pl.ds(pl.multiple_of((2 * (u + i) + core) * LANES, LANES), LANES)
            for i in range(width)
        ]
        b0 = [b0_ref[:, pick] for pick in picks]
        b1 = [b1_ref[:, pick] for pick in picks]
        if width == 2:
            b0, b1 = jnp.concatenate(b0, axis=1), jnp.concatenate(b1, axis=1)
        else:
            b0, b1 = b0[0], b1[0]
        total = mm(a0, b0) + mm(a1, b1)
        for i in range(width):
            stage_ref[pl.ds(u + i, bm, stride=count), :] = total[
                :, i * LANES : (i + 1) * LANES
            ]
        u += width
    out_ref[...] = stage_ref[...].astype(BF16)


def flat_grad(flat, total_rows, core, a, b, rows_from, rows_to, place, bm=128):
    a0, a1 = a
    b0, b1 = b
    depth = a0.shape[0]
    columns = b0.shape[1]
    count = columns // UNIT
    out_rows = bm * count
    first = rows_from // bm
    steps = (rows_to - rows_from) // bm

    in_specs = [
        pl.BlockSpec(memory_space=pltpu.SMEM),
        pl.BlockSpec((depth, bm), lambda i: (0, first + i)),
        pl.BlockSpec((depth, bm), lambda i: (0, first + i)),
        pl.BlockSpec((depth, columns), lambda i: (0, 0)),
        pl.BlockSpec((depth, columns), lambda i: (0, 0)),
    ]
    operands = [core, a0, a1, b0, b1]
    aliases = {}
    if flat is not None:
        in_specs.append(pl.BlockSpec(memory_space=pl.ANY))
        operands.append(flat)
        aliases = {5: 0}
    return pl.pallas_call(
        functools.partial(flat_kernel, columns=columns),
        grid=(steps,),
        in_specs=in_specs,
        out_specs=pl.BlockSpec(
            (pl.Element(out_rows), pl.Element(LANES)),
            lambda i: (pl.multiple_of(place + i * out_rows, LANES), 0),
        ),
        out_shape=jax.ShapeDtypeStruct((total_rows, LANES), BF16),
        scratch_shapes=[pltpu.VMEM((out_rows, LANES), F32)],
        input_output_aliases=aliases,
        compiler_params=pltpu.CompilerParams(vmem_limit_bytes=40 * 1024 * 1024),
        cost_estimate=cost(
            2 * 2 * depth * (rows_to - rows_from) * columns // 2,
            4 * depth * (rows_to - rows_from + columns) + 2 * steps * out_rows * LANES,
        ),
        name="flat_grad",
    )(*operands)


def flat_half(core, total_rows, work):
    flat = None
    place = 0
    for a, b, low, high in work:
        flat = flat_grad(flat, total_rows, core, a, b, low, high, place)
        place += (high - low) * b[0].shape[1] // UNIT
    return flat


def dp_swap(block, bit):
    count = lax.axis_size("dp")
    return lax.ppermute(block, "dp", [(i, i ^ bit) for i in range(count)])


def stream_swap(block):
    return lax.ppermute(block, "stream", [(0, 1), (1, 0)])


def pick(block, index, axis=0):
    return lax.dynamic_index_in_dim(block, index, axis, keepdims=False)


def plus(a, b):
    return (a.astype(F32) + b.astype(F32)).astype(BF16)


def line_step(block, step, span, toward):
    count = lax.axis_size("dp")
    route = []
    for i in range(count):
        at = (i >> 2) % span
        if toward > 0 and at <= step and at + 1 < span:
            route.append((i, i + 4))
        if toward < 0 and span - 1 - at <= step and at > 0:
            route.append((i, i - 4))
    return lax.ppermute(block, "dp", route)


def reduce_scatter(flat):
    count = lax.axis_size("dp")
    me = lax.axis_index("dp")
    span = count // 4
    rows = flat.shape[0] // (2 * span)
    y = (me >> 1) & 1
    blocks = flat.reshape(span, 2, rows, LANES)
    total = plus(pick(blocks, y, 1), dp_swap(pick(blocks, 1 - y, 1), 2))
    while span > 4:
        half = span // 2
        upper = (me >> 2) // half % 2
        halves = total.reshape(2, half, rows, LANES)
        total = plus(pick(halves, upper), dp_swap(pick(halves, 1 - upper), 4 * half))
        span = half
    at = (me >> 2) % span
    up = down = None
    for step in range(span - 1):
        to_up = pick(total, jnp.clip(span - 1 - step + at, 0, span - 1))
        to_down = pick(total, jnp.clip(step - (span - 1) + at, 0, span - 1))
        up = line_step(to_up if up is None else plus(to_up, up), step, span, 1)
        down = line_step(to_down if down is None else plus(to_down, down), step, span, -1)
    result = pick(total, at).astype(F32)
    if up is not None:
        result = result + up.astype(F32) + down.astype(F32)
    return result


def share_of(result):
    core = lax.axis_index("dp") & 1
    halves = result.reshape(2, result.shape[0] // 2, LANES)
    mine = pick(halves, core)
    far = dp_swap(pick(halves, 1 - core), 1)
    first = jnp.where(core == 0, mine, far)
    second = jnp.where(core == 0, far, mine)
    return jnp.stack([first, second], axis=1).reshape(-1)


def normed(tensor):
    centred = tensor - jnp.mean(tensor, axis=-1, keepdims=True)
    inverse = lax.rsqrt(jnp.mean(centred * centred, axis=-1, keepdims=True) + 1e-05)
    return centred * inverse, inverse


def normed_back(grad, n, inverse, gain_row):
    scaled = grad * gain_row
    low = jnp.mean(scaled, axis=-1, keepdims=True)
    tilt = jnp.mean(scaled * n, axis=-1, keepdims=True)
    return (scaled - low - n * tilt) * inverse, jnp.sum(grad * n, axis=0)


def gelu_and_slope(u):
    share = 0.5 * (1.0 + lax.erf(u * 0.7071067811865476))
    slope = share + u * (0.3989422804014327 * jnp.exp(-0.5 * u * u))
    return (u * share).astype(BF16), slope


def stream_layer(states, context, cot, lens, weights, gains, heads, fixed, pairs):
    attend_w, up_w, down_w, qkv_w, output_w = weights
    width = states.shape[1]
    size = width // heads
    heads_in = LANES // size
    blocks = width // LANES
    scaling = size ** (-0.5)
    n1, inv1 = normed(states.astype(F32) + mm(context, attend_w))
    h1 = n1 * gains[0]
    h1_low = h1.astype(BF16)
    hidden_low, slope = gelu_and_slope(mm(h1_low, up_w))
    n2, inv2 = normed(h1 + mm(hidden_low, down_w))
    h2 = n2 * gains[1]
    h2_low = h2.astype(BF16)
    packed = mm(h2_low, qkv_w).astype(BF16)
    cols = (0, blocks, 2 * blocks)
    z = attend(lens, packed, packed, packed, cols, pairs, blocks, heads_in, fixed, scaling)
    n3, inv3 = normed(h2 + mm(z, output_w))
    result = n3 * gains[2]
    de, dg2 = normed_back(cot, n3, inv3, gains[2])
    de_low = de.astype(BF16)
    dz = mm_nt(de_low, output_w).astype(BF16)
    dr = attend_back(
        lens, packed, packed, packed, dz, cols, pairs, blocks, heads_in, fixed, scaling, True
    )
    dh2 = de + mm_nt(dr, qkv_w)
    db, dg1 = normed_back(dh2, n2, inv2, gains[1])
    db_low = db.astype(BF16)
    du = (mm_nt(db_low, down_w) * slope).astype(BF16)
    dh1 = db + mm_nt(du, up_w)
    da, dg0 = normed_back(dh1, n1, inv1, gains[0])
    da_low = da.astype(BF16)
    dc = mm_nt(da_low, attend_w).astype(BF16)
    sides = {
        "attend": (context, da_low),
        "up": (h1_low, du),
        "down": (hidden_low, db_low),
        "qkv": (h2_low, dr),
        "output": (z, de_low),
    }
    return result, da, dc, sides, jnp.stack((dg0, dg1, dg2))


def with_far(sides):
    near, far = {}, {}
    for name, (a, b) in sides.items():
        near[name] = (a, b)
        far[name] = (dp_swap(a, 1), dp_swap(b, 1))
    return {
        name: ((near[name][0], far[name][0]), (near[name][1], far[name][1])) for name in sides
    }


def local(
    text_states,
    image_states,
    caption_lengths,
    text_query,
    text_keyval,
    text_attend,
    text_up,
    text_down,
    text_qkv,
    text_output,
    text_gains,
    image_query,
    image_keyval,
    image_attend,
    image_up,
    image_down,
    image_qkv,
    image_output,
    image_gains,
    text_cotangent,
    image_cotangent,
):
    own_pairs = caption_lengths.shape[0]
    own_text = text_states.shape[0]
    text_len = own_text // own_pairs
    regions = image_states.shape[0] // own_pairs
    padded = -(-regions // 16) * 16
    own_image = own_pairs * padded
    pairs = 2 * own_pairs
    d_i = image_states.shape[1]
    stream = lax.axis_index("stream")
    core = (lax.axis_index("dp") & 1).astype(jnp.int32).reshape(1)

    def padded_rows(block):
        block = block.reshape(own_pairs, regions, d_i)
        return jnp.pad(block, ((0, 0), (0, padded - regions), (0, 0))).reshape(own_image, d_i)

    def trimmed(block):
        return block.reshape(own_pairs, padded, d_i)[:, :regions].reshape(-1, d_i)

    image_near = padded_rows(image_states)
    image_cot_near = padded_rows(image_cotangent)
    image_all = jnp.concatenate([stream_swap(image_near), image_near])
    text_all = jnp.concatenate([text_states, stream_swap(text_states)])
    lens = jnp.concatenate([caption_lengths, stream_swap(caption_lengths)])
    image_cot = jnp.concatenate([stream_swap(image_cot_near), image_cot_near])
    text_cot = jnp.concatenate([text_cotangent, stream_swap(text_cotangent)])

    positions = lax.broadcasted_iota(jnp.int32, (pairs, text_len), 1)
    valid = (positions < lens[:, None]).reshape(pairs * text_len, 1).astype(F32)

    co_blocks = D_C // LANES
    co_scale = (D_C // H_C) ** (-0.5)

    text_kv = mm(text_all, text_keyval).astype(BF16)
    image_q = mm(image_all, image_query).astype(BF16)
    ci = attend(lens, image_q, text_kv, text_kv, (0, 0, co_blocks), pairs, co_blocks, 1, None, co_scale)
    image_out, image_da, image_dc, image_sides, image_dg = stream_layer(
        image_all,
        ci,
        image_cot.astype(F32),
        lens,
        (image_attend, image_up, image_down, image_qkv, image_output),
        image_gains,
        H_I,
        regions,
        pairs,
    )
    image_dq, text_dkv = attend_back(
        lens, image_q, text_kv, text_kv, image_dc, (0, 0, co_blocks), pairs, co_blocks, 1, None, co_scale, False
    )

    image_kv = mm(image_all, image_keyval).astype(BF16)
    text_q = mm(text_all, text_query).astype(BF16)
    ct = attend(lens, text_q, image_kv, image_kv, (0, 0, co_blocks), pairs, co_blocks, 1, regions, co_scale)
    text_out, text_da, text_dc, text_sides, text_dg = stream_layer(
        text_all,
        ct,
        text_cot.astype(F32) * valid,
        lens,
        (text_attend, text_up, text_down, text_qkv, text_output),
        text_gains,
        H_T,
        None,
        pairs,
    )
    text_dq, image_dkv = attend_back(
        lens, text_q, image_kv, image_kv, text_dc, (0, 0, co_blocks), pairs, co_blocks, 1, regions, co_scale, False
    )

    text_result = (text_out[:own_text] * valid[:own_text]).astype(BF16)
    image_result = trimmed(image_out[own_image:].astype(BF16))
    text_grad = (
        text_da[:own_text]
        + mm_nt(text_dq[:own_text], text_query)
        + mm_nt(text_dkv[:own_text], text_keyval)
    ).astype(BF16)
    image_grad = trimmed(
        (
            image_da[own_image:]
            + mm_nt(image_dq[own_image:], image_query)
            + mm_nt(image_dkv[own_image:], image_keyval)
        ).astype(BF16)
    )

    image_sides["query"] = (image_all, image_dq)
    image_sides["keyval"] = (image_all, image_dkv)
    text_sides["query"] = (text_all, text_dq)
    text_sides["keyval"] = (text_all, text_dkv)

    def halves(sides, width):
        both = with_far(sides)
        total = sum(a[0].shape[1] * b[0].shape[1] for a, b in both.values())
        total_rows = total // (2 * UNIT)
        names = ("query", "keyval", "attend", "up", "down", "qkv", "output")
        first, second, filled = [], [], 0
        for name in names:
            a, b = both[name]
            m, n = a[0].shape[1], b[0].shape[1]
            room = min(max((total // 2 - filled) // n, 0), m)
            if room:
                first.append((a, b, 0, room))
            if room < m:
                second.append((a, b, room, m))
            filled += m * n
        return lax.cond(
            stream == 0,
            lambda: flat_half(core, total_rows, first),
            lambda: flat_half(core, total_rows, second),
        )

    image_share = share_of(reduce_scatter(halves(image_sides, d_i)))
    text_share = share_of(reduce_scatter(halves(text_sides, text_states.shape[1])))
    text_gain_sum, image_gain_sum = lax.psum((text_dg, image_dg), "dp")
    return (
        text_result,
        image_result,
        text_grad,
        image_grad,
        text_share,
        image_share,
        text_gain_sum,
        image_gain_sum,
    )


def solution(mesh):
    split = P(("stream", "dp"), None)
    flat = P(("stream", "dp"))
    whole = P()
    return jax.shard_map(
        local,
        mesh=mesh,
        in_specs=(split, split, flat) + (whole,) * 16 + (split, split),
        out_specs=(split, split, split, split, flat, flat, whole, whole),
        check_vma=False,
    )
```

```python
import functools

import jax
import jax.numpy as jnp
from jax import lax
from jax.experimental import pallas as pl
from jax.experimental.pallas import tpu as pltpu
from jax.sharding import PartitionSpec as P

H_T = 12
H_I = 8
H_C = 8
D_C = 1024
LANES = 128
UNIT = 256
masked_score = -1e30
F32 = jnp.float32
BF16 = jnp.bfloat16


def mm(a, b):
    return jnp.dot(a, b, preferred_element_type=F32)


def mm_nt(a, b):
    return lax.dot_general(a, b, (((1,), (1,)), ((), ())), preferred_element_type=F32)


def mm_tn(a, b):
    return lax.dot_general(a, b, (((0,), (0,)), ((), ())), preferred_element_type=F32)


def cost(flops, nbytes, trans=0):
    return pl.CostEstimate(
        flops=int(flops), bytes_accessed=int(nbytes), transcendentals=int(trans)
    )


def lane_block(ref, rows, block):
    return ref[rows, pl.ds(pl.multiple_of(block * LANES, LANES), LANES)]


def put_block(ref, rows, block, value):
    ref[rows, pl.ds(pl.multiple_of(block * LANES, LANES), LANES)] = value


def split_heads(block, heads_in):
    if heads_in == 1:
        return block
    lanes = lax.broadcasted_iota(jnp.int32, block.shape, 1)
    zero = jnp.zeros_like(block)
    low = lanes < LANES // 2
    return jnp.concatenate([jnp.where(low, block, zero), jnp.where(low, zero, block)], axis=0)


def side_by_side(block, heads_in):
    if heads_in == 1:
        return block
    rows = block.shape[0] // 2
    return jnp.concatenate([block[:rows], block[rows:]], axis=1)


def attend_kernel(
    lens_ref, q_ref, k_ref, v_ref, o_ref, *, pairs, blocks, cols, heads_in, fixed, scaling
):
    ql = q_ref.shape[0] // pairs
    kl = k_ref.shape[0] // pairs
    chain = heads_in * ql
    keys = lax.broadcasted_iota(jnp.int32, (chain, kl), 1)
    if fixed is None:
        masks = [keys < lens_ref[p] for p in range(pairs)]
    else:
        masks = [keys < fixed] * pairs

    @pl.loop(0, blocks)
    def _(j):
        scores = []
        for p in range(pairs):
            q = split_heads(lane_block(q_ref, slice(p * ql, (p + 1) * ql), cols[0] + j), heads_in)
            k = lane_block(k_ref, slice(p * kl, (p + 1) * kl), cols[1] + j)
            scores.append(jnp.where(masks[p], mm_nt(q, k) * scaling, masked_score))
        s = jnp.concatenate(scores, axis=0)
        raised = jnp.exp(s - jnp.max(s, axis=-1, keepdims=True))
        w = (raised * (1.0 / jnp.sum(raised, axis=-1, keepdims=True))).astype(BF16)
        for p in range(pairs):
            v = split_heads(lane_block(v_ref, slice(p * kl, (p + 1) * kl), cols[2] + j), heads_in)
            o = mm(side_by_side(w[p * chain : (p + 1) * chain], heads_in), v)
            put_block(o_ref, slice(p * ql, (p + 1) * ql), j, o.astype(BF16))


def attend(lens, q, k, v, cols, pairs, blocks, heads_in, fixed, scaling):
    rows = q.shape[0]
    krows = k.shape[0]
    same = k is v
    vmem = pl.BlockSpec(memory_space=pltpu.VMEM)
    operands = [lens, q, k] if same else [lens, q, k, v]
    if q is k:
        operands = [lens, q]

    def body(lens_ref, *refs, **kw):
        refs = list(refs)
        o_ref = refs.pop()
        while len(refs) < 3:
            refs.append(refs[-1])
        attend_kernel(lens_ref, *refs, o_ref, **kw)

    return pl.pallas_call(
        functools.partial(
            body,
            pairs=pairs,
            blocks=blocks,
            cols=cols,
            heads_in=heads_in,
            fixed=fixed,
            scaling=scaling,
        ),
        in_specs=[pl.BlockSpec(memory_space=pltpu.SMEM)] + [vmem] * (len(operands) - 1),
        out_specs=vmem,
        out_shape=jax.ShapeDtypeStruct((rows, blocks * LANES), BF16),
        compiler_params=pltpu.CompilerParams(vmem_limit_bytes=24 * 1024 * 1024),
        cost_estimate=cost(
            16 * blocks * heads_in * rows * krows // pairs * LANES,
            4 * blocks * LANES * (rows + krows),
            blocks * heads_in * rows * krows // pairs,
        ),
        name="attend",
    )(*operands)


def attend_back_kernel(
    lens_ref,
    q_ref,
    k_ref,
    v_ref,
    g_ref,
    dq_ref,
    dk_ref,
    dv_ref,
    *,
    pairs,
    blocks,
    cols,
    out_cols,
    heads_in,
    fixed,
    scaling,
):
    ql = q_ref.shape[0] // pairs
    kl = k_ref.shape[0] // pairs
    keys = lax.broadcasted_iota(jnp.int32, (heads_in * kl, ql), 0)
    if heads_in == 2:
        keys = jnp.where(keys >= kl, keys - kl, keys)
    if fixed is None:
        masks = [keys < lens_ref[p] for p in range(pairs)]
    else:
        masks = [keys < fixed] * pairs

    @pl.loop(0, blocks)
    def _(j):
        scores, slopes = [], []
        for p in range(pairs):
            qs, ks = slice(p * ql, (p + 1) * ql), slice(p * kl, (p + 1) * kl)
            q, g = lane_block(q_ref, qs, cols[0] + j), lane_block(g_ref, qs, j)
            k = split_heads(lane_block(k_ref, ks, cols[1] + j), heads_in)
            v = split_heads(lane_block(v_ref, ks, cols[2] + j), heads_in)
            scores.append(jnp.where(masks[p], mm_nt(k, q) * scaling, masked_score))
            slopes.append(mm_nt(v, g))
        stacked = (pairs * heads_in, kl, ql)
        s = jnp.concatenate(scores, axis=0).reshape(stacked)
        dp = jnp.concatenate(slopes, axis=0).reshape(stacked)
        raised = jnp.exp(s - jnp.max(s, axis=1, keepdims=True))
        w = raised * (1.0 / jnp.sum(raised, axis=1, keepdims=True))
        inner = jnp.sum(w * dp, axis=1, keepdims=True)
        ds = (w * (dp - inner)).astype(BF16).reshape(-1, ql)
        w = w.astype(BF16).reshape(-1, ql)
        chain = heads_in * kl
        for p in range(pairs):
            qs, ks = slice(p * ql, (p + 1) * ql), slice(p * kl, (p + 1) * kl)
            own = slice(p * chain, (p + 1) * chain)
            q = split_heads(lane_block(q_ref, qs, cols[0] + j), heads_in)
            g = split_heads(lane_block(g_ref, qs, j), heads_in)
            k = split_heads(lane_block(k_ref, ks, cols[1] + j), heads_in)
            dq = mm_tn(ds[own], k) * scaling
            dk = mm(side_by_side(ds[own], heads_in), q) * scaling
            dv = mm(side_by_side(w[own], heads_in), g)
            put_block(dq_ref, qs, out_cols[0] + j, dq.astype(BF16))
            put_block(dk_ref, ks, out_cols[1] + j, dk.astype(BF16))
            put_block(dv_ref, ks, out_cols[2] + j, dv.astype(BF16))


def attend_back(lens, q, k, v, g, cols, pairs, blocks, heads_in, fixed, scaling, packed):
    rows = q.shape[0]
    krows = k.shape[0]
    vmem = pl.BlockSpec(memory_space=pltpu.VMEM)
    width = blocks * LANES
    if packed:
        operands = [lens, q, g]
        out_cols = (0, blocks, 2 * blocks)
        out_shape = jax.ShapeDtypeStruct((rows, 3 * width), BF16)
        out_specs = vmem
    else:
        operands = [lens, q, k, g]
        out_cols = (0, 0, blocks)
        out_shape = [
            jax.ShapeDtypeStruct((rows, width), BF16),
            jax.ShapeDtypeStruct((krows, 2 * width), BF16),
        ]
        out_specs = [vmem, vmem]

    def body(lens_ref, *refs, **kw):
        if packed:
            q_ref, g_ref, out_ref = refs
            ins, outs = (q_ref, q_ref, q_ref, g_ref), (out_ref,) * 3
        else:
            q_ref, k_ref, g_ref, dq_ref, dkv_ref = refs
            ins, outs = (q_ref, k_ref, k_ref, g_ref), (dq_ref, dkv_ref, dkv_ref)
        attend_back_kernel(lens_ref, *ins, *outs, **kw)

    return pl.pallas_call(
        functools.partial(
            body,
            pairs=pairs,
            blocks=blocks,
            cols=cols,
            out_cols=out_cols,
            heads_in=heads_in,
            fixed=fixed,
            scaling=scaling,
        ),
        in_specs=[pl.BlockSpec(memory_space=pltpu.SMEM)] + [vmem] * (len(operands) - 1),
        out_specs=out_specs,
        out_shape=out_shape,
        compiler_params=pltpu.CompilerParams(vmem_limit_bytes=24 * 1024 * 1024),
        cost_estimate=cost(
            40 * blocks * heads_in * rows * krows // pairs * LANES,
            8 * blocks * LANES * (rows + krows),
            blocks * heads_in * rows * krows // pairs,
        ),
        name="attend_back",
    )(*operands)


def flat_kernel(
    side_ref, a0_ref, a1_ref, b0_ref, b1_ref, *rest, place, bm, low, units, quarter
):
    out_ref, stage_ref, low_ref, b_ref, sem = rest[-5:]
    core = side_ref[0]
    depth = a0_ref.shape[0]
    for u in range(units):
        at = 2 * u + core
        if quarter:
            at = 4 * u + 2 * side_ref[1] + core
        chosen = pl.ds(pl.multiple_of(at * LANES, LANES), LANES)
        b_ref[:depth, u * LANES : (u + 1) * LANES] = b0_ref[:, chosen]
        b_ref[depth:, u * LANES : (u + 1) * LANES] = b1_ref[:, chosen]
    rows = bm * units
    steps = (low[1] - low[0]) // bm

    def copy(i):
        return pltpu.make_async_copy(
            low_ref.at[i % 2], out_ref.at[pl.ds(place + i * rows, rows)], sem.at[i % 2]
        )

    for i in range(steps):
        columns = slice(low[0] + i * bm, low[0] + (i + 1) * bm)
        a = jnp.concatenate([a0_ref[:, columns], a1_ref[:, columns]], axis=0).T
        for u0 in range(0, units, 4):
            u1 = min(u0 + 4, units)
            total = mm(a, b_ref[:, u0 * LANES : u1 * LANES])
            for u in range(u0, u1):
                stage_ref[pl.ds(u, bm, stride=units), :] = total[
                    :, (u - u0) * LANES : (u - u0 + 1) * LANES
                ]
        if i >= 2:
            copy(i - 2).wait()
        low_ref[i % 2] = stage_ref[...].astype(BF16)
        copy(i).start()
    for i in range(max(steps - 2, 0), steps):
        copy(i).wait()


def flat_grad(flat, total_rows, side, a, b, low, high, place, quarter=False):
    a0, a1 = a
    b0, b1 = b
    depth = a0.shape[0]
    columns = b0.shape[1]
    units = columns // (2 * UNIT if quarter else UNIT)
    most = 512 if units <= 8 else 384
    bm = LANES
    for size in range(LANES, most + 1, LANES):
        if (high - low) % size == 0:
            bm = size
    out_rows = bm * units
    vmem = pl.BlockSpec(memory_space=pltpu.VMEM)
    in_specs = [pl.BlockSpec(memory_space=pltpu.SMEM)] + [vmem] * 4
    operands = [side, a0, a1, b0, b1]
    aliases = {}
    if flat is not None:
        in_specs.append(pl.BlockSpec(memory_space=pl.ANY))
        operands.append(flat)
        aliases = {5: 0}
    return pl.pallas_call(
        functools.partial(
            flat_kernel, place=place, bm=bm, low=(low, high), units=units, quarter=quarter
        ),
        in_specs=in_specs,
        out_specs=pl.BlockSpec(memory_space=pl.ANY),
        out_shape=jax.ShapeDtypeStruct((total_rows, LANES), BF16),
        scratch_shapes=[
            pltpu.VMEM((out_rows, LANES), F32),
            pltpu.VMEM((2, out_rows, LANES), BF16),
            pltpu.VMEM((2 * depth, units * LANES), BF16),
            pltpu.SemaphoreType.DMA((2,)),
        ],
        input_output_aliases=aliases,
        compiler_params=pltpu.CompilerParams(vmem_limit_bytes=24 * 1024 * 1024),
        cost_estimate=cost(
            4 * depth * (high - low) * units * LANES,
            4 * depth * (high - low + columns) + 2 * (high - low) * units * LANES,
        ),
        name="flat_grad",
    )(*operands)


def flat_half(side, total_rows, work):
    flat = None
    place = 0
    for a, b, low, high in work:
        if a is None:
            place += b
            continue
        flat = flat_grad(flat, total_rows, side, a, b, low, high, place)
        place += (high - low) * b[0].shape[1] // UNIT
    return flat


def dp_swap(block, bit):
    count = lax.axis_size("dp")
    return lax.ppermute(block, "dp", [(i, i ^ bit) for i in range(count)])


def stream_swap(block):
    return lax.ppermute(block, "stream", [(0, 1), (1, 0)])


def pick(block, index, axis=0):
    return lax.dynamic_index_in_dim(block, index, axis, keepdims=False)


def plus(a, b):
    return (a.astype(F32) + b.astype(F32)).astype(BF16)


def halved(block, bits, order):
    me = lax.axis_index("dp")
    left = list(bits)
    for step, bit in enumerate(order):
        axis = left.index(bit)
        left.remove(bit)
        mine = (me >> bit) & 1
        keep = pick(block, mine, axis)
        far = dp_swap(pick(block, 1 - mine, axis), 1 << bit)
        if step + 1 < len(order):
            block = plus(keep, far)
        else:
            block = keep.astype(F32) + far.astype(F32)
    return block


def reduce_scatter(flat, cuts):
    count = lax.axis_size("dp")
    top = count.bit_length() - 2
    bits = tuple(range(top, 0, -1))
    chips = count // 2
    rows = flat.shape[0] // chips
    blocks = flat.reshape((2,) * len(bits) + (rows, LANES))
    natural = tuple(range(1, top + 1))
    turned = natural[1:2] + natural[:1] + natural[2:]
    done, start = [], 0
    for share, turn in cuts:
        part = lax.slice_in_dim(blocks, start, start + rows * share // 8, axis=len(bits))
        start += rows * share // 8
        done.append(halved(part, bits, turned if turn else natural))
    return jnp.concatenate(done) if len(done) > 1 else done[0]


def share_of(result):
    core = lax.axis_index("dp") & 1
    halves = result.reshape(2, result.shape[0] // 2, LANES)
    mine = pick(halves, core)
    far = dp_swap(pick(halves, 1 - core), 1)
    return interleaved(mine, far, core).reshape(-1)


def interleaved(mine, far, odd):
    first = jnp.where(odd == 0, mine, far)
    second = jnp.where(odd == 0, far, mine)
    return jnp.stack([first, second], axis=1).reshape(-1, LANES)


def normed(tensor):
    centred = tensor - jnp.mean(tensor, axis=-1, keepdims=True)
    inverse = lax.rsqrt(jnp.mean(centred * centred, axis=-1, keepdims=True) + 1e-05)
    return centred * inverse, inverse


def normed_back(grad, n, inverse, gain_row):
    scaled = grad * gain_row
    low = jnp.mean(scaled, axis=-1, keepdims=True)
    tilt = jnp.mean(scaled * n, axis=-1, keepdims=True)
    return (scaled - low - n * tilt) * inverse, jnp.sum(grad * n, axis=0)


def gelu_and_slope(u):
    share = 0.5 * (1.0 + lax.erf(u * 0.7071067811865476))
    slope = share + u * (0.3989422804014327 * jnp.exp(-0.5 * u * u))
    return (u * share).astype(BF16), slope


def stream_layer(states, context, cot, lens, weights, gains, heads, fixed, pairs):
    attend_w, up_w, down_w, qkv_w, output_w = weights
    width = states.shape[1]
    size = width // heads
    heads_in = LANES // size
    blocks = width // LANES
    scaling = size ** (-0.5)
    n1, inv1 = normed(states.astype(F32) + mm(context, attend_w))
    h1 = n1 * gains[0]
    h1_low = h1.astype(BF16)
    hidden_low, slope = gelu_and_slope(mm(h1_low, up_w))
    n2, inv2 = normed(h1 + mm(hidden_low, down_w))
    h2 = n2 * gains[1]
    h2_low = h2.astype(BF16)
    packed = mm(h2_low, qkv_w).astype(BF16)
    cols = (0, blocks, 2 * blocks)
    z = attend(lens, packed, packed, packed, cols, pairs, blocks, heads_in, fixed, scaling)
    n3, inv3 = normed(h2 + mm(z, output_w))
    result = n3 * gains[2]
    de, dg2 = normed_back(cot, n3, inv3, gains[2])
    de_low = de.astype(BF16)
    dz = mm_nt(de_low, output_w).astype(BF16)
    dr = attend_back(
        lens, packed, packed, packed, dz, cols, pairs, blocks, heads_in, fixed, scaling, True
    )
    dh2 = de + mm_nt(dr, qkv_w)
    db, dg1 = normed_back(dh2, n2, inv2, gains[1])
    db_low = db.astype(BF16)
    du = (mm_nt(db_low, down_w) * slope).astype(BF16)
    dh1 = db + mm_nt(du, up_w)
    da, dg0 = normed_back(dh1, n1, inv1, gains[0])
    da_low = da.astype(BF16)
    dc = mm_nt(da_low, attend_w).astype(BF16)
    sides = {
        "attend": (context, da_low),
        "up": (h1_low, du),
        "down": (hidden_low, db_low),
        "qkv": (h2_low, dr),
        "output": (z, de_low),
    }
    return result, da, dc, sides, jnp.stack((dg0, dg1, dg2))


def with_far(sides):
    return {name: ((a, dp_swap(a, 1)), (b, dp_swap(b, 1))) for name, (a, b) in sides.items()}


NAMES = ("query", "keyval", "attend", "up", "down", "qkv", "output")


def half_work(both, sizes, total):
    first, second, filled = [], [], 0
    for name in NAMES:
        m, n = sizes[name]
        a, b = both.get(name, (None, m * n // UNIT))
        room = min(max((total // 2 - filled) // n, 0), m)
        if room:
            first.append((a, b, 0, room))
        if room < m:
            second.append((a, b, room, m))
        filled += m * n
    return first, second


def spread(count, regions, padded, offset, rows):
    target = lax.broadcasted_iota(jnp.int32, (rows, count * regions), 0) - offset
    source = lax.broadcasted_iota(jnp.int32, (rows, count * regions), 1)
    return (target == source // regions * padded + source % regions).astype(BF16)


def local(
    text_states,
    image_states,
    caption_lengths,
    text_query,
    text_keyval,
    text_attend,
    text_up,
    text_down,
    text_qkv,
    text_output,
    text_gains,
    image_query,
    image_keyval,
    image_attend,
    image_up,
    image_down,
    image_qkv,
    image_output,
    image_gains,
    text_cotangent,
    image_cotangent,
):
    own_pairs = caption_lengths.shape[0]
    own_text = text_states.shape[0]
    text_len = own_text // own_pairs
    regions = image_states.shape[0] // own_pairs
    padded = -(-regions // 16) * 16
    own_image = own_pairs * padded
    pairs = 2 * own_pairs
    d_t, d_i = text_states.shape[1], image_states.shape[1]
    stream = lax.axis_index("stream")
    core = lax.axis_index("dp") & 1
    side = jnp.stack([core, stream]).astype(jnp.int32)

    far_put = spread(own_pairs, regions, padded, 0, 2 * own_image)
    near_put = spread(own_pairs, regions, padded, own_image, 2 * own_image)
    trim = near_put[own_image:].T

    def both_images(near):
        return (mm(far_put, stream_swap(near)) + mm(near_put, near)).astype(BF16)

    image_all = both_images(image_states)
    text_all = jnp.concatenate([text_states, stream_swap(text_states)])
    lens = jnp.concatenate([caption_lengths, stream_swap(caption_lengths)])
    image_cot = both_images(image_cotangent)
    text_cot = jnp.concatenate([text_cotangent, stream_swap(text_cotangent)])

    positions = lax.broadcasted_iota(jnp.int32, (pairs, text_len), 1)
    valid = (positions < lens[:, None]).reshape(pairs * text_len, 1).astype(F32)

    co_blocks = D_C // LANES
    co_cols = (0, 0, co_blocks)
    co_scale = (D_C // H_C) ** (-0.5)

    text_kv = mm(text_all, text_keyval).astype(BF16)
    image_q = mm(image_all, image_query).astype(BF16)
    ci = attend(lens, image_q, text_kv, text_kv, co_cols, pairs, co_blocks, 1, None, co_scale)
    image_out, image_da, image_dc, image_sides, image_dg = stream_layer(
        image_all,
        ci,
        image_cot.astype(F32),
        lens,
        (image_attend, image_up, image_down, image_qkv, image_output),
        image_gains,
        H_I,
        regions,
        pairs,
    )
    image_dq, text_dkv = attend_back(
        lens, image_q, text_kv, text_kv, image_dc, co_cols, pairs, co_blocks, 1, None, co_scale, False
    )
    image_sides["query"] = (image_all, image_dq)

    def sizes_of(*weights):
        return {name: weight.shape for name, weight in zip(NAMES, weights)}

    def gather_half(sides, sizes):
        both = with_far(sides)
        total = sum(m * n for m, n in sizes.values())
        total_rows = total // (2 * UNIT)
        first, second = half_work(both, sizes, total)
        return lax.cond(
            stream == 0,
            lambda: flat_half(side, total_rows, first),
            lambda: flat_half(side, total_rows, second),
        )

    image_sizes = sizes_of(
        image_query, image_keyval, image_attend, image_up, image_down, image_qkv, image_output
    )
    text_sizes = sizes_of(
        text_query, text_keyval, text_attend, text_up, text_down, text_qkv, text_output
    )
    early = lax.axis_size("dp") == 16
    if early:
        image_flat = gather_half(image_sides, image_sizes)

    image_kv = mm(image_all, image_keyval).astype(BF16)
    text_q = mm(text_all, text_query).astype(BF16)
    ct = attend(lens, text_q, image_kv, image_kv, co_cols, pairs, co_blocks, 1, regions, co_scale)
    if early:
        ct, image_flat = lax.optimization_barrier((ct, image_flat))
        image_part = reduce_scatter(image_flat, ((4, False), (4, True)))
    text_out, text_da, text_dc, text_sides, text_dg = stream_layer(
        text_all,
        ct,
        text_cot.astype(F32) * valid,
        lens,
        (text_attend, text_up, text_down, text_qkv, text_output),
        text_gains,
        H_T,
        None,
        pairs,
    )
    text_dq, image_dkv = attend_back(
        lens, text_q, image_kv, image_kv, text_dc, co_cols, pairs, co_blocks, 1, regions, co_scale, False
    )

    text_result = (text_out[:own_text] * valid[:own_text]).astype(BF16)
    image_result = mm(trim, image_out[own_image:].astype(BF16)).astype(BF16)
    text_grad = (
        text_da[:own_text]
        + mm_nt(text_dq[:own_text], text_query)
        + mm_nt(text_dkv[:own_text], text_keyval)
    ).astype(BF16)
    image_grad = (
        image_da[own_image:]
        + mm_nt(image_dq[own_image:], image_query)
        + mm_nt(image_dkv[own_image:], image_keyval)
    ).astype(BF16)
    image_grad = mm(trim, image_grad).astype(BF16)

    text_sides["query"] = (text_all, text_dq)
    text_sides["keyval"] = (text_all, text_dkv)
    if early:
        late = late_keyval(side, image_all, image_dkv)
        image_part = merged_keyval(image_part, late)
        cuts = ((2, False), (2, True), (2, False), (2, False))
    else:
        image_sides["keyval"] = (image_all, image_dkv)
        image_part = reduce_scatter(gather_half(image_sides, image_sizes), ((8, False),))
        cuts = ((8, False),)
    text_part = reduce_scatter(gather_half(text_sides, text_sizes), cuts)
    image_share = share_of(image_part)
    text_share = share_of(text_part)
    text_gain_sum, image_gain_sum = lax.psum((text_dg, image_dg), "dp")
    return (
        text_result,
        image_result,
        text_grad,
        image_grad,
        text_share,
        image_share,
        text_gain_sum,
        image_gain_sum,
    )


def late_keyval(side, states, grads):
    me = lax.axis_index("dp")
    far = (dp_swap(states, 1), dp_swap(grads, 1))
    flat = flat_grad(
        None, 4 * 1280, side, (states, far[0]), (grads, far[1]), 0, states.shape[1], 768, True
    )
    blocks = flat.reshape(2, 2, 1280, LANES)
    y = (me >> 1) & 1
    odd = (me >> 2) & 1
    total = plus(pick(blocks, 1 - y, 1), dp_swap(pick(blocks, y, 1), 2))
    own = jnp.where(y == 1, odd, 1 - odd)
    total = plus(pick(total, own), dp_swap(pick(total, 1 - own), 4))
    route = []
    for i in range(16):
        z, y_of = i >> 2, (i >> 1) & 1
        goal = 1 if z & 1 else (0 if y_of else 2)
        if z != goal:
            route.append((i, goal * 4 + (i & 3)))
    total = plus(total, lax.ppermute(total, "dp", route))
    far = lax.ppermute(total, "stream", [(1, 0)])
    return jnp.stack([total, far], axis=1).reshape(2 * 1280, LANES)


def merged_keyval(part, late):
    chip = lax.axis_index("dp") >> 1
    low = jnp.where(chip == 1, 1536, 0)
    high = jnp.where((chip >= 1) & (chip <= 4), jnp.where(chip == 4, 2048, 2560), 0)
    high = jnp.where(lax.axis_index("stream") == 0, high, 0)
    rows = lax.broadcasted_iota(jnp.int32, (part.shape[0], 1), 0)
    return jnp.where((rows >= low) & (rows < high), late.astype(F32), part)


def solution(mesh):
    split = P(("stream", "dp"), None)
    flat = P(("stream", "dp"))
    whole = P()
    return jax.shard_map(
        local,
        mesh=mesh,
        in_specs=(split, split, flat) + (whole,) * 16 + (split, split),
        out_specs=(split, split, split, split, flat, flat, whole, whole),
        check_vma=False,
    )
```

```python
import functools

import jax
import jax.numpy as jnp
from jax import lax
from jax.experimental import pallas as pl
from jax.experimental.pallas import tpu as pltpu
from jax.sharding import PartitionSpec as P

H_T = 12
H_I = 8
H_C = 8
D_C = 1024
LANES = 128
UNIT = 256
masked_score = -1e30
F32 = jnp.float32
BF16 = jnp.bfloat16


def mm(a, b):
    return jnp.dot(a, b, preferred_element_type=F32)


def mm_nt(a, b):
    return lax.dot_general(a, b, (((1,), (1,)), ((), ())), preferred_element_type=F32)


def mm_tn(a, b):
    return lax.dot_general(a, b, (((0,), (0,)), ((), ())), preferred_element_type=F32)


def cost(flops, nbytes, trans=0):
    return pl.CostEstimate(
        flops=int(flops), bytes_accessed=int(nbytes), transcendentals=int(trans)
    )


def lane_block(ref, rows, block):
    return ref[rows, pl.ds(pl.multiple_of(block * LANES, LANES), LANES)]


def put_block(ref, rows, block, value):
    ref[rows, pl.ds(pl.multiple_of(block * LANES, LANES), LANES)] = value


def split_heads(block, heads_in):
    if heads_in == 1:
        return block
    lanes = lax.broadcasted_iota(jnp.int32, block.shape, 1)
    zero = jnp.zeros_like(block)
    low = lanes < LANES // 2
    return jnp.concatenate([jnp.where(low, block, zero), jnp.where(low, zero, block)], axis=0)


def side_by_side(block, heads_in):
    if heads_in == 1:
        return block
    rows = block.shape[0] // 2
    return jnp.concatenate([block[:rows], block[rows:]], axis=1)


def attend_kernel(
    lens_ref, q_ref, k_ref, v_ref, o_ref, *, pairs, blocks, cols, heads_in, fixed, scaling
):
    ql = q_ref.shape[0] // pairs
    kl = k_ref.shape[0] // pairs
    chain = heads_in * ql
    keys = lax.broadcasted_iota(jnp.int32, (chain, kl), 1)
    if fixed is None:
        masks = [keys < lens_ref[p] for p in range(pairs)]
    else:
        masks = [keys < fixed] * pairs

    @pl.loop(0, blocks)
    def _(j):
        scores = []
        for p in range(pairs):
            q = split_heads(lane_block(q_ref, slice(p * ql, (p + 1) * ql), cols[0] + j), heads_in)
            k = lane_block(k_ref, slice(p * kl, (p + 1) * kl), cols[1] + j)
            scores.append(jnp.where(masks[p], mm_nt(q, k) * scaling, masked_score))
        s = jnp.concatenate(scores, axis=0)
        raised = jnp.exp(s - jnp.max(s, axis=-1, keepdims=True))
        w = (raised * (1.0 / jnp.sum(raised, axis=-1, keepdims=True))).astype(BF16)
        for p in range(pairs):
            v = split_heads(lane_block(v_ref, slice(p * kl, (p + 1) * kl), cols[2] + j), heads_in)
            o = mm(side_by_side(w[p * chain : (p + 1) * chain], heads_in), v)
            put_block(o_ref, slice(p * ql, (p + 1) * ql), j, o.astype(BF16))


def attend(lens, q, k, v, cols, pairs, blocks, heads_in, fixed, scaling):
    rows = q.shape[0]
    krows = k.shape[0]
    same = k is v
    vmem = pl.BlockSpec(memory_space=pltpu.VMEM)
    operands = [lens, q, k] if same else [lens, q, k, v]
    if q is k:
        operands = [lens, q]

    def body(lens_ref, *refs, **kw):
        refs = list(refs)
        o_ref = refs.pop()
        while len(refs) < 3:
            refs.append(refs[-1])
        attend_kernel(lens_ref, *refs, o_ref, **kw)

    return pl.pallas_call(
        functools.partial(
            body,
            pairs=pairs,
            blocks=blocks,
            cols=cols,
            heads_in=heads_in,
            fixed=fixed,
            scaling=scaling,
        ),
        in_specs=[pl.BlockSpec(memory_space=pltpu.SMEM)] + [vmem] * (len(operands) - 1),
        out_specs=vmem,
        out_shape=jax.ShapeDtypeStruct((rows, blocks * LANES), BF16),
        compiler_params=pltpu.CompilerParams(vmem_limit_bytes=24 * 1024 * 1024),
        cost_estimate=cost(
            16 * blocks * heads_in * rows * krows // pairs * LANES,
            4 * blocks * LANES * (rows + krows),
            blocks * heads_in * rows * krows // pairs,
        ),
        name="attend",
    )(*operands)


def attend_back_kernel(
    lens_ref,
    q_ref,
    k_ref,
    v_ref,
    g_ref,
    dq_ref,
    dk_ref,
    dv_ref,
    *,
    pairs,
    blocks,
    cols,
    out_cols,
    heads_in,
    fixed,
    scaling,
):
    ql = q_ref.shape[0] // pairs
    kl = k_ref.shape[0] // pairs
    keys = lax.broadcasted_iota(jnp.int32, (heads_in * kl, ql), 0)
    if heads_in == 2:
        keys = jnp.where(keys >= kl, keys - kl, keys)
    if fixed is None:
        masks = [keys < lens_ref[p] for p in range(pairs)]
    else:
        masks = [keys < fixed] * pairs

    @pl.loop(0, blocks)
    def _(j):
        scores, slopes = [], []
        for p in range(pairs):
            qs, ks = slice(p * ql, (p + 1) * ql), slice(p * kl, (p + 1) * kl)
            q, g = lane_block(q_ref, qs, cols[0] + j), lane_block(g_ref, qs, j)
            k = split_heads(lane_block(k_ref, ks, cols[1] + j), heads_in)
            v = split_heads(lane_block(v_ref, ks, cols[2] + j), heads_in)
            scores.append(jnp.where(masks[p], mm_nt(k, q) * scaling, masked_score))
            slopes.append(mm_nt(v, g))
        stacked = (pairs * heads_in, kl, ql)
        s = jnp.concatenate(scores, axis=0).reshape(stacked)
        dp = jnp.concatenate(slopes, axis=0).reshape(stacked)
        raised = jnp.exp(s - jnp.max(s, axis=1, keepdims=True))
        w = raised * (1.0 / jnp.sum(raised, axis=1, keepdims=True))
        inner = jnp.sum(w * dp, axis=1, keepdims=True)
        ds = (w * (dp - inner)).astype(BF16).reshape(-1, ql)
        w = w.astype(BF16).reshape(-1, ql)
        chain = heads_in * kl
        for p in range(pairs):
            qs, ks = slice(p * ql, (p + 1) * ql), slice(p * kl, (p + 1) * kl)
            own = slice(p * chain, (p + 1) * chain)
            q = split_heads(lane_block(q_ref, qs, cols[0] + j), heads_in)
            g = split_heads(lane_block(g_ref, qs, j), heads_in)
            k = split_heads(lane_block(k_ref, ks, cols[1] + j), heads_in)
            dq = mm_tn(ds[own], k) * scaling
            dk = mm(side_by_side(ds[own], heads_in), q) * scaling
            dv = mm(side_by_side(w[own], heads_in), g)
            put_block(dq_ref, qs, out_cols[0] + j, dq.astype(BF16))
            put_block(dk_ref, ks, out_cols[1] + j, dk.astype(BF16))
            put_block(dv_ref, ks, out_cols[2] + j, dv.astype(BF16))


def attend_back(lens, q, k, v, g, cols, pairs, blocks, heads_in, fixed, scaling, packed):
    rows = q.shape[0]
    krows = k.shape[0]
    vmem = pl.BlockSpec(memory_space=pltpu.VMEM)
    width = blocks * LANES
    if packed:
        operands = [lens, q, g]
        out_cols = (0, blocks, 2 * blocks)
        out_shape = jax.ShapeDtypeStruct((rows, 3 * width), BF16)
        out_specs = vmem
    else:
        operands = [lens, q, k, g]
        out_cols = (0, 0, blocks)
        out_shape = [
            jax.ShapeDtypeStruct((rows, width), BF16),
            jax.ShapeDtypeStruct((krows, 2 * width), BF16),
        ]
        out_specs = [vmem, vmem]

    def body(lens_ref, *refs, **kw):
        if packed:
            q_ref, g_ref, out_ref = refs
            ins, outs = (q_ref, q_ref, q_ref, g_ref), (out_ref,) * 3
        else:
            q_ref, k_ref, g_ref, dq_ref, dkv_ref = refs
            ins, outs = (q_ref, k_ref, k_ref, g_ref), (dq_ref, dkv_ref, dkv_ref)
        attend_back_kernel(lens_ref, *ins, *outs, **kw)

    return pl.pallas_call(
        functools.partial(
            body,
            pairs=pairs,
            blocks=blocks,
            cols=cols,
            out_cols=out_cols,
            heads_in=heads_in,
            fixed=fixed,
            scaling=scaling,
        ),
        in_specs=[pl.BlockSpec(memory_space=pltpu.SMEM)] + [vmem] * (len(operands) - 1),
        out_specs=out_specs,
        out_shape=out_shape,
        compiler_params=pltpu.CompilerParams(vmem_limit_bytes=24 * 1024 * 1024),
        cost_estimate=cost(
            40 * blocks * heads_in * rows * krows // pairs * LANES,
            8 * blocks * LANES * (rows + krows),
            blocks * heads_in * rows * krows // pairs,
        ),
        name="attend_back",
    )(*operands)


def flat_kernel(
    side_ref, a0_ref, a1_ref, b0_ref, b1_ref, *rest, place, bm, low, units, quarter
):
    out_ref, stage_ref, low_ref, b_ref, sem = rest[-5:]
    core = side_ref[0]
    depth = a0_ref.shape[0]
    for u in range(units):
        at = 2 * u + core
        if quarter:
            at = 4 * u + 2 * side_ref[1] + core
        chosen = pl.ds(pl.multiple_of(at * LANES, LANES), LANES)
        b_ref[:depth, u * LANES : (u + 1) * LANES] = b0_ref[:, chosen]
        b_ref[depth:, u * LANES : (u + 1) * LANES] = b1_ref[:, chosen]
    rows = bm * units
    steps = (low[1] - low[0]) // bm

    def copy(i):
        return pltpu.make_async_copy(
            low_ref.at[i % 2], out_ref.at[pl.ds(place + i * rows, rows)], sem.at[i % 2]
        )

    for i in range(steps):
        columns = slice(low[0] + i * bm, low[0] + (i + 1) * bm)
        a = jnp.concatenate([a0_ref[:, columns], a1_ref[:, columns]], axis=0).T
        for u0 in range(0, units, 4):
            u1 = min(u0 + 4, units)
            total = mm(a, b_ref[:, u0 * LANES : u1 * LANES])
            for u in range(u0, u1):
                stage_ref[pl.ds(u, bm, stride=units), :] = total[
                    :, (u - u0) * LANES : (u - u0 + 1) * LANES
                ]
        if i >= 2:
            copy(i - 2).wait()
        low_ref[i % 2] = stage_ref[...].astype(BF16)
        copy(i).start()
    for i in range(max(steps - 2, 0), steps):
        copy(i).wait()


def flat_grad(flat, total_rows, side, a, b, low, high, place, quarter=False):
    a0, a1 = a
    b0, b1 = b
    depth = a0.shape[0]
    columns = b0.shape[1]
    units = columns // (2 * UNIT if quarter else UNIT)
    most = 512 if units <= 8 else 384
    bm = LANES
    for size in range(LANES, most + 1, LANES):
        if (high - low) % size == 0:
            bm = size
    out_rows = bm * units
    vmem = pl.BlockSpec(memory_space=pltpu.VMEM)
    in_specs = [pl.BlockSpec(memory_space=pltpu.SMEM)] + [vmem] * 4
    operands = [side, a0, a1, b0, b1]
    aliases = {}
    if flat is not None:
        in_specs.append(pl.BlockSpec(memory_space=pl.ANY))
        operands.append(flat)
        aliases = {5: 0}
    return pl.pallas_call(
        functools.partial(
            flat_kernel, place=place, bm=bm, low=(low, high), units=units, quarter=quarter
        ),
        in_specs=in_specs,
        out_specs=pl.BlockSpec(memory_space=pl.ANY),
        out_shape=jax.ShapeDtypeStruct((total_rows, LANES), BF16),
        scratch_shapes=[
            pltpu.VMEM((out_rows, LANES), F32),
            pltpu.VMEM((2, out_rows, LANES), BF16),
            pltpu.VMEM((2 * depth, units * LANES), BF16),
            pltpu.SemaphoreType.DMA((2,)),
        ],
        input_output_aliases=aliases,
        compiler_params=pltpu.CompilerParams(vmem_limit_bytes=24 * 1024 * 1024),
        cost_estimate=cost(
            4 * depth * (high - low) * units * LANES,
            4 * depth * (high - low + columns) + 2 * (high - low) * units * LANES,
        ),
        name="flat_grad",
    )(*operands)


def flat_half(side, total_rows, work):
    flat = None
    place = 0
    for a, b, low, high in work:
        if a is None:
            place += b
            continue
        flat = flat_grad(flat, total_rows, side, a, b, low, high, place)
        place += (high - low) * b[0].shape[1] // UNIT
    return flat


def dp_swap(block, bit):
    count = lax.axis_size("dp")
    return lax.ppermute(block, "dp", [(i, i ^ bit) for i in range(count)])


def stream_swap(block):
    return lax.ppermute(block, "stream", [(0, 1), (1, 0)])


def pick(block, index, axis=0):
    return lax.dynamic_index_in_dim(block, index, axis, keepdims=False)


def plus(a, b):
    return (a.astype(F32) + b.astype(F32)).astype(BF16)


def tied(*values):
    return lax.optimization_barrier(values)


def scatter_parts(flat, cuts):
    count = lax.axis_size("dp")
    top = count.bit_length() - 2
    bits = tuple(range(top, 0, -1))
    rows = flat.shape[0] // (count // 2)
    blocks = flat.reshape((2,) * len(bits) + (rows, LANES))
    natural = tuple(range(1, top + 1))
    turned = natural[1:2] + natural[:1] + natural[2:]
    parts, start = [], 0
    for share, turn in cuts:
        part = lax.slice_in_dim(blocks, start, start + rows * share // 8, axis=len(bits))
        start += rows * share // 8
        parts.append((part, bits, turned if turn else natural))
    return parts


def scatter_step(parts):
    me = lax.axis_index("dp")
    done = []
    for block, left, order in parts:
        bit = order[0]
        axis = left.index(bit)
        mine = (me >> bit) & 1
        keep = pick(block, mine, axis)
        far = dp_swap(pick(block, 1 - mine, axis), 1 << bit)
        block = plus(keep, far) if len(order) > 1 else keep.astype(F32) + far.astype(F32)
        done.append((block, left[:axis] + left[axis + 1 :], order[1:]))
    return done


def tied_parts(value, parts):
    value, *blocks = tied(value, *(block for block, _, _ in parts))
    return value, [(block, *part[1:]) for block, part in zip(blocks, parts)]


def scatter_end(parts):
    while parts[0][2]:
        parts = scatter_step(parts)
    blocks = [block for block, _, _ in parts]
    return jnp.concatenate(blocks) if len(blocks) > 1 else blocks[0]


def reduce_scatter(flat, cuts):
    return scatter_end(scatter_parts(flat, cuts))


def share_of(result):
    core = lax.axis_index("dp") & 1
    halves = result.reshape(2, result.shape[0] // 2, LANES)
    mine = pick(halves, core)
    far = dp_swap(pick(halves, 1 - core), 1)
    return interleaved(mine, far, core).reshape(-1)


def interleaved(mine, far, odd):
    first = jnp.where(odd == 0, mine, far)
    second = jnp.where(odd == 0, far, mine)
    return jnp.stack([first, second], axis=1).reshape(-1, LANES)


def normed(tensor):
    centred = tensor - jnp.mean(tensor, axis=-1, keepdims=True)
    inverse = lax.rsqrt(jnp.mean(centred * centred, axis=-1, keepdims=True) + 1e-05)
    return centred * inverse, inverse


def normed_back(grad, n, inverse, gain_row):
    scaled = grad * gain_row
    low = jnp.mean(scaled, axis=-1, keepdims=True)
    tilt = jnp.mean(scaled * n, axis=-1, keepdims=True)
    return (scaled - low - n * tilt) * inverse, jnp.sum(grad * n, axis=0)


def gelu_and_slope(u):
    share = 0.5 * (1.0 + lax.erf(u * 0.7071067811865476))
    slope = share + u * (0.3989422804014327 * jnp.exp(-0.5 * u * u))
    return (u * share).astype(BF16), slope


def stream_layer(
    states, context, cot, lens, weights, gains, heads, fixed, pairs, hook=lambda name, value: value
):
    attend_w, up_w, down_w, qkv_w, output_w = weights
    width = states.shape[1]
    size = width // heads
    heads_in = LANES // size
    blocks = width // LANES
    scaling = size ** (-0.5)
    n1, inv1 = normed(states.astype(F32) + mm(context, attend_w))
    h1 = n1 * gains[0]
    h1_low = h1.astype(BF16)
    hidden_low, slope = gelu_and_slope(mm(h1_low, up_w))
    n2, inv2 = normed(h1 + mm(hidden_low, down_w))
    h2 = n2 * gains[1]
    h2_low = h2.astype(BF16)
    packed = mm(h2_low, qkv_w).astype(BF16)
    cols = (0, blocks, 2 * blocks)
    z = attend(lens, packed, packed, packed, cols, pairs, blocks, heads_in, fixed, scaling)
    n3, inv3 = normed(h2 + mm(z, output_w))
    result = n3 * gains[2]
    de, dg2 = normed_back(cot, n3, inv3, gains[2])
    de_low = de.astype(BF16)
    dz = mm_nt(de_low, output_w).astype(BF16)
    dr = attend_back(
        lens, packed, packed, packed, dz, cols, pairs, blocks, heads_in, fixed, scaling, True
    )
    dr = hook("dr", dr)
    dh2 = de + mm_nt(dr, qkv_w)
    db, dg1 = normed_back(dh2, n2, inv2, gains[1])
    db_low = db.astype(BF16)
    du = (mm_nt(db_low, down_w) * slope).astype(BF16)
    dh1 = db + mm_nt(du, up_w)
    da, dg0 = normed_back(dh1, n1, inv1, gains[0])
    da_low = hook("da", da.astype(BF16))
    dc = mm_nt(da_low, attend_w).astype(BF16)
    sides = {
        "attend": (context, da_low),
        "up": (h1_low, du),
        "down": (hidden_low, db_low),
        "qkv": (h2_low, dr),
        "output": (z, de_low),
    }
    return result, da, dc, sides, jnp.stack((dg0, dg1, dg2))


def with_far(sides):
    return {name: ((a, dp_swap(a, 1)), (b, dp_swap(b, 1))) for name, (a, b) in sides.items()}


NAMES = ("query", "keyval", "attend", "up", "down", "qkv", "output")


def half_work(both, sizes, total):
    first, second, filled = [], [], 0
    for name in NAMES:
        m, n = sizes[name]
        a, b = both.get(name, (None, m * n // UNIT))
        room = min(max((total // 2 - filled) // n, 0), m)
        if room:
            first.append((a, b, 0, room))
        if room < m:
            second.append((a, b, room, m))
        filled += m * n
    return first, second


def spread(count, regions, padded, offset, rows):
    target = lax.broadcasted_iota(jnp.int32, (rows, count * regions), 0) - offset
    source = lax.broadcasted_iota(jnp.int32, (rows, count * regions), 1)
    return (target == source // regions * padded + source % regions).astype(BF16)


def local(
    text_states,
    image_states,
    caption_lengths,
    text_query,
    text_keyval,
    text_attend,
    text_up,
    text_down,
    text_qkv,
    text_output,
    text_gains,
    image_query,
    image_keyval,
    image_attend,
    image_up,
    image_down,
    image_qkv,
    image_output,
    image_gains,
    text_cotangent,
    image_cotangent,
):
    own_pairs = caption_lengths.shape[0]
    own_text = text_states.shape[0]
    text_len = own_text // own_pairs
    regions = image_states.shape[0] // own_pairs
    padded = -(-regions // 16) * 16
    own_image = own_pairs * padded
    pairs = 2 * own_pairs
    d_t, d_i = text_states.shape[1], image_states.shape[1]
    stream = lax.axis_index("stream")
    core = lax.axis_index("dp") & 1
    side = jnp.stack([core, stream]).astype(jnp.int32)

    far_put = spread(own_pairs, regions, padded, 0, 2 * own_image)
    near_put = spread(own_pairs, regions, padded, own_image, 2 * own_image)
    trim = near_put[own_image:].T

    def both_images(near):
        return (mm(far_put, stream_swap(near)) + mm(near_put, near)).astype(BF16)

    image_all = both_images(image_states)
    text_all = jnp.concatenate([text_states, stream_swap(text_states)])
    lens = jnp.concatenate([caption_lengths, stream_swap(caption_lengths)])
    image_cot = both_images(image_cotangent)
    text_cot = jnp.concatenate([text_cotangent, stream_swap(text_cotangent)])

    positions = lax.broadcasted_iota(jnp.int32, (pairs, text_len), 1)
    valid = (positions < lens[:, None]).reshape(pairs * text_len, 1).astype(F32)

    co_blocks = D_C // LANES
    co_cols = (0, 0, co_blocks)
    co_scale = (D_C // H_C) ** (-0.5)

    text_kv = mm(text_all, text_keyval).astype(BF16)
    image_q = mm(image_all, image_query).astype(BF16)
    ci = attend(lens, image_q, text_kv, text_kv, co_cols, pairs, co_blocks, 1, None, co_scale)
    image_out, image_da, image_dc, image_sides, image_dg = stream_layer(
        image_all,
        ci,
        image_cot.astype(F32),
        lens,
        (image_attend, image_up, image_down, image_qkv, image_output),
        image_gains,
        H_I,
        regions,
        pairs,
    )
    image_dq, text_dkv = attend_back(
        lens, image_q, text_kv, text_kv, image_dc, co_cols, pairs, co_blocks, 1, None, co_scale, False
    )
    image_sides["query"] = (image_all, image_dq)

    def sizes_of(*weights):
        return {name: weight.shape for name, weight in zip(NAMES, weights)}

    def gather_half(sides, sizes):
        both = with_far(sides)
        total = sum(m * n for m, n in sizes.values())
        total_rows = total // (2 * UNIT)
        first, second = half_work(both, sizes, total)
        return lax.cond(
            stream == 0,
            lambda: flat_half(side, total_rows, first),
            lambda: flat_half(side, total_rows, second),
        )

    image_sizes = sizes_of(
        image_query, image_keyval, image_attend, image_up, image_down, image_qkv, image_output
    )
    text_sizes = sizes_of(
        text_query, text_keyval, text_attend, text_up, text_down, text_qkv, text_output
    )
    early = lax.axis_size("dp") == 16
    if early:
        image_flat = gather_half(image_sides, image_sizes)

    image_kv = mm(image_all, image_keyval).astype(BF16)
    text_q = mm(text_all, text_query).astype(BF16)
    ct = attend(lens, text_q, image_kv, image_kv, co_cols, pairs, co_blocks, 1, regions, co_scale)
    if early:
        ct, image_flat = lax.optimization_barrier((ct, image_flat))
        running = {"parts": scatter_step(scatter_parts(image_flat, ((4, False), (4, True))))}

    def hook(name, value):
        if not early:
            return value
        value, parts = tied_parts(value, running["parts"])
        running["parts"] = scatter_step(parts)
        return value

    text_out, text_da, text_dc, text_sides, text_dg = stream_layer(
        text_all,
        ct,
        text_cot.astype(F32) * valid,
        lens,
        (text_attend, text_up, text_down, text_qkv, text_output),
        text_gains,
        H_T,
        None,
        pairs,
        hook,
    )
    gains = gain_step(pack_gains(text_dg, image_dg), 1)
    text_dc, gains = tied(text_dc, gains)
    gains = gain_step(gains, 2)
    text_dq, image_dkv = attend_back(
        lens, text_q, image_kv, image_kv, text_dc, co_cols, pairs, co_blocks, 1, regions, co_scale, False
    )

    text_dq, image_dkv, gains = tied(text_dq, image_dkv, gains)
    bit = 4
    while bit < lax.axis_size("dp"):
        gains = gain_step(gains, bit)
        bit *= 2

    text_sides["query"] = (text_all, text_dq)
    text_sides["keyval"] = (text_all, text_dkv)
    if early:
        late = late_start(side, image_all, image_dkv)
        text_flat, late = tied(gather_half(text_sides, text_sizes), late)
        late = late_end(late)
        text_parts = scatter_step(
            scatter_parts(text_flat, ((2, False), (2, True), (2, False), (2, False)))
        )
        image_part = merged_keyval(scatter_end(running["parts"]), late)
    else:
        image_sides["keyval"] = (image_all, image_dkv)
        image_part = reduce_scatter(gather_half(image_sides, image_sizes), ((8, False),))
        text_flat = gather_half(text_sides, text_sizes)
        text_parts = scatter_parts(text_flat, ((8, False),))

    text_da, image_da, text_out, image_out, text_flat = tied(
        text_da, image_da, text_out, image_out, text_flat
    )
    text_result = (text_out[:own_text] * valid[:own_text]).astype(BF16)
    image_result = mm(trim, image_out[own_image:].astype(BF16)).astype(BF16)
    text_grad = (
        text_da[:own_text]
        + mm_nt(text_dq[:own_text], text_query)
        + mm_nt(text_dkv[:own_text], text_keyval)
    ).astype(BF16)
    image_grad = (
        image_da[own_image:]
        + mm_nt(image_dq[own_image:], image_query)
        + mm_nt(image_dkv[own_image:], image_keyval)
    ).astype(BF16)
    image_grad = mm(trim, image_grad).astype(BF16)

    image_share = share_of(image_part)
    text_share = share_of(scatter_end(text_parts))
    text_gain_sum, image_gain_sum = unpack_gains(gains, text_dg.shape[1])
    return (
        text_result,
        image_result,
        text_grad,
        image_grad,
        text_share,
        image_share,
        text_gain_sum,
        image_gain_sum,
    )


def pack_gains(text_dg, image_dg):
    return jnp.concatenate([text_dg, image_dg], axis=1)


def gain_step(gains, bit):
    return gains + dp_swap(gains, bit)


def unpack_gains(gains, width):
    return gains[:, :width], gains[:, width:]


def late_start(side, states, grads):
    me = lax.axis_index("dp")
    far = (dp_swap(states, 1), dp_swap(grads, 1))
    flat = flat_grad(
        None, 4 * 1280, side, (states, far[0]), (grads, far[1]), 0, states.shape[1], 768, True
    )
    blocks = flat.reshape(2, 2, 1280, LANES)
    y = (me >> 1) & 1
    return plus(pick(blocks, 1 - y, 1), dp_swap(pick(blocks, y, 1), 2))


def late_end(total):
    me = lax.axis_index("dp")
    y = (me >> 1) & 1
    odd = (me >> 2) & 1
    own = jnp.where(y == 1, odd, 1 - odd)
    total = plus(pick(total, own), dp_swap(pick(total, 1 - own), 4))
    route = []
    for i in range(16):
        z, y_of = i >> 2, (i >> 1) & 1
        goal = 1 if z & 1 else (0 if y_of else 2)
        if z != goal:
            route.append((i, goal * 4 + (i & 3)))
    total = plus(total, lax.ppermute(total, "dp", route))
    far = lax.ppermute(total, "stream", [(1, 0)])
    return jnp.stack([total, far], axis=1).reshape(2 * 1280, LANES)


def merged_keyval(part, late):
    chip = lax.axis_index("dp") >> 1
    low = jnp.where(chip == 1, 1536, 0)
    high = jnp.where((chip >= 1) & (chip <= 4), jnp.where(chip == 4, 2048, 2560), 0)
    high = jnp.where(lax.axis_index("stream") == 0, high, 0)
    rows = lax.broadcasted_iota(jnp.int32, (part.shape[0], 1), 0)
    return jnp.where((rows >= low) & (rows < high), late.astype(F32), part)


def solution(mesh):
    split = P(("stream", "dp"), None)
    flat = P(("stream", "dp"))
    whole = P()
    return jax.shard_map(
        local,
        mesh=mesh,
        in_specs=(split, split, flat) + (whole,) * 16 + (split, split),
        out_specs=(split, split, split, split, flat, flat, whole, whole),
        check_vma=False,
    )
```

```python
import functools

import jax
import jax.numpy as jnp
from jax import lax
from jax.experimental import pallas as pl
from jax.experimental.pallas import tpu as pltpu
from jax.sharding import PartitionSpec as P

H_T = 12
H_I = 8
H_C = 8
D_C = 1024
LANES = 128
UNIT = 256
masked_score = -1e30
F32 = jnp.float32
BF16 = jnp.bfloat16


def mm(a, b):
    return jnp.dot(a, b, preferred_element_type=F32)


def mm_nt(a, b):
    return lax.dot_general(a, b, (((1,), (1,)), ((), ())), preferred_element_type=F32)


def mm_tn(a, b):
    return lax.dot_general(a, b, (((0,), (0,)), ((), ())), preferred_element_type=F32)


def cost(flops, nbytes, trans=0):
    return pl.CostEstimate(
        flops=int(flops), bytes_accessed=int(nbytes), transcendentals=int(trans)
    )


def lane_block(ref, rows, block):
    return ref[rows, pl.ds(pl.multiple_of(block * LANES, LANES), LANES)]


def put_block(ref, rows, block, value):
    ref[rows, pl.ds(pl.multiple_of(block * LANES, LANES), LANES)] = value


def split_heads(block, heads_in):
    if heads_in == 1:
        return block
    lanes = lax.broadcasted_iota(jnp.int32, block.shape, 1)
    zero = jnp.zeros_like(block)
    low = lanes < LANES // 2
    return jnp.concatenate([jnp.where(low, block, zero), jnp.where(low, zero, block)], axis=0)


def side_by_side(block, heads_in):
    if heads_in == 1:
        return block
    rows = block.shape[0] // 2
    return jnp.concatenate([block[:rows], block[rows:]], axis=1)


def attend_kernel(
    lens_ref, q_ref, k_ref, v_ref, o_ref, *, pairs, blocks, cols, heads_in, fixed, scaling
):
    ql = q_ref.shape[0] // pairs
    kl = k_ref.shape[0] // pairs
    chain = heads_in * ql
    keys = lax.broadcasted_iota(jnp.int32, (chain, kl), 1)
    if fixed is None:
        masks = [keys < lens_ref[p] for p in range(pairs)]
    else:
        masks = [keys < fixed] * pairs

    @pl.loop(0, blocks)
    def _(j):
        scores = []
        for p in range(pairs):
            q = split_heads(lane_block(q_ref, slice(p * ql, (p + 1) * ql), cols[0] + j), heads_in)
            k = lane_block(k_ref, slice(p * kl, (p + 1) * kl), cols[1] + j)
            scores.append(jnp.where(masks[p], mm_nt(q, k) * scaling, masked_score))
        s = jnp.concatenate(scores, axis=0)
        raised = jnp.exp(s - jnp.max(s, axis=-1, keepdims=True))
        w = (raised * (1.0 / jnp.sum(raised, axis=-1, keepdims=True))).astype(BF16)
        for p in range(pairs):
            v = split_heads(lane_block(v_ref, slice(p * kl, (p + 1) * kl), cols[2] + j), heads_in)
            o = mm(side_by_side(w[p * chain : (p + 1) * chain], heads_in), v)
            put_block(o_ref, slice(p * ql, (p + 1) * ql), j, o.astype(BF16))


def attend(lens, q, k, v, cols, pairs, blocks, heads_in, fixed, scaling):
    rows = q.shape[0]
    krows = k.shape[0]
    same = k is v
    vmem = pl.BlockSpec(memory_space=pltpu.VMEM)
    operands = [lens, q, k] if same else [lens, q, k, v]
    if q is k:
        operands = [lens, q]

    def body(lens_ref, *refs, **kw):
        refs = list(refs)
        o_ref = refs.pop()
        while len(refs) < 3:
            refs.append(refs[-1])
        attend_kernel(lens_ref, *refs, o_ref, **kw)

    return pl.pallas_call(
        functools.partial(
            body,
            pairs=pairs,
            blocks=blocks,
            cols=cols,
            heads_in=heads_in,
            fixed=fixed,
            scaling=scaling,
        ),
        in_specs=[pl.BlockSpec(memory_space=pltpu.SMEM)] + [vmem] * (len(operands) - 1),
        out_specs=vmem,
        out_shape=jax.ShapeDtypeStruct((rows, blocks * LANES), BF16),
        compiler_params=pltpu.CompilerParams(vmem_limit_bytes=24 * 1024 * 1024),
        cost_estimate=cost(1000, 1000),
        name="attend",
    )(*operands)


def attend_back_kernel(
    lens_ref,
    q_ref,
    k_ref,
    v_ref,
    g_ref,
    dq_ref,
    dk_ref,
    dv_ref,
    *,
    pairs,
    blocks,
    cols,
    out_cols,
    heads_in,
    fixed,
    scaling,
):
    ql = q_ref.shape[0] // pairs
    kl = k_ref.shape[0] // pairs
    keys = lax.broadcasted_iota(jnp.int32, (heads_in * kl, ql), 0)
    if heads_in == 2:
        keys = jnp.where(keys >= kl, keys - kl, keys)
    if fixed is None:
        masks = [keys < lens_ref[p] for p in range(pairs)]
    else:
        masks = [keys < fixed] * pairs

    @pl.loop(0, blocks)
    def _(j):
        scores, slopes = [], []
        for p in range(pairs):
            qs, ks = slice(p * ql, (p + 1) * ql), slice(p * kl, (p + 1) * kl)
            q, g = lane_block(q_ref, qs, cols[0] + j), lane_block(g_ref, qs, j)
            k = split_heads(lane_block(k_ref, ks, cols[1] + j), heads_in)
            v = split_heads(lane_block(v_ref, ks, cols[2] + j), heads_in)
            scores.append(jnp.where(masks[p], mm_nt(k, q) * scaling, masked_score))
            slopes.append(mm_nt(v, g))
        stacked = (pairs * heads_in, kl, ql)
        s = jnp.concatenate(scores, axis=0).reshape(stacked)
        dp = jnp.concatenate(slopes, axis=0).reshape(stacked)
        raised = jnp.exp(s - jnp.max(s, axis=1, keepdims=True))
        w = raised * (1.0 / jnp.sum(raised, axis=1, keepdims=True))
        inner = jnp.sum(w * dp, axis=1, keepdims=True)
        ds = (w * (dp - inner)).astype(BF16).reshape(-1, ql)
        w = w.astype(BF16).reshape(-1, ql)
        chain = heads_in * kl
        for p in range(pairs):
            qs, ks = slice(p * ql, (p + 1) * ql), slice(p * kl, (p + 1) * kl)
            own = slice(p * chain, (p + 1) * chain)
            q = split_heads(lane_block(q_ref, qs, cols[0] + j), heads_in)
            g = split_heads(lane_block(g_ref, qs, j), heads_in)
            k = split_heads(lane_block(k_ref, ks, cols[1] + j), heads_in)
            dq = mm_tn(ds[own], k) * scaling
            dk = mm(side_by_side(ds[own], heads_in), q) * scaling
            dv = mm(side_by_side(w[own], heads_in), g)
            put_block(dq_ref, qs, out_cols[0] + j, dq.astype(BF16))
            put_block(dk_ref, ks, out_cols[1] + j, dk.astype(BF16))
            put_block(dv_ref, ks, out_cols[2] + j, dv.astype(BF16))


def attend_back(lens, q, k, v, g, cols, pairs, blocks, heads_in, fixed, scaling, packed):
    rows = q.shape[0]
    krows = k.shape[0]
    vmem = pl.BlockSpec(memory_space=pltpu.VMEM)
    width = blocks * LANES
    if packed:
        operands = [lens, q, g]
        out_cols = (0, blocks, 2 * blocks)
        out_shape = jax.ShapeDtypeStruct((rows, 3 * width), BF16)
        out_specs = vmem
    else:
        operands = [lens, q, k, g]
        out_cols = (0, 0, blocks)
        out_shape = [
            jax.ShapeDtypeStruct((rows, width), BF16),
            jax.ShapeDtypeStruct((krows, 2 * width), BF16),
        ]
        out_specs = [vmem, vmem]

    def body(lens_ref, *refs, **kw):
        if packed:
            q_ref, g_ref, out_ref = refs
            ins, outs = (q_ref, q_ref, q_ref, g_ref), (out_ref,) * 3
        else:
            q_ref, k_ref, g_ref, dq_ref, dkv_ref = refs
            ins, outs = (q_ref, k_ref, k_ref, g_ref), (dq_ref, dkv_ref, dkv_ref)
        attend_back_kernel(lens_ref, *ins, *outs, **kw)

    return pl.pallas_call(
        functools.partial(
            body,
            pairs=pairs,
            blocks=blocks,
            cols=cols,
            out_cols=out_cols,
            heads_in=heads_in,
            fixed=fixed,
            scaling=scaling,
        ),
        in_specs=[pl.BlockSpec(memory_space=pltpu.SMEM)] + [vmem] * (len(operands) - 1),
        out_specs=out_specs,
        out_shape=out_shape,
        compiler_params=pltpu.CompilerParams(vmem_limit_bytes=24 * 1024 * 1024),
        cost_estimate=cost(1000, 1000),
        name="attend_back",
    )(*operands)


def flat_kernel(
    side_ref, a0_ref, a1_ref, b0_ref, b1_ref, *rest, place, bm, low, units, quarter
):
    out_ref, stage_ref, low_ref, b_ref, sem = rest[-5:]
    core = side_ref[0]
    depth = a0_ref.shape[0]
    for u in range(units):
        at = 2 * u + core
        if quarter:
            at = 4 * u + 2 * side_ref[1] + core
        chosen = pl.ds(pl.multiple_of(at * LANES, LANES), LANES)
        b_ref[:depth, u * LANES : (u + 1) * LANES] = b0_ref[:, chosen]
        b_ref[depth:, u * LANES : (u + 1) * LANES] = b1_ref[:, chosen]
    rows = bm * units
    steps = (low[1] - low[0]) // bm

    def copy(i):
        return pltpu.make_async_copy(
            low_ref.at[i % 2], out_ref.at[pl.ds(place + i * rows, rows)], sem.at[i % 2]
        )

    for i in range(steps):
        columns = slice(low[0] + i * bm, low[0] + (i + 1) * bm)
        a = jnp.concatenate([a0_ref[:, columns], a1_ref[:, columns]], axis=0).T
        for u0 in range(0, units, 4):
            u1 = min(u0 + 4, units)
            total = mm(a, b_ref[:, u0 * LANES : u1 * LANES])
            for u in range(u0, u1):
                stage_ref[pl.ds(u, bm, stride=units), :] = total[
                    :, (u - u0) * LANES : (u - u0 + 1) * LANES
                ]
        if i >= 2:
            copy(i - 2).wait()
        low_ref[i % 2] = stage_ref[...].astype(BF16)
        copy(i).start()
    for i in range(max(steps - 2, 0), steps):
        copy(i).wait()


def flat_grad(flat, total_rows, side, a, b, low, high, place, quarter=False):
    a0, a1 = a
    b0, b1 = b
    depth = a0.shape[0]
    columns = b0.shape[1]
    units = columns // (2 * UNIT if quarter else UNIT)
    most = 512 if units <= 8 else 384
    bm = LANES
    for size in range(LANES, most + 1, LANES):
        if (high - low) % size == 0:
            bm = size
    out_rows = bm * units
    vmem = pl.BlockSpec(memory_space=pltpu.VMEM)
    in_specs = [pl.BlockSpec(memory_space=pltpu.SMEM)] + [vmem] * 4
    operands = [side, a0, a1, b0, b1]
    aliases = {}
    if flat is not None:
        in_specs.append(pl.BlockSpec(memory_space=pl.ANY))
        operands.append(flat)
        aliases = {5: 0}
    return pl.pallas_call(
        functools.partial(
            flat_kernel, place=place, bm=bm, low=(low, high), units=units, quarter=quarter
        ),
        in_specs=in_specs,
        out_specs=pl.BlockSpec(memory_space=pl.ANY),
        out_shape=jax.ShapeDtypeStruct((total_rows, LANES), BF16),
        scratch_shapes=[
            pltpu.VMEM((out_rows, LANES), F32),
            pltpu.VMEM((2, out_rows, LANES), BF16),
            pltpu.VMEM((2 * depth, units * LANES), BF16),
            pltpu.SemaphoreType.DMA((2,)),
        ],
        input_output_aliases=aliases,
        compiler_params=pltpu.CompilerParams(vmem_limit_bytes=24 * 1024 * 1024),
        cost_estimate=cost(1000, 1000),
        name="flat_grad",
    )(*operands)


def flat_half(side, total_rows, work):
    flat = None
    place = 0
    for a, b, low, high in work:
        if a is None:
            place += b
            continue
        flat = flat_grad(flat, total_rows, side, a, b, low, high, place)
        place += (high - low) * b[0].shape[1] // UNIT
    return flat


def dp_swap(block, bit):
    count = lax.axis_size("dp")
    return lax.ppermute(block, "dp", [(i, i ^ bit) for i in range(count)])


def stream_swap(block):
    return lax.ppermute(block, "stream", [(0, 1), (1, 0)])


def pick(block, index, axis=0):
    return lax.dynamic_index_in_dim(block, index, axis, keepdims=False)


def plus(a, b):
    return (a.astype(F32) + b.astype(F32)).astype(BF16)


def tied(*values):
    return lax.optimization_barrier(values)


def scatter_parts(flat, cuts):
    count = lax.axis_size("dp")
    top = count.bit_length() - 2
    bits = tuple(range(top, 0, -1))
    rows = flat.shape[0] // (count // 2)
    blocks = flat.reshape((2,) * len(bits) + (rows, LANES))
    natural = tuple(range(1, top + 1))
    turned = natural[1:2] + natural[:1] + natural[2:]
    parts, start = [], 0
    for share, turn in cuts:
        part = lax.slice_in_dim(blocks, start, start + rows * share // 8, axis=len(bits))
        start += rows * share // 8
        parts.append((part, bits, turned if turn else natural))
    return parts


def scatter_step(parts):
    me = lax.axis_index("dp")
    done = []
    for block, left, order in parts:
        bit = order[0]
        axis = left.index(bit)
        mine = (me >> bit) & 1
        keep = pick(block, mine, axis)
        far = dp_swap(pick(block, 1 - mine, axis), 1 << bit)
        block = plus(keep, far) if len(order) > 1 else keep.astype(F32) + far.astype(F32)
        done.append((block, left[:axis] + left[axis + 1 :], order[1:]))
    return done


def tied_parts(value, parts):
    value, *blocks = tied(value, *(block for block, _, _ in parts))
    return value, [(block, *part[1:]) for block, part in zip(blocks, parts)]


def scatter_end(parts):
    while parts[0][2]:
        parts = scatter_step(parts)
    blocks = [block for block, _, _ in parts]
    return jnp.concatenate(blocks) if len(blocks) > 1 else blocks[0]


def reduce_scatter(flat, cuts):
    return scatter_end(scatter_parts(flat, cuts))


def share_of(result):
    core = lax.axis_index("dp") & 1
    halves = result.reshape(2, result.shape[0] // 2, LANES)
    mine = pick(halves, core)
    far = dp_swap(pick(halves, 1 - core), 1)
    return interleaved(mine, far, core).reshape(-1)


def interleaved(mine, far, odd):
    first = jnp.where(odd == 0, mine, far)
    second = jnp.where(odd == 0, far, mine)
    return jnp.stack([first, second], axis=1).reshape(-1, LANES)


CHUNK = 64
ROWS = 128
WIDEST = 1024
WIDEST_GELU = 1024


def tiles(columns, body, widest=None):
    size = max(c for c in range(LANES, (widest or WIDEST) + 1, LANES) if columns % c == 0)
    if size == columns:
        return body(slice(0, columns))

    @pl.loop(0, columns // size)
    def _(j):
        body(pl.ds(pl.multiple_of(j * size, size), size))


def row_chunks(rows, body):
    size = ROWS if rows % ROWS == 0 else CHUNK

    @pl.loop(0, rows // size)
    def _(i):
        body(i * size, pl.ds(pl.multiple_of(i * size, size), size), size)


def normed_chunk(a):
    centred = a - jnp.mean(a, axis=-1, keepdims=True)
    inverse = lax.rsqrt(jnp.mean(centred * centred, axis=-1, keepdims=True) + 1e-05)
    return centred * inverse, inverse


def normed_back_chunk(grad, n, inverse, gain_row):
    scaled = grad * gain_row
    low = jnp.mean(scaled, axis=-1, keepdims=True)
    tilt = jnp.mean(scaled * n, axis=-1, keepdims=True)
    return (scaled - low - n * tilt) * inverse, jnp.sum(grad * n, axis=0, keepdims=True)


def co_kernel(
    lens_ref, x_ref, o_ref, g_ref, wq_ref, wkv_ref, wat_ref,
    q_ref, kv_ref, c_ref, n_ref, inv_ref, h_ref, a_ref, *, pairs, fixed, scaling,
):
    rows, width = x_ref.shape

    def kv_tile(cols):
        kv_ref[:, cols] = mm(o_ref[...], wkv_ref[:, cols]).astype(BF16)

    def q_tile(cols):
        q_ref[:, cols] = mm(x_ref[...], wq_ref[:, cols]).astype(BF16)

    def a_tile(cols):
        a_ref[:, cols] = x_ref[:, cols].astype(F32) + mm(c_ref[...], wat_ref[:, cols])

    def norm(i, at, size):
        n, inverse = normed_chunk(a_ref[at, :])
        n_ref[at, :] = n
        inv_ref[at, :] = jnp.broadcast_to(inverse, (size, LANES))
        h_ref[at, :] = (n * g_ref[0:1, :]).astype(BF16)

    tiles(kv_ref.shape[1], kv_tile)
    tiles(q_ref.shape[1], q_tile)
    blocks = q_ref.shape[1] // LANES
    attend_kernel(
        lens_ref, q_ref, kv_ref, kv_ref, c_ref, pairs=pairs, blocks=blocks,
        cols=(0, 0, blocks), heads_in=1, fixed=fixed, scaling=scaling,
    )
    tiles(width, a_tile)
    row_chunks(rows, norm)


def mlp_kernel(
    h1_ref, n1_ref, g_ref, wup_ref, wdown_ref, wqkv_ref,
    hid_ref, slope_ref, n_ref, inv_ref, h_ref, r_ref, a_ref,
):
    rows, width = n1_ref.shape

    def up_tile(cols):
        u_all = mm(h1_ref[...], wup_ref[:, cols])
        for at in range(0, rows, CHUNK):
            u = u_all[at : at + CHUNK]
            share = 0.5 + 0.5 * lax.erf(u * 0.7071067811865476)
            hid_ref[at : at + CHUNK, cols] = (u * share).astype(BF16)
            slope = share + u * (0.3989422804014327 * jnp.exp(-0.5 * u * u))
            slope_ref[at : at + CHUNK, cols] = slope.astype(BF16)

    def down_tile(cols):
        a_ref[:, cols] = n1_ref[:, cols] * g_ref[0:1, cols] + mm(hid_ref[...], wdown_ref[:, cols])

    def norm(i, at, size):
        n, inverse = normed_chunk(a_ref[at, :])
        n_ref[at, :] = n
        inv_ref[at, :] = jnp.broadcast_to(inverse, (size, LANES))
        h_ref[at, :] = (n * g_ref[1:2, :]).astype(BF16)

    def qkv_tile(cols):
        r_ref[:, cols] = mm(h_ref[...], wqkv_ref[:, cols]).astype(BF16)

    tiles(wup_ref.shape[1], up_tile, WIDEST_GELU)
    tiles(width, down_tile)
    row_chunks(rows, norm)
    tiles(r_ref.shape[1], qkv_tile)


def self_kernel(
    lens_ref, r_ref, n2_ref, g_ref, wout_ref, cot_ref,
    z_ref, y_ref, de_ref, de_low_ref, dr_ref, dg_ref, a_ref, dz_ref,
    *, pairs, heads_in, fixed, scaling,
):
    rows, width = n2_ref.shape
    blocks = width // LANES
    cols = (0, blocks, 2 * blocks)
    shared = dict(
        pairs=pairs, blocks=blocks, cols=cols, heads_in=heads_in, fixed=fixed, scaling=scaling
    )

    def out_tile(at):
        a_ref[:, at] = n2_ref[:, at] * g_ref[1:2, at] + mm(z_ref[...], wout_ref[:, at])

    def last(start, at, size):
        n, inverse = normed_chunk(a_ref[at, :])
        y = n * g_ref[2:3, :]
        grad = cot_ref[at, :].astype(F32)
        if fixed is None:
            slots = rows // pairs
            place = lax.broadcasted_iota(jnp.int32, (size, 1), 0) + lax.rem(start, slots)
            valid = (place < lens_ref[lax.div(start, slots)]).astype(F32)
            y, grad = y * valid, grad * valid
        y_ref[at, :] = y.astype(BF16)
        de, dg = normed_back_chunk(grad, n, inverse, g_ref[2:3, :])
        de_ref[at, :] = de
        de_low_ref[at, :] = de.astype(BF16)
        dg_ref[...] += dg

    def dz_tile(at):
        dz_ref[:, at] = mm_nt(de_low_ref[...], wout_ref[at, :]).astype(BF16)

    attend_kernel(lens_ref, r_ref, r_ref, r_ref, z_ref, **shared)
    tiles(width, out_tile)
    dg_ref[...] = jnp.zeros_like(dg_ref)
    row_chunks(rows, last)
    tiles(width, dz_tile)
    attend_back_kernel(
        lens_ref, r_ref, r_ref, r_ref, dz_ref, dr_ref, dr_ref, dr_ref, out_cols=cols, **shared
    )


def back_kernel(
    dr_ref, de_ref, n2_ref, inv2_ref, n1_ref, inv1_ref, g_ref, slope_ref,
    wqkv_ref, wdown_ref, wup_ref, wat_ref,
    db_low_ref, du_ref, da_ref, da_low_ref, dc_ref, dg_ref, a_ref, db_ref,
):
    rows, width = n1_ref.shape
    dg_ref[...] = jnp.zeros_like(dg_ref)

    def second_tile(at):
        a_ref[:, at] = de_ref[:, at] + mm_nt(dr_ref[...], wqkv_ref[at, :])

    def second_norm(i, at, size):
        db, dg = normed_back_chunk(a_ref[at, :], n2_ref[at, :], inv2_ref[at, 0:1], g_ref[1:2, :])
        db_ref[at, :] = db
        db_low_ref[at, :] = db.astype(BF16)
        dg_ref[1:2, :] += dg

    def du_tile(at):
        grad = mm_nt(db_low_ref[...], wdown_ref[at, :])
        du_ref[:, at] = (grad * slope_ref[:, at].astype(F32)).astype(BF16)

    def first_tile(at):
        a_ref[:, at] = db_ref[:, at] + mm_nt(du_ref[...], wup_ref[at, :])

    def first_norm(i, at, size):
        da, dg = normed_back_chunk(a_ref[at, :], n1_ref[at, :], inv1_ref[at, 0:1], g_ref[0:1, :])
        da_ref[at, :] = da
        da_low_ref[at, :] = da.astype(BF16)
        dg_ref[0:1, :] += dg

    def dc_tile(at):
        dc_ref[:, at] = mm_nt(da_low_ref[...], wat_ref[at, :]).astype(BF16)

    tiles(width, second_tile)
    row_chunks(rows, second_norm)
    tiles(du_ref.shape[1], du_tile, WIDEST_GELU)
    tiles(width, first_tile)
    row_chunks(rows, first_norm)
    tiles(dc_ref.shape[1], dc_tile)


def fused(kernel, operands, outs, scratch, name, smem_first=False, limit=20):
    vmem = pl.BlockSpec(memory_space=pltpu.VMEM)
    in_specs = [vmem] * len(operands)
    if smem_first:
        in_specs[0] = pl.BlockSpec(memory_space=pltpu.SMEM)
    return pl.pallas_call(
        kernel,
        in_specs=in_specs,
        out_specs=[vmem] * len(outs),
        out_shape=[jax.ShapeDtypeStruct(shape, kind) for shape, kind in outs],
        scratch_shapes=[pltpu.VMEM(shape, kind) for shape, kind in scratch],
        compiler_params=pltpu.CompilerParams(vmem_limit_bytes=limit * 1024 * 1024),
        cost_estimate=cost(1000, 1000),
        name=name,
    )(*operands)


def co_forward(lens, states, other, gains, query_w, keyval_w, attend_w, pairs, fixed):
    rows, width = states.shape
    orows = other.shape[0]
    return fused(
        functools.partial(co_kernel, pairs=pairs, fixed=fixed, scaling=(D_C // H_C) ** (-0.5)),
        (lens, states, other, gains, query_w, keyval_w, attend_w),
        [
            ((rows, D_C), BF16),
            ((orows, 2 * D_C), BF16),
            ((rows, D_C), BF16),
            ((rows, width), F32),
            ((rows, LANES), F32),
            ((rows, width), BF16),
        ],
        [((rows, width), F32)],
        "co_forward",
        True,
    )


def mlp_forward(h1, n1, gains, up_w, down_w, qkv_w):
    rows, width = n1.shape
    hidden = up_w.shape[1]
    return fused(
        mlp_kernel,
        (h1, n1, gains, up_w, down_w, qkv_w),
        [
            ((rows, hidden), BF16),
            ((rows, hidden), BF16),
            ((rows, width), F32),
            ((rows, LANES), F32),
            ((rows, width), BF16),
            ((rows, 3 * width), BF16),
        ],
        [((rows, width), F32)],
        "mlp_forward",
    )


def self_turn(lens, r, n2, gains, output_w, cot, pairs, heads, fixed):
    rows, width = n2.shape
    size = width // heads
    return fused(
        functools.partial(
            self_kernel, pairs=pairs, heads_in=LANES // size, fixed=fixed, scaling=size ** (-0.5)
        ),
        (lens, r, n2, gains, output_w, cot),
        [
            ((rows, width), BF16),
            ((rows, width), BF16),
            ((rows, width), F32),
            ((rows, width), BF16),
            ((rows, 3 * width), BF16),
            ((1, width), F32),
        ],
        [((rows, width), F32), ((rows, width), BF16)],
        "self_turn",
        True,
    )


def rest_back(dr, de, n2, inv2, n1, inv1, gains, slope, qkv_w, down_w, up_w, attend_w):
    rows, width = n1.shape
    return fused(
        back_kernel,
        (dr, de, n2, inv2, n1, inv1, gains, slope, qkv_w, down_w, up_w, attend_w),
        [
            ((rows, width), BF16),
            ((rows, up_w.shape[1]), BF16),
            ((rows, width), F32),
            ((rows, width), BF16),
            ((rows, D_C), BF16),
            ((2, width), F32),
        ],
        [((rows, width), F32), ((rows, width), F32)],
        "rest_back",
    )


class Exchange:
    def __init__(self):
        self.far = {}
        self.pending = []
        self.parts = None

    def send(self, **arrays):
        for name, array in arrays.items():
            self.far[name] = dp_swap(array, 1)
            self.pending.append(name)

    def settle(self, value, **arrays):
        names, self.pending = self.pending, []
        if names:
            value, *got = tied(value, *(self.far[name] for name in names))
            self.far.update(zip(names, got))
        self.send(**arrays)
        return value

    def pair(self, name, array):
        return array, self.far[name]


def stream_forward(
    lens, states, other, cot, weights, gains, heads, fixed, other_fixed, pairs, moves, hook
):
    query_w, other_keyval_w, attend_w, up_w, down_w, qkv_w, output_w = weights
    q, kv, context, n1, inv1, h1 = co_forward(
        lens, states, other, gains, query_w, other_keyval_w, attend_w, pairs, other_fixed
    )
    h1 = hook("co", moves.settle(h1, context=context, h1=h1))
    hidden, slope, n2, inv2, h2, r = mlp_forward(h1, n1, gains, up_w, down_w, qkv_w)
    r = hook("mlp", moves.settle(r, hidden=hidden, h2=h2))
    z, result, de, de_low, dr, dg2 = self_turn(
        lens, r, n2, gains, output_w, cot, pairs, heads, fixed
    )
    dr = hook("self", moves.settle(dr, z=z, de=de_low, dr=dr))
    db, du, da, da_low, dc, dg = rest_back(
        dr, de, n2, inv2, n1, inv1, gains, slope, qkv_w, down_w, up_w, attend_w
    )
    dc = hook("back", moves.settle(dc, db=db, du=du, da=da_low))

    def sides(dq):
        return {
            "query": (moves.pair("states", states), moves.pair("dq", dq)),
            "attend": (moves.pair("context", context), moves.pair("da", da_low)),
            "up": (moves.pair("h1", h1), moves.pair("du", du)),
            "down": (moves.pair("hidden", hidden), moves.pair("db", db)),
            "qkv": (moves.pair("h2", h2), moves.pair("dr", dr)),
            "output": (moves.pair("z", z), moves.pair("de", de_low)),
        }

    return result, da, dc, q, kv, sides, jnp.concatenate([dg, dg2])


NAMES = ("query", "keyval", "attend", "up", "down", "qkv", "output")


def half_work(both, sizes, total):
    first, second, filled = [], [], 0
    for name in NAMES:
        m, n = sizes[name]
        a, b = both.get(name, (None, m * n // UNIT))
        room = min(max((total // 2 - filled) // n, 0), m)
        if room:
            first.append((a, b, 0, room))
        if room < m:
            second.append((a, b, room, m))
        filled += m * n
    return first, second


def spread(count, regions, padded, offset, rows):
    target = lax.broadcasted_iota(jnp.int32, (rows, count * regions), 0) - offset
    source = lax.broadcasted_iota(jnp.int32, (rows, count * regions), 1)
    return (target == source // regions * padded + source % regions).astype(BF16)


def local(
    text_states,
    image_states,
    caption_lengths,
    text_query,
    text_keyval,
    text_attend,
    text_up,
    text_down,
    text_qkv,
    text_output,
    text_gains,
    image_query,
    image_keyval,
    image_attend,
    image_up,
    image_down,
    image_qkv,
    image_output,
    image_gains,
    text_cotangent,
    image_cotangent,
):
    own_pairs = caption_lengths.shape[0]
    own_text = text_states.shape[0]
    text_len = own_text // own_pairs
    regions = image_states.shape[0] // own_pairs
    padded = -(-regions // 16) * 16
    own_image = own_pairs * padded
    pairs = 2 * own_pairs
    d_t, d_i = text_states.shape[1], image_states.shape[1]
    stream = lax.axis_index("stream")
    core = lax.axis_index("dp") & 1
    side = jnp.stack([core, stream]).astype(jnp.int32)

    far_put = spread(own_pairs, regions, padded, 0, 2 * own_image)
    near_put = spread(own_pairs, regions, padded, own_image, 2 * own_image)
    trim = near_put[own_image:].T

    def both_images(near):
        return (mm(far_put, stream_swap(near)) + mm(near_put, near)).astype(BF16)

    image_all = both_images(image_states)
    text_all = jnp.concatenate([text_states, stream_swap(text_states)])
    lens = jnp.concatenate([caption_lengths, stream_swap(caption_lengths)])
    image_cot = both_images(image_cotangent)
    text_cot = jnp.concatenate([text_cotangent, stream_swap(text_cotangent)])

    co_blocks = D_C // LANES
    co_cols = (0, 0, co_blocks)
    co_scale = (D_C // H_C) ** (-0.5)

    image_moves, text_moves = Exchange(), Exchange()
    image_moves.send(states=image_all)
    image_out, image_da, image_dc, image_q, text_kv, image_sides, image_dg = stream_forward(
        lens,
        image_all,
        text_all,
        image_cot,
        (image_query, text_keyval, image_attend, image_up, image_down, image_qkv, image_output),
        image_gains,
        H_I,
        regions,
        None,
        pairs,
        image_moves,
        lambda name, value: value,
    )
    image_dq, text_dkv = attend_back(
        lens, image_q, text_kv, text_kv, image_dc, co_cols, pairs, co_blocks, 1, None, co_scale, False
    )
    image_moves.send(dq=image_dq)
    image_sides = image_sides(image_dq)
    text_moves.send(states=text_all, dkv=text_dkv)

    def sizes_of(*weights):
        return {name: weight.shape for name, weight in zip(NAMES, weights)}

    def gather_half(both, sizes):
        total = sum(m * n for m, n in sizes.values())
        total_rows = total // (2 * UNIT)
        first, second = half_work(both, sizes, total)
        return lax.cond(
            stream == 0,
            lambda: flat_half(side, total_rows, first),
            lambda: flat_half(side, total_rows, second),
        )

    image_sizes = sizes_of(
        image_query, image_keyval, image_attend, image_up, image_down, image_qkv, image_output
    )
    text_sizes = sizes_of(
        text_query, text_keyval, text_attend, text_up, text_down, text_qkv, text_output
    )
    early = lax.axis_size("dp") == 16
    if early:
        image_flat = gather_half(image_sides, image_sizes)

    running = {}

    def hook(name, value):
        if not early:
            return value
        if name == "co":
            value, flat = tied(value, image_flat)
            running["parts"] = scatter_step(scatter_parts(flat, ((4, False), (4, True))))
        if name == "back":
            value, parts = tied_parts(value, running["parts"])
            running["parts"] = scatter_step(parts)
        return value

    text_out, text_da, text_dc, text_q, image_kv, text_sides, text_dg = stream_forward(
        lens,
        text_all,
        image_all,
        text_cot,
        (text_query, image_keyval, text_attend, text_up, text_down, text_qkv, text_output),
        text_gains,
        H_T,
        None,
        regions,
        pairs,
        text_moves,
        hook,
    )
    gains = gain_step(pack_gains(text_dg, image_dg), 1)
    text_dc, gains = tied(text_dc, gains)
    gains = gain_step(gains, 2)
    text_dq, image_dkv = attend_back(
        lens, text_q, image_kv, image_kv, text_dc, co_cols, pairs, co_blocks, 1, regions, co_scale, False
    )

    text_dq, image_dkv, gains = tied(text_dq, image_dkv, gains)
    bit = 4
    while bit < lax.axis_size("dp"):
        gains = gain_step(gains, bit)
        bit *= 2

    image_moves.send(dkv=image_dkv)
    text_moves.send(dq=text_dq)
    text_sides = text_sides(text_dq)
    text_sides["keyval"] = (text_moves.pair("states", text_all), text_moves.pair("dkv", text_dkv))
    if early:
        late = late_start(
            side, image_moves.pair("states", image_all), image_moves.pair("dkv", image_dkv)
        )
        text_flat, late = tied(gather_half(text_sides, text_sizes), late)
        late = late_end(late)
        text_parts = scatter_step(
            scatter_parts(text_flat, ((2, False), (2, True), (2, False), (2, False)))
        )
        image_part = merged_keyval(scatter_end(running["parts"]), late)
    else:
        image_sides["keyval"] = (
            image_moves.pair("states", image_all),
            image_moves.pair("dkv", image_dkv),
        )
        image_part = reduce_scatter(gather_half(image_sides, image_sizes), ((8, False),))
        text_flat = gather_half(text_sides, text_sizes)
        text_parts = scatter_parts(text_flat, ((8, False),))

    text_da, image_da, text_out, image_out, text_flat = tied(
        text_da, image_da, text_out, image_out, text_flat
    )
    text_result = text_out[:own_text]
    image_result = mm(trim, image_out[own_image:]).astype(BF16)
    text_grad = (
        text_da[:own_text]
        + mm_nt(text_dq[:own_text], text_query)
        + mm_nt(text_dkv[:own_text], text_keyval)
    ).astype(BF16)
    image_grad = (
        image_da[own_image:]
        + mm_nt(image_dq[own_image:], image_query)
        + mm_nt(image_dkv[own_image:], image_keyval)
    ).astype(BF16)
    image_grad = mm(trim, image_grad).astype(BF16)

    image_share = share_of(image_part)
    text_share = share_of(scatter_end(text_parts))
    text_gain_sum, image_gain_sum = unpack_gains(gains, text_dg.shape[1])
    return (
        text_result,
        image_result,
        text_grad,
        image_grad,
        text_share,
        image_share,
        text_gain_sum,
        image_gain_sum,
    )


def pack_gains(text_dg, image_dg):
    return jnp.concatenate([text_dg, image_dg], axis=1)


def gain_step(gains, bit):
    return gains + dp_swap(gains, bit)


def unpack_gains(gains, width):
    return gains[:, :width], gains[:, width:]


def late_start(side, states, grads):
    me = lax.axis_index("dp")
    flat = flat_grad(None, 4 * 1280, side, states, grads, 0, states[0].shape[1], 768, True)
    blocks = flat.reshape(2, 2, 1280, LANES)
    y = (me >> 1) & 1
    return plus(pick(blocks, 1 - y, 1), dp_swap(pick(blocks, y, 1), 2))


def late_end(total):
    me = lax.axis_index("dp")
    y = (me >> 1) & 1
    odd = (me >> 2) & 1
    own = jnp.where(y == 1, odd, 1 - odd)
    total = plus(pick(total, own), dp_swap(pick(total, 1 - own), 4))
    route = []
    for i in range(16):
        z, y_of = i >> 2, (i >> 1) & 1
        goal = 1 if z & 1 else (0 if y_of else 2)
        if z != goal:
            route.append((i, goal * 4 + (i & 3)))
    total = plus(total, lax.ppermute(total, "dp", route))
    far = lax.ppermute(total, "stream", [(1, 0)])
    return jnp.stack([total, far], axis=1).reshape(2 * 1280, LANES)


def merged_keyval(part, late):
    chip = lax.axis_index("dp") >> 1
    low = jnp.where(chip == 1, 1536, 0)
    high = jnp.where((chip >= 1) & (chip <= 4), jnp.where(chip == 4, 2048, 2560), 0)
    high = jnp.where(lax.axis_index("stream") == 0, high, 0)
    rows = lax.broadcasted_iota(jnp.int32, (part.shape[0], 1), 0)
    return jnp.where((rows >= low) & (rows < high), late.astype(F32), part)


def solution(mesh):
    split = P(("stream", "dp"), None)
    flat = P(("stream", "dp"))
    whole = P()
    return jax.shard_map(
        local,
        mesh=mesh,
        in_specs=(split, split, flat) + (whole,) * 16 + (split, split),
        out_specs=(split, split, split, split, flat, flat, whole, whole),
        check_vma=False,
    )
```

```python
import functools

import jax
import jax.numpy as jnp
from jax import lax
from jax.experimental import pallas as pl
from jax.experimental.pallas import tpu as pltpu
from jax.sharding import PartitionSpec as P

H_T = 12
H_I = 8
H_C = 8
D_C = 1024
LANES = 128
UNIT = 256
masked_score = -1e30
F32 = jnp.float32
BF16 = jnp.bfloat16


def mm(a, b):
    return jnp.dot(a, b, preferred_element_type=F32)


def mm_nt(a, b):
    return lax.dot_general(a, b, (((1,), (1,)), ((), ())), preferred_element_type=F32)


def mm_tn(a, b):
    return lax.dot_general(a, b, (((0,), (0,)), ((), ())), preferred_element_type=F32)


def cost(us):
    return pl.CostEstimate(flops=int(us * 1e9), bytes_accessed=1000, transcendentals=0)


def lane_block(ref, rows, block):
    return ref[rows, pl.ds(pl.multiple_of(block * LANES, LANES), LANES)]


def put_block(ref, rows, block, value):
    ref[rows, pl.ds(pl.multiple_of(block * LANES, LANES), LANES)] = value


def split_heads(block, heads_in):
    if heads_in == 1:
        return block
    lanes = lax.broadcasted_iota(jnp.int32, block.shape, 1)
    zero = jnp.zeros_like(block)
    low = lanes < LANES // 2
    return jnp.concatenate([jnp.where(low, block, zero), jnp.where(low, zero, block)], axis=0)


def side_by_side(block, heads_in):
    if heads_in == 1:
        return block
    rows = block.shape[0] // 2
    return jnp.concatenate([block[:rows], block[rows:]], axis=1)


def attend_kernel(
    lens_ref, q_ref, k_ref, v_ref, o_ref, *, pairs, blocks, cols, heads_in, fixed, scaling
):
    ql = q_ref.shape[0] // pairs
    kl = k_ref.shape[0] // pairs
    chain = heads_in * ql
    keys = lax.broadcasted_iota(jnp.int32, (chain, kl), 1)
    if fixed is None:
        masks = [keys < lens_ref[p] for p in range(pairs)]
    else:
        masks = [keys < fixed] * pairs

    @pl.loop(0, blocks)
    def _(j):
        scores = []
        for p in range(pairs):
            q = split_heads(lane_block(q_ref, slice(p * ql, (p + 1) * ql), cols[0] + j), heads_in)
            k = lane_block(k_ref, slice(p * kl, (p + 1) * kl), cols[1] + j)
            scores.append(jnp.where(masks[p], mm_nt(q, k) * scaling, masked_score))
        s = jnp.concatenate(scores, axis=0)
        raised = jnp.exp(s - jnp.max(s, axis=-1, keepdims=True))
        w = (raised * (1.0 / jnp.sum(raised, axis=-1, keepdims=True))).astype(BF16)
        for p in range(pairs):
            v = split_heads(lane_block(v_ref, slice(p * kl, (p + 1) * kl), cols[2] + j), heads_in)
            o = mm(side_by_side(w[p * chain : (p + 1) * chain], heads_in), v)
            put_block(o_ref, slice(p * ql, (p + 1) * ql), j, o.astype(BF16))


def attend(lens, q, k, v, cols, pairs, blocks, heads_in, fixed, scaling):
    rows = q.shape[0]
    krows = k.shape[0]
    same = k is v
    vmem = pl.BlockSpec(memory_space=pltpu.VMEM)
    operands = [lens, q, k] if same else [lens, q, k, v]
    if q is k:
        operands = [lens, q]

    def body(lens_ref, *refs, **kw):
        refs = list(refs)
        o_ref = refs.pop()
        while len(refs) < 3:
            refs.append(refs[-1])
        attend_kernel(lens_ref, *refs, o_ref, **kw)

    return pl.pallas_call(
        functools.partial(
            body,
            pairs=pairs,
            blocks=blocks,
            cols=cols,
            heads_in=heads_in,
            fixed=fixed,
            scaling=scaling,
        ),
        in_specs=[pl.BlockSpec(memory_space=pltpu.SMEM)] + [vmem] * (len(operands) - 1),
        out_specs=vmem,
        out_shape=jax.ShapeDtypeStruct((rows, blocks * LANES), BF16),
        compiler_params=pltpu.CompilerParams(vmem_limit_bytes=24 * 1024 * 1024),
        cost_estimate=cost(5),
        name="attend",
    )(*operands)


def attend_back_kernel(
    lens_ref,
    q_ref,
    k_ref,
    v_ref,
    g_ref,
    dq_ref,
    dk_ref,
    dv_ref,
    *,
    pairs,
    blocks,
    cols,
    out_cols,
    heads_in,
    fixed,
    scaling,
):
    ql = q_ref.shape[0] // pairs
    kl = k_ref.shape[0] // pairs
    keys = lax.broadcasted_iota(jnp.int32, (heads_in * kl, ql), 0)
    if heads_in == 2:
        keys = jnp.where(keys >= kl, keys - kl, keys)
    if fixed is None:
        masks = [keys < lens_ref[p] for p in range(pairs)]
    else:
        masks = [keys < fixed] * pairs

    @pl.loop(0, blocks)
    def _(j):
        scores, slopes = [], []
        for p in range(pairs):
            qs, ks = slice(p * ql, (p + 1) * ql), slice(p * kl, (p + 1) * kl)
            q, g = lane_block(q_ref, qs, cols[0] + j), lane_block(g_ref, qs, j)
            k = split_heads(lane_block(k_ref, ks, cols[1] + j), heads_in)
            v = split_heads(lane_block(v_ref, ks, cols[2] + j), heads_in)
            scores.append(jnp.where(masks[p], mm_nt(k, q) * scaling, masked_score))
            slopes.append(mm_nt(v, g))
        stacked = (pairs * heads_in, kl, ql)
        s = jnp.concatenate(scores, axis=0).reshape(stacked)
        dp = jnp.concatenate(slopes, axis=0).reshape(stacked)
        raised = jnp.exp(s - jnp.max(s, axis=1, keepdims=True))
        w = raised * (1.0 / jnp.sum(raised, axis=1, keepdims=True))
        inner = jnp.sum(w * dp, axis=1, keepdims=True)
        ds = (w * (dp - inner)).astype(BF16).reshape(-1, ql)
        w = w.astype(BF16).reshape(-1, ql)
        chain = heads_in * kl
        for p in range(pairs):
            qs, ks = slice(p * ql, (p + 1) * ql), slice(p * kl, (p + 1) * kl)
            own = slice(p * chain, (p + 1) * chain)
            q = split_heads(lane_block(q_ref, qs, cols[0] + j), heads_in)
            g = split_heads(lane_block(g_ref, qs, j), heads_in)
            k = split_heads(lane_block(k_ref, ks, cols[1] + j), heads_in)
            dq = mm_tn(ds[own], k) * scaling
            dk = mm(side_by_side(ds[own], heads_in), q) * scaling
            dv = mm(side_by_side(w[own], heads_in), g)
            put_block(dq_ref, qs, out_cols[0] + j, dq.astype(BF16))
            put_block(dk_ref, ks, out_cols[1] + j, dk.astype(BF16))
            put_block(dv_ref, ks, out_cols[2] + j, dv.astype(BF16))


def attend_back(lens, q, k, v, g, cols, pairs, blocks, heads_in, fixed, scaling, packed):
    rows = q.shape[0]
    krows = k.shape[0]
    vmem = pl.BlockSpec(memory_space=pltpu.VMEM)
    width = blocks * LANES
    if packed:
        operands = [lens, q, g]
        out_cols = (0, blocks, 2 * blocks)
        out_shape = jax.ShapeDtypeStruct((rows, 3 * width), BF16)
        out_specs = vmem
    else:
        operands = [lens, q, k, g]
        out_cols = (0, 0, blocks)
        out_shape = [
            jax.ShapeDtypeStruct((rows, width), BF16),
            jax.ShapeDtypeStruct((krows, 2 * width), BF16),
        ]
        out_specs = [vmem, vmem]

    def body(lens_ref, *refs, **kw):
        if packed:
            q_ref, g_ref, out_ref = refs
            ins, outs = (q_ref, q_ref, q_ref, g_ref), (out_ref,) * 3
        else:
            q_ref, k_ref, g_ref, dq_ref, dkv_ref = refs
            ins, outs = (q_ref, k_ref, k_ref, g_ref), (dq_ref, dkv_ref, dkv_ref)
        attend_back_kernel(lens_ref, *ins, *outs, **kw)

    return pl.pallas_call(
        functools.partial(
            body,
            pairs=pairs,
            blocks=blocks,
            cols=cols,
            out_cols=out_cols,
            heads_in=heads_in,
            fixed=fixed,
            scaling=scaling,
        ),
        in_specs=[pl.BlockSpec(memory_space=pltpu.SMEM)] + [vmem] * (len(operands) - 1),
        out_specs=out_specs,
        out_shape=out_shape,
        compiler_params=pltpu.CompilerParams(vmem_limit_bytes=24 * 1024 * 1024),
        cost_estimate=cost(6),
        name="attend_back",
    )(*operands)


class Job:
    def __init__(self, a, b, low, high, place):
        self.a, self.b = a, b
        self.low, self.count = low, high - low
        self.columns = b[3]
        self.place = place


def flat_kernel(side_ref, *refs, plans, found, quarter, resident):
    out_ref, chosen_ref, stage_ref = refs[len(found) : len(found) + 3]
    core = side_ref[0]
    depth = chosen_ref.shape[0] // 2
    if not resident:
        a_buf, b_buf, in_sem = refs[-3:]

    def loads(jobs, k):
        job, slot = jobs[k], k % 2
        copies = []
        for side, buf, start, width in (
            (job.a, a_buf, job.a[2] + job.low, job.count),
            (job.b, b_buf, job.b[2], job.columns),
        ):
            for half in range(2):
                copies.append(
                    pltpu.make_async_copy(
                        refs[found[id(side[half])]].at[:, start : start + width],
                        buf.at[slot, half * depth : (half + 1) * depth, 0:width],
                        in_sem.at[slot, len(copies)],
                    )
                )
        return copies

    def run(jobs):
        if not resident:
            for copy in loads(jobs, 0):
                copy.start()
        for k, job in enumerate(jobs):
            if resident:
                a_refs = [refs[found[id(job.a[half])]] for half in range(2)]
                b_refs = [refs[found[id(job.b[half])]] for half in range(2)]
                a_first, b_first = job.a[2] + job.low, job.b[2]
            else:
                if k + 1 < len(jobs):
                    for copy in loads(jobs, k + 1):
                        copy.start()
                for copy in loads(jobs, k):
                    copy.wait()
                halves = [slice(0, depth), slice(depth, 2 * depth)]
                a_refs = [a_buf.at[k % 2, half] for half in halves]
                b_refs = [b_buf.at[k % 2, half] for half in halves]
                a_first = b_first = 0
            units = job.columns // (2 * UNIT if quarter else UNIT)
            for u in range(units):
                at = 4 * u + 2 * side_ref[1] + core if quarter else 2 * u + core
                block = pl.ds(pl.multiple_of(at * LANES + b_first, LANES), LANES)
                for half in range(2):
                    chosen_ref[half * depth : (half + 1) * depth, u * LANES : (u + 1) * LANES] = (
                        b_refs[half][:, block]
                    )
            bm = best_rows(job.count, units)
            rows = bm * units
            for i in range(job.count // bm):
                columns = slice(a_first + i * bm, a_first + (i + 1) * bm)
                a = jnp.concatenate([a_ref[:, columns] for a_ref in a_refs], axis=0).T
                for u0 in range(0, units, 4):
                    u1 = min(u0 + 4, units)
                    total = mm(a, chosen_ref[:, u0 * LANES : u1 * LANES])
                    for u in range(u0, u1):
                        stage_ref[pl.ds(u, bm, stride=units), :] = total[
                            :, (u - u0) * LANES : (u - u0 + 1) * LANES
                        ]
                first = job.place + i * rows
                out_ref[first : first + rows, :] = stage_ref[:rows].astype(BF16)

    if len(plans) == 1:
        run(plans[0])
    else:
        for side, jobs in enumerate(plans):

            @pl.when(side_ref[1] == side)
            def _(jobs=jobs):
                run(jobs)


def best_rows(count, units):
    most = 512 if units <= 8 else 384
    return max(size for size in range(LANES, most + 1, LANES) if count % size == 0)


def flat_grads(side, total_rows, plans, us, quarter=False, resident=True):
    arrays, found = [], {}
    jobs = [job for plan in plans for job in plan]
    for job in jobs:
        for array in (*job.a[:2], *job.b[:2]):
            if id(array) not in found:
                found[id(array)] = len(arrays)
                arrays.append(array)
    depth = 2 * arrays[0].shape[0]
    widest = max(job.columns for job in jobs)
    tallest = max(job.count for job in jobs)
    factor = 2 * UNIT if quarter else UNIT
    rows = max(best_rows(job.count, job.columns // factor) * job.columns // factor for job in jobs)
    held = 2 * depth * widest * LANES // factor + 4 * rows * LANES
    scratch = [
        pltpu.VMEM((depth, widest * LANES // factor), BF16),
        pltpu.VMEM((rows, LANES), F32),
    ]
    if not resident:
        held += 4 * depth * (tallest + widest)
        scratch += [
            pltpu.VMEM((2, depth, tallest), BF16),
            pltpu.VMEM((2, depth, widest), BF16),
            pltpu.SemaphoreType.DMA((2, 4)),
        ]
    place = pltpu.VMEM if resident else pltpu.HBM
    return pl.pallas_call(
        functools.partial(
            flat_kernel, plans=plans, found=found, quarter=quarter, resident=resident
        ),
        in_specs=[pl.BlockSpec(memory_space=pltpu.SMEM)]
        + [pl.BlockSpec(memory_space=place)] * len(arrays),
        out_specs=pl.BlockSpec(memory_space=pltpu.VMEM),
        out_shape=jax.ShapeDtypeStruct((total_rows, LANES), BF16),
        scratch_shapes=scratch,
        compiler_params=pltpu.CompilerParams(vmem_limit_bytes=held + 6 * 1024 * 1024),
        cost_estimate=cost(us),
        name="flat_grads",
    )(side, *arrays)


def dp_swap(block, bit):
    count = lax.axis_size("dp")
    return lax.ppermute(block, "dp", [(i, i ^ bit) for i in range(count)])


def stream_swap(block):
    return lax.ppermute(block, "stream", [(0, 1), (1, 0)])


def pick(block, index, axis=0):
    return lax.dynamic_index_in_dim(block, index, axis, keepdims=False)


def plus(a, b):
    return (a.astype(F32) + b.astype(F32)).astype(BF16)


def tied(*values):
    return lax.optimization_barrier(values)


def scatter_parts(flat, cuts):
    count = lax.axis_size("dp")
    top = count.bit_length() - 2
    bits = tuple(range(top, 0, -1))
    rows = flat.shape[0] // (count // 2)
    blocks = flat.reshape((2,) * len(bits) + (rows, LANES))
    natural = tuple(range(1, top + 1))
    turned = natural[1:2] + natural[:1] + natural[2:]
    parts, start = [], 0
    for share, turn in cuts:
        part = lax.slice_in_dim(blocks, start, start + rows * share // 8, axis=len(bits))
        start += rows * share // 8
        parts.append((part, bits, turned if turn else natural))
    return parts


def scatter_step(parts):
    me = lax.axis_index("dp")
    done = []
    for block, left, order in parts:
        bit = order[0]
        axis = left.index(bit)
        mine = (me >> bit) & 1
        keep = pick(block, mine, axis)
        far = dp_swap(pick(block, 1 - mine, axis), 1 << bit)
        block = plus(keep, far) if len(order) > 1 else keep.astype(F32) + far.astype(F32)
        done.append((block, left[:axis] + left[axis + 1 :], order[1:]))
    return done


def scatter_end(parts):
    while parts[0][2]:
        parts = scatter_step(parts)
    blocks = [block for block, _, _ in parts]
    return jnp.concatenate(blocks) if len(blocks) > 1 else blocks[0]


def reduce_scatter(flat, cuts):
    return scatter_end(scatter_parts(flat, cuts))


def share_of(result):
    core = lax.axis_index("dp") & 1
    halves = result.reshape(2, result.shape[0] // 2, LANES)
    mine = pick(halves, core)
    far = dp_swap(pick(halves, 1 - core), 1)
    first = jnp.where(core == 0, mine, far)
    second = jnp.where(core == 0, far, mine)
    return jnp.stack([first, second], axis=1).reshape(-1)


def choices(stream):
    me = lax.axis_index("dp")
    y, odd = (me >> 1) & 1, (me >> 2) & 1
    own = jnp.where(y == 1, odd, 1 - odd)
    values = [me & 1, y, odd, (me >> 3) & 1, 1 - y, own, stream, me >> 1]
    return jnp.stack(values).astype(jnp.int32)


LATE_Y, LATE_OWN, STREAM, CHIP = 4, 5, 6, 7


def split_kernel(choice_ref, flat_ref, *refs, chunk, cuts):
    for k, (start, rows, bases, weight, which) in enumerate(cuts):
        mine = choice_ref[which]
        for i, base in enumerate(bases):
            for out_ref, index in ((refs[2 * k], mine), (refs[2 * k + 1], 1 - mine)):
                first = (base + index * weight) * chunk + start
                out_ref[i] = flat_ref[pl.ds(pl.multiple_of(first, 16), rows), :]


def split(choice, flat, chunk, cuts):
    shapes = [
        jax.ShapeDtypeStruct((len(bases), rows, LANES), BF16)
        for _, rows, bases, _, _ in cuts
        for _ in range(2)
    ]
    return pl.pallas_call(
        functools.partial(split_kernel, chunk=chunk, cuts=cuts),
        in_specs=[
            pl.BlockSpec(memory_space=pltpu.SMEM),
            pl.BlockSpec(memory_space=pltpu.VMEM),
        ],
        out_specs=[pl.BlockSpec(memory_space=pltpu.VMEM)] * len(shapes),
        out_shape=shapes,
        compiler_params=pltpu.CompilerParams(vmem_limit_bytes=4 * 1024 * 1024),
        cost_estimate=cost(3),
        name="split",
    )(choice, flat)


def paced(came, leaving, values=()):
    got = tied(*(item.far for item in came), *(item.out for item in leaving), *values)
    for item, array in zip(came, got):
        item.far = array
    for item, array in zip(leaving, got[len(came) :]):
        item.out = array
    return got[len(came) + len(leaving) :]


def added(a_ref, b_ref, index):
    return a_ref[index].astype(F32) + b_ref[index].astype(F32)


def add_split_kernel(choice_ref, keep_ref, far_ref, stay_ref, send_ref, *, pre, post, which):
    mine = choice_ref[which]
    for p in range(pre):
        for q in range(post):
            at = p * post + q
            for out_ref, index in ((stay_ref, mine), (send_ref, 1 - mine)):
                out_ref[at] = added(keep_ref, far_ref, (2 * p + index) * post + q).astype(BF16)


def add_split(choice, keep, far, pre, post, which):
    shape = jax.ShapeDtypeStruct((pre * post,) + keep.shape[1:], BF16)
    vmem = pl.BlockSpec(memory_space=pltpu.VMEM)
    return pl.pallas_call(
        functools.partial(add_split_kernel, pre=pre, post=post, which=which),
        in_specs=[pl.BlockSpec(memory_space=pltpu.SMEM), vmem, vmem],
        out_specs=[vmem] * 2,
        out_shape=[shape] * 2,
        compiler_params=pltpu.CompilerParams(vmem_limit_bytes=8 * 1024 * 1024),
        cost_estimate=cost(1),
        name="add_split",
    )(choice, keep, far)


def piece_set(choice, flat, orders, shares=None):
    chunk = flat.shape[0] // 8
    shares = shares or (1,) * len(orders)
    unit = chunk // sum(shares)
    cuts, pieces, start = [], [], 0
    for order, share in zip(orders, shares):
        rows = unit * share
        bits = [3, 2, 1]
        bits.remove(order[0])
        bases = tuple(
            sum(((n >> (1 - at)) & 1) << (b - 1) for at, b in enumerate(bits)) for n in range(4)
        )
        cuts.append((start, rows, bases, 1 << (order[0] - 1), order[0]))
        start += rows
        pieces.append(Piece(choice, bits, order))
    arrays = split(choice, flat, chunk, tuple(cuts))
    for i, piece in enumerate(pieces):
        piece.keep, piece.out = arrays[2 * i : 2 * i + 2]
    return pieces


class Piece:
    def __init__(self, choice, bits, order):
        self.choice = choice
        self.bits = bits
        self.order = list(order)

    def send(self):
        self.far = dp_swap(self.out, 1 << self.order.pop(0))

    def turn(self):
        bit = self.order[0]
        at = self.bits.index(bit)
        self.bits.remove(bit)
        pre = 1 << at
        self.keep, self.out = add_split(
            self.choice, self.keep, self.far, pre, self.keep.shape[0] // (2 * pre), bit
        )


def after(value, pieces, name="far"):
    value, *got = tied(value, *(getattr(piece, name) for piece in pieces))
    for piece, array in zip(pieces, got):
        setattr(piece, name, array)
    return value


def finish_kernel(choice_ref, *refs, counts):
    refs = list(refs)
    pairs = [[(refs.pop(0), refs.pop(0)) for _ in range(count)] for count in counts]
    near_ref, far_ref = refs.pop(0), refs.pop(0)
    out_ref, send_ref, *totals, joined_ref = refs
    for total_ref, group in zip(totals, pairs):
        row = 0
        for keep_ref, came_ref in group:
            rows = keep_ref.shape[1]
            total_ref[row : row + rows] = added(keep_ref, came_ref, 0)
            row += rows
    half = near_ref.shape[0]
    joined_ref[pl.ds(0, half, stride=2), :] = near_ref[...].astype(F32)
    joined_ref[pl.ds(1, half, stride=2), :] = far_ref[...].astype(F32)
    image_ref = totals[0]
    rows = image_ref.shape[0]
    chip = choice_ref[CHIP]
    first = jnp.where(chip == 1, 1536, 0)
    last = jnp.where(chip == 4, 2048, rows)
    here = (chip >= 1) & (chip <= 4) & (choice_ref[STREAM] == 0)
    last = jnp.where(here, last, 0)
    at = lax.broadcasted_iota(jnp.int32, (rows, 1), 0)
    image_ref[...] = jnp.where((at >= first) & (at < last), joined_ref[...], image_ref[...])
    core = choice_ref[0]
    row = 0
    for total_ref in totals:
        half = total_ref.shape[0] // 2
        for ref, index in ((out_ref, core), (send_ref, 1 - core)):
            ref[row : row + half, :] = total_ref[pl.ds(pl.multiple_of(index * half, 8), half), :]
        row += half


def join_kernel(choice_ref, near_ref, far_ref, *outs):
    core = choice_ref[0]
    row = 0
    for out_ref in outs:
        half = out_ref.shape[0] // 2
        out_ref[pl.ds(core, half, stride=2), :] = near_ref[row : row + half, :]
        out_ref[pl.ds(1 - core, half, stride=2), :] = far_ref[row : row + half, :]
        row += half


def finished(choice, image_pieces, late, text_pieces):
    groups = (image_pieces, text_pieces)
    sizes = [sum(piece.keep.shape[1] for piece in group) for group in groups]
    vmem = pl.BlockSpec(memory_space=pltpu.VMEM)
    smem = pl.BlockSpec(memory_space=pltpu.SMEM)
    operands = [ref for group in groups for piece in group for ref in (piece.keep, piece.far)]
    operands += list(late)
    half = jax.ShapeDtypeStruct((sum(sizes) // 2, LANES), F32)
    near, send = pl.pallas_call(
        functools.partial(finish_kernel, counts=[len(group) for group in groups]),
        in_specs=[smem] + [vmem] * len(operands),
        out_specs=[vmem] * 2,
        out_shape=[half] * 2,
        scratch_shapes=[pltpu.VMEM((rows, LANES), F32) for rows in (*sizes, sizes[0])],
        compiler_params=pltpu.CompilerParams(vmem_limit_bytes=16 * 1024 * 1024),
        cost_estimate=cost(3),
        name="finish",
    )(choice, *operands)
    joined = pl.pallas_call(
        join_kernel,
        in_specs=[smem, vmem, vmem],
        out_specs=[vmem] * 2,
        out_shape=[jax.ShapeDtypeStruct((rows, LANES), F32) for rows in sizes],
        compiler_params=pltpu.CompilerParams(vmem_limit_bytes=8 * 1024 * 1024),
        cost_estimate=cost(2),
        name="join",
    )(choice, near, dp_swap(send, 1))
    return [block.reshape(-1) for block in joined]


CHUNK = 64
ROWS = 128
WIDEST = 1024
WIDEST_GELU = 1024


def tiles(columns, body, widest=None):
    size = max(c for c in range(LANES, (widest or WIDEST) + 1, LANES) if columns % c == 0)
    if size == columns:
        return body(slice(0, columns))

    @pl.loop(0, columns // size)
    def _(j):
        body(pl.ds(pl.multiple_of(j * size, size), size))


def views(pack_ref, *widths):
    found, start = [], 0
    for width in widths:
        found.append(pack_ref.at[:, start : start + width])
        start += width
    return found


def row_chunks(rows, body):
    size = ROWS if rows % ROWS == 0 else CHUNK

    @pl.loop(0, rows // size)
    def _(i):
        body(i * size, pl.ds(pl.multiple_of(i * size, size), size), size)


def normed_chunk(a):
    centred = a - jnp.mean(a, axis=-1, keepdims=True)
    inverse = lax.rsqrt(jnp.mean(centred * centred, axis=-1, keepdims=True) + 1e-05)
    return centred * inverse, inverse


def normed_back_chunk(grad, n, inverse, gain_row):
    scaled = grad * gain_row
    low = jnp.mean(scaled, axis=-1, keepdims=True)
    tilt = jnp.mean(scaled * n, axis=-1, keepdims=True)
    return (scaled - low - n * tilt) * inverse, jnp.sum(grad * n, axis=0, keepdims=True)


def co_kernel(
    lens_ref, x_ref, o_ref, g_ref, wq_ref, wkv_ref, wat_ref,
    q_ref, kv_ref, pack_ref, n_ref, inv_ref, a_ref, *, pairs, fixed, scaling,
):
    rows, width = x_ref.shape
    c_ref, h_ref = views(pack_ref, D_C, width)

    def kv_tile(cols):
        kv_ref[:, cols] = mm(o_ref[...], wkv_ref[:, cols]).astype(BF16)

    def q_tile(cols):
        q_ref[:, cols] = mm(x_ref[...], wq_ref[:, cols]).astype(BF16)

    def a_tile(cols):
        a_ref[:, cols] = x_ref[:, cols].astype(F32) + mm(c_ref[...], wat_ref[:, cols])

    def norm(i, at, size):
        n, inverse = normed_chunk(a_ref[at, :])
        n_ref[at, :] = n
        inv_ref[at, :] = jnp.broadcast_to(inverse, (size, LANES))
        h_ref[at, :] = (n * g_ref[0:1, :]).astype(BF16)

    tiles(kv_ref.shape[1], kv_tile)
    tiles(q_ref.shape[1], q_tile)
    blocks = q_ref.shape[1] // LANES
    attend_kernel(
        lens_ref, q_ref, kv_ref, kv_ref, c_ref, pairs=pairs, blocks=blocks,
        cols=(0, 0, blocks), heads_in=1, fixed=fixed, scaling=scaling,
    )
    tiles(width, a_tile)
    row_chunks(rows, norm)


def mlp_kernel(
    pack1_ref, n1_ref, g_ref, wup_ref, wdown_ref, wqkv_ref,
    pack_ref, slope_ref, n_ref, inv_ref, r_ref, a_ref,
):
    rows, width = n1_ref.shape
    _, h1_ref = views(pack1_ref, D_C, width)
    hid_ref, h_ref = views(pack_ref, wup_ref.shape[1], width)

    def up_tile(cols):
        u_all = mm(h1_ref[...], wup_ref[:, cols])
        for at in range(0, rows, CHUNK):
            u = u_all[at : at + CHUNK]
            share = 0.5 + 0.5 * lax.erf(u * 0.7071067811865476)
            hid_ref[at : at + CHUNK, cols] = (u * share).astype(BF16)
            slope = share + u * (0.3989422804014327 * jnp.exp(-0.5 * u * u))
            slope_ref[at : at + CHUNK, cols] = slope.astype(BF16)

    def down_tile(cols):
        a_ref[:, cols] = n1_ref[:, cols] * g_ref[0:1, cols] + mm(hid_ref[...], wdown_ref[:, cols])

    def norm(i, at, size):
        n, inverse = normed_chunk(a_ref[at, :])
        n_ref[at, :] = n
        inv_ref[at, :] = jnp.broadcast_to(inverse, (size, LANES))
        h_ref[at, :] = (n * g_ref[1:2, :]).astype(BF16)

    def qkv_tile(cols):
        r_ref[:, cols] = mm(h_ref[...], wqkv_ref[:, cols]).astype(BF16)

    tiles(wup_ref.shape[1], up_tile, WIDEST_GELU)
    tiles(width, down_tile)
    row_chunks(rows, norm)
    tiles(r_ref.shape[1], qkv_tile)


def self_kernel(
    lens_ref, r_ref, n2_ref, g_ref, wout_ref, cot_ref,
    pack_ref, y_ref, de_ref, dg_ref, a_ref, dz_ref,
    *, pairs, heads_in, fixed, scaling,
):
    rows, width = n2_ref.shape
    z_ref, de_low_ref, dr_ref = views(pack_ref, width, width, 3 * width)
    blocks = width // LANES
    cols = (0, blocks, 2 * blocks)
    shared = dict(
        pairs=pairs, blocks=blocks, cols=cols, heads_in=heads_in, fixed=fixed, scaling=scaling
    )

    def out_tile(at):
        a_ref[:, at] = n2_ref[:, at] * g_ref[1:2, at] + mm(z_ref[...], wout_ref[:, at])

    def last(start, at, size):
        n, inverse = normed_chunk(a_ref[at, :])
        y = n * g_ref[2:3, :]
        grad = cot_ref[at, :].astype(F32)
        if fixed is None:
            slots = rows // pairs
            place = lax.broadcasted_iota(jnp.int32, (size, 1), 0) + lax.rem(start, slots)
            valid = (place < lens_ref[lax.div(start, slots)]).astype(F32)
            y, grad = y * valid, grad * valid
        y_ref[at, :] = y.astype(BF16)
        de, dg = normed_back_chunk(grad, n, inverse, g_ref[2:3, :])
        de_ref[at, :] = de
        de_low_ref[at, :] = de.astype(BF16)
        dg_ref[...] += dg

    def dz_tile(at):
        dz_ref[:, at] = mm_nt(de_low_ref[...], wout_ref[at, :]).astype(BF16)

    attend_kernel(lens_ref, r_ref, r_ref, r_ref, z_ref, **shared)
    tiles(width, out_tile)
    dg_ref[...] = jnp.zeros_like(dg_ref)
    row_chunks(rows, last)
    tiles(width, dz_tile)
    attend_back_kernel(
        lens_ref, r_ref, r_ref, r_ref, dz_ref, dr_ref, dr_ref, dr_ref, out_cols=cols, **shared
    )


def back_kernel(
    pack3_ref, de_ref, n2_ref, inv2_ref, n1_ref, inv1_ref, g_ref, slope_ref,
    wqkv_ref, wdown_ref, wup_ref, wat_ref,
    pack_ref, da_ref, dc_ref, dg_ref, a_ref, db_ref,
):
    rows, width = n1_ref.shape
    _, _, dr_ref = views(pack3_ref, width, width, 3 * width)
    db_low_ref, du_ref, da_low_ref = views(pack_ref, width, slope_ref.shape[1], width)
    dg_ref[...] = jnp.zeros_like(dg_ref)

    def second_tile(at):
        a_ref[:, at] = de_ref[:, at] + mm_nt(dr_ref[...], wqkv_ref[at, :])

    def second_norm(i, at, size):
        db, dg = normed_back_chunk(a_ref[at, :], n2_ref[at, :], inv2_ref[at, 0:1], g_ref[1:2, :])
        db_ref[at, :] = db
        db_low_ref[at, :] = db.astype(BF16)
        dg_ref[1:2, :] += dg

    def du_tile(at):
        grad = mm_nt(db_low_ref[...], wdown_ref[at, :])
        du_ref[:, at] = (grad * slope_ref[:, at].astype(F32)).astype(BF16)

    def first_tile(at):
        a_ref[:, at] = db_ref[:, at] + mm_nt(du_ref[...], wup_ref[at, :])

    def first_norm(i, at, size):
        da, dg = normed_back_chunk(a_ref[at, :], n1_ref[at, :], inv1_ref[at, 0:1], g_ref[0:1, :])
        da_ref[at, :] = da
        da_low_ref[at, :] = da.astype(BF16)
        dg_ref[0:1, :] += dg

    def dc_tile(at):
        dc_ref[:, at] = mm_nt(da_low_ref[...], wat_ref[at, :]).astype(BF16)

    tiles(width, second_tile)
    row_chunks(rows, second_norm)
    tiles(du_ref.shape[1], du_tile, WIDEST_GELU)
    tiles(width, first_tile)
    row_chunks(rows, first_norm)
    tiles(dc_ref.shape[1], dc_tile)


def fused(kernel, operands, outs, scratch, name, us, smem_first=False, limit=14):
    vmem = pl.BlockSpec(memory_space=pltpu.VMEM)
    in_specs = [vmem] * len(operands)
    if smem_first:
        in_specs[0] = pl.BlockSpec(memory_space=pltpu.SMEM)
    return pl.pallas_call(
        kernel,
        in_specs=in_specs,
        out_specs=[vmem] * len(outs),
        out_shape=[jax.ShapeDtypeStruct(shape, kind) for shape, kind in outs],
        scratch_shapes=[pltpu.VMEM(shape, kind) for shape, kind in scratch],
        compiler_params=pltpu.CompilerParams(vmem_limit_bytes=limit * 1024 * 1024),
        cost_estimate=cost(us),
        name=name,
    )(*operands)


def co_forward(lens, states, other, gains, query_w, keyval_w, attend_w, pairs, fixed):
    rows, width = states.shape
    orows = other.shape[0]
    return fused(
        functools.partial(co_kernel, pairs=pairs, fixed=fixed, scaling=(D_C // H_C) ** (-0.5)),
        (lens, states, other, gains, query_w, keyval_w, attend_w),
        [
            ((rows, D_C), BF16),
            ((orows, 2 * D_C), BF16),
            ((rows, D_C + width), BF16),
            ((rows, width), F32),
            ((rows, LANES), F32),
        ],
        [((rows, width), F32)],
        "co_forward",
        9,
        True,
    )


def mlp_forward(pack1, n1, gains, up_w, down_w, qkv_w):
    rows, width = n1.shape
    hidden = up_w.shape[1]
    return fused(
        mlp_kernel,
        (pack1, n1, gains, up_w, down_w, qkv_w),
        [
            ((rows, hidden + width), BF16),
            ((rows, hidden), BF16),
            ((rows, width), F32),
            ((rows, LANES), F32),
            ((rows, 3 * width), BF16),
        ],
        [((rows, width), F32)],
        "mlp_forward",
        rows / 40,
    )


def self_turn(lens, r, n2, gains, output_w, cot, pairs, heads, fixed):
    rows, width = n2.shape
    size = width // heads
    return fused(
        functools.partial(
            self_kernel, pairs=pairs, heads_in=LANES // size, fixed=fixed, scaling=size ** (-0.5)
        ),
        (lens, r, n2, gains, output_w, cot),
        [
            ((rows, 5 * width), BF16),
            ((rows, width), BF16),
            ((rows, width), F32),
            ((1, width), F32),
        ],
        [((rows, width), F32), ((rows, width), BF16)],
        "self_turn",
        rows / 128 + 9,
        True,
    )


def rest_back(pack3, de, n2, inv2, n1, inv1, gains, slope, qkv_w, down_w, up_w, attend_w):
    rows, width = n1.shape
    return fused(
        back_kernel,
        (pack3, de, n2, inv2, n1, inv1, gains, slope, qkv_w, down_w, up_w, attend_w),
        [
            ((rows, 2 * width + up_w.shape[1]), BF16),
            ((rows, width), F32),
            ((rows, D_C), BF16),
            ((2, width), F32),
        ],
        [((rows, width), F32), ((rows, width), F32)],
        "rest_back",
        rows / 36,
    )


class Exchange:
    def __init__(self):
        self.far = {}
        self.pending = []
        self.parts = None

    def send(self, **arrays):
        for name, array in arrays.items():
            self.far[name] = dp_swap(array, 1)
            self.pending.append(name)

    def settle(self, value):
        names, self.pending = self.pending, []
        if names:
            value, *got = tied(value, *(self.far[name] for name in names))
            self.far.update(zip(names, got))
        return value

    def pair(self, name, array, start=0, width=None):
        return array, self.far[name], start, width or array.shape[1]


def stream_forward(
    lens, states, other, cot, weights, gains, heads, fixed, other_fixed, pairs, moves, hook
):
    query_w, other_keyval_w, attend_w, up_w, down_w, qkv_w, output_w = weights
    q, kv, pack1, n1, inv1 = co_forward(
        lens, states, other, gains, query_w, other_keyval_w, attend_w, pairs, other_fixed
    )
    pack1 = moves.settle(hook("co", pack1))
    moves.send(pack1=pack1)
    pack2, slope, n2, inv2, r = mlp_forward(pack1, n1, gains, up_w, down_w, qkv_w)
    r, pack2 = tied(moves.settle(hook("mlp", r)), pack2)
    moves.send(pack2=pack2)
    pack3, result, de, dg2 = self_turn(lens, r, n2, gains, output_w, cot, pairs, heads, fixed)
    pack3 = moves.settle(hook("self", pack3))
    moves.send(pack3=pack3)
    pack4, da, dc, dg = rest_back(
        pack3, de, n2, inv2, n1, inv1, gains, slope, qkv_w, down_w, up_w, attend_w
    )
    dc, pack4 = tied(moves.settle(hook("back", dc)), pack4)
    moves.send(pack4=pack4)
    width, hidden = up_w.shape

    def sides(dq):
        def side(number, start, count):
            pack = (pack1, pack2, pack3, pack4)[number - 1]
            return moves.pair("pack%d" % number, pack, start, count)

        return {
            "query": (moves.pair("states", states), moves.pair("dq", dq)),
            "attend": (side(1, 0, D_C), side(4, width + hidden, width)),
            "up": (side(1, D_C, width), side(4, width, hidden)),
            "down": (side(2, 0, hidden), side(4, 0, width)),
            "qkv": (side(2, hidden, width), side(3, 2 * width, 3 * width)),
            "output": (side(3, 0, width), side(3, width, width)),
        }

    return result, da, dc, q, kv, sides, jnp.concatenate([dg, dg2])


NAMES = ("query", "keyval", "attend", "up", "down", "qkv", "output")


def half_jobs(both, sizes, total):
    plans, filled = ([], []), 0
    for name in NAMES:
        m, n = sizes[name]
        room = min(max((total // 2 - filled) // n, 0), m)
        for plan, low, high in ((plans[0], 0, room), (plans[1], room, m)):
            if low < high and name in both:
                start = filled + low * n - (0 if plan is plans[0] else total // 2)
                step = 1536 if (high - low) > 1536 else high - low
                for at in range(low, high, step):
                    place = (start + (at - low) * n) // UNIT
                    plan.append(Job(*both[name], at, at + step, place))
        filled += m * n
    return plans


def spread(count, regions, padded, offset, rows):
    target = lax.broadcasted_iota(jnp.int32, (rows, count * regions), 0) - offset
    source = lax.broadcasted_iota(jnp.int32, (rows, count * regions), 1)
    return (target == source // regions * padded + source % regions).astype(BF16)


def local(
    text_states,
    image_states,
    caption_lengths,
    text_query,
    text_keyval,
    text_attend,
    text_up,
    text_down,
    text_qkv,
    text_output,
    text_gains,
    image_query,
    image_keyval,
    image_attend,
    image_up,
    image_down,
    image_qkv,
    image_output,
    image_gains,
    text_cotangent,
    image_cotangent,
):
    own_pairs = caption_lengths.shape[0]
    own_text = text_states.shape[0]
    text_len = own_text // own_pairs
    regions = image_states.shape[0] // own_pairs
    padded = -(-regions // 16) * 16
    own_image = own_pairs * padded
    pairs = 2 * own_pairs
    d_t, d_i = text_states.shape[1], image_states.shape[1]
    stream = lax.axis_index("stream")
    core = lax.axis_index("dp") & 1
    side = jnp.stack([core, stream]).astype(jnp.int32)

    far_put = spread(own_pairs, regions, padded, 0, 2 * own_image)
    near_put = spread(own_pairs, regions, padded, own_image, 2 * own_image)
    trim = near_put[own_image:].T

    def both_images(near):
        return (mm(far_put, stream_swap(near)) + mm(near_put, near)).astype(BF16)

    choice = choices(stream)
    image_all = both_images(image_states)
    far_text = stream_swap(text_states)
    text_all = jnp.concatenate([text_states, far_text])
    lens = jnp.concatenate([caption_lengths, stream_swap(caption_lengths)])
    image_cotangent, text_cotangent, text_all = tied(image_cotangent, text_cotangent, text_all)
    image_cot = both_images(image_cotangent)
    far_text_cot = stream_swap(text_cotangent)

    co_blocks = D_C // LANES
    co_cols = (0, 0, co_blocks)
    co_scale = (D_C // H_C) ** (-0.5)

    image_moves, text_moves = Exchange(), Exchange()
    image_moves.send(states=image_all)
    cots = [far_text_cot]

    def image_hook(name, value):
        if name == "self":
            value, cots[0] = tied(value, cots[0])
        return value

    image_out, image_da, image_dc, image_q, text_kv, image_sides, image_dg = stream_forward(
        lens,
        image_all,
        text_all,
        image_cot,
        (image_query, text_keyval, image_attend, image_up, image_down, image_qkv, image_output),
        image_gains,
        H_I,
        regions,
        None,
        pairs,
        image_moves,
        image_hook,
    )
    image_dq, text_dkv = attend_back(
        lens, image_q, text_kv, text_kv, image_dc, co_cols, pairs, co_blocks, 1, None, co_scale, False
    )
    image_moves.send(dq=image_dq)
    image_sides = image_sides(image_dq)
    text_moves.send(states=text_all, dkv=text_dkv)

    def sizes_of(*weights):
        return {name: weight.shape for name, weight in zip(NAMES, weights)}

    def gather_half(both, sizes):
        total = sum(m * n for m, n in sizes.values())
        total_rows = total // (2 * UNIT)
        plans = half_jobs(both, sizes, total)
        image = both["query"][0][0] is image_all
        return flat_grads(side, total_rows, plans, 6 if image else 14, resident=image)

    image_sizes = sizes_of(
        image_query, image_keyval, image_attend, image_up, image_down, image_qkv, image_output
    )
    text_sizes = sizes_of(
        text_query, text_keyval, text_attend, text_up, text_down, text_qkv, text_output
    )
    early = lax.axis_size("dp") == 16
    if early:
        image_flat = gather_half(image_sides, image_sizes)

    pieces = []

    def hook(name, value):
        if not early:
            return value
        if name == "co":
            value, flat = tied(value, image_flat)
            pieces.extend(piece_set(choice, flat, ((1, 2, 3), (2, 1, 3), (1, 2, 3), (2, 1, 3))))
            value = after(value, pieces, "out")
            for piece in pieces[:2]:
                piece.send()
        if name == "mlp":
            value = after(value, pieces[:2])
            for piece in pieces[:2]:
                piece.turn()
            for piece in pieces[2:]:
                piece.send()
            value = after(value, pieces[:2], "out")
        if name == "self":
            value = after(value, pieces[2:])
            for piece in pieces[2:]:
                piece.turn()
            for piece in pieces:
                piece.send()
        if name == "back":
            value = after(value, pieces)
            for piece in pieces:
                piece.turn()
            for piece in pieces:
                piece.send()
        return value

    text_out, text_da, text_dc, text_q, image_kv, text_sides, text_dg = stream_forward(
        lens,
        text_all,
        image_all,
        jnp.concatenate([text_cotangent, cots[0]]),
        (text_query, image_keyval, text_attend, text_up, text_down, text_qkv, text_output),
        text_gains,
        H_T,
        None,
        regions,
        pairs,
        text_moves,
        hook,
    )
    gains = pack_gains(text_dg, image_dg)
    bits = [1 << b for b in range(lax.axis_size("dp").bit_length() - 1)]
    gains = gain_step(gains, bits.pop())
    text_dq, image_dkv = attend_back(
        lens, text_q, image_kv, image_kv, text_dc, co_cols, pairs, co_blocks, 1, regions, co_scale, False
    )

    text_dq, image_dkv, gains = tied(text_dq, image_dkv, gains)
    gains = gain_step(gains, bits.pop())

    image_moves.send(dkv=image_dkv)
    text_moves.send(dq=text_dq)
    text_sides = text_sides(text_dq)
    text_sides["keyval"] = (text_moves.pair("states", text_all), text_moves.pair("dkv", text_dkv))
    if early:
        late = Late(
            choice,
            side,
            image_moves.pair("states", image_all),
            image_moves.pair("dkv", image_dkv),
        )
        near_dq, *rest = text_sides["query"][1]
        near_dq, late.out, gains = tied(near_dq, late.out, gains)
        text_sides["query"] = (text_sides["query"][0], (near_dq, *rest))
        late.send(2)
        gains = gain_step(gains, bits.pop())
        text_flat = gather_half(text_sides, text_sizes)
        text_flat, gains = tied(after(text_flat, pieces + [late]), gains)
        text_pieces = piece_set(
            choice, text_flat, ((1, 2, 3), (1, 2, 3), (1, 2, 3), (2, 1, 3)), (48, 48, 24, 36)
        )
    else:
        image_sides["keyval"] = (
            image_moves.pair("states", image_all),
            image_moves.pair("dkv", image_dkv),
        )
        image_part = reduce_scatter(gather_half(image_sides, image_sizes), ((8, False),))
        text_flat = gather_half(text_sides, text_sizes)
        text_part = reduce_scatter(text_flat, ((8, False),))
    while bits:
        gains = gain_step(gains, bits.pop())

    near = [
        block[:own_text] for block in (text_da, text_dq, text_dkv, text_out)
    ] + [block[own_image:] for block in (image_da, image_dq, image_dkv, image_out)]
    if early:
        first, *near = tied(text_pieces[0].out, *near)
        text_pieces[0].out = first
    text_da, text_dq, text_dkv, text_result, image_da, image_dq, image_dkv, image_out = near
    image_result = mm(trim, image_out).astype(BF16)
    text_grad = (text_da + mm_nt(text_dq, text_query) + mm_nt(text_dkv, text_keyval)).astype(BF16)
    image_grad = (
        image_da + mm_nt(image_dq, image_query) + mm_nt(image_dkv, image_keyval)
    ).astype(BF16)
    image_grad = mm(trim, image_grad).astype(BF16)

    if early:
        one, two, three, turned = text_pieces
        one.send()
        turned.send()
        late.turn(LATE_OWN)
        text_grad, image_grad, image_result, gains = paced(
            (one, turned), (two, late), (text_grad, image_grad, image_result, gains)
        )
        one.turn()
        two.send()
        one.send()
        late.send(4)
        paced((one, two, late), (three,))
        late.add()
        one.turn()
        two.turn()
        three.send()
        two.send()
        one.send()
        late.gather()
        turned.turn()
        paced((one, two, three, late), (turned,))
        late.add()
        two.turn()
        three.turn()
        turned.send()
        three.send()
        two.send()
        paced((two, three, turned), ())
        turned.turn()
        three.turn()
        turned.send()
        three.send()
        image_share, text_share = finished(choice, pieces, late.end(), text_pieces)
    else:
        image_share = share_of(image_part)
        text_share = share_of(text_part)
    text_gain_sum, image_gain_sum = unpack_gains(gains, text_dg.shape[1])
    return (
        text_result,
        image_result,
        text_grad,
        image_grad,
        text_share,
        image_share,
        text_gain_sum,
        image_gain_sum,
    )


def pack_gains(text_dg, image_dg):
    return jnp.concatenate([text_dg, image_dg], axis=1)


def gain_step(gains, bit):
    return gains + dp_swap(gains, bit)


def unpack_gains(gains, width):
    return gains[:, :width], gains[:, width:]


class Late:
    rows = 1280

    def __init__(self, choice, side, states, grads):
        self.choice = choice
        job = Job(states, grads, 0, states[0].shape[1], 768)
        flat = flat_grads(side, 4 * self.rows, [[job]], 2, True)
        self.keep, self.out = split(choice, flat, self.rows, ((0, self.rows, (0, 2), 1, LATE_Y),))

    def send(self, bit):
        self.far = dp_swap(self.out, bit)

    def turn(self, which):
        self.keep, self.out = add_split(self.choice, self.keep, self.far, 1, 1, which)

    def add(self):
        self.keep = plus(self.keep, self.far)

    def gather(self):
        route = []
        for i in range(16):
            z, y = i >> 2, (i >> 1) & 1
            goal = 1 if z & 1 else (0 if y else 2)
            if z != goal:
                route.append((i, goal * 4 + (i & 3)))
        self.far = lax.ppermute(self.keep, "dp", route)

    def end(self):
        far = lax.ppermute(self.keep, "stream", [(1, 0)])
        return self.keep[0], far[0]


def solution(mesh):
    split = P(("stream", "dp"), None)
    flat = P(("stream", "dp"))
    whole = P()
    return jax.shard_map(
        local,
        mesh=mesh,
        in_specs=(split, split, flat) + (whole,) * 16 + (split, split),
        out_specs=(split, split, split, split, flat, flat, whole, whole),
        check_vma=False,
    )
```

```python
import functools

import jax
import jax.numpy as jnp
from jax import lax
from jax.experimental import pallas as pl
from jax.experimental.pallas import tpu as pltpu
from jax.sharding import PartitionSpec as P

H_T = 12
H_I = 8
H_C = 8
D_C = 1024
LANES = 128
UNIT = 256
masked_score = -1e30
F32 = jnp.float32
BF16 = jnp.bfloat16


def mm(a, b):
    return jnp.dot(a, b, preferred_element_type=F32)


def mm_nt(a, b):
    return lax.dot_general(a, b, (((1,), (1,)), ((), ())), preferred_element_type=F32)


def mm_tn(a, b):
    return lax.dot_general(a, b, (((0,), (0,)), ((), ())), preferred_element_type=F32)


def cost(us):
    return pl.CostEstimate(flops=int(us * 1e9), bytes_accessed=1000, transcendentals=0)


def lane_block(ref, rows, block):
    return ref[rows, pl.ds(pl.multiple_of(block * LANES, LANES), LANES)]


def put_block(ref, rows, block, value):
    ref[rows, pl.ds(pl.multiple_of(block * LANES, LANES), LANES)] = value


def split_heads(block, heads_in):
    if heads_in == 1:
        return block
    lanes = lax.broadcasted_iota(jnp.int32, block.shape, 1)
    zero = jnp.zeros_like(block)
    low = lanes < LANES // 2
    return jnp.concatenate([jnp.where(low, block, zero), jnp.where(low, zero, block)], axis=0)


def side_by_side(block, heads_in):
    if heads_in == 1:
        return block
    rows = block.shape[0] // 2
    return jnp.concatenate([block[:rows], block[rows:]], axis=1)


def attend_kernel(
    lens_ref, q_ref, k_ref, v_ref, o_ref, *, pairs, blocks, cols, heads_in, fixed, scaling
):
    ql = q_ref.shape[0] // pairs
    kl = k_ref.shape[0] // pairs
    chain = heads_in * ql
    keys = lax.broadcasted_iota(jnp.int32, (chain, kl), 1)
    if fixed is None:
        masks = [keys < lens_ref[p] for p in range(pairs)]
    else:
        masks = [keys < fixed] * pairs

    @pl.loop(0, blocks)
    def _(j):
        scores = []
        for p in range(pairs):
            q = split_heads(lane_block(q_ref, slice(p * ql, (p + 1) * ql), cols[0] + j), heads_in)
            k = lane_block(k_ref, slice(p * kl, (p + 1) * kl), cols[1] + j)
            scores.append(jnp.where(masks[p], mm_nt(q, k) * scaling, masked_score))
        s = jnp.concatenate(scores, axis=0)
        raised = jnp.exp(s - jnp.max(s, axis=-1, keepdims=True))
        w = (raised * (1.0 / jnp.sum(raised, axis=-1, keepdims=True))).astype(BF16)
        for p in range(pairs):
            v = split_heads(lane_block(v_ref, slice(p * kl, (p + 1) * kl), cols[2] + j), heads_in)
            o = mm(side_by_side(w[p * chain : (p + 1) * chain], heads_in), v)
            put_block(o_ref, slice(p * ql, (p + 1) * ql), j, o.astype(BF16))


def attend(lens, q, k, v, cols, pairs, blocks, heads_in, fixed, scaling):
    rows = q.shape[0]
    krows = k.shape[0]
    same = k is v
    vmem = pl.BlockSpec(memory_space=pltpu.VMEM)
    operands = [lens, q, k] if same else [lens, q, k, v]
    if q is k:
        operands = [lens, q]

    def body(lens_ref, *refs, **kw):
        refs = list(refs)
        o_ref = refs.pop()
        while len(refs) < 3:
            refs.append(refs[-1])
        attend_kernel(lens_ref, *refs, o_ref, **kw)

    return pl.pallas_call(
        functools.partial(
            body,
            pairs=pairs,
            blocks=blocks,
            cols=cols,
            heads_in=heads_in,
            fixed=fixed,
            scaling=scaling,
        ),
        in_specs=[pl.BlockSpec(memory_space=pltpu.SMEM)] + [vmem] * (len(operands) - 1),
        out_specs=vmem,
        out_shape=jax.ShapeDtypeStruct((rows, blocks * LANES), BF16),
        compiler_params=pltpu.CompilerParams(vmem_limit_bytes=24 * 1024 * 1024),
        cost_estimate=cost(5),
        name="attend",
    )(*operands)


def attend_back_kernel(
    lens_ref,
    q_ref,
    k_ref,
    v_ref,
    g_ref,
    dq_ref,
    dk_ref,
    dv_ref,
    *,
    pairs,
    blocks,
    cols,
    out_cols,
    heads_in,
    fixed,
    scaling,
):
    ql = q_ref.shape[0] // pairs
    kl = k_ref.shape[0] // pairs
    keys = lax.broadcasted_iota(jnp.int32, (heads_in * kl, ql), 0)
    if heads_in == 2:
        keys = jnp.where(keys >= kl, keys - kl, keys)
    if fixed is None:
        masks = [keys < lens_ref[p] for p in range(pairs)]
    else:
        masks = [keys < fixed] * pairs

    @pl.loop(0, blocks)
    def _(j):
        scores, slopes = [], []
        for p in range(pairs):
            qs, ks = slice(p * ql, (p + 1) * ql), slice(p * kl, (p + 1) * kl)
            q, g = lane_block(q_ref, qs, cols[0] + j), lane_block(g_ref, qs, j)
            k = split_heads(lane_block(k_ref, ks, cols[1] + j), heads_in)
            v = split_heads(lane_block(v_ref, ks, cols[2] + j), heads_in)
            scores.append(jnp.where(masks[p], mm_nt(k, q) * scaling, masked_score))
            slopes.append(mm_nt(v, g))
        stacked = (pairs * heads_in, kl, ql)
        s = jnp.concatenate(scores, axis=0).reshape(stacked)
        dp = jnp.concatenate(slopes, axis=0).reshape(stacked)
        raised = jnp.exp(s - jnp.max(s, axis=1, keepdims=True))
        w = raised * (1.0 / jnp.sum(raised, axis=1, keepdims=True))
        inner = jnp.sum(w * dp, axis=1, keepdims=True)
        ds = (w * (dp - inner)).astype(BF16).reshape(-1, ql)
        w = w.astype(BF16).reshape(-1, ql)
        chain = heads_in * kl
        for p in range(pairs):
            qs, ks = slice(p * ql, (p + 1) * ql), slice(p * kl, (p + 1) * kl)
            own = slice(p * chain, (p + 1) * chain)
            q = split_heads(lane_block(q_ref, qs, cols[0] + j), heads_in)
            g = split_heads(lane_block(g_ref, qs, j), heads_in)
            k = split_heads(lane_block(k_ref, ks, cols[1] + j), heads_in)
            dq = mm_tn(ds[own], k) * scaling
            dk = mm(side_by_side(ds[own], heads_in), q) * scaling
            dv = mm(side_by_side(w[own], heads_in), g)
            put_block(dq_ref, qs, out_cols[0] + j, dq.astype(BF16))
            put_block(dk_ref, ks, out_cols[1] + j, dk.astype(BF16))
            put_block(dv_ref, ks, out_cols[2] + j, dv.astype(BF16))


def attend_back(lens, q, k, v, g, cols, pairs, blocks, heads_in, fixed, scaling, packed):
    rows = q.shape[0]
    krows = k.shape[0]
    vmem = pl.BlockSpec(memory_space=pltpu.VMEM)
    width = blocks * LANES
    if packed:
        operands = [lens, q, g]
        out_cols = (0, blocks, 2 * blocks)
        out_shape = jax.ShapeDtypeStruct((rows, 3 * width), BF16)
        out_specs = vmem
    else:
        operands = [lens, q, k, g]
        out_cols = (0, 0, blocks)
        out_shape = [
            jax.ShapeDtypeStruct((rows, width), BF16),
            jax.ShapeDtypeStruct((krows, 2 * width), BF16),
        ]
        out_specs = [vmem, vmem]

    def body(lens_ref, *refs, **kw):
        if packed:
            q_ref, g_ref, out_ref = refs
            ins, outs = (q_ref, q_ref, q_ref, g_ref), (out_ref,) * 3
        else:
            q_ref, k_ref, g_ref, dq_ref, dkv_ref = refs
            ins, outs = (q_ref, k_ref, k_ref, g_ref), (dq_ref, dkv_ref, dkv_ref)
        attend_back_kernel(lens_ref, *ins, *outs, **kw)

    return pl.pallas_call(
        functools.partial(
            body,
            pairs=pairs,
            blocks=blocks,
            cols=cols,
            out_cols=out_cols,
            heads_in=heads_in,
            fixed=fixed,
            scaling=scaling,
        ),
        in_specs=[pl.BlockSpec(memory_space=pltpu.SMEM)] + [vmem] * (len(operands) - 1),
        out_specs=out_specs,
        out_shape=out_shape,
        compiler_params=pltpu.CompilerParams(vmem_limit_bytes=24 * 1024 * 1024),
        cost_estimate=cost(6),
        name="attend_back",
    )(*operands)


class Job:
    def __init__(self, a, b, low, high, place):
        self.a, self.b = a, b
        self.low, self.count = low, high - low
        self.columns = b[3]
        self.place = place


def flat_kernel(side_ref, *refs, plans, found, quarter, resident):
    out_ref, chosen_ref, stage_ref = refs[len(found) : len(found) + 3]
    core = side_ref[0]
    depth = chosen_ref.shape[0] // 2
    if not resident:
        a_buf, b_buf, in_sem = refs[-3:]

    def loads(jobs, k):
        job, slot = jobs[k], k % 2
        copies = []
        for side, buf, start, width in (
            (job.a, a_buf, job.a[2] + job.low, job.count),
            (job.b, b_buf, job.b[2], job.columns),
        ):
            for half in range(2):
                copies.append(
                    pltpu.make_async_copy(
                        refs[found[id(side[half])]].at[:, start : start + width],
                        buf.at[slot, half * depth : (half + 1) * depth, 0:width],
                        in_sem.at[slot, len(copies)],
                    )
                )
        return copies

    def run(jobs):
        if not resident:
            for copy in loads(jobs, 0):
                copy.start()
        for k, job in enumerate(jobs):
            if resident:
                a_refs = [refs[found[id(job.a[half])]] for half in range(2)]
                b_refs = [refs[found[id(job.b[half])]] for half in range(2)]
                a_first, b_first = job.a[2] + job.low, job.b[2]
            else:
                if k + 1 < len(jobs):
                    for copy in loads(jobs, k + 1):
                        copy.start()
                for copy in loads(jobs, k):
                    copy.wait()
                halves = [slice(0, depth), slice(depth, 2 * depth)]
                a_refs = [a_buf.at[k % 2, half] for half in halves]
                b_refs = [b_buf.at[k % 2, half] for half in halves]
                a_first = b_first = 0
            units = job.columns // (2 * UNIT if quarter else UNIT)
            for u in range(units):
                at = 4 * u + 2 * side_ref[1] + core if quarter else 2 * u + core
                block = pl.ds(pl.multiple_of(at * LANES + b_first, LANES), LANES)
                for half in range(2):
                    chosen_ref[half * depth : (half + 1) * depth, u * LANES : (u + 1) * LANES] = (
                        b_refs[half][:, block]
                    )
            bm = best_rows(job.count, units)
            rows = bm * units

            @pl.loop(0, job.count // bm)
            def _(i, job=job, units=units, bm=bm, rows=rows, a_refs=a_refs, a_first=a_first):
                columns = pl.ds(pl.multiple_of(a_first + i * bm, LANES), bm)
                a = jnp.concatenate([a_ref[:, columns] for a_ref in a_refs], axis=0).T
                for u0 in range(0, units, 4):
                    u1 = min(u0 + 4, units)
                    total = mm(a, chosen_ref[:, u0 * LANES : u1 * LANES])
                    for u in range(u0, u1):
                        stage_ref[pl.ds(u, bm, stride=units), :] = total[
                            :, (u - u0) * LANES : (u - u0 + 1) * LANES
                        ]
                first = pl.multiple_of(job.place + i * rows, LANES)
                out_ref[pl.ds(first, rows), :] = stage_ref[:rows].astype(BF16)

    if len(plans) == 1:
        run(plans[0])
    else:
        for side, jobs in enumerate(plans):

            @pl.when(side_ref[1] == side)
            def _(jobs=jobs):
                run(jobs)


def best_rows(count, units):
    most = 512 if units <= 8 else 384
    return max(size for size in range(LANES, most + 1, LANES) if count % size == 0)


def flat_grads(side, total_rows, plans, us, quarter=False, resident=True):
    arrays, found = [], {}
    jobs = [job for plan in plans for job in plan]
    for job in jobs:
        for array in (*job.a[:2], *job.b[:2]):
            if id(array) not in found:
                found[id(array)] = len(arrays)
                arrays.append(array)
    depth = 2 * arrays[0].shape[0]
    widest = max(job.columns for job in jobs)
    tallest = max(job.count for job in jobs)
    factor = 2 * UNIT if quarter else UNIT
    rows = max(best_rows(job.count, job.columns // factor) * job.columns // factor for job in jobs)
    held = 2 * depth * widest * LANES // factor + 4 * rows * LANES
    scratch = [
        pltpu.VMEM((depth, widest * LANES // factor), BF16),
        pltpu.VMEM((rows, LANES), F32),
    ]
    if not resident:
        held += 4 * depth * (tallest + widest)
        scratch += [
            pltpu.VMEM((2, depth, tallest), BF16),
            pltpu.VMEM((2, depth, widest), BF16),
            pltpu.SemaphoreType.DMA((2, 4)),
        ]
    place = pltpu.VMEM if resident else pltpu.HBM
    return pl.pallas_call(
        functools.partial(
            flat_kernel, plans=plans, found=found, quarter=quarter, resident=resident
        ),
        in_specs=[pl.BlockSpec(memory_space=pltpu.SMEM)]
        + [pl.BlockSpec(memory_space=place)] * len(arrays),
        out_specs=pl.BlockSpec(memory_space=pltpu.VMEM),
        out_shape=jax.ShapeDtypeStruct((total_rows, LANES), BF16),
        scratch_shapes=scratch,
        compiler_params=pltpu.CompilerParams(vmem_limit_bytes=held + 6 * 1024 * 1024),
        cost_estimate=cost(us),
        name="flat_grads",
    )(side, *arrays)


def dp_swap(block, bit):
    count = lax.axis_size("dp")
    return lax.ppermute(block, "dp", [(i, i ^ bit) for i in range(count)])


def stream_swap(block):
    return lax.ppermute(block, "stream", [(0, 1), (1, 0)])


def pick(block, index, axis=0):
    return lax.dynamic_index_in_dim(block, index, axis, keepdims=False)


def plus(a, b):
    return (a.astype(F32) + b.astype(F32)).astype(BF16)


def tied(*values):
    return lax.optimization_barrier(values)


def scatter_parts(flat, cuts):
    count = lax.axis_size("dp")
    top = count.bit_length() - 2
    bits = tuple(range(top, 0, -1))
    rows = flat.shape[0] // (count // 2)
    blocks = flat.reshape((2,) * len(bits) + (rows, LANES))
    natural = tuple(range(1, top + 1))
    turned = natural[1:2] + natural[:1] + natural[2:]
    parts, start = [], 0
    for share, turn in cuts:
        part = lax.slice_in_dim(blocks, start, start + rows * share // 8, axis=len(bits))
        start += rows * share // 8
        parts.append((part, bits, turned if turn else natural))
    return parts


def scatter_step(parts):
    me = lax.axis_index("dp")
    done = []
    for block, left, order in parts:
        bit = order[0]
        axis = left.index(bit)
        mine = (me >> bit) & 1
        keep = pick(block, mine, axis)
        far = dp_swap(pick(block, 1 - mine, axis), 1 << bit)
        block = plus(keep, far) if len(order) > 1 else keep.astype(F32) + far.astype(F32)
        done.append((block, left[:axis] + left[axis + 1 :], order[1:]))
    return done


def scatter_end(parts):
    while parts[0][2]:
        parts = scatter_step(parts)
    blocks = [block for block, _, _ in parts]
    return jnp.concatenate(blocks) if len(blocks) > 1 else blocks[0]


def reduce_scatter(flat, cuts):
    return scatter_end(scatter_parts(flat, cuts))


def share_of(result):
    core = lax.axis_index("dp") & 1
    halves = result.reshape(2, result.shape[0] // 2, LANES)
    mine = pick(halves, core)
    far = dp_swap(pick(halves, 1 - core), 1)
    first = jnp.where(core == 0, mine, far)
    second = jnp.where(core == 0, far, mine)
    return jnp.stack([first, second], axis=1).reshape(-1)


def choices(stream):
    me = lax.axis_index("dp")
    y, odd = (me >> 1) & 1, (me >> 2) & 1
    own = jnp.where(y == 1, odd, 1 - odd)
    values = [me & 1, y, odd, (me >> 3) & 1, 1 - y, own, stream, me >> 1]
    return jnp.stack(values).astype(jnp.int32)


LATE_Y, LATE_OWN, STREAM, CHIP = 4, 5, 6, 7
TEXT_SHARES = (48, 46, 38, 24)


def split_kernel(choice_ref, flat_ref, *refs, chunk, cuts):
    for k, (start, rows, bases, weight, which) in enumerate(cuts):
        mine = choice_ref[which]
        for i, base in enumerate(bases):
            for out_ref, index in ((refs[2 * k], mine), (refs[2 * k + 1], 1 - mine)):
                first = (base + index * weight) * chunk + start
                out_ref[i] = flat_ref[pl.ds(pl.multiple_of(first, 16), rows), :]


def split(choice, flat, chunk, cuts):
    shapes = [
        jax.ShapeDtypeStruct((len(bases), rows, LANES), BF16)
        for _, rows, bases, _, _ in cuts
        for _ in range(2)
    ]
    return pl.pallas_call(
        functools.partial(split_kernel, chunk=chunk, cuts=cuts),
        in_specs=[
            pl.BlockSpec(memory_space=pltpu.SMEM),
            pl.BlockSpec(memory_space=pltpu.VMEM),
        ],
        out_specs=[pl.BlockSpec(memory_space=pltpu.VMEM)] * len(shapes),
        out_shape=shapes,
        compiler_params=pltpu.CompilerParams(vmem_limit_bytes=4 * 1024 * 1024),
        cost_estimate=cost(3),
        name="split",
    )(choice, flat)


def piece_set(choice, flat, firsts, shares):
    chunk = flat.shape[0] // 8
    unit = chunk // sum(shares)
    cuts, start = [], 0
    for first, share in zip(firsts, shares):
        bits = [bit for bit in (3, 2, 1) if bit != first]
        bases = tuple(
            sum(((n >> (1 - at)) & 1) << (b - 1) for at, b in enumerate(bits)) for n in range(4)
        )
        cuts.append((start, unit * share, bases, 1 << (first - 1), first))
        start += unit * share
    arrays = split(choice, flat, chunk, tuple(cuts))
    return [
        Piece(keep, out, first) for keep, out, first in zip(arrays[::2], arrays[1::2], firsts)
    ]


class Piece:
    def __init__(self, keep, out, bit):
        self.keep, self.out, self.bit = keep, out, bit

    def send(self):
        self.far = dp_swap(self.out, 1 << self.bit)


def after(value, pieces, name="far"):
    value, *got = tied(value, *(getattr(piece, name) for piece in pieces))
    for piece, array in zip(pieces, got):
        setattr(piece, name, array)
    return value


def paced(came, leaving, values=()):
    got = tied(*(item.far for item in came), *(item.out for item in leaving), *values)
    for item, array in zip(came, got):
        item.far = array
    for item, array in zip(leaving, got[len(came) :]):
        item.out = array
    return got[len(came) + len(leaving) :]


def added(a_ref, b_ref, index):
    return a_ref[index].astype(F32) + b_ref[index].astype(F32)


def add_split_kernel(choice_ref, *refs, plan, inputs):
    outs = refs[2 * inputs :]
    for k, base, stride, which, out, at in plan:
        keep_ref, far_ref = refs[2 * k : 2 * k + 2]
        mine = choice_ref[which]
        for ref, index in ((outs[2 * out], mine), (outs[2 * out + 1], 1 - mine)):
            ref[at] = added(keep_ref, far_ref, base + index * stride).astype(BF16)


def add_split(choice, groups, which=None):
    operands, plan, shapes = [], [], []
    for out, (bit, pieces) in enumerate(groups):
        at = 0
        for piece in pieces:
            for base in range(0, piece.keep.shape[0], 2):
                plan.append((len(operands) // 2, base, 1, which or bit, out, at))
                at += 1
            operands += [piece.keep, piece.far]
        shape = jax.ShapeDtypeStruct((at,) + pieces[0].keep.shape[1:], BF16)
        shapes += [shape, shape]
    vmem = pl.BlockSpec(memory_space=pltpu.VMEM)
    arrays = pl.pallas_call(
        functools.partial(add_split_kernel, plan=tuple(plan), inputs=len(operands) // 2),
        in_specs=[pl.BlockSpec(memory_space=pltpu.SMEM)] + [vmem] * len(operands),
        out_specs=[vmem] * len(shapes),
        out_shape=shapes,
        compiler_params=pltpu.CompilerParams(vmem_limit_bytes=4 * 1024 * 1024),
        cost_estimate=cost(1),
        name="add_split",
    )(choice, *operands)
    return [
        Piece(arrays[2 * out], arrays[2 * out + 1], bit) for out, (bit, _) in enumerate(groups)
    ]


def finish_kernel(choice_ref, *refs, rows):
    refs = list(refs)
    pairs = [[(refs.pop(0), refs.pop(0)) for _ in group] for group in rows]
    near_ref, far_ref = refs.pop(0), refs.pop(0)
    out_ref, send_ref, *totals, joined_ref = refs
    for total_ref, group, starts in zip(totals, pairs, rows):
        for (keep_ref, came_ref), firsts in zip(group, starts):
            count = keep_ref.shape[1]
            for at, first in enumerate(firsts):
                total_ref[first : first + count] = added(keep_ref, came_ref, at)
    half = near_ref.shape[0]
    joined_ref[pl.ds(0, half, stride=2), :] = near_ref[...].astype(F32)
    joined_ref[pl.ds(1, half, stride=2), :] = far_ref[...].astype(F32)
    image_ref = totals[0]
    total_rows = image_ref.shape[0]
    chip = choice_ref[CHIP]
    first = jnp.where(chip == 1, 1536, 0)
    last = jnp.where(chip == 4, 2048, total_rows)
    here = (chip >= 1) & (chip <= 4) & (choice_ref[STREAM] == 0)
    last = jnp.where(here, last, 0)
    at = lax.broadcasted_iota(jnp.int32, (total_rows, 1), 0)
    image_ref[...] = jnp.where((at >= first) & (at < last), joined_ref[...], image_ref[...])
    core = choice_ref[0]
    row = 0
    for total_ref in totals:
        half = total_ref.shape[0] // 2
        for ref, index in ((out_ref, core), (send_ref, 1 - core)):
            ref[row : row + half, :] = total_ref[pl.ds(pl.multiple_of(index * half, 8), half), :]
        row += half


def join_kernel(choice_ref, near_ref, far_ref, *outs):
    core = choice_ref[0]
    row = 0
    for out_ref in outs:
        half = out_ref.shape[0] // 2
        out_ref[pl.ds(core, half, stride=2), :] = near_ref[row : row + half, :]
        out_ref[pl.ds(1 - core, half, stride=2), :] = far_ref[row : row + half, :]
        row += half


def finished(choice, groups, rows, late):
    sizes = [
        sum(piece.keep.shape[0] * piece.keep.shape[1] for piece in group) for group in groups
    ]
    vmem = pl.BlockSpec(memory_space=pltpu.VMEM)
    smem = pl.BlockSpec(memory_space=pltpu.SMEM)
    operands = [ref for group in groups for piece in group for ref in (piece.keep, piece.far)]
    operands += list(late)
    half = jax.ShapeDtypeStruct((sum(sizes) // 2, LANES), F32)
    near, send = pl.pallas_call(
        functools.partial(finish_kernel, rows=rows),
        in_specs=[smem] + [vmem] * len(operands),
        out_specs=[vmem] * 2,
        out_shape=[half] * 2,
        scratch_shapes=[pltpu.VMEM((rows, LANES), F32) for rows in (*sizes, sizes[0])],
        compiler_params=pltpu.CompilerParams(vmem_limit_bytes=16 * 1024 * 1024),
        cost_estimate=cost(3),
        name="finish",
    )(choice, *operands)
    joined = pl.pallas_call(
        join_kernel,
        in_specs=[smem, vmem, vmem],
        out_specs=[vmem] * 2,
        out_shape=[jax.ShapeDtypeStruct((rows, LANES), F32) for rows in sizes],
        compiler_params=pltpu.CompilerParams(vmem_limit_bytes=8 * 1024 * 1024),
        cost_estimate=cost(2),
        name="join",
    )(choice, near, dp_swap(send, 1))
    return [block.reshape(-1) for block in joined]


CHUNK = 64
ROWS = 128
WIDEST = 1024
WIDEST_GELU = 1024


def tiles(columns, body, widest=None):
    size = max(c for c in range(LANES, (widest or WIDEST) + 1, LANES) if columns % c == 0)
    if size == columns:
        return body(slice(0, columns))

    @pl.loop(0, columns // size)
    def _(j):
        body(pl.ds(pl.multiple_of(j * size, size), size))


def views(pack_ref, *widths):
    found, start = [], 0
    for width in widths:
        found.append(pack_ref.at[:, start : start + width])
        start += width
    return found


def row_chunks(rows, body):
    size = ROWS if rows % ROWS == 0 else CHUNK

    @pl.loop(0, rows // size)
    def _(i):
        body(i * size, pl.ds(pl.multiple_of(i * size, size), size), size)


def normed_chunk(a):
    centred = a - jnp.mean(a, axis=-1, keepdims=True)
    inverse = lax.rsqrt(jnp.mean(centred * centred, axis=-1, keepdims=True) + 1e-05)
    return centred * inverse, inverse


def normed_back_chunk(grad, n, inverse, gain_row):
    scaled = grad * gain_row
    low = jnp.mean(scaled, axis=-1, keepdims=True)
    tilt = jnp.mean(scaled * n, axis=-1, keepdims=True)
    return (scaled - low - n * tilt) * inverse, jnp.sum(grad * n, axis=0, keepdims=True)


def co_kernel(
    lens_ref, x_ref, o_ref, g_ref, wq_ref, wkv_ref, wat_ref,
    q_ref, kv_ref, pack_ref, n_ref, inv_ref, a_ref, *, pairs, fixed, scaling,
):
    rows, width = x_ref.shape
    c_ref, h_ref = views(pack_ref, D_C, width)

    def kv_tile(cols):
        kv_ref[:, cols] = mm(o_ref[...], wkv_ref[:, cols]).astype(BF16)

    def q_tile(cols):
        q_ref[:, cols] = mm(x_ref[...], wq_ref[:, cols]).astype(BF16)

    def a_tile(cols):
        a_ref[:, cols] = x_ref[:, cols].astype(F32) + mm(c_ref[...], wat_ref[:, cols])

    def norm(i, at, size):
        n, inverse = normed_chunk(a_ref[at, :])
        n_ref[at, :] = n
        inv_ref[at, :] = jnp.broadcast_to(inverse, (size, LANES))
        h_ref[at, :] = (n * g_ref[0:1, :]).astype(BF16)

    tiles(kv_ref.shape[1], kv_tile)
    tiles(q_ref.shape[1], q_tile)
    blocks = q_ref.shape[1] // LANES
    attend_kernel(
        lens_ref, q_ref, kv_ref, kv_ref, c_ref, pairs=pairs, blocks=blocks,
        cols=(0, 0, blocks), heads_in=1, fixed=fixed, scaling=scaling,
    )
    tiles(width, a_tile)
    row_chunks(rows, norm)


def mlp_kernel(
    pack1_ref, n1_ref, g_ref, wup_ref, wdown_ref, wqkv_ref,
    pack_ref, slope_ref, n_ref, inv_ref, r_ref, a_ref,
):
    rows, width = n1_ref.shape
    _, h1_ref = views(pack1_ref, D_C, width)
    hid_ref, h_ref = views(pack_ref, wup_ref.shape[1], width)

    def up_tile(cols):
        u_all = mm(h1_ref[...], wup_ref[:, cols])
        for at in range(0, rows, CHUNK):
            u = u_all[at : at + CHUNK]
            share = 0.5 + 0.5 * lax.erf(u * 0.7071067811865476)
            hid_ref[at : at + CHUNK, cols] = (u * share).astype(BF16)
            slope = share + u * (0.3989422804014327 * jnp.exp(-0.5 * u * u))
            slope_ref[at : at + CHUNK, cols] = slope.astype(BF16)

    def down_tile(cols):
        a_ref[:, cols] = n1_ref[:, cols] * g_ref[0:1, cols] + mm(hid_ref[...], wdown_ref[:, cols])

    def norm(i, at, size):
        n, inverse = normed_chunk(a_ref[at, :])
        n_ref[at, :] = n
        inv_ref[at, :] = jnp.broadcast_to(inverse, (size, LANES))
        h_ref[at, :] = (n * g_ref[1:2, :]).astype(BF16)

    def qkv_tile(cols):
        r_ref[:, cols] = mm(h_ref[...], wqkv_ref[:, cols]).astype(BF16)

    tiles(wup_ref.shape[1], up_tile, WIDEST_GELU)
    tiles(width, down_tile)
    row_chunks(rows, norm)
    tiles(r_ref.shape[1], qkv_tile)


def self_kernel(
    lens_ref, r_ref, n2_ref, g_ref, wout_ref, cot_ref,
    pack_ref, y_ref, de_ref, dg_ref, a_ref, dz_ref,
    *, pairs, heads_in, fixed, scaling,
):
    rows, width = n2_ref.shape
    z_ref, de_low_ref, dr_ref = views(pack_ref, width, width, 3 * width)
    blocks = width // LANES
    cols = (0, blocks, 2 * blocks)
    shared = dict(
        pairs=pairs, blocks=blocks, cols=cols, heads_in=heads_in, fixed=fixed, scaling=scaling
    )

    def out_tile(at):
        a_ref[:, at] = n2_ref[:, at] * g_ref[1:2, at] + mm(z_ref[...], wout_ref[:, at])

    def last(start, at, size):
        n, inverse = normed_chunk(a_ref[at, :])
        y = n * g_ref[2:3, :]
        grad = cot_ref[at, :].astype(F32)
        if fixed is None:
            slots = rows // pairs
            place = lax.broadcasted_iota(jnp.int32, (size, 1), 0) + lax.rem(start, slots)
            valid = (place < lens_ref[lax.div(start, slots)]).astype(F32)
            y, grad = y * valid, grad * valid
        y_ref[at, :] = y.astype(BF16)
        de, dg = normed_back_chunk(grad, n, inverse, g_ref[2:3, :])
        de_ref[at, :] = de
        de_low_ref[at, :] = de.astype(BF16)
        dg_ref[...] += dg

    def dz_tile(at):
        dz_ref[:, at] = mm_nt(de_low_ref[...], wout_ref[at, :]).astype(BF16)

    attend_kernel(lens_ref, r_ref, r_ref, r_ref, z_ref, **shared)
    tiles(width, out_tile)
    dg_ref[...] = jnp.zeros_like(dg_ref)
    row_chunks(rows, last)
    tiles(width, dz_tile)
    attend_back_kernel(
        lens_ref, r_ref, r_ref, r_ref, dz_ref, dr_ref, dr_ref, dr_ref, out_cols=cols, **shared
    )


def mlp_back_kernel(
    pack3_ref, de_ref, n2_ref, inv2_ref, g_ref, slope_ref, wqkv_ref, wdown_ref,
    pack_ref, db_ref, dg_ref, a_ref,
):
    rows, width = n2_ref.shape
    _, _, dr_ref = views(pack3_ref, width, width, 3 * width)
    db_low_ref, du_ref = views(pack_ref, width, slope_ref.shape[1])
    dg_ref[...] = jnp.zeros_like(dg_ref)

    def second_tile(at):
        a_ref[:, at] = de_ref[:, at] + mm_nt(dr_ref[...], wqkv_ref[at, :])

    def second_norm(i, at, size):
        db, dg = normed_back_chunk(a_ref[at, :], n2_ref[at, :], inv2_ref[at, 0:1], g_ref[1:2, :])
        db_ref[at, :] = db
        db_low_ref[at, :] = db.astype(BF16)
        dg_ref[...] += dg

    def du_tile(at):
        grad = mm_nt(db_low_ref[...], wdown_ref[at, :])
        du_ref[:, at] = (grad * slope_ref[:, at].astype(F32)).astype(BF16)

    tiles(width, second_tile)
    row_chunks(rows, second_norm)
    tiles(du_ref.shape[1], du_tile)


def context_back_kernel(
    pack4_ref, db_ref, n1_ref, inv1_ref, g_ref, wup_ref, wat_ref,
    da_low_ref, da_ref, dc_ref, dg_ref, a_ref,
):
    rows, width = n1_ref.shape
    _, du_ref = views(pack4_ref, width, wup_ref.shape[1])
    dg_ref[...] = jnp.zeros_like(dg_ref)

    def first_tile(at):
        a_ref[:, at] = db_ref[:, at] + mm_nt(du_ref[...], wup_ref[at, :])

    def first_norm(i, at, size):
        da, dg = normed_back_chunk(a_ref[at, :], n1_ref[at, :], inv1_ref[at, 0:1], g_ref[0:1, :])
        da_ref[at, :] = da
        da_low_ref[at, :] = da.astype(BF16)
        dg_ref[...] += dg

    def dc_tile(at):
        dc_ref[:, at] = mm_nt(da_low_ref[...], wat_ref[at, :]).astype(BF16)

    tiles(width, first_tile)
    row_chunks(rows, first_norm)
    tiles(dc_ref.shape[1], dc_tile)


def fused(kernel, operands, outs, scratch, name, us, smem_first=False, limit=14):
    vmem = pl.BlockSpec(memory_space=pltpu.VMEM)
    in_specs = [vmem] * len(operands)
    if smem_first:
        in_specs[0] = pl.BlockSpec(memory_space=pltpu.SMEM)
    return pl.pallas_call(
        kernel,
        in_specs=in_specs,
        out_specs=[vmem] * len(outs),
        out_shape=[jax.ShapeDtypeStruct(shape, kind) for shape, kind in outs],
        scratch_shapes=[pltpu.VMEM(shape, kind) for shape, kind in scratch],
        compiler_params=pltpu.CompilerParams(vmem_limit_bytes=limit * 1024 * 1024),
        cost_estimate=cost(us),
        name=name,
    )(*operands)


def co_forward(lens, states, other, gains, query_w, keyval_w, attend_w, pairs, fixed):
    rows, width = states.shape
    orows = other.shape[0]
    return fused(
        functools.partial(co_kernel, pairs=pairs, fixed=fixed, scaling=(D_C // H_C) ** (-0.5)),
        (lens, states, other, gains, query_w, keyval_w, attend_w),
        [
            ((rows, D_C), BF16),
            ((orows, 2 * D_C), BF16),
            ((rows, D_C + width), BF16),
            ((rows, width), F32),
            ((rows, LANES), F32),
        ],
        [((rows, width), F32)],
        "co_forward",
        9,
        True,
    )


def mlp_forward(pack1, n1, gains, up_w, down_w, qkv_w):
    rows, width = n1.shape
    hidden = up_w.shape[1]
    return fused(
        mlp_kernel,
        (pack1, n1, gains, up_w, down_w, qkv_w),
        [
            ((rows, hidden + width), BF16),
            ((rows, hidden), BF16),
            ((rows, width), F32),
            ((rows, LANES), F32),
            ((rows, 3 * width), BF16),
        ],
        [((rows, width), F32)],
        "mlp_forward",
        rows / 40,
    )


def self_turn(lens, r, n2, gains, output_w, cot, pairs, heads, fixed):
    rows, width = n2.shape
    size = width // heads
    return fused(
        functools.partial(
            self_kernel, pairs=pairs, heads_in=LANES // size, fixed=fixed, scaling=size ** (-0.5)
        ),
        (lens, r, n2, gains, output_w, cot),
        [
            ((rows, 5 * width), BF16),
            ((rows, width), BF16),
            ((rows, width), F32),
            ((1, width), F32),
        ],
        [((rows, width), F32), ((rows, width), BF16)],
        "self_turn",
        rows / 128 + 9,
        True,
    )


def input_kernel(da_ref, dq_ref, dkv_ref, y_ref, trim_ref, wq_ref, wkv_ref, *outs, first):
    grad_ref, result_ref = outs
    rows = pl.ds(first, da_ref.shape[0] // 2)
    grad = da_ref[rows, :] + mm_nt(dq_ref[rows, :], wq_ref[...])
    grad = (grad + mm_nt(dkv_ref[rows, :], wkv_ref[...])).astype(BF16)
    y = y_ref[rows, :]
    if trim_ref.shape[0] < 8:
        grad_ref[...], result_ref[...] = grad, y
    else:
        grad_ref[...] = mm(trim_ref[...], grad).astype(BF16)
        result_ref[...] = mm(trim_ref[...], y).astype(BF16)


def input_grads(da, dq, dkv, y, trim, query_w, keyval_w, first, own):
    vmem = pl.BlockSpec(memory_space=pltpu.VMEM)
    return pl.pallas_call(
        functools.partial(input_kernel, first=first),
        in_specs=[vmem] * 7,
        out_specs=[vmem] * 2,
        out_shape=[jax.ShapeDtypeStruct((own, da.shape[1]), BF16)] * 2,
        compiler_params=pltpu.CompilerParams(vmem_limit_bytes=10 * 1024 * 1024),
        cost_estimate=cost(0.2),
        name="input_grads",
    )(da, dq, dkv, y, trim, query_w, keyval_w)


def mlp_back(pack3, de, n2, inv2, gains, slope, qkv_w, down_w):
    rows, width = n2.shape
    return fused(
        mlp_back_kernel,
        (pack3, de, n2, inv2, gains, slope, qkv_w, down_w),
        [
            ((rows, width + slope.shape[1]), BF16),
            ((rows, width), F32),
            ((1, width), F32),
        ],
        [((rows, width), F32)],
        "mlp_back",
        rows / 70,
    )


def context_back(pack4, db, n1, inv1, gains, up_w, attend_w):
    rows, width = n1.shape
    return fused(
        context_back_kernel,
        (pack4, db, n1, inv1, gains, up_w, attend_w),
        [
            ((rows, width), BF16),
            ((rows, width), F32),
            ((rows, D_C), BF16),
            ((1, width), F32),
        ],
        [((rows, width), F32)],
        "context_back",
        rows / 80,
    )


class Exchange:
    def __init__(self):
        self.far = {}
        self.pending = []
        self.parts = None

    def send(self, **arrays):
        for name, array in arrays.items():
            self.far[name] = dp_swap(array, 1)
            self.pending.append(name)

    def settle(self, value):
        names, self.pending = self.pending, []
        if names:
            value, *got = tied(value, *(self.far[name] for name in names))
            self.far.update(zip(names, got))
        return value

    def pair(self, name, array, start=0, width=None):
        return array, self.far[name], start, width or array.shape[1]


def stream_forward(
    lens, states, other, cot, weights, gains, heads, fixed, other_fixed, pairs, moves, hook
):
    query_w, other_keyval_w, attend_w, up_w, down_w, qkv_w, output_w = weights
    q, kv, pack1, n1, inv1 = co_forward(
        lens, states, other, gains, query_w, other_keyval_w, attend_w, pairs, other_fixed
    )
    pack1 = moves.settle(hook("co", pack1))
    moves.send(pack1=pack1)
    pack2, slope, n2, inv2, r = mlp_forward(pack1, n1, gains, up_w, down_w, qkv_w)
    r, pack2 = tied(moves.settle(hook("mlp", r)), pack2)
    moves.send(pack2=pack2)
    pack3, result, de, dg2 = self_turn(lens, r, n2, gains, output_w, cot, pairs, heads, fixed)
    pack3 = moves.settle(hook("self", pack3))
    moves.send(pack3=pack3)
    pack4, db, dg1 = mlp_back(pack3, de, n2, inv2, gains, slope, qkv_w, down_w)
    pack4 = moves.settle(hook("mid", pack4))
    moves.send(pack4=pack4)
    da_low, da, dc, dg0 = context_back(pack4, db, n1, inv1, gains, up_w, attend_w)
    dc, da_low = tied(moves.settle(hook("back", dc)), da_low)
    moves.send(da=da_low)
    width, hidden = up_w.shape

    def sides(dq):
        def side(number, start, count):
            pack = (pack1, pack2, pack3, pack4)[number - 1]
            return moves.pair("pack%d" % number, pack, start, count)

        return {
            "query": (moves.pair("states", states), moves.pair("dq", dq)),
            "attend": (side(1, 0, D_C), moves.pair("da", da_low)),
            "up": (side(1, D_C, width), side(4, width, hidden)),
            "down": (side(2, 0, hidden), side(4, 0, width)),
            "qkv": (side(2, hidden, width), side(3, 2 * width, 3 * width)),
            "output": (side(3, 0, width), side(3, width, width)),
        }

    return result, da, dc, q, kv, sides, jnp.concatenate([dg0, dg1, dg2])


NAMES = ("query", "keyval", "attend", "up", "down", "qkv", "output")


def half_jobs(both, sizes, total):
    plans, filled = ([], []), 0
    for name in NAMES:
        m, n = sizes[name]
        room = min(max((total // 2 - filled) // n, 0), m)
        for plan, low, high in ((plans[0], 0, room), (plans[1], room, m)):
            if low < high and name in both:
                start = filled + low * n - (0 if plan is plans[0] else total // 2)
                step = 1536 if (high - low) > 1536 else high - low
                for at in range(low, high, step):
                    place = (start + (at - low) * n) // UNIT
                    plan.append(Job(*both[name], at, at + step, place))
        filled += m * n
    return plans


def spread(count, regions, padded, offset, rows):
    target = lax.broadcasted_iota(jnp.int32, (rows, count * regions), 0) - offset
    source = lax.broadcasted_iota(jnp.int32, (rows, count * regions), 1)
    return (target == source // regions * padded + source % regions).astype(BF16)


def local(
    text_states,
    image_states,
    caption_lengths,
    text_query,
    text_keyval,
    text_attend,
    text_up,
    text_down,
    text_qkv,
    text_output,
    text_gains,
    image_query,
    image_keyval,
    image_attend,
    image_up,
    image_down,
    image_qkv,
    image_output,
    image_gains,
    text_cotangent,
    image_cotangent,
):
    own_pairs = caption_lengths.shape[0]
    own_text = text_states.shape[0]
    text_len = own_text // own_pairs
    regions = image_states.shape[0] // own_pairs
    padded = -(-regions // 16) * 16
    own_image = own_pairs * padded
    pairs = 2 * own_pairs
    d_t, d_i = text_states.shape[1], image_states.shape[1]
    stream = lax.axis_index("stream")
    core = lax.axis_index("dp") & 1
    side = jnp.stack([core, stream]).astype(jnp.int32)

    far_put = spread(own_pairs, regions, padded, 0, 2 * own_image)
    near_put = spread(own_pairs, regions, padded, own_image, 2 * own_image)
    trim = near_put[own_image:].T

    def both_images(near):
        return (mm(far_put, stream_swap(near)) + mm(near_put, near)).astype(BF16)

    choice = choices(stream)
    image_all = both_images(image_states)
    far_text = stream_swap(text_states)
    text_all = jnp.concatenate([text_states, far_text])
    lens = jnp.concatenate([caption_lengths, stream_swap(caption_lengths)])
    image_cotangent, text_cotangent, text_all = tied(image_cotangent, text_cotangent, text_all)
    image_cot = both_images(image_cotangent)
    far_text_cot = stream_swap(text_cotangent)

    co_blocks = D_C // LANES
    co_cols = (0, 0, co_blocks)
    co_scale = (D_C // H_C) ** (-0.5)

    image_moves, text_moves = Exchange(), Exchange()
    image_moves.send(states=image_all)
    cots = [far_text_cot]

    def image_hook(name, value):
        if name == "self":
            value, cots[0] = tied(value, cots[0])
        return value

    image_out, image_da, image_dc, image_q, text_kv, image_sides, image_dg = stream_forward(
        lens,
        image_all,
        text_all,
        image_cot,
        (image_query, text_keyval, image_attend, image_up, image_down, image_qkv, image_output),
        image_gains,
        H_I,
        regions,
        None,
        pairs,
        image_moves,
        image_hook,
    )
    image_dq, text_dkv = attend_back(
        lens, image_q, text_kv, text_kv, image_dc, co_cols, pairs, co_blocks, 1, None, co_scale, False
    )
    image_moves.send(dq=image_dq)
    image_sides = image_sides(image_dq)
    text_moves.send(states=text_all, dkv=text_dkv)

    def sizes_of(*weights):
        return {name: weight.shape for name, weight in zip(NAMES, weights)}

    def gather_half(both, sizes):
        total = sum(m * n for m, n in sizes.values())
        total_rows = total // (2 * UNIT)
        plans = half_jobs(both, sizes, total)
        image = both["query"][0][0] is image_all
        return flat_grads(side, total_rows, plans, 6 if image else 14, resident=image)

    image_sizes = sizes_of(
        image_query, image_keyval, image_attend, image_up, image_down, image_qkv, image_output
    )
    text_sizes = sizes_of(
        text_query, text_keyval, text_attend, text_up, text_down, text_qkv, text_output
    )
    early = lax.axis_size("dp") == 16
    if early:
        image_flat = gather_half(image_sides, image_sizes)

    pieces = []

    def hook(name, value):
        if not early:
            return value
        if name == "co":
            value, flat = tied(value, image_flat)
            pieces.extend(piece_set(choice, flat, (1, 2, 1, 2), (1, 1, 1, 1)))
            value = after(value, pieces, "out")
            for piece in pieces[:2]:
                piece.send()
        if name == "mlp":
            (value,) = paced(pieces[:2], pieces[2:], (value,))
            for piece in pieces[2:]:
                piece.send()
        if name == "self":
            (value,) = paced(pieces[2:], (), (value,))
            pieces[:] = add_split(choice, ((2, pieces[0::2]), (1, pieces[1::2])))
            for piece in pieces:
                piece.send()
        if name == "back":
            (value,) = paced(pieces, (), (value,))
            pieces[:] = add_split(choice, ((3, pieces),))
            pieces[0].send()
        return value

    text_out, text_da, text_dc, text_q, image_kv, text_sides, text_dg = stream_forward(
        lens,
        text_all,
        image_all,
        jnp.concatenate([text_cotangent, cots[0]]),
        (text_query, image_keyval, text_attend, text_up, text_down, text_qkv, text_output),
        text_gains,
        H_T,
        None,
        regions,
        pairs,
        text_moves,
        hook,
    )
    gains = pack_gains(text_dg, image_dg)
    bits = [1 << b for b in range(lax.axis_size("dp").bit_length() - 1)]
    text_dq, image_dkv = attend_back(
        lens, text_q, image_kv, image_kv, text_dc, co_cols, pairs, co_blocks, 1, regions, co_scale, False
    )

    image_moves.send(dkv=image_dkv)
    text_moves.send(dq=text_dq)
    text_sides = text_sides(text_dq)
    text_sides["keyval"] = (text_moves.pair("states", text_all), text_moves.pair("dkv", text_dkv))

    def all_input_grads(text_dq, image_dq):
        text = input_grads(
            text_da, text_dq, text_dkv, text_out, trim[:1], text_query, text_keyval, 0, own_text
        )
        image = input_grads(
            image_da,
            image_dq,
            image_dkv,
            image_out,
            trim,
            image_query,
            image_keyval,
            own_image,
            own_pairs * regions,
        )
        return (*text, *image)

    if early:
        late = Late(
            choice,
            side,
            image_moves.pair("states", image_all),
            image_moves.pair("dkv", image_dkv),
        )
        near_dq, *rest = text_sides["query"][1]
        near_dq, late.out = tied(near_dq, late.out)
        text_sides["query"] = (text_sides["query"][0], (near_dq, *rest))
        late.send()
        text_flat = gather_half(text_sides, text_sizes)
        text_flat = after(text_flat, pieces + [late])
        text_pieces = piece_set(choice, text_flat, (1, 1, 1, 1), TEXT_SHARES)
        one, two, three, four = text_pieces
        late.turn()
        one.out, late.out, text_dq, image_dq, gains = tied(
            one.out, late.out, text_dq, image_dq, gains
        )
        one.send()
        late.send()
        gains = gain_step(gains, bits.pop())
        grads = all_input_grads(text_dq, image_dq)
        *grads, gains = paced((one, late), (two,), (*grads, gains))
        (one,) = add_split(choice, ((2, (one,)),))
        late.add(gather=True)
        two.send()
        one.send()
        gains = gain_step(gains, bits.pop())
        (gains,) = paced((one, two, late), (three,), (gains,))
        (one,) = add_split(choice, ((3, (one,)),))
        (two,) = add_split(choice, ((2, (two,)),))
        late.add()
        three.send()
        two.send()
        one.send()
        gains = gain_step(gains, bits.pop())
        (gains,) = paced((one, two, three, late), (four,), (gains,))
        (two,) = add_split(choice, ((3, (two,)),))
        (three,) = add_split(choice, ((2, (three,)),))
        four.send()
        three.send()
        two.send()
        gains = gain_step(gains, bits.pop())
        (gains,) = paced((two, three, four), (), (gains,))
        (three,) = add_split(choice, ((3, (three,)),))
        (four,) = add_split(choice, ((2, (four,)),))
        three.send()
        four.send()
        paced((three, four), ())
        (four,) = add_split(choice, ((3, (four,)),))
        four.send()
        unit = image_flat.shape[0] // 8 // 4
        starts, row = [], 0
        for piece in (one, two, three, four):
            starts.append((row,))
            row += piece.keep.shape[1]
        image_share, text_share = finished(
            choice,
            (pieces, (one, two, three, four)),
            (((0, 2 * unit, unit, 3 * unit),), tuple(starts)),
            (late.keep[0], late.far[0]),
        )
    else:
        image_sides["keyval"] = (
            image_moves.pair("states", image_all),
            image_moves.pair("dkv", image_dkv),
        )
        image_share = share_of(
            reduce_scatter(gather_half(image_sides, image_sizes), ((8, False),))
        )
        text_share = share_of(reduce_scatter(gather_half(text_sides, text_sizes), ((8, False),)))
        grads = all_input_grads(text_dq, image_dq)
        while bits:
            gains = gain_step(gains, bits.pop())
    text_grad, text_result, image_grad, image_result = grads
    text_gain_sum, image_gain_sum = unpack_gains(gains, text_dg.shape[1])
    return (
        text_result,
        image_result,
        text_grad,
        image_grad,
        text_share,
        image_share,
        text_gain_sum,
        image_gain_sum,
    )


def pack_gains(text_dg, image_dg):
    return jnp.concatenate([text_dg, image_dg], axis=1)


def gain_step(gains, bit):
    return gains + dp_swap(gains, bit)


def unpack_gains(gains, width):
    return gains[:, :width], gains[:, width:]


class Late:
    rows = 1280

    def __init__(self, choice, side, states, grads):
        self.choice = choice
        job = Job(states, grads, 0, states[0].shape[1], 768)
        flat = flat_grads(side, 4 * self.rows, [[job]], 2, True)
        self.keep, self.out = split(choice, flat, self.rows, ((0, self.rows, (0, 2), 1, LATE_Y),))
        self.bit = 2

    def send(self):
        self.far = dp_swap(self.out, self.bit)

    def turn(self):
        (piece,) = add_split(self.choice, ((LATE_OWN, (self,)),))
        self.keep, self.out, self.bit = piece.keep, piece.out, 4

    def add(self, gather=False):
        self.keep = plus(self.keep, self.far)
        if gather:
            route = []
            for i in range(16):
                z, y = i >> 2, (i >> 1) & 1
                goal = 1 if z & 1 else (0 if y else 2)
                if z != goal:
                    route.append((i, goal * 4 + (i & 3)))
            self.far = lax.ppermute(self.keep, "dp", route)
        else:
            self.far = lax.ppermute(self.keep, "stream", [(1, 0)])


def solution(mesh):
    split = P(("stream", "dp"), None)
    flat = P(("stream", "dp"))
    whole = P()
    return jax.shard_map(
        local,
        mesh=mesh,
        in_specs=(split, split, flat) + (whole,) * 16 + (split, split),
        out_specs=(split, split, split, split, flat, flat, whole, whole),
        check_vma=False,
    )
```

```python
import functools

import jax
import jax.numpy as jnp
from jax import lax
from jax.experimental import pallas as pl
from jax.experimental.pallas import tpu as pltpu
from jax.sharding import PartitionSpec as P

H_T = 12
H_I = 8
H_C = 8
D_C = 1024
LANES = 128
UNIT = 256
masked_score = -1e30
F32 = jnp.float32
BF16 = jnp.bfloat16


def mm(a, b):
    return jnp.dot(a, b, preferred_element_type=F32)


def mm_nt(a, b):
    return lax.dot_general(a, b, (((1,), (1,)), ((), ())), preferred_element_type=F32)


def mm_tn(a, b):
    return lax.dot_general(a, b, (((0,), (0,)), ((), ())), preferred_element_type=F32)


def cost(us):
    return pl.CostEstimate(flops=int(us * 1e9), bytes_accessed=1000, transcendentals=0)


def lane_block(ref, rows, block):
    return ref[rows, pl.ds(pl.multiple_of(block * LANES, LANES), LANES)]


def put_block(ref, rows, block, value):
    ref[rows, pl.ds(pl.multiple_of(block * LANES, LANES), LANES)] = value


def split_heads(block, heads_in):
    if heads_in == 1:
        return block
    lanes = lax.broadcasted_iota(jnp.int32, block.shape, 1)
    zero = jnp.zeros_like(block)
    low = lanes < LANES // 2
    return jnp.concatenate([jnp.where(low, block, zero), jnp.where(low, zero, block)], axis=0)


def side_by_side(block, heads_in):
    if heads_in == 1:
        return block
    rows = block.shape[0] // 2
    return jnp.concatenate([block[:rows], block[rows:]], axis=1)


def attend_kernel(
    lens_ref, q_ref, k_ref, v_ref, o_ref, *, pairs, blocks, cols, heads_in, fixed, scaling
):
    ql = q_ref.shape[0] // pairs
    kl = k_ref.shape[0] // pairs
    chain = heads_in * ql
    keys = lax.broadcasted_iota(jnp.int32, (chain, kl), 1)
    if fixed is None:
        masks = [keys < lens_ref[p] for p in range(pairs)]
    else:
        masks = [keys < fixed] * pairs

    @pl.loop(0, blocks)
    def _(j):
        scores = []
        for p in range(pairs):
            q = split_heads(lane_block(q_ref, slice(p * ql, (p + 1) * ql), cols[0] + j), heads_in)
            k = lane_block(k_ref, slice(p * kl, (p + 1) * kl), cols[1] + j)
            scores.append(jnp.where(masks[p], mm_nt(q, k) * scaling, masked_score))
        s = jnp.concatenate(scores, axis=0)
        raised = jnp.exp(s - jnp.max(s, axis=-1, keepdims=True))
        w = (raised * (1.0 / jnp.sum(raised, axis=-1, keepdims=True))).astype(BF16)
        for p in range(pairs):
            v = split_heads(lane_block(v_ref, slice(p * kl, (p + 1) * kl), cols[2] + j), heads_in)
            o = mm(side_by_side(w[p * chain : (p + 1) * chain], heads_in), v)
            put_block(o_ref, slice(p * ql, (p + 1) * ql), j, o.astype(BF16))


def attend(lens, q, k, v, cols, pairs, blocks, heads_in, fixed, scaling):
    rows = q.shape[0]
    krows = k.shape[0]
    same = k is v
    vmem = pl.BlockSpec(memory_space=pltpu.VMEM)
    operands = [lens, q, k] if same else [lens, q, k, v]
    if q is k:
        operands = [lens, q]

    def body(lens_ref, *refs, **kw):
        refs = list(refs)
        o_ref = refs.pop()
        while len(refs) < 3:
            refs.append(refs[-1])
        attend_kernel(lens_ref, *refs, o_ref, **kw)

    return pl.pallas_call(
        functools.partial(
            body,
            pairs=pairs,
            blocks=blocks,
            cols=cols,
            heads_in=heads_in,
            fixed=fixed,
            scaling=scaling,
        ),
        in_specs=[pl.BlockSpec(memory_space=pltpu.SMEM)] + [vmem] * (len(operands) - 1),
        out_specs=vmem,
        out_shape=jax.ShapeDtypeStruct((rows, blocks * LANES), BF16),
        compiler_params=pltpu.CompilerParams(vmem_limit_bytes=10 * 1024 * 1024),
        cost_estimate=cost(5),
        name="attend",
    )(*operands)


def attend_back_kernel(
    lens_ref,
    q_ref,
    k_ref,
    v_ref,
    g_ref,
    dq_ref,
    dk_ref,
    dv_ref,
    *,
    pairs,
    blocks,
    cols,
    out_cols,
    heads_in,
    fixed,
    scaling,
):
    ql = q_ref.shape[0] // pairs
    kl = k_ref.shape[0] // pairs
    keys = lax.broadcasted_iota(jnp.int32, (heads_in * kl, ql), 0)
    if heads_in == 2:
        keys = jnp.where(keys >= kl, keys - kl, keys)
    if fixed is None:
        masks = [keys < lens_ref[p] for p in range(pairs)]
    else:
        masks = [keys < fixed] * pairs

    @pl.loop(0, blocks)
    def _(j):
        scores, slopes = [], []
        for p in range(pairs):
            qs, ks = slice(p * ql, (p + 1) * ql), slice(p * kl, (p + 1) * kl)
            q, g = lane_block(q_ref, qs, cols[0] + j), lane_block(g_ref, qs, j)
            k = split_heads(lane_block(k_ref, ks, cols[1] + j), heads_in)
            v = split_heads(lane_block(v_ref, ks, cols[2] + j), heads_in)
            scores.append(jnp.where(masks[p], mm_nt(k, q) * scaling, masked_score))
            slopes.append(mm_nt(v, g))
        stacked = (pairs * heads_in, kl, ql)
        s = jnp.concatenate(scores, axis=0).reshape(stacked)
        dp = jnp.concatenate(slopes, axis=0).reshape(stacked)
        raised = jnp.exp(s - jnp.max(s, axis=1, keepdims=True))
        w = raised * (1.0 / jnp.sum(raised, axis=1, keepdims=True))
        inner = jnp.sum(w * dp, axis=1, keepdims=True)
        ds = (w * (dp - inner)).astype(BF16).reshape(-1, ql)
        w = w.astype(BF16).reshape(-1, ql)
        chain = heads_in * kl
        for p in range(pairs):
            qs, ks = slice(p * ql, (p + 1) * ql), slice(p * kl, (p + 1) * kl)
            own = slice(p * chain, (p + 1) * chain)
            q = split_heads(lane_block(q_ref, qs, cols[0] + j), heads_in)
            g = split_heads(lane_block(g_ref, qs, j), heads_in)
            k = split_heads(lane_block(k_ref, ks, cols[1] + j), heads_in)
            dq = mm_tn(ds[own], k) * scaling
            dk = mm(side_by_side(ds[own], heads_in), q) * scaling
            dv = mm(side_by_side(w[own], heads_in), g)
            put_block(dq_ref, qs, out_cols[0] + j, dq.astype(BF16))
            put_block(dk_ref, ks, out_cols[1] + j, dk.astype(BF16))
            put_block(dv_ref, ks, out_cols[2] + j, dv.astype(BF16))


def attend_back(lens, q, k, v, g, cols, pairs, blocks, heads_in, fixed, scaling, packed):
    rows = q.shape[0]
    krows = k.shape[0]
    vmem = pl.BlockSpec(memory_space=pltpu.VMEM)
    width = blocks * LANES
    if packed:
        operands = [lens, q, g]
        out_cols = (0, blocks, 2 * blocks)
        out_shape = jax.ShapeDtypeStruct((rows, 3 * width), BF16)
        out_specs = vmem
    else:
        operands = [lens, q, k, g]
        out_cols = (0, 0, blocks)
        out_shape = [
            jax.ShapeDtypeStruct((rows, width), BF16),
            jax.ShapeDtypeStruct((krows, 2 * width), BF16),
        ]
        out_specs = [vmem, vmem]

    def body(lens_ref, *refs, **kw):
        if packed:
            q_ref, g_ref, out_ref = refs
            ins, outs = (q_ref, q_ref, q_ref, g_ref), (out_ref,) * 3
        else:
            q_ref, k_ref, g_ref, dq_ref, dkv_ref = refs
            ins, outs = (q_ref, k_ref, k_ref, g_ref), (dq_ref, dkv_ref, dkv_ref)
        attend_back_kernel(lens_ref, *ins, *outs, **kw)

    return pl.pallas_call(
        functools.partial(
            body,
            pairs=pairs,
            blocks=blocks,
            cols=cols,
            out_cols=out_cols,
            heads_in=heads_in,
            fixed=fixed,
            scaling=scaling,
        ),
        in_specs=[pl.BlockSpec(memory_space=pltpu.SMEM)] + [vmem] * (len(operands) - 1),
        out_specs=out_specs,
        out_shape=out_shape,
        compiler_params=pltpu.CompilerParams(vmem_limit_bytes=10 * 1024 * 1024),
        cost_estimate=cost(6),
        name="attend_back",
    )(*operands)


class Job:
    def __init__(self, a, b, low, high, place):
        self.a, self.b = a, b
        self.low, self.count = low, high - low
        self.columns = b[3]
        self.place = place


def flat_kernel(side_ref, *refs, plans, found, quarter, resident):
    out_ref, chosen_ref, stage_ref = refs[len(found) : len(found) + 3]
    core = side_ref[0]
    depth = chosen_ref.shape[0] // 2
    if not resident:
        a_buf, b_buf, in_sem = refs[-3:]

    def loads(jobs, k):
        job, slot = jobs[k], k % 2
        copies = []
        for side, buf, start, width in (
            (job.a, a_buf, job.a[2] + job.low, job.count),
            (job.b, b_buf, job.b[2], job.columns),
        ):
            for half in range(2):
                copies.append(
                    pltpu.make_async_copy(
                        refs[found[id(side[half])]].at[:, start : start + width],
                        buf.at[slot, half * depth : (half + 1) * depth, 0:width],
                        in_sem.at[slot, len(copies)],
                    )
                )
        return copies

    def run(jobs):
        if not resident:
            for copy in loads(jobs, 0):
                copy.start()
        for k, job in enumerate(jobs):
            if resident:
                a_refs = [refs[found[id(job.a[half])]] for half in range(2)]
                b_refs = [refs[found[id(job.b[half])]] for half in range(2)]
                a_first, b_first = job.a[2] + job.low, job.b[2]
            else:
                if k + 1 < len(jobs):
                    for copy in loads(jobs, k + 1):
                        copy.start()
                for copy in loads(jobs, k):
                    copy.wait()
                halves = [slice(0, depth), slice(depth, 2 * depth)]
                a_refs = [a_buf.at[k % 2, half] for half in halves]
                b_refs = [b_buf.at[k % 2, half] for half in halves]
                a_first = b_first = 0
            units = job.columns // (2 * UNIT if quarter else UNIT)
            for u in range(units):
                at = 4 * u + 2 * side_ref[1] + core if quarter else 2 * u + core
                block = pl.ds(pl.multiple_of(at * LANES + b_first, LANES), LANES)
                for half in range(2):
                    chosen_ref[half * depth : (half + 1) * depth, u * LANES : (u + 1) * LANES] = (
                        b_refs[half][:, block]
                    )
            bm = best_rows(job.count, units)
            rows = bm * units

            @pl.loop(0, job.count // bm)
            def _(i, job=job, units=units, bm=bm, rows=rows, a_refs=a_refs, a_first=a_first):
                columns = pl.ds(pl.multiple_of(a_first + i * bm, LANES), bm)
                a = jnp.concatenate([a_ref[:, columns] for a_ref in a_refs], axis=0).T
                for u0 in range(0, units, 4):
                    u1 = min(u0 + 4, units)
                    total = mm(a, chosen_ref[:, u0 * LANES : u1 * LANES])
                    for u in range(u0, u1):
                        stage_ref[pl.ds(u, bm, stride=units), :] = total[
                            :, (u - u0) * LANES : (u - u0 + 1) * LANES
                        ]
                first = pl.multiple_of(job.place + i * rows, LANES)
                out_ref[pl.ds(first, rows), :] = stage_ref[:rows].astype(BF16)

    if len(plans) == 1:
        run(plans[0])
    else:
        for side, jobs in enumerate(plans):

            @pl.when(side_ref[1] == side)
            def _(jobs=jobs):
                run(jobs)


def best_rows(count, units):
    most = 512 if units <= 8 else 384
    return max(size for size in range(LANES, most + 1, LANES) if count % size == 0)


def flat_grads(side, total_rows, plans, us, quarter=False, resident=True):
    arrays, found = [], {}
    jobs = [job for plan in plans for job in plan]
    for job in jobs:
        for array in (*job.a[:2], *job.b[:2]):
            if id(array) not in found:
                found[id(array)] = len(arrays)
                arrays.append(array)
    depth = 2 * arrays[0].shape[0]
    widest = max(job.columns for job in jobs)
    tallest = max(job.count for job in jobs)
    factor = 2 * UNIT if quarter else UNIT
    rows = max(best_rows(job.count, job.columns // factor) * job.columns // factor for job in jobs)
    held = 2 * depth * widest * LANES // factor + 4 * rows * LANES
    scratch = [
        pltpu.VMEM((depth, widest * LANES // factor), BF16),
        pltpu.VMEM((rows, LANES), F32),
    ]
    if not resident:
        held += 4 * depth * (tallest + widest)
        scratch += [
            pltpu.VMEM((2, depth, tallest), BF16),
            pltpu.VMEM((2, depth, widest), BF16),
            pltpu.SemaphoreType.DMA((2, 4)),
        ]
    place = pltpu.VMEM if resident else pltpu.HBM
    return pl.pallas_call(
        functools.partial(
            flat_kernel, plans=plans, found=found, quarter=quarter, resident=resident
        ),
        in_specs=[pl.BlockSpec(memory_space=pltpu.SMEM)]
        + [pl.BlockSpec(memory_space=place)] * len(arrays),
        out_specs=pl.BlockSpec(memory_space=pltpu.VMEM),
        out_shape=jax.ShapeDtypeStruct((total_rows, LANES), BF16),
        scratch_shapes=scratch,
        compiler_params=pltpu.CompilerParams(vmem_limit_bytes=held + (7 if resident else 8) * 1024 * 1024),
        cost_estimate=cost(us),
        name="flat_grads",
    )(side, *arrays)


def dp_swap(block, bit):
    count = lax.axis_size("dp")
    return lax.ppermute(block, "dp", [(i, i ^ bit) for i in range(count)])


def stream_swap(block):
    return lax.ppermute(block, "stream", [(0, 1), (1, 0)])


def pick(block, index, axis=0):
    return lax.dynamic_index_in_dim(block, index, axis, keepdims=False)


def plus(a, b):
    return (a.astype(F32) + b.astype(F32)).astype(BF16)


def tied(*values):
    return lax.optimization_barrier(values)


def scatter_parts(flat, cuts):
    count = lax.axis_size("dp")
    top = count.bit_length() - 2
    bits = tuple(range(top, 0, -1))
    rows = flat.shape[0] // (count // 2)
    blocks = flat.reshape((2,) * len(bits) + (rows, LANES))
    natural = tuple(range(1, top + 1))
    turned = natural[1:2] + natural[:1] + natural[2:]
    parts, start = [], 0
    for share, turn in cuts:
        part = lax.slice_in_dim(blocks, start, start + rows * share // 8, axis=len(bits))
        start += rows * share // 8
        parts.append((part, bits, turned if turn else natural))
    return parts


def scatter_step(parts):
    me = lax.axis_index("dp")
    done = []
    for block, left, order in parts:
        bit = order[0]
        axis = left.index(bit)
        mine = (me >> bit) & 1
        keep = pick(block, mine, axis)
        far = dp_swap(pick(block, 1 - mine, axis), 1 << bit)
        block = plus(keep, far) if len(order) > 1 else keep.astype(F32) + far.astype(F32)
        done.append((block, left[:axis] + left[axis + 1 :], order[1:]))
    return done


def scatter_end(parts):
    while parts[0][2]:
        parts = scatter_step(parts)
    blocks = [block for block, _, _ in parts]
    return jnp.concatenate(blocks) if len(blocks) > 1 else blocks[0]


def reduce_scatter(flat, cuts):
    return scatter_end(scatter_parts(flat, cuts))


def share_of(result):
    core = lax.axis_index("dp") & 1
    halves = result.reshape(2, result.shape[0] // 2, LANES)
    mine = pick(halves, core)
    far = dp_swap(pick(halves, 1 - core), 1)
    first = jnp.where(core == 0, mine, far)
    second = jnp.where(core == 0, far, mine)
    return jnp.stack([first, second], axis=1).reshape(-1)


def choices(stream):
    me = lax.axis_index("dp")
    y, odd = (me >> 1) & 1, (me >> 2) & 1
    own = jnp.where(y == 1, odd, 1 - odd)
    values = [me & 1, y, odd, (me >> 3) & 1, 1 - y, own, stream, me >> 1]
    return jnp.stack(values).astype(jnp.int32)


LATE_Y, LATE_OWN, STREAM, CHIP = 4, 5, 6, 7
TEXT_SHARES = (48, 46, 38, 24)


def split_kernel(choice_ref, flat_ref, *refs, chunk, cuts):
    for k, (start, rows, bases, weight, which) in enumerate(cuts):
        mine = choice_ref[which]
        for i, base in enumerate(bases):
            for out_ref, index in ((refs[2 * k], mine), (refs[2 * k + 1], 1 - mine)):
                first = (base + index * weight) * chunk + start
                out_ref[i] = flat_ref[pl.ds(pl.multiple_of(first, 16), rows), :]


def split(choice, flat, chunk, cuts):
    shapes = [
        jax.ShapeDtypeStruct((len(bases), rows, LANES), BF16)
        for _, rows, bases, _, _ in cuts
        for _ in range(2)
    ]
    return pl.pallas_call(
        functools.partial(split_kernel, chunk=chunk, cuts=cuts),
        in_specs=[
            pl.BlockSpec(memory_space=pltpu.SMEM),
            pl.BlockSpec(memory_space=pltpu.VMEM),
        ],
        out_specs=[pl.BlockSpec(memory_space=pltpu.VMEM)] * len(shapes),
        out_shape=shapes,
        compiler_params=pltpu.CompilerParams(vmem_limit_bytes=8 * 1024 * 1024),
        cost_estimate=cost(3),
        name="split",
    )(choice, flat)


def piece_set(choice, flat, firsts, shares):
    chunk = flat.shape[0] // 8
    unit = chunk // sum(shares)
    cuts, start = [], 0
    for first, share in zip(firsts, shares):
        bits = [bit for bit in (3, 2, 1) if bit != first]
        bases = tuple(
            sum(((n >> (1 - at)) & 1) << (b - 1) for at, b in enumerate(bits)) for n in range(4)
        )
        cuts.append((start, unit * share, bases, 1 << (first - 1), first))
        start += unit * share
    arrays = split(choice, flat, chunk, tuple(cuts))
    return [
        Piece(keep, out, first) for keep, out, first in zip(arrays[::2], arrays[1::2], firsts)
    ]


class Piece:
    def __init__(self, keep, out, bit):
        self.keep, self.out, self.bit = keep, out, bit

    def send(self):
        self.far = dp_swap(self.out, 1 << self.bit)


def after(value, pieces, name="far"):
    value, *got = tied(value, *(getattr(piece, name) for piece in pieces))
    for piece, array in zip(pieces, got):
        setattr(piece, name, array)
    return value


def paced(came, leaving, values=()):
    got = tied(*(item.far for item in came), *(item.out for item in leaving), *values)
    for item, array in zip(came, got):
        item.far = array
    for item, array in zip(leaving, got[len(came) :]):
        item.out = array
    return got[len(came) + len(leaving) :]


def added(a_ref, b_ref, index):
    return a_ref[index].astype(F32) + b_ref[index].astype(F32)


def add_split_kernel(choice_ref, *refs, plan, inputs):
    outs = refs[2 * inputs :]
    for k, base, stride, which, out, at in plan:
        keep_ref, far_ref = refs[2 * k : 2 * k + 2]
        mine = choice_ref[which]
        for ref, index in ((outs[2 * out], mine), (outs[2 * out + 1], 1 - mine)):
            ref[at] = added(keep_ref, far_ref, base + index * stride).astype(BF16)


def add_split(choice, groups, which=None):
    operands, plan, shapes = [], [], []
    for out, (bit, pieces) in enumerate(groups):
        at = 0
        for piece in pieces:
            for base in range(0, piece.keep.shape[0], 2):
                plan.append((len(operands) // 2, base, 1, which or bit, out, at))
                at += 1
            operands += [piece.keep, piece.far]
        shape = jax.ShapeDtypeStruct((at,) + pieces[0].keep.shape[1:], BF16)
        shapes += [shape, shape]
    vmem = pl.BlockSpec(memory_space=pltpu.VMEM)
    arrays = pl.pallas_call(
        functools.partial(add_split_kernel, plan=tuple(plan), inputs=len(operands) // 2),
        in_specs=[pl.BlockSpec(memory_space=pltpu.SMEM)] + [vmem] * len(operands),
        out_specs=[vmem] * len(shapes),
        out_shape=shapes,
        compiler_params=pltpu.CompilerParams(vmem_limit_bytes=8 * 1024 * 1024),
        cost_estimate=cost(1),
        name="add_split",
    )(choice, *operands)
    return [
        Piece(arrays[2 * out], arrays[2 * out + 1], bit) for out, (bit, _) in enumerate(groups)
    ]


def finish_kernel(choice_ref, *refs, rows):
    refs = list(refs)
    pairs = [[(refs.pop(0), refs.pop(0)) for _ in group] for group in rows]
    near_ref, far_ref = refs.pop(0), refs.pop(0)
    out_ref, send_ref, *totals, joined_ref = refs
    for total_ref, group, starts in zip(totals, pairs, rows):
        for (keep_ref, came_ref), firsts in zip(group, starts):
            count = keep_ref.shape[1]
            for at, first in enumerate(firsts):
                total_ref[first : first + count] = added(keep_ref, came_ref, at)
    half = near_ref.shape[0]
    joined_ref[pl.ds(0, half, stride=2), :] = near_ref[...].astype(F32)
    joined_ref[pl.ds(1, half, stride=2), :] = far_ref[...].astype(F32)
    image_ref = totals[0]
    total_rows = image_ref.shape[0]
    chip = choice_ref[CHIP]
    first = jnp.where(chip == 1, 1536, 0)
    last = jnp.where(chip == 4, 2048, total_rows)
    here = (chip >= 1) & (chip <= 4) & (choice_ref[STREAM] == 0)
    last = jnp.where(here, last, 0)
    at = lax.broadcasted_iota(jnp.int32, (total_rows, 1), 0)
    image_ref[...] = jnp.where((at >= first) & (at < last), joined_ref[...], image_ref[...])
    core = choice_ref[0]
    row = 0
    for total_ref in totals:
        half = total_ref.shape[0] // 2
        for ref, index in ((out_ref, core), (send_ref, 1 - core)):
            ref[row : row + half, :] = total_ref[pl.ds(pl.multiple_of(index * half, 8), half), :]
        row += half


def join_kernel(choice_ref, near_ref, far_ref, *outs):
    core = choice_ref[0]
    row = 0
    for out_ref in outs:
        half = out_ref.shape[0] // 2
        out_ref[pl.ds(core, half, stride=2), :] = near_ref[row : row + half, :]
        out_ref[pl.ds(1 - core, half, stride=2), :] = far_ref[row : row + half, :]
        row += half


def finished(choice, groups, rows, late):
    sizes = [
        sum(piece.keep.shape[0] * piece.keep.shape[1] for piece in group) for group in groups
    ]
    vmem = pl.BlockSpec(memory_space=pltpu.VMEM)
    smem = pl.BlockSpec(memory_space=pltpu.SMEM)
    operands = [ref for group in groups for piece in group for ref in (piece.keep, piece.far)]
    operands += list(late)
    half = jax.ShapeDtypeStruct((sum(sizes) // 2, LANES), F32)
    near, send = pl.pallas_call(
        functools.partial(finish_kernel, rows=rows),
        in_specs=[smem] + [vmem] * len(operands),
        out_specs=[vmem] * 2,
        out_shape=[half] * 2,
        scratch_shapes=[pltpu.VMEM((rows, LANES), F32) for rows in (*sizes, sizes[0])],
        compiler_params=pltpu.CompilerParams(vmem_limit_bytes=12 * 1024 * 1024),
        cost_estimate=cost(3),
        name="finish",
    )(choice, *operands)
    joined = pl.pallas_call(
        join_kernel,
        in_specs=[smem, vmem, vmem],
        out_specs=[vmem] * 2,
        out_shape=[jax.ShapeDtypeStruct((rows, LANES), F32) for rows in sizes],
        compiler_params=pltpu.CompilerParams(vmem_limit_bytes=12 * 1024 * 1024),
        cost_estimate=cost(2),
        name="join",
    )(choice, near, dp_swap(send, 1))
    return [block.reshape(-1) for block in joined]


CHUNK = 64
ROWS = 128
WIDEST = 1024
WIDEST_GELU = 1024


def tiles(columns, body, widest=None):
    size = max(c for c in range(LANES, (widest or WIDEST) + 1, LANES) if columns % c == 0)
    if size == columns:
        return body(slice(0, columns))

    @pl.loop(0, columns // size)
    def _(j):
        body(pl.ds(pl.multiple_of(j * size, size), size))


def views(pack_ref, *widths):
    found, start = [], 0
    for width in widths:
        found.append(pack_ref.at[:, start : start + width])
        start += width
    return found


def row_chunks(rows, body):
    size = ROWS if rows % ROWS == 0 else CHUNK

    @pl.loop(0, rows // size)
    def _(i):
        body(i * size, pl.ds(pl.multiple_of(i * size, size), size), size)


def normed_chunk(a):
    centred = a - jnp.mean(a, axis=-1, keepdims=True)
    inverse = lax.rsqrt(jnp.mean(centred * centred, axis=-1, keepdims=True) + 1e-05)
    return centred * inverse, inverse


def normed_back_chunk(grad, n, inverse, gain_row):
    scaled = grad * gain_row
    low = jnp.mean(scaled, axis=-1, keepdims=True)
    tilt = jnp.mean(scaled * n, axis=-1, keepdims=True)
    return (scaled - low - n * tilt) * inverse, jnp.sum(grad * n, axis=0, keepdims=True)


def co_kernel(
    lens_ref, x_ref, given_ref, source_ref, g_ref, wmade_ref, wat_ref,
    made_ref, pack_ref, n_ref, inv_ref, a_ref, *, pairs, fixed, scaling, makes_kv,
):
    rows, width = x_ref.shape
    c_ref, h_ref = views(pack_ref, D_C, width)

    def made_tile(cols):
        made_ref[:, cols] = mm(source_ref[...], wmade_ref[:, cols]).astype(BF16)

    def a_tile(cols):
        a_ref[:, cols] = x_ref[:, cols].astype(F32) + mm(c_ref[...], wat_ref[:, cols])

    def norm(i, at, size):
        n, inverse = normed_chunk(a_ref[at, :])
        n_ref[at, :] = n
        inv_ref[at, :] = jnp.broadcast_to(inverse, (size, LANES))
        h_ref[at, :] = (n * g_ref[0:1, :]).astype(BF16)

    tiles(made_ref.shape[1], made_tile)
    q_ref, kv_ref = (given_ref, made_ref) if makes_kv else (made_ref, given_ref)
    blocks = q_ref.shape[1] // LANES
    attend_kernel(
        lens_ref, q_ref, kv_ref, kv_ref, c_ref, pairs=pairs, blocks=blocks,
        cols=(0, 0, blocks), heads_in=1, fixed=fixed, scaling=scaling,
    )
    tiles(width, a_tile)
    row_chunks(rows, norm)


def mlp_kernel(
    pack1_ref, n1_ref, g_ref, wup_ref, wdown_ref, wqkv_ref,
    pack_ref, slope_ref, n_ref, inv_ref, r_ref, a_ref,
):
    rows, width = n1_ref.shape
    _, h1_ref = views(pack1_ref, D_C, width)
    hid_ref, h_ref = views(pack_ref, wup_ref.shape[1], width)

    def up_tile(cols):
        u_all = mm(h1_ref[...], wup_ref[:, cols])
        for at in range(0, rows, CHUNK):
            u = u_all[at : at + CHUNK]
            share = 0.5 + 0.5 * lax.erf(u * 0.7071067811865476)
            hid_ref[at : at + CHUNK, cols] = (u * share).astype(BF16)
            slope = share + u * (0.3989422804014327 * jnp.exp(-0.5 * u * u))
            slope_ref[at : at + CHUNK, cols] = slope.astype(BF16)

    def down_tile(cols):
        a_ref[:, cols] = n1_ref[:, cols] * g_ref[0:1, cols] + mm(hid_ref[...], wdown_ref[:, cols])

    def norm(i, at, size):
        n, inverse = normed_chunk(a_ref[at, :])
        n_ref[at, :] = n
        inv_ref[at, :] = jnp.broadcast_to(inverse, (size, LANES))
        h_ref[at, :] = (n * g_ref[1:2, :]).astype(BF16)

    def qkv_tile(cols):
        r_ref[:, cols] = mm(h_ref[...], wqkv_ref[:, cols]).astype(BF16)

    tiles(wup_ref.shape[1], up_tile, WIDEST_GELU)
    tiles(width, down_tile)
    row_chunks(rows, norm)
    tiles(r_ref.shape[1], qkv_tile)


def self_kernel(
    lens_ref, r_ref, n2_ref, g_ref, wout_ref, cot_ref,
    pack_ref, y_ref, de_ref, dg_ref, a_ref, dz_ref,
    *, pairs, heads_in, fixed, scaling,
):
    rows, width = n2_ref.shape
    z_ref, de_low_ref, dr_ref = views(pack_ref, width, width, 3 * width)
    blocks = width // LANES
    cols = (0, blocks, 2 * blocks)
    shared = dict(
        pairs=pairs, blocks=blocks, cols=cols, heads_in=heads_in, fixed=fixed, scaling=scaling
    )

    def out_tile(at):
        a_ref[:, at] = n2_ref[:, at] * g_ref[1:2, at] + mm(z_ref[...], wout_ref[:, at])

    def last(start, at, size):
        n, inverse = normed_chunk(a_ref[at, :])
        y = n * g_ref[2:3, :]
        grad = cot_ref[at, :].astype(F32)
        if fixed is None:
            slots = rows // pairs
            place = lax.broadcasted_iota(jnp.int32, (size, 1), 0) + lax.rem(start, slots)
            valid = (place < lens_ref[lax.div(start, slots)]).astype(F32)
            y, grad = y * valid, grad * valid
        y_ref[at, :] = y.astype(BF16)
        de, dg = normed_back_chunk(grad, n, inverse, g_ref[2:3, :])
        de_ref[at, :] = de
        de_low_ref[at, :] = de.astype(BF16)
        dg_ref[...] += dg

    def dz_tile(at):
        dz_ref[:, at] = mm_nt(de_low_ref[...], wout_ref[at, :]).astype(BF16)

    attend_kernel(lens_ref, r_ref, r_ref, r_ref, z_ref, **shared)
    tiles(width, out_tile)
    dg_ref[...] = jnp.zeros_like(dg_ref)
    row_chunks(rows, last)
    tiles(width, dz_tile)
    attend_back_kernel(
        lens_ref, r_ref, r_ref, r_ref, dz_ref, dr_ref, dr_ref, dr_ref, out_cols=cols, **shared
    )


def mlp_back_kernel(
    pack3_ref, de_ref, n2_ref, inv2_ref, g_ref, slope_ref, wqkv_ref, wdown_ref,
    pack_ref, db_ref, dg_ref, a_ref,
):
    rows, width = n2_ref.shape
    _, _, dr_ref = views(pack3_ref, width, width, 3 * width)
    db_low_ref, du_ref = views(pack_ref, width, slope_ref.shape[1])
    dg_ref[...] = jnp.zeros_like(dg_ref)

    def second_tile(at):
        a_ref[:, at] = de_ref[:, at] + mm_nt(dr_ref[...], wqkv_ref[at, :])

    def second_norm(i, at, size):
        db, dg = normed_back_chunk(a_ref[at, :], n2_ref[at, :], inv2_ref[at, 0:1], g_ref[1:2, :])
        db_ref[at, :] = db
        db_low_ref[at, :] = db.astype(BF16)
        dg_ref[...] += dg

    def du_tile(at):
        grad = mm_nt(db_low_ref[...], wdown_ref[at, :])
        du_ref[:, at] = (grad * slope_ref[:, at].astype(F32)).astype(BF16)

    tiles(width, second_tile)
    row_chunks(rows, second_norm)
    tiles(du_ref.shape[1], du_tile)


def context_back_kernel(
    pack4_ref, db_ref, n1_ref, inv1_ref, g_ref, wup_ref, wat_ref,
    da_low_ref, da_ref, dc_ref, dg_ref, a_ref,
):
    rows, width = n1_ref.shape
    _, du_ref = views(pack4_ref, width, wup_ref.shape[1])
    dg_ref[...] = jnp.zeros_like(dg_ref)

    def first_tile(at):
        a_ref[:, at] = db_ref[:, at] + mm_nt(du_ref[...], wup_ref[at, :])

    def first_norm(i, at, size):
        da, dg = normed_back_chunk(a_ref[at, :], n1_ref[at, :], inv1_ref[at, 0:1], g_ref[0:1, :])
        da_ref[at, :] = da
        da_low_ref[at, :] = da.astype(BF16)
        dg_ref[...] += dg

    def dc_tile(at):
        dc_ref[:, at] = mm_nt(da_low_ref[...], wat_ref[at, :]).astype(BF16)

    tiles(width, first_tile)
    row_chunks(rows, first_norm)
    tiles(dc_ref.shape[1], dc_tile)


def fused(kernel, operands, outs, scratch, name, us, smem_first=False, limit=11):
    vmem = pl.BlockSpec(memory_space=pltpu.VMEM)
    in_specs = [vmem] * len(operands)
    if smem_first:
        in_specs[0] = pl.BlockSpec(memory_space=pltpu.SMEM)
    return pl.pallas_call(
        kernel,
        in_specs=in_specs,
        out_specs=[vmem] * len(outs),
        out_shape=[jax.ShapeDtypeStruct(shape, kind) for shape, kind in outs],
        scratch_shapes=[pltpu.VMEM(shape, kind) for shape, kind in scratch],
        compiler_params=pltpu.CompilerParams(vmem_limit_bytes=limit * 1024 * 1024),
        cost_estimate=cost(us),
        name=name,
    )(*operands)


def co_forward(lens, states, given, source, gains, made_w, attend_w, pairs, fixed):
    rows, width = states.shape
    made, pack1, n1, inv1 = fused(
        functools.partial(
            co_kernel,
            pairs=pairs,
            fixed=fixed,
            scaling=(D_C // H_C) ** (-0.5),
            makes_kv=made_w.shape[1] == 2 * D_C,
        ),
        (lens, states, given, source, gains, made_w, attend_w),
        [
            ((source.shape[0], made_w.shape[1]), BF16),
            ((rows, D_C + width), BF16),
            ((rows, width), F32),
            ((rows, LANES), F32),
        ],
        [((rows, width), F32)],
        "co_forward",
        7,
        True,
    )
    return made, pack1, n1, inv1


def mlp_forward(pack1, n1, gains, up_w, down_w, qkv_w):
    rows, width = n1.shape
    hidden = up_w.shape[1]
    return fused(
        mlp_kernel,
        (pack1, n1, gains, up_w, down_w, qkv_w),
        [
            ((rows, hidden + width), BF16),
            ((rows, hidden), BF16),
            ((rows, width), F32),
            ((rows, LANES), F32),
            ((rows, 3 * width), BF16),
        ],
        [((rows, width), F32)],
        "mlp_forward",
        rows / 40,
    )


def self_turn(lens, r, n2, gains, output_w, cot, pairs, heads, fixed):
    rows, width = n2.shape
    size = width // heads
    return fused(
        functools.partial(
            self_kernel, pairs=pairs, heads_in=LANES // size, fixed=fixed, scaling=size ** (-0.5)
        ),
        (lens, r, n2, gains, output_w, cot),
        [
            ((rows, 5 * width), BF16),
            ((rows, width), BF16),
            ((rows, width), F32),
            ((1, width), F32),
        ],
        [((rows, width), F32), ((rows, width), BF16)],
        "self_turn",
        rows / 128 + 9,
        True,
    )


def input_kernel(da_ref, dq_ref, dkv_ref, y_ref, trim_ref, wq_ref, wkv_ref, *outs, first):
    grad_ref, result_ref = outs
    rows = pl.ds(first, da_ref.shape[0] // 2)
    grad = da_ref[rows, :] + mm_nt(dq_ref[rows, :], wq_ref[...])
    grad = (grad + mm_nt(dkv_ref[rows, :], wkv_ref[...])).astype(BF16)
    y = y_ref[rows, :]
    if trim_ref.shape[0] < 8:
        grad_ref[...], result_ref[...] = grad, y
    else:
        grad_ref[...] = mm(trim_ref[...], grad).astype(BF16)
        result_ref[...] = mm(trim_ref[...], y).astype(BF16)


def input_grads(da, dq, dkv, y, trim, query_w, keyval_w, first, own):
    vmem = pl.BlockSpec(memory_space=pltpu.VMEM)
    return pl.pallas_call(
        functools.partial(input_kernel, first=first),
        in_specs=[vmem] * 7,
        out_specs=[vmem] * 2,
        out_shape=[jax.ShapeDtypeStruct((own, da.shape[1]), BF16)] * 2,
        compiler_params=pltpu.CompilerParams(vmem_limit_bytes=10 * 1024 * 1024),
        cost_estimate=cost(0.2),
        name="input_grads",
    )(da, dq, dkv, y, trim, query_w, keyval_w)


def mlp_back(pack3, de, n2, inv2, gains, slope, qkv_w, down_w):
    rows, width = n2.shape
    return fused(
        mlp_back_kernel,
        (pack3, de, n2, inv2, gains, slope, qkv_w, down_w),
        [
            ((rows, width + slope.shape[1]), BF16),
            ((rows, width), F32),
            ((1, width), F32),
        ],
        [((rows, width), F32)],
        "mlp_back",
        rows / 70,
    )


def context_back(pack4, db, n1, inv1, gains, up_w, attend_w):
    rows, width = n1.shape
    return fused(
        context_back_kernel,
        (pack4, db, n1, inv1, gains, up_w, attend_w),
        [
            ((rows, width), BF16),
            ((rows, width), F32),
            ((rows, D_C), BF16),
            ((1, width), F32),
        ],
        [((rows, width), F32)],
        "context_back",
        rows / 80,
    )


class Exchange:
    def __init__(self):
        self.far = {}
        self.pending = []
        self.parts = None

    def send(self, **arrays):
        for name, array in arrays.items():
            self.far[name] = dp_swap(array, 1)
            self.pending.append(name)

    def settle(self, value):
        names, self.pending = self.pending, []
        if names:
            value, *got = tied(value, *(self.far[name] for name in names))
            self.far.update(zip(names, got))
        return value

    def pair(self, name, array, start=0, width=None):
        return array, self.far[name], start, width or array.shape[1]


def stream_forward(
    lens, states, given, source, cot, weights, gains, heads, fixed, other_fixed, pairs, moves, hook
):
    made_w, attend_w, up_w, down_w, qkv_w, output_w = weights
    made, pack1, n1, inv1 = co_forward(
        lens, states, given, source, gains, made_w, attend_w, pairs, other_fixed
    )
    pack1 = moves.settle(hook("co", pack1))
    moves.send(pack1=pack1)
    pack2, slope, n2, inv2, r = mlp_forward(pack1, n1, gains, up_w, down_w, qkv_w)
    r, pack2 = tied(moves.settle(hook("mlp", r)), pack2)
    moves.send(pack2=pack2)
    pack3, result, de, dg2 = self_turn(lens, r, n2, gains, output_w, cot, pairs, heads, fixed)
    pack3 = moves.settle(hook("self", pack3))
    moves.send(pack3=pack3)
    pack4, db, dg1 = mlp_back(pack3, de, n2, inv2, gains, slope, qkv_w, down_w)
    pack4 = moves.settle(hook("mid", pack4))
    moves.send(pack4=pack4)
    da_low, da, dc, dg0 = context_back(pack4, db, n1, inv1, gains, up_w, attend_w)
    dc = moves.settle(hook("back", dc))
    width, hidden = up_w.shape

    def sides(dq, da_low):
        def side(number, start, count):
            pack = (pack1, pack2, pack3, pack4)[number - 1]
            return moves.pair("pack%d" % number, pack, start, count)

        return {
            "query": (moves.pair("states", states), moves.pair("dq", dq)),
            "attend": (side(1, 0, D_C), moves.pair("da", da_low)),
            "up": (side(1, D_C, width), side(4, width, hidden)),
            "down": (side(2, 0, hidden), side(4, 0, width)),
            "qkv": (side(2, hidden, width), side(3, 2 * width, 3 * width)),
            "output": (side(3, 0, width), side(3, width, width)),
        }

    return result, (da, da_low), dc, made, sides, jnp.concatenate([dg0, dg1, dg2])


NAMES = ("query", "keyval", "attend", "up", "down", "qkv", "output")


def half_jobs(both, sizes, total):
    plans, filled = ([], []), 0
    for name in NAMES:
        m, n = sizes[name]
        room = min(max((total // 2 - filled) // n, 0), m)
        for plan, low, high in ((plans[0], 0, room), (plans[1], room, m)):
            if low < high and name in both:
                start = filled + low * n - (0 if plan is plans[0] else total // 2)
                step = min(high - low, 1024)
                for at in range(low, high, step):
                    place = (start + (at - low) * n) // UNIT
                    plan.append(Job(*both[name], at, at + step, place))
        filled += m * n
    return plans


def spread(count, regions, padded, offset, rows):
    target = lax.broadcasted_iota(jnp.int32, (rows, count * regions), 0) - offset
    source = lax.broadcasted_iota(jnp.int32, (rows, count * regions), 1)
    return (target == source // regions * padded + source % regions).astype(BF16)


def local(
    text_states,
    image_states,
    caption_lengths,
    text_query,
    text_keyval,
    text_attend,
    text_up,
    text_down,
    text_qkv,
    text_output,
    text_gains,
    image_query,
    image_keyval,
    image_attend,
    image_up,
    image_down,
    image_qkv,
    image_output,
    image_gains,
    text_cotangent,
    image_cotangent,
):
    own_pairs = caption_lengths.shape[0]
    own_text = text_states.shape[0]
    text_len = own_text // own_pairs
    regions = image_states.shape[0] // own_pairs
    padded = -(-regions // 16) * 16
    own_image = own_pairs * padded
    pairs = 2 * own_pairs
    d_t, d_i = text_states.shape[1], image_states.shape[1]
    stream = lax.axis_index("stream")
    core = lax.axis_index("dp") & 1
    side = jnp.stack([core, stream]).astype(jnp.int32)

    far_put = spread(own_pairs, regions, padded, 0, 2 * own_image)
    near_put = spread(own_pairs, regions, padded, own_image, 2 * own_image)
    trim = near_put[own_image:].T

    def both_images(near):
        return (mm(far_put, stream_swap(near)) + mm(near_put, near)).astype(BF16)

    choice = choices(stream)
    image_all = both_images(image_states)
    image_q = mm(image_all, image_query).astype(BF16)
    image_kv = mm(image_all, image_keyval).astype(BF16)
    far_text, far_lens, image_q, image_kv = tied(
        stream_swap(text_states), stream_swap(caption_lengths), image_q, image_kv
    )
    text_all = jnp.concatenate([text_states, far_text])
    lens = jnp.concatenate([caption_lengths, far_lens])
    image_cotangent, text_cotangent, text_all = tied(image_cotangent, text_cotangent, text_all)
    image_cot = both_images(image_cotangent)
    far_text_cot = stream_swap(text_cotangent)

    co_blocks = D_C // LANES
    co_cols = (0, 0, co_blocks)
    co_scale = (D_C // H_C) ** (-0.5)

    image_moves, text_moves = Exchange(), Exchange()
    image_moves.send(states=image_all)
    cots = [far_text_cot]

    def image_hook(name, value):
        if name == "self":
            value, cots[0] = tied(value, cots[0])
        return value

    image_out, (image_da, image_da_low), image_dc, text_kv, image_sides, image_dg = stream_forward(
        lens,
        image_all,
        image_q,
        text_all,
        image_cot,
        (text_keyval, image_attend, image_up, image_down, image_qkv, image_output),
        image_gains,
        H_I,
        regions,
        None,
        pairs,
        image_moves,
        image_hook,
    )
    image_dq, text_dkv = attend_back(
        lens, image_q, text_kv, text_kv, image_dc, co_cols, pairs, co_blocks, 1, None, co_scale, False,
    )
    image_moves.send(dq=image_dq, da=image_da_low)
    image_sides = image_sides(image_dq, image_da_low)
    text_moves.send(states=text_all, dkv=text_dkv)

    def sizes_of(*weights):
        return {name: weight.shape for name, weight in zip(NAMES, weights)}

    def gather_half(both, sizes):
        total = sum(m * n for m, n in sizes.values())
        total_rows = total // (2 * UNIT)
        plans = half_jobs(both, sizes, total)
        image = both["query"][0][0] is image_all
        return flat_grads(side, total_rows, plans, 6 if image else 14, resident=image)

    image_sizes = sizes_of(
        image_query, image_keyval, image_attend, image_up, image_down, image_qkv, image_output
    )
    text_sizes = sizes_of(
        text_query, text_keyval, text_attend, text_up, text_down, text_qkv, text_output
    )
    early = lax.axis_size("dp") == 16
    if early:
        image_flat = gather_half(image_sides, image_sizes)

    pieces = []

    def hook(name, value):
        if not early:
            return value
        if name == "co":
            value, flat = tied(value, image_flat)
            pieces.extend(piece_set(choice, flat, (1, 2, 1, 2), (1, 1, 1, 1)))
            value = after(value, pieces, "out")
            for piece in pieces[:2]:
                piece.send()
        if name == "mlp":
            (value,) = paced(pieces[:2], pieces[2:], (value,))
            for piece in pieces[2:]:
                piece.send()
        if name == "self":
            (value,) = paced(pieces[2:], (), (value,))
            pieces[:] = add_split(choice, ((2, pieces[0::2]), (1, pieces[1::2])))
            for piece in pieces:
                piece.send()
        return value

    text_out, (text_da, text_da_low), text_dc, text_q, text_sides, text_dg = stream_forward(
        lens,
        text_all,
        image_kv,
        text_all,
        jnp.concatenate([text_cotangent, cots[0]]),
        (text_query, text_attend, text_up, text_down, text_qkv, text_output),
        text_gains,
        H_T,
        None,
        regions,
        pairs,
        text_moves,
        hook,
    )
    gains = pack_gains(text_dg, image_dg)
    bits = [1 << b for b in range(lax.axis_size("dp").bit_length() - 1)]
    text_dq, image_dkv = attend_back(
        lens, text_q, image_kv, image_kv, text_dc, co_cols, pairs, co_blocks, 1, regions, co_scale, False
    )

    if early:
        image_dkv, text_dq, text_da_low = paced(pieces, (), (image_dkv, text_dq, text_da_low))
        pieces[:] = add_split(choice, ((3, pieces[:1]), (3, pieces[1:])))
        pieces[0].send()
    image_moves.send(dkv=image_dkv)
    text_moves.send(dq=text_dq, da=text_da_low)
    text_sides = text_sides(text_dq, text_da_low)
    text_sides["keyval"] = (text_moves.pair("states", text_all), text_moves.pair("dkv", text_dkv))

    def all_input_grads(text_dq, image_dq):
        text = input_grads(
            text_da, text_dq, text_dkv, text_out, trim[:1], text_query, text_keyval, 0, own_text
        )
        image = input_grads(
            image_da,
            image_dq,
            image_dkv,
            image_out,
            trim,
            image_query,
            image_keyval,
            own_image,
            own_pairs * regions,
        )
        return (*text, *image)

    if early:
        late = Late(
            choice,
            side,
            image_moves.pair("states", image_all),
            image_moves.pair("dkv", image_dkv),
        )
        near_dq, *rest = text_sides["query"][1]
        near_dq, late.out = tied(near_dq, late.out)
        text_sides["query"] = (text_sides["query"][0], (near_dq, *rest))
        late.send()
        text_flat = gather_half(text_sides, text_sizes)
        text_flat = after(text_flat, [late, pieces[0]])
        text_pieces = piece_set(choice, text_flat, (1, 1, 1, 1), TEXT_SHARES)
        one, two, three, four = text_pieces
        late.turn()
        one.out, late.out, pieces[1].out, text_dq, image_dq, gains = tied(
            one.out, late.out, pieces[1].out, text_dq, image_dq, gains
        )
        one.send()
        late.send()
        pieces[1].send()
        gains = gain_step(gains, bits.pop())
        grads = all_input_grads(text_dq, image_dq)
        *grads, gains = paced((one, late, pieces[1]), (two,), (*grads, gains))
        (one,) = add_split(choice, ((2, (one,)),))
        late.add(gather=True)
        two.send()
        one.send()
        gains = gain_step(gains, bits.pop())
        (gains,) = paced((one, two, late), (three,), (gains,))
        (one,) = add_split(choice, ((3, (one,)),))
        (two,) = add_split(choice, ((2, (two,)),))
        late.add()
        three.send()
        two.send()
        one.send()
        gains = gain_step(gains, bits.pop())
        (gains,) = paced((one, two, three, late), (four,), (gains,))
        (two,) = add_split(choice, ((3, (two,)),))
        (three,) = add_split(choice, ((2, (three,)),))
        four.send()
        three.send()
        two.send()
        gains = gain_step(gains, bits.pop())
        (gains,) = paced((two, three, four), (), (gains,))
        (three,) = add_split(choice, ((3, (three,)),))
        (four,) = add_split(choice, ((2, (four,)),))
        three.send()
        four.send()
        paced((three, four), ())
        (four,) = add_split(choice, ((3, (four,)),))
        four.send()
        unit = image_flat.shape[0] // 8 // 4
        starts, row = [], 0
        for piece in (one, two, three, four):
            starts.append((row,))
            row += piece.keep.shape[1]
        image_share, text_share = finished(
            choice,
            (pieces, (one, two, three, four)),
            (((0, 2 * unit), (unit, 3 * unit)), tuple(starts)),
            (late.keep[0], late.far[0]),
        )
    else:
        image_sides["keyval"] = (
            image_moves.pair("states", image_all),
            image_moves.pair("dkv", image_dkv),
        )
        image_share = share_of(
            reduce_scatter(gather_half(image_sides, image_sizes), ((8, False),))
        )
        text_share = share_of(reduce_scatter(gather_half(text_sides, text_sizes), ((8, False),)))
        grads = all_input_grads(text_dq, image_dq)
        while bits:
            gains = gain_step(gains, bits.pop())
    text_grad, text_result, image_grad, image_result = grads
    text_gain_sum, image_gain_sum = unpack_gains(gains, text_dg.shape[1])
    return (
        text_result,
        image_result,
        text_grad,
        image_grad,
        text_share,
        image_share,
        text_gain_sum,
        image_gain_sum,
    )


def pack_gains(text_dg, image_dg):
    return jnp.concatenate([text_dg, image_dg], axis=1)


def gain_step(gains, bit):
    return gains + dp_swap(gains, bit)


def unpack_gains(gains, width):
    return gains[:, :width], gains[:, width:]


class Late:
    rows = 1280

    def __init__(self, choice, side, states, grads):
        self.choice = choice
        job = Job(states, grads, 0, states[0].shape[1], 768)
        flat = flat_grads(side, 4 * self.rows, [[job]], 2, True)
        self.keep, self.out = split(choice, flat, self.rows, ((0, self.rows, (0, 2), 1, LATE_Y),))
        self.bit = 2

    def send(self):
        self.far = dp_swap(self.out, self.bit)

    def turn(self):
        (piece,) = add_split(self.choice, ((LATE_OWN, (self,)),))
        self.keep, self.out, self.bit = piece.keep, piece.out, 4

    def add(self, gather=False):
        self.keep = plus(self.keep, self.far)
        if gather:
            route = []
            for i in range(16):
                z, y = i >> 2, (i >> 1) & 1
                goal = 1 if z & 1 else (0 if y else 2)
                if z != goal:
                    route.append((i, goal * 4 + (i & 3)))
            self.far = lax.ppermute(self.keep, "dp", route)
        else:
            self.far = lax.ppermute(self.keep, "stream", [(1, 0)])


def solution(mesh):
    split = P(("stream", "dp"), None)
    flat = P(("stream", "dp"))
    whole = P()
    return jax.shard_map(
        local,
        mesh=mesh,
        in_specs=(split, split, flat) + (whole,) * 16 + (split, split),
        out_specs=(split, split, split, split, flat, flat, whole, whole),
        check_vma=False,
    )
```

```python
import functools

import jax
import jax.numpy as jnp
from jax import lax
from jax.experimental import pallas as pl
from jax.experimental.pallas import tpu as pltpu
from jax.sharding import PartitionSpec as P

H_T = 12
H_I = 8
H_C = 8
D_C = 1024
LANES = 128
UNIT = 256
masked_score = -1e30
F32 = jnp.float32
BF16 = jnp.bfloat16


def mm(a, b):
    return jnp.dot(a, b, preferred_element_type=F32)


def mm_nt(a, b):
    return lax.dot_general(a, b, (((1,), (1,)), ((), ())), preferred_element_type=F32)


def mm_tn(a, b):
    return lax.dot_general(a, b, (((0,), (0,)), ((), ())), preferred_element_type=F32)


def cost(us):
    return pl.CostEstimate(flops=int(us * 10e9), bytes_accessed=1000, transcendentals=0)


def lane_block(ref, rows, block):
    return ref[rows, pl.ds(pl.multiple_of(block * LANES, LANES), LANES)]


def put_block(ref, rows, block, value):
    ref[rows, pl.ds(pl.multiple_of(block * LANES, LANES), LANES)] = value


def split_heads(block, heads_in):
    if heads_in == 1:
        return block
    lanes = lax.broadcasted_iota(jnp.int32, block.shape, 1)
    zero = jnp.zeros_like(block)
    low = lanes < LANES // 2
    return jnp.concatenate([jnp.where(low, block, zero), jnp.where(low, zero, block)], axis=0)


def side_by_side(block, heads_in):
    if heads_in == 1:
        return block
    rows = block.shape[0] // 2
    return jnp.concatenate([block[:rows], block[rows:]], axis=1)


def attend_kernel(
    lens_ref, q_ref, k_ref, v_ref, o_ref, *, pairs, blocks, cols, heads_in, fixed, scaling
):
    ql = q_ref.shape[0] // pairs
    kl = k_ref.shape[0] // pairs
    chain = heads_in * ql
    keys = lax.broadcasted_iota(jnp.int32, (chain, kl), 1)
    if fixed is None:
        masks = [keys < lens_ref[p] for p in range(pairs)]
    else:
        masks = [keys < fixed] * pairs

    @pl.loop(0, blocks)
    def _(j):
        scores = []
        for p in range(pairs):
            q = split_heads(lane_block(q_ref, slice(p * ql, (p + 1) * ql), cols[0] + j), heads_in)
            k = lane_block(k_ref, slice(p * kl, (p + 1) * kl), cols[1] + j)
            scores.append(jnp.where(masks[p], mm_nt(q, k) * scaling, masked_score))
        s = jnp.concatenate(scores, axis=0)
        raised = jnp.exp(s - jnp.max(s, axis=-1, keepdims=True))
        w = (raised * (1.0 / jnp.sum(raised, axis=-1, keepdims=True))).astype(BF16)
        for p in range(pairs):
            v = split_heads(lane_block(v_ref, slice(p * kl, (p + 1) * kl), cols[2] + j), heads_in)
            o = mm(side_by_side(w[p * chain : (p + 1) * chain], heads_in), v)
            put_block(o_ref, slice(p * ql, (p + 1) * ql), j, o.astype(BF16))


def attend(lens, q, k, v, cols, pairs, blocks, heads_in, fixed, scaling):
    rows = q.shape[0]
    krows = k.shape[0]
    same = k is v
    vmem = pl.BlockSpec(memory_space=pltpu.VMEM)
    operands = [lens, q, k] if same else [lens, q, k, v]
    if q is k:
        operands = [lens, q]

    def body(lens_ref, *refs, **kw):
        refs = list(refs)
        o_ref = refs.pop()
        while len(refs) < 3:
            refs.append(refs[-1])
        attend_kernel(lens_ref, *refs, o_ref, **kw)

    return pl.pallas_call(
        functools.partial(
            body,
            pairs=pairs,
            blocks=blocks,
            cols=cols,
            heads_in=heads_in,
            fixed=fixed,
            scaling=scaling,
        ),
        in_specs=[pl.BlockSpec(memory_space=pltpu.SMEM)] + [vmem] * (len(operands) - 1),
        out_specs=vmem,
        out_shape=jax.ShapeDtypeStruct((rows, blocks * LANES), BF16),
        compiler_params=pltpu.CompilerParams(vmem_limit_bytes=10 * 1024 * 1024),
        cost_estimate=cost(5),
        name="attend",
    )(*operands)


def attend_back_kernel(
    lens_ref,
    q_ref,
    k_ref,
    v_ref,
    g_ref,
    dq_ref,
    dk_ref,
    dv_ref,
    *,
    pairs,
    blocks,
    cols,
    out_cols,
    heads_in,
    fixed,
    scaling,
):
    ql = q_ref.shape[0] // pairs
    kl = k_ref.shape[0] // pairs
    keys = lax.broadcasted_iota(jnp.int32, (heads_in * kl, ql), 0)
    if heads_in == 2:
        keys = jnp.where(keys >= kl, keys - kl, keys)
    if fixed is None:
        masks = [keys < lens_ref[p] for p in range(pairs)]
    else:
        masks = [keys < fixed] * pairs

    @pl.loop(0, blocks)
    def _(j):
        scores, slopes = [], []
        for p in range(pairs):
            qs, ks = slice(p * ql, (p + 1) * ql), slice(p * kl, (p + 1) * kl)
            q, g = lane_block(q_ref, qs, cols[0] + j), lane_block(g_ref, qs, j)
            k = split_heads(lane_block(k_ref, ks, cols[1] + j), heads_in)
            v = split_heads(lane_block(v_ref, ks, cols[2] + j), heads_in)
            scores.append(jnp.where(masks[p], mm_nt(k, q) * scaling, masked_score))
            slopes.append(mm_nt(v, g))
        stacked = (pairs * heads_in, kl, ql)
        s = jnp.concatenate(scores, axis=0).reshape(stacked)
        dp = jnp.concatenate(slopes, axis=0).reshape(stacked)
        raised = jnp.exp(s - jnp.max(s, axis=1, keepdims=True))
        w = raised * (1.0 / jnp.sum(raised, axis=1, keepdims=True))
        inner = jnp.sum(w * dp, axis=1, keepdims=True)
        ds = (w * (dp - inner)).astype(BF16).reshape(-1, ql)
        w = w.astype(BF16).reshape(-1, ql)
        chain = heads_in * kl
        for p in range(pairs):
            qs, ks = slice(p * ql, (p + 1) * ql), slice(p * kl, (p + 1) * kl)
            own = slice(p * chain, (p + 1) * chain)
            q = split_heads(lane_block(q_ref, qs, cols[0] + j), heads_in)
            g = split_heads(lane_block(g_ref, qs, j), heads_in)
            k = split_heads(lane_block(k_ref, ks, cols[1] + j), heads_in)
            dq = mm_tn(ds[own], k) * scaling
            dk = mm(side_by_side(ds[own], heads_in), q) * scaling
            dv = mm(side_by_side(w[own], heads_in), g)
            put_block(dq_ref, qs, out_cols[0] + j, dq.astype(BF16))
            put_block(dk_ref, ks, out_cols[1] + j, dk.astype(BF16))
            put_block(dv_ref, ks, out_cols[2] + j, dv.astype(BF16))


def attend_back(lens, q, k, v, g, cols, pairs, blocks, heads_in, fixed, scaling, packed):
    rows = q.shape[0]
    krows = k.shape[0]
    vmem = pl.BlockSpec(memory_space=pltpu.VMEM)
    width = blocks * LANES
    if packed:
        operands = [lens, q, g]
        out_cols = (0, blocks, 2 * blocks)
        out_shape = jax.ShapeDtypeStruct((rows, 3 * width), BF16)
        out_specs = vmem
    else:
        operands = [lens, q, k, g]
        out_cols = (0, 0, blocks)
        out_shape = [
            jax.ShapeDtypeStruct((rows, width), BF16),
            jax.ShapeDtypeStruct((krows, 2 * width), BF16),
        ]
        out_specs = [vmem, vmem]

    def body(lens_ref, *refs, **kw):
        if packed:
            q_ref, g_ref, out_ref = refs
            ins, outs = (q_ref, q_ref, q_ref, g_ref), (out_ref,) * 3
        else:
            q_ref, k_ref, g_ref, dq_ref, dkv_ref = refs
            ins, outs = (q_ref, k_ref, k_ref, g_ref), (dq_ref, dkv_ref, dkv_ref)
        attend_back_kernel(lens_ref, *ins, *outs, **kw)

    return pl.pallas_call(
        functools.partial(
            body,
            pairs=pairs,
            blocks=blocks,
            cols=cols,
            out_cols=out_cols,
            heads_in=heads_in,
            fixed=fixed,
            scaling=scaling,
        ),
        in_specs=[pl.BlockSpec(memory_space=pltpu.SMEM)] + [vmem] * (len(operands) - 1),
        out_specs=out_specs,
        out_shape=out_shape,
        compiler_params=pltpu.CompilerParams(vmem_limit_bytes=10 * 1024 * 1024),
        cost_estimate=cost(6),
        name="attend_back",
    )(*operands)


class Job:
    def __init__(self, a, b, low, high, place):
        self.a, self.b = a, b
        self.low, self.count = low, high - low
        self.columns = b[3]
        self.place = place


def flat_kernel(side_ref, *refs, plans, found, quarter, resident):
    out_ref, chosen_ref, stage_ref = refs[len(found) : len(found) + 3]
    core = side_ref[0]
    depth = chosen_ref.shape[0] // 2
    if not resident:
        a_buf, b_buf, in_sem = refs[-3:]

    def loads(jobs, k):
        job, slot = jobs[k], k % 2
        copies = []
        for side, buf, start, width in (
            (job.a, a_buf, job.a[2] + job.low, job.count),
            (job.b, b_buf, job.b[2], job.columns),
        ):
            for half in range(2):
                copies.append(
                    pltpu.make_async_copy(
                        refs[found[id(side[half])]].at[:, start : start + width],
                        buf.at[slot, half * depth : (half + 1) * depth, 0:width],
                        in_sem.at[slot, len(copies)],
                    )
                )
        return copies

    def run(jobs):
        if not resident:
            for copy in loads(jobs, 0):
                copy.start()
        for k, job in enumerate(jobs):
            if resident:
                a_refs = [refs[found[id(job.a[half])]] for half in range(2)]
                b_refs = [refs[found[id(job.b[half])]] for half in range(2)]
                a_first, b_first = job.a[2] + job.low, job.b[2]
            else:
                if k + 1 < len(jobs):
                    for copy in loads(jobs, k + 1):
                        copy.start()
                for copy in loads(jobs, k):
                    copy.wait()
                halves = [slice(0, depth), slice(depth, 2 * depth)]
                a_refs = [a_buf.at[k % 2, half] for half in halves]
                b_refs = [b_buf.at[k % 2, half] for half in halves]
                a_first = b_first = 0
            units = job.columns // (2 * UNIT if quarter else UNIT)
            for u in range(units):
                at = 4 * u + 2 * side_ref[1] + core if quarter else 2 * u + core
                block = pl.ds(pl.multiple_of(at * LANES + b_first, LANES), LANES)
                for half in range(2):
                    chosen_ref[half * depth : (half + 1) * depth, u * LANES : (u + 1) * LANES] = (
                        b_refs[half][:, block]
                    )
            bm = best_rows(job.count, units)
            rows = bm * units

            @pl.loop(0, job.count // bm)
            def _(i, job=job, units=units, bm=bm, rows=rows, a_refs=a_refs, a_first=a_first):
                columns = pl.ds(pl.multiple_of(a_first + i * bm, LANES), bm)
                a = jnp.concatenate([a_ref[:, columns] for a_ref in a_refs], axis=0).T
                for u0 in range(0, units, 12):
                    u1 = min(u0 + 12, units)
                    total = mm(a, chosen_ref[:, u0 * LANES : u1 * LANES])
                    for u in range(u0, u1):
                        stage_ref[pl.ds(u, bm, stride=units), :] = total[
                            :, (u - u0) * LANES : (u - u0 + 1) * LANES
                        ]
                first = pl.multiple_of(job.place + i * rows, LANES)
                out_ref[pl.ds(first, rows), :] = stage_ref[:rows].astype(BF16)

    if len(plans) == 1:
        run(plans[0])
    else:
        for side, jobs in enumerate(plans):

            @pl.when(side_ref[1] == side)
            def _(jobs=jobs):
                run(jobs)


def best_rows(count, units):
    most = 512 if units <= 8 else 384
    return max(size for size in range(LANES, most + 1, LANES) if count % size == 0)


def flat_grads(side, total_rows, plans, us, quarter=False, resident=True):
    arrays, found = [], {}
    jobs = [job for plan in plans for job in plan]
    for job in jobs:
        for array in (*job.a[:2], *job.b[:2]):
            if id(array) not in found:
                found[id(array)] = len(arrays)
                arrays.append(array)
    depth = 2 * arrays[0].shape[0]
    widest = max(job.columns for job in jobs)
    tallest = max(job.count for job in jobs)
    factor = 2 * UNIT if quarter else UNIT
    rows = max(best_rows(job.count, job.columns // factor) * job.columns // factor for job in jobs)
    held = 2 * depth * widest * LANES // factor + 4 * rows * LANES
    scratch = [
        pltpu.VMEM((depth, widest * LANES // factor), BF16),
        pltpu.VMEM((rows, LANES), F32),
    ]
    if not resident:
        held += 4 * depth * (tallest + widest)
        scratch += [
            pltpu.VMEM((2, depth, tallest), BF16),
            pltpu.VMEM((2, depth, widest), BF16),
            pltpu.SemaphoreType.DMA((2, 4)),
        ]
    place = pltpu.VMEM if resident else pltpu.HBM
    return pl.pallas_call(
        functools.partial(
            flat_kernel, plans=plans, found=found, quarter=quarter, resident=resident
        ),
        in_specs=[pl.BlockSpec(memory_space=pltpu.SMEM)]
        + [pl.BlockSpec(memory_space=place)] * len(arrays),
        out_specs=pl.BlockSpec(memory_space=pltpu.VMEM),
        out_shape=jax.ShapeDtypeStruct((total_rows, LANES), BF16),
        scratch_shapes=scratch,
        compiler_params=pltpu.CompilerParams(vmem_limit_bytes=held + (8 if resident else 10) * 1024 * 1024),
        cost_estimate=cost(us),
        name="flat_grads",
    )(side, *arrays)


def dp_swap(block, bit):
    count = lax.axis_size("dp")
    return lax.ppermute(block, "dp", [(i, i ^ bit) for i in range(count)])


def stream_swap(block):
    return lax.ppermute(block, "stream", [(0, 1), (1, 0)])


def pick(block, index, axis=0):
    return lax.dynamic_index_in_dim(block, index, axis, keepdims=False)


def plus(a, b):
    return (a.astype(F32) + b.astype(F32)).astype(BF16)


def tied(*values):
    return lax.optimization_barrier(values)


def scatter_parts(flat, cuts):
    count = lax.axis_size("dp")
    top = count.bit_length() - 2
    bits = tuple(range(top, 0, -1))
    rows = flat.shape[0] // (count // 2)
    blocks = flat.reshape((2,) * len(bits) + (rows, LANES))
    natural = tuple(range(1, top + 1))
    turned = natural[1:2] + natural[:1] + natural[2:]
    parts, start = [], 0
    for share, turn in cuts:
        part = lax.slice_in_dim(blocks, start, start + rows * share // 8, axis=len(bits))
        start += rows * share // 8
        parts.append((part, bits, turned if turn else natural))
    return parts


def scatter_step(parts):
    me = lax.axis_index("dp")
    done = []
    for block, left, order in parts:
        bit = order[0]
        axis = left.index(bit)
        mine = (me >> bit) & 1
        keep = pick(block, mine, axis)
        far = dp_swap(pick(block, 1 - mine, axis), 1 << bit)
        block = plus(keep, far) if len(order) > 1 else keep.astype(F32) + far.astype(F32)
        done.append((block, left[:axis] + left[axis + 1 :], order[1:]))
    return done


def scatter_end(parts):
    while parts[0][2]:
        parts = scatter_step(parts)
    blocks = [block for block, _, _ in parts]
    return jnp.concatenate(blocks) if len(blocks) > 1 else blocks[0]


def reduce_scatter(flat, cuts):
    return scatter_end(scatter_parts(flat, cuts))


def share_of(result):
    core = lax.axis_index("dp") & 1
    halves = result.reshape(2, result.shape[0] // 2, LANES)
    mine = pick(halves, core)
    far = dp_swap(pick(halves, 1 - core), 1)
    first = jnp.where(core == 0, mine, far)
    second = jnp.where(core == 0, far, mine)
    return jnp.stack([first, second], axis=1).reshape(-1)


def choices(stream):
    me = lax.axis_index("dp")
    y, odd = (me >> 1) & 1, (me >> 2) & 1
    own = jnp.where(y == 1, odd, 1 - odd)
    values = [me & 1, y, odd, (me >> 3) & 1, 1 - y, own, stream, me >> 1]
    return jnp.stack(values).astype(jnp.int32)


LATE_Y, LATE_OWN, STREAM, CHIP = 4, 5, 6, 7
TEXT_SHARES = (48, 46, 38, 24)


def split_kernel(choice_ref, flat_ref, *refs, chunk, cuts):
    for k, (start, rows, bases, weight, which) in enumerate(cuts):
        mine = choice_ref[which]
        for i, base in enumerate(bases):
            for out_ref, index in ((refs[2 * k], mine), (refs[2 * k + 1], 1 - mine)):
                first = (base + index * weight) * chunk + start
                out_ref[i] = flat_ref[pl.ds(pl.multiple_of(first, 16), rows), :]


def split(choice, flat, chunk, cuts):
    shapes = [
        jax.ShapeDtypeStruct((len(bases), rows, LANES), BF16)
        for _, rows, bases, _, _ in cuts
        for _ in range(2)
    ]
    return pl.pallas_call(
        functools.partial(split_kernel, chunk=chunk, cuts=cuts),
        in_specs=[
            pl.BlockSpec(memory_space=pltpu.SMEM),
            pl.BlockSpec(memory_space=pltpu.VMEM),
        ],
        out_specs=[pl.BlockSpec(memory_space=pltpu.VMEM)] * len(shapes),
        out_shape=shapes,
        compiler_params=pltpu.CompilerParams(vmem_limit_bytes=8 * 1024 * 1024),
        cost_estimate=cost(3),
        name="split",
    )(choice, flat)


def piece_set(choice, flat, firsts, shares):
    chunk = flat.shape[0] // 8
    unit = chunk // sum(shares)
    cuts, start = [], 0
    for first, share in zip(firsts, shares):
        bits = [bit for bit in (3, 2, 1) if bit != first]
        bases = tuple(
            sum(((n >> (1 - at)) & 1) << (b - 1) for at, b in enumerate(bits)) for n in range(4)
        )
        cuts.append((start, unit * share, bases, 1 << (first - 1), first))
        start += unit * share
    arrays = split(choice, flat, chunk, tuple(cuts))
    return [
        Piece(keep, out, first) for keep, out, first in zip(arrays[::2], arrays[1::2], firsts)
    ]


class Piece:
    def __init__(self, keep, out, bit):
        self.keep, self.out, self.bit = keep, out, bit

    def send(self):
        self.far = dp_swap(self.out, 1 << self.bit)


def after(value, pieces, name="far"):
    value, *got = tied(value, *(getattr(piece, name) for piece in pieces))
    for piece, array in zip(pieces, got):
        setattr(piece, name, array)
    return value


def paced(came, leaving, values=()):
    got = tied(*(item.far for item in came), *(item.out for item in leaving), *values)
    for item, array in zip(came, got):
        item.far = array
    for item, array in zip(leaving, got[len(came) :]):
        item.out = array
    return got[len(came) + len(leaving) :]


def added(a_ref, b_ref, index):
    return a_ref[index].astype(F32) + b_ref[index].astype(F32)


def add_split_kernel(choice_ref, *refs, plan, inputs):
    outs = refs[2 * inputs :]
    for k, base, stride, which, out, at in plan:
        keep_ref, far_ref = refs[2 * k : 2 * k + 2]
        mine = choice_ref[which]
        for ref, index in ((outs[2 * out], mine), (outs[2 * out + 1], 1 - mine)):
            ref[at] = added(keep_ref, far_ref, base + index * stride).astype(BF16)


def add_split(choice, groups, which=None):
    operands, plan, shapes = [], [], []
    for out, (bit, pieces) in enumerate(groups):
        at = 0
        for piece in pieces:
            for base in range(0, piece.keep.shape[0], 2):
                plan.append((len(operands) // 2, base, 1, which or bit, out, at))
                at += 1
            operands += [piece.keep, piece.far]
        shape = jax.ShapeDtypeStruct((at,) + pieces[0].keep.shape[1:], BF16)
        shapes += [shape, shape]
    vmem = pl.BlockSpec(memory_space=pltpu.VMEM)
    arrays = pl.pallas_call(
        functools.partial(add_split_kernel, plan=tuple(plan), inputs=len(operands) // 2),
        in_specs=[pl.BlockSpec(memory_space=pltpu.SMEM)] + [vmem] * len(operands),
        out_specs=[vmem] * len(shapes),
        out_shape=shapes,
        compiler_params=pltpu.CompilerParams(vmem_limit_bytes=8 * 1024 * 1024),
        cost_estimate=cost(1),
        name="add_split",
    )(choice, *operands)
    return [
        Piece(arrays[2 * out], arrays[2 * out + 1], bit) for out, (bit, _) in enumerate(groups)
    ]


def finish_kernel(choice_ref, *refs, rows):
    refs = list(refs)
    pairs = [[(refs.pop(0), refs.pop(0)) for _ in group] for group in rows]
    near_ref, far_ref = refs.pop(0), refs.pop(0)
    out_ref, send_ref, *totals, joined_ref = refs
    for total_ref, group, starts in zip(totals, pairs, rows):
        for (keep_ref, came_ref), firsts in zip(group, starts):
            count = keep_ref.shape[1]
            for at, first in enumerate(firsts):
                total_ref[first : first + count] = added(keep_ref, came_ref, at)
    half = near_ref.shape[0]
    joined_ref[pl.ds(0, half, stride=2), :] = near_ref[...].astype(F32)
    joined_ref[pl.ds(1, half, stride=2), :] = far_ref[...].astype(F32)
    image_ref = totals[0]
    total_rows = image_ref.shape[0]
    chip = choice_ref[CHIP]
    first = jnp.where(chip == 1, 1536, 0)
    last = jnp.where(chip == 4, 2048, total_rows)
    here = (chip >= 1) & (chip <= 4) & (choice_ref[STREAM] == 0)
    last = jnp.where(here, last, 0)
    at = lax.broadcasted_iota(jnp.int32, (total_rows, 1), 0)
    image_ref[...] = jnp.where((at >= first) & (at < last), joined_ref[...], image_ref[...])
    core = choice_ref[0]
    row = 0
    for total_ref in totals:
        half = total_ref.shape[0] // 2
        for ref, index in ((out_ref, core), (send_ref, 1 - core)):
            ref[row : row + half, :] = total_ref[pl.ds(pl.multiple_of(index * half, 8), half), :]
        row += half


def join_kernel(choice_ref, near_ref, far_ref, *outs):
    core = choice_ref[0]
    row = 0
    for out_ref in outs:
        half = out_ref.shape[0] // 2
        out_ref[pl.ds(core, half, stride=2), :] = near_ref[row : row + half, :]
        out_ref[pl.ds(1 - core, half, stride=2), :] = far_ref[row : row + half, :]
        row += half


def finished(choice, groups, rows, late):
    sizes = [
        sum(piece.keep.shape[0] * piece.keep.shape[1] for piece in group) for group in groups
    ]
    vmem = pl.BlockSpec(memory_space=pltpu.VMEM)
    smem = pl.BlockSpec(memory_space=pltpu.SMEM)
    operands = [ref for group in groups for piece in group for ref in (piece.keep, piece.far)]
    operands += list(late)
    half = jax.ShapeDtypeStruct((sum(sizes) // 2, LANES), F32)
    near, send = pl.pallas_call(
        functools.partial(finish_kernel, rows=rows),
        in_specs=[smem] + [vmem] * len(operands),
        out_specs=[vmem] * 2,
        out_shape=[half] * 2,
        scratch_shapes=[pltpu.VMEM((rows, LANES), F32) for rows in (*sizes, sizes[0])],
        compiler_params=pltpu.CompilerParams(vmem_limit_bytes=12 * 1024 * 1024),
        cost_estimate=cost(3),
        name="finish",
    )(choice, *operands)
    joined = pl.pallas_call(
        join_kernel,
        in_specs=[smem, vmem, vmem],
        out_specs=[vmem] * 2,
        out_shape=[jax.ShapeDtypeStruct((rows, LANES), F32) for rows in sizes],
        compiler_params=pltpu.CompilerParams(vmem_limit_bytes=12 * 1024 * 1024),
        cost_estimate=cost(2),
        name="join",
    )(choice, near, dp_swap(send, 1))
    return [block.reshape(-1) for block in joined]


CHUNK = 64
ROWS = 128
WIDEST = 1024
WIDEST_GELU = 1024


def tiles(columns, body, widest=None):
    size = max(c for c in range(LANES, (widest or WIDEST) + 1, LANES) if columns % c == 0)
    if size == columns:
        return body(slice(0, columns))

    @pl.loop(0, columns // size)
    def _(j):
        body(pl.ds(pl.multiple_of(j * size, size), size))


def views(pack_ref, *widths):
    found, start = [], 0
    for width in widths:
        found.append(pack_ref.at[:, start : start + width])
        start += width
    return found


def row_chunks(rows, body):
    size = ROWS if rows % ROWS == 0 else CHUNK

    @pl.loop(0, rows // size)
    def _(i):
        body(i * size, pl.ds(pl.multiple_of(i * size, size), size), size)


def normed_chunk(a):
    centred = a - jnp.mean(a, axis=-1, keepdims=True)
    inverse = lax.rsqrt(jnp.mean(centred * centred, axis=-1, keepdims=True) + 1e-05)
    return centred * inverse, inverse


def normed_back_chunk(grad, n, inverse, gain_row):
    scaled = grad * gain_row
    low = jnp.mean(scaled, axis=-1, keepdims=True)
    tilt = jnp.mean(scaled * n, axis=-1, keepdims=True)
    return (scaled - low - n * tilt) * inverse, jnp.sum(grad * n, axis=0, keepdims=True)


def co_kernel(
    lens_ref, x_ref, given_ref, source_ref, g_ref, wmade_ref, wat_ref,
    made_ref, pack_ref, n_ref, inv_ref, a_ref, *, pairs, fixed, scaling, makes_kv,
):
    rows, width = x_ref.shape
    c_ref, h_ref = views(pack_ref, D_C, width)

    def made_tile(cols):
        made_ref[:, cols] = mm(source_ref[...], wmade_ref[:, cols]).astype(BF16)

    def a_tile(cols):
        a_ref[:, cols] = x_ref[:, cols].astype(F32) + mm(c_ref[...], wat_ref[:, cols])

    def norm(i, at, size):
        n, inverse = normed_chunk(a_ref[at, :])
        n_ref[at, :] = n
        inv_ref[at, :] = jnp.broadcast_to(inverse, (size, LANES))
        h_ref[at, :] = (n * g_ref[0:1, :]).astype(BF16)

    tiles(made_ref.shape[1], made_tile)
    q_ref, kv_ref = (given_ref, made_ref) if makes_kv else (made_ref, given_ref)
    blocks = q_ref.shape[1] // LANES
    attend_kernel(
        lens_ref, q_ref, kv_ref, kv_ref, c_ref, pairs=pairs, blocks=blocks,
        cols=(0, 0, blocks), heads_in=1, fixed=fixed, scaling=scaling,
    )
    tiles(width, a_tile)
    row_chunks(rows, norm)


def mlp_kernel(
    pack1_ref, n1_ref, g_ref, wup_ref, wdown_ref, wqkv_ref,
    pack_ref, slope_ref, n_ref, inv_ref, r_ref, a_ref,
):
    rows, width = n1_ref.shape
    _, h1_ref = views(pack1_ref, D_C, width)
    hid_ref, h_ref = views(pack_ref, wup_ref.shape[1], width)

    def up_tile(cols):
        u_all = mm(h1_ref[...], wup_ref[:, cols])
        for at in range(0, rows, CHUNK):
            u = u_all[at : at + CHUNK]
            share = 0.5 + 0.5 * lax.erf(u * 0.7071067811865476)
            hid_ref[at : at + CHUNK, cols] = (u * share).astype(BF16)
            slope = share + u * (0.3989422804014327 * jnp.exp(-0.5 * u * u))
            slope_ref[at : at + CHUNK, cols] = slope.astype(BF16)

    def down_tile(cols):
        a_ref[:, cols] = n1_ref[:, cols] * g_ref[0:1, cols] + mm(hid_ref[...], wdown_ref[:, cols])

    def norm(i, at, size):
        n, inverse = normed_chunk(a_ref[at, :])
        n_ref[at, :] = n
        inv_ref[at, :] = jnp.broadcast_to(inverse, (size, LANES))
        h_ref[at, :] = (n * g_ref[1:2, :]).astype(BF16)

    def qkv_tile(cols):
        r_ref[:, cols] = mm(h_ref[...], wqkv_ref[:, cols]).astype(BF16)

    tiles(wup_ref.shape[1], up_tile, WIDEST_GELU)
    tiles(width, down_tile)
    row_chunks(rows, norm)
    tiles(r_ref.shape[1], qkv_tile)


def self_kernel(
    lens_ref, r_ref, n2_ref, g_ref, wout_ref, cot_ref,
    pack_ref, y_ref, de_ref, dg_ref, a_ref, dz_ref,
    *, pairs, heads_in, fixed, scaling,
):
    rows, width = n2_ref.shape
    z_ref, de_low_ref, dr_ref = views(pack_ref, width, width, 3 * width)
    blocks = width // LANES
    cols = (0, blocks, 2 * blocks)
    shared = dict(
        pairs=pairs, blocks=blocks, cols=cols, heads_in=heads_in, fixed=fixed, scaling=scaling
    )

    def out_tile(at):
        a_ref[:, at] = n2_ref[:, at] * g_ref[1:2, at] + mm(z_ref[...], wout_ref[:, at])

    def last(start, at, size):
        n, inverse = normed_chunk(a_ref[at, :])
        y = n * g_ref[2:3, :]
        grad = cot_ref[at, :].astype(F32)
        if fixed is None:
            slots = rows // pairs
            place = lax.broadcasted_iota(jnp.int32, (size, 1), 0) + lax.rem(start, slots)
            valid = (place < lens_ref[lax.div(start, slots)]).astype(F32)
            y, grad = y * valid, grad * valid
        y_ref[at, :] = y.astype(BF16)
        de, dg = normed_back_chunk(grad, n, inverse, g_ref[2:3, :])
        de_ref[at, :] = de
        de_low_ref[at, :] = de.astype(BF16)
        dg_ref[...] += dg

    def dz_tile(at):
        dz_ref[:, at] = mm_nt(de_low_ref[...], wout_ref[at, :]).astype(BF16)

    attend_kernel(lens_ref, r_ref, r_ref, r_ref, z_ref, **shared)
    tiles(width, out_tile)
    dg_ref[...] = jnp.zeros_like(dg_ref)
    row_chunks(rows, last)
    tiles(width, dz_tile)
    attend_back_kernel(
        lens_ref, r_ref, r_ref, r_ref, dz_ref, dr_ref, dr_ref, dr_ref, out_cols=cols, **shared
    )


def mlp_back_kernel(
    pack3_ref, de_ref, n2_ref, inv2_ref, g_ref, slope_ref, wqkv_ref, wdown_ref,
    pack_ref, db_ref, dg_ref, a_ref,
):
    rows, width = n2_ref.shape
    _, _, dr_ref = views(pack3_ref, width, width, 3 * width)
    db_low_ref, du_ref = views(pack_ref, width, slope_ref.shape[1])
    dg_ref[...] = jnp.zeros_like(dg_ref)

    def second_tile(at):
        a_ref[:, at] = de_ref[:, at] + mm_nt(dr_ref[...], wqkv_ref[at, :])

    def second_norm(i, at, size):
        db, dg = normed_back_chunk(a_ref[at, :], n2_ref[at, :], inv2_ref[at, 0:1], g_ref[1:2, :])
        db_ref[at, :] = db
        db_low_ref[at, :] = db.astype(BF16)
        dg_ref[...] += dg

    def du_tile(at):
        grad = mm_nt(db_low_ref[...], wdown_ref[at, :])
        du_ref[:, at] = (grad * slope_ref[:, at].astype(F32)).astype(BF16)

    tiles(width, second_tile)
    row_chunks(rows, second_norm)
    tiles(du_ref.shape[1], du_tile)


def context_back_kernel(
    pack4_ref, db_ref, n1_ref, inv1_ref, g_ref, wup_ref, wat_ref,
    da_low_ref, da_ref, dc_ref, dg_ref, a_ref,
):
    rows, width = n1_ref.shape
    _, du_ref = views(pack4_ref, width, wup_ref.shape[1])
    dg_ref[...] = jnp.zeros_like(dg_ref)

    def first_tile(at):
        a_ref[:, at] = db_ref[:, at] + mm_nt(du_ref[...], wup_ref[at, :])

    def first_norm(i, at, size):
        da, dg = normed_back_chunk(a_ref[at, :], n1_ref[at, :], inv1_ref[at, 0:1], g_ref[0:1, :])
        da_ref[at, :] = da
        da_low_ref[at, :] = da.astype(BF16)
        dg_ref[...] += dg

    def dc_tile(at):
        dc_ref[:, at] = mm_nt(da_low_ref[...], wat_ref[at, :]).astype(BF16)

    tiles(width, first_tile)
    row_chunks(rows, first_norm)
    tiles(dc_ref.shape[1], dc_tile)


def fused(kernel, operands, outs, scratch, name, us, smem_first=False, limit=11):
    vmem = pl.BlockSpec(memory_space=pltpu.VMEM)
    in_specs = [vmem] * len(operands)
    if smem_first:
        in_specs[0] = pl.BlockSpec(memory_space=pltpu.SMEM)
    return pl.pallas_call(
        kernel,
        in_specs=in_specs,
        out_specs=[vmem] * len(outs),
        out_shape=[jax.ShapeDtypeStruct(shape, kind) for shape, kind in outs],
        scratch_shapes=[pltpu.VMEM(shape, kind) for shape, kind in scratch],
        compiler_params=pltpu.CompilerParams(vmem_limit_bytes=limit * 1024 * 1024),
        cost_estimate=cost(us),
        name=name,
    )(*operands)


def co_forward(lens, states, given, source, gains, made_w, attend_w, pairs, fixed):
    rows, width = states.shape
    made, pack1, n1, inv1 = fused(
        functools.partial(
            co_kernel,
            pairs=pairs,
            fixed=fixed,
            scaling=(D_C // H_C) ** (-0.5),
            makes_kv=made_w.shape[1] == 2 * D_C,
        ),
        (lens, states, given, source, gains, made_w, attend_w),
        [
            ((source.shape[0], made_w.shape[1]), BF16),
            ((rows, D_C + width), BF16),
            ((rows, width), F32),
            ((rows, LANES), F32),
        ],
        [((rows, width), F32)],
        "co_forward",
        7,
        True,
    )
    return made, pack1, n1, inv1


def mlp_forward(pack1, n1, gains, up_w, down_w, qkv_w):
    rows, width = n1.shape
    hidden = up_w.shape[1]
    return fused(
        mlp_kernel,
        (pack1, n1, gains, up_w, down_w, qkv_w),
        [
            ((rows, hidden + width), BF16),
            ((rows, hidden), BF16),
            ((rows, width), F32),
            ((rows, LANES), F32),
            ((rows, 3 * width), BF16),
        ],
        [((rows, width), F32)],
        "mlp_forward",
        rows / 40,
    )


def self_turn(lens, r, n2, gains, output_w, cot, pairs, heads, fixed):
    rows, width = n2.shape
    size = width // heads
    return fused(
        functools.partial(
            self_kernel, pairs=pairs, heads_in=LANES // size, fixed=fixed, scaling=size ** (-0.5)
        ),
        (lens, r, n2, gains, output_w, cot),
        [
            ((rows, 5 * width), BF16),
            ((rows, width), BF16),
            ((rows, width), F32),
            ((1, width), F32),
        ],
        [((rows, width), F32), ((rows, width), BF16)],
        "self_turn",
        rows / 128 + 9,
        True,
    )


def input_kernel(da_ref, dq_ref, dkv_ref, y_ref, trim_ref, wq_ref, wkv_ref, *outs, first):
    grad_ref, result_ref = outs
    rows = pl.ds(first, da_ref.shape[0] // 2)
    grad = da_ref[rows, :] + mm_nt(dq_ref[rows, :], wq_ref[...])
    grad = (grad + mm_nt(dkv_ref[rows, :], wkv_ref[...])).astype(BF16)
    y = y_ref[rows, :]
    if trim_ref.shape[0] < 8:
        grad_ref[...], result_ref[...] = grad, y
    else:
        grad_ref[...] = mm(trim_ref[...], grad).astype(BF16)
        result_ref[...] = mm(trim_ref[...], y).astype(BF16)


def input_grads(da, dq, dkv, y, trim, query_w, keyval_w, first, own):
    vmem = pl.BlockSpec(memory_space=pltpu.VMEM)
    return pl.pallas_call(
        functools.partial(input_kernel, first=first),
        in_specs=[vmem] * 7,
        out_specs=[vmem] * 2,
        out_shape=[jax.ShapeDtypeStruct((own, da.shape[1]), BF16)] * 2,
        compiler_params=pltpu.CompilerParams(vmem_limit_bytes=10 * 1024 * 1024),
        cost_estimate=cost(0.2),
        name="input_grads",
    )(da, dq, dkv, y, trim, query_w, keyval_w)


def mlp_back(pack3, de, n2, inv2, gains, slope, qkv_w, down_w):
    rows, width = n2.shape
    return fused(
        mlp_back_kernel,
        (pack3, de, n2, inv2, gains, slope, qkv_w, down_w),
        [
            ((rows, width + slope.shape[1]), BF16),
            ((rows, width), F32),
            ((1, width), F32),
        ],
        [((rows, width), F32)],
        "mlp_back",
        rows / 70,
    )


def context_back(pack4, db, n1, inv1, gains, up_w, attend_w):
    rows, width = n1.shape
    return fused(
        context_back_kernel,
        (pack4, db, n1, inv1, gains, up_w, attend_w),
        [
            ((rows, width), BF16),
            ((rows, width), F32),
            ((rows, D_C), BF16),
            ((1, width), F32),
        ],
        [((rows, width), F32)],
        "context_back",
        rows / 80,
    )


class Exchange:
    def __init__(self):
        self.far = {}
        self.pending = []
        self.parts = None

    def send(self, **arrays):
        for name, array in arrays.items():
            self.far[name] = dp_swap(array, 1)
            self.pending.append(name)

    def settle(self, value):
        names, self.pending = self.pending, []
        if names:
            value, *got = tied(value, *(self.far[name] for name in names))
            self.far.update(zip(names, got))
        return value

    def pair(self, name, array, start=0, width=None):
        return array, self.far[name], start, width or array.shape[1]


def stream_forward(
    lens, states, given, source, cot, weights, gains, heads, fixed, other_fixed, pairs, moves, hook
):
    made_w, attend_w, up_w, down_w, qkv_w, output_w = weights
    made, pack1, n1, inv1 = co_forward(
        lens, states, given, source, gains, made_w, attend_w, pairs, other_fixed
    )
    pack1 = moves.settle(hook("co", pack1))
    moves.send(pack1=pack1)
    pack2, slope, n2, inv2, r = mlp_forward(pack1, n1, gains, up_w, down_w, qkv_w)
    r, pack2 = tied(moves.settle(hook("mlp", r)), pack2)
    moves.send(pack2=pack2)
    pack3, result, de, dg2 = self_turn(lens, r, n2, gains, output_w, cot, pairs, heads, fixed)
    pack3 = moves.settle(hook("self", pack3))
    moves.send(pack3=pack3)
    pack4, db, dg1 = mlp_back(pack3, de, n2, inv2, gains, slope, qkv_w, down_w)
    pack4 = moves.settle(hook("mid", pack4))
    moves.send(pack4=pack4)
    da_low, da, dc, dg0 = context_back(pack4, db, n1, inv1, gains, up_w, attend_w)
    dc = moves.settle(hook("back", dc))
    width, hidden = up_w.shape

    def sides(dq, da_low):
        def side(number, start, count):
            pack = (pack1, pack2, pack3, pack4)[number - 1]
            return moves.pair("pack%d" % number, pack, start, count)

        return {
            "query": (moves.pair("states", states), moves.pair("dq", dq)),
            "attend": (side(1, 0, D_C), moves.pair("da", da_low)),
            "up": (side(1, D_C, width), side(4, width, hidden)),
            "down": (side(2, 0, hidden), side(4, 0, width)),
            "qkv": (side(2, hidden, width), side(3, 2 * width, 3 * width)),
            "output": (side(3, 0, width), side(3, width, width)),
        }

    return result, (da, da_low), dc, made, sides, jnp.concatenate([dg0, dg1, dg2])


NAMES = ("query", "keyval", "attend", "up", "down", "qkv", "output")


def half_jobs(both, sizes, total):
    plans, filled = ([], []), 0
    for name in NAMES:
        m, n = sizes[name]
        room = min(max((total // 2 - filled) // n, 0), m)
        for plan, low, high in ((plans[0], 0, room), (plans[1], room, m)):
            if low < high and name in both:
                start = filled + low * n - (0 if plan is plans[0] else total // 2)
                step = min(high - low, 1024)
                for at in range(low, high, step):
                    place = (start + (at - low) * n) // UNIT
                    plan.append(Job(*both[name], at, at + step, place))
        filled += m * n
    return plans


def spread(count, regions, padded, offset, rows):
    target = lax.broadcasted_iota(jnp.int32, (rows, count * regions), 0) - offset
    source = lax.broadcasted_iota(jnp.int32, (rows, count * regions), 1)
    return (target == source // regions * padded + source % regions).astype(BF16)


def local(
    text_states,
    image_states,
    caption_lengths,
    text_query,
    text_keyval,
    text_attend,
    text_up,
    text_down,
    text_qkv,
    text_output,
    text_gains,
    image_query,
    image_keyval,
    image_attend,
    image_up,
    image_down,
    image_qkv,
    image_output,
    image_gains,
    text_cotangent,
    image_cotangent,
):
    own_pairs = caption_lengths.shape[0]
    own_text = text_states.shape[0]
    text_len = own_text // own_pairs
    regions = image_states.shape[0] // own_pairs
    padded = -(-regions // 16) * 16
    own_image = own_pairs * padded
    pairs = 2 * own_pairs
    d_t, d_i = text_states.shape[1], image_states.shape[1]
    stream = lax.axis_index("stream")
    core = lax.axis_index("dp") & 1
    side = jnp.stack([core, stream]).astype(jnp.int32)

    far_put = spread(own_pairs, regions, padded, 0, 2 * own_image)
    near_put = spread(own_pairs, regions, padded, own_image, 2 * own_image)
    trim = near_put[own_image:].T

    def both_images(near):
        return (mm(far_put, stream_swap(near)) + mm(near_put, near)).astype(BF16)

    choice = choices(stream)
    image_all = both_images(image_states)
    image_q = mm(image_all, image_query).astype(BF16)
    image_kv = mm(image_all, image_keyval).astype(BF16)
    far_text, far_lens, image_q, image_kv = tied(
        stream_swap(text_states), stream_swap(caption_lengths), image_q, image_kv
    )
    text_all = jnp.concatenate([text_states, far_text])
    lens = jnp.concatenate([caption_lengths, far_lens])
    image_cotangent, text_cotangent, text_all = tied(image_cotangent, text_cotangent, text_all)
    image_cot = both_images(image_cotangent)
    far_text_cot = stream_swap(text_cotangent)

    co_blocks = D_C // LANES
    co_cols = (0, 0, co_blocks)
    co_scale = (D_C // H_C) ** (-0.5)

    image_moves, text_moves = Exchange(), Exchange()
    image_moves.send(states=image_all)
    cots = [far_text_cot]

    def image_hook(name, value):
        if name == "self":
            value, cots[0] = tied(value, cots[0])
        return value

    image_out, (image_da, image_da_low), image_dc, text_kv, image_sides, image_dg = stream_forward(
        lens,
        image_all,
        image_q,
        text_all,
        image_cot,
        (text_keyval, image_attend, image_up, image_down, image_qkv, image_output),
        image_gains,
        H_I,
        regions,
        None,
        pairs,
        image_moves,
        image_hook,
    )
    image_dq, text_dkv = attend_back(
        lens, image_q, text_kv, text_kv, image_dc, co_cols, pairs, co_blocks, 1, None, co_scale, False,
    )
    image_moves.send(dq=image_dq, da=image_da_low)
    image_sides = image_sides(image_dq, image_da_low)
    text_moves.send(states=text_all, dkv=text_dkv)

    def sizes_of(*weights):
        return {name: weight.shape for name, weight in zip(NAMES, weights)}

    def gather_half(both, sizes):
        total = sum(m * n for m, n in sizes.values())
        total_rows = total // (2 * UNIT)
        plans = half_jobs(both, sizes, total)
        image = both["query"][0][0] is image_all
        return flat_grads(side, total_rows, plans, 6 if image else 14, resident=image)

    image_sizes = sizes_of(
        image_query, image_keyval, image_attend, image_up, image_down, image_qkv, image_output
    )
    text_sizes = sizes_of(
        text_query, text_keyval, text_attend, text_up, text_down, text_qkv, text_output
    )
    early = lax.axis_size("dp") == 16
    if early:
        image_flat = gather_half(image_sides, image_sizes)

    pieces = []

    def hook(name, value):
        if not early:
            return value
        if name == "co":
            value, flat = tied(value, image_flat)
            pieces.extend(piece_set(choice, flat, (1, 2, 1, 2), (1, 1, 1, 1)))
            value = after(value, pieces, "out")
            for piece in pieces[:2]:
                piece.send()
        if name == "mlp":
            (value,) = paced(pieces[:2], pieces[2:], (value,))
            for piece in pieces[2:]:
                piece.send()
        if name == "self":
            (value,) = paced(pieces[2:], (), (value,))
            pieces[:] = add_split(choice, ((2, pieces[0::2]), (1, pieces[1::2])))
            for piece in pieces:
                piece.send()
        return value

    text_out, (text_da, text_da_low), text_dc, text_q, text_sides, text_dg = stream_forward(
        lens,
        text_all,
        image_kv,
        text_all,
        jnp.concatenate([text_cotangent, cots[0]]),
        (text_query, text_attend, text_up, text_down, text_qkv, text_output),
        text_gains,
        H_T,
        None,
        regions,
        pairs,
        text_moves,
        hook,
    )
    gains = pack_gains(text_dg, image_dg)
    bits = [1 << b for b in range(lax.axis_size("dp").bit_length() - 1)]
    text_dq, image_dkv = attend_back(
        lens, text_q, image_kv, image_kv, text_dc, co_cols, pairs, co_blocks, 1, regions, co_scale, False
    )

    if early:
        image_dkv, text_dq, text_da_low = paced(pieces, (), (image_dkv, text_dq, text_da_low))
        pieces[:] = add_split(choice, ((3, pieces[:1]), (3, pieces[1:])))
        pieces[0].send()
    image_moves.send(dkv=image_dkv)
    text_moves.send(dq=text_dq, da=text_da_low)
    text_sides = text_sides(text_dq, text_da_low)
    text_sides["keyval"] = (text_moves.pair("states", text_all), text_moves.pair("dkv", text_dkv))

    def all_input_grads(text_dq, image_dq):
        text = input_grads(
            text_da, text_dq, text_dkv, text_out, trim[:1], text_query, text_keyval, 0, own_text
        )
        image = input_grads(
            image_da,
            image_dq,
            image_dkv,
            image_out,
            trim,
            image_query,
            image_keyval,
            own_image,
            own_pairs * regions,
        )
        return (*text, *image)

    if early:
        late = Late(
            choice,
            side,
            image_moves.pair("states", image_all),
            image_moves.pair("dkv", image_dkv),
        )
        near_dq, *rest = text_sides["query"][1]
        near_dq, late.out = tied(near_dq, late.out)
        text_sides["query"] = (text_sides["query"][0], (near_dq, *rest))
        late.send()
        text_flat = gather_half(text_sides, text_sizes)
        text_flat = after(text_flat, [late, pieces[0]])
        text_pieces = piece_set(choice, text_flat, (1, 1, 1, 1), TEXT_SHARES)
        one, two, three, four = text_pieces
        late.turn()
        one.out, late.out, pieces[1].out, text_dq, image_dq, gains = tied(
            one.out, late.out, pieces[1].out, text_dq, image_dq, gains
        )
        one.send()
        late.send()
        pieces[1].send()
        gains = gain_step(gains, bits.pop())
        grads = all_input_grads(text_dq, image_dq)
        *grads, gains = paced((one, late, pieces[1]), (two,), (*grads, gains))
        (one,) = add_split(choice, ((2, (one,)),))
        late.add(gather=True)
        two.send()
        one.send()
        gains = gain_step(gains, bits.pop())
        (gains,) = paced((one, two, late), (three,), (gains,))
        (one,) = add_split(choice, ((3, (one,)),))
        (two,) = add_split(choice, ((2, (two,)),))
        late.add()
        three.send()
        two.send()
        one.send()
        gains = gain_step(gains, bits.pop())
        (gains,) = paced((one, two, three, late), (four,), (gains,))
        (two,) = add_split(choice, ((3, (two,)),))
        (three,) = add_split(choice, ((2, (three,)),))
        four.send()
        three.send()
        two.send()
        gains = gain_step(gains, bits.pop())
        (gains,) = paced((two, three, four), (), (gains,))
        (three,) = add_split(choice, ((3, (three,)),))
        (four,) = add_split(choice, ((2, (four,)),))
        three.send()
        four.send()
        paced((three, four), ())
        (four,) = add_split(choice, ((3, (four,)),))
        four.send()
        unit = image_flat.shape[0] // 8 // 4
        starts, row = [], 0
        for piece in (one, two, three, four):
            starts.append((row,))
            row += piece.keep.shape[1]
        image_share, text_share = finished(
            choice,
            (pieces, (one, two, three, four)),
            (((0, 2 * unit), (unit, 3 * unit)), tuple(starts)),
            (late.keep[0], late.far[0]),
        )
    else:
        image_sides["keyval"] = (
            image_moves.pair("states", image_all),
            image_moves.pair("dkv", image_dkv),
        )
        image_share = share_of(
            reduce_scatter(gather_half(image_sides, image_sizes), ((8, False),))
        )
        text_share = share_of(reduce_scatter(gather_half(text_sides, text_sizes), ((8, False),)))
        grads = all_input_grads(text_dq, image_dq)
        while bits:
            gains = gain_step(gains, bits.pop())
    text_grad, text_result, image_grad, image_result = grads
    text_gain_sum, image_gain_sum = unpack_gains(gains, text_dg.shape[1])
    return (
        text_result,
        image_result,
        text_grad,
        image_grad,
        text_share,
        image_share,
        text_gain_sum,
        image_gain_sum,
    )


def pack_gains(text_dg, image_dg):
    return jnp.concatenate([text_dg, image_dg], axis=1)


def gain_step(gains, bit):
    return gains + dp_swap(gains, bit)


def unpack_gains(gains, width):
    return gains[:, :width], gains[:, width:]


class Late:
    rows = 1280

    def __init__(self, choice, side, states, grads):
        self.choice = choice
        job = Job(states, grads, 0, states[0].shape[1], 768)
        flat = flat_grads(side, 4 * self.rows, [[job]], 2, True)
        self.keep, self.out = split(choice, flat, self.rows, ((0, self.rows, (0, 2), 1, LATE_Y),))
        self.bit = 2

    def send(self):
        self.far = dp_swap(self.out, self.bit)

    def turn(self):
        (piece,) = add_split(self.choice, ((LATE_OWN, (self,)),))
        self.keep, self.out, self.bit = piece.keep, piece.out, 4

    def add(self, gather=False):
        self.keep = plus(self.keep, self.far)
        if gather:
            route = []
            for i in range(16):
                z, y = i >> 2, (i >> 1) & 1
                goal = 1 if z & 1 else (0 if y else 2)
                if z != goal:
                    route.append((i, goal * 4 + (i & 3)))
            self.far = lax.ppermute(self.keep, "dp", route)
        else:
            self.far = lax.ppermute(self.keep, "stream", [(1, 0)])


def solution(mesh):
    split = P(("stream", "dp"), None)
    flat = P(("stream", "dp"))
    whole = P()
    return jax.shard_map(
        local,
        mesh=mesh,
        in_specs=(split, split, flat) + (whole,) * 16 + (split, split),
        out_specs=(split, split, split, split, flat, flat, whole, whole),
        check_vma=False,
    )
```

```python
import functools

import jax
import jax.numpy as jnp
from jax import lax
from jax.experimental import pallas as pl
from jax.experimental.pallas import tpu as pltpu
from jax.sharding import PartitionSpec as P

H_T = 12
H_I = 8
H_C = 8
D_C = 1024
LANES = 128
UNIT = 256
masked_score = -1e30
F32 = jnp.float32
BF16 = jnp.bfloat16


def mm(a, b):
    return jnp.dot(a, b, preferred_element_type=F32)


def mm_nt(a, b):
    return lax.dot_general(a, b, (((1,), (1,)), ((), ())), preferred_element_type=F32)


def mm_tn(a, b):
    return lax.dot_general(a, b, (((0,), (0,)), ((), ())), preferred_element_type=F32)


def cost(us):
    return pl.CostEstimate(flops=int(us * 10e9), bytes_accessed=1000, transcendentals=0)


def lane_block(ref, rows, block):
    return ref[rows, pl.ds(pl.multiple_of(block * LANES, LANES), LANES)]


def put_block(ref, rows, block, value):
    ref[rows, pl.ds(pl.multiple_of(block * LANES, LANES), LANES)] = value


def split_heads(block, heads_in):
    if heads_in == 1:
        return block
    lanes = lax.broadcasted_iota(jnp.int32, block.shape, 1)
    zero = jnp.zeros_like(block)
    low = lanes < LANES // 2
    return jnp.concatenate([jnp.where(low, block, zero), jnp.where(low, zero, block)], axis=0)


def side_by_side(block, heads_in):
    if heads_in == 1:
        return block
    rows = block.shape[0] // 2
    return jnp.concatenate([block[:rows], block[rows:]], axis=1)


def attend_kernel(
    lens_ref, q_ref, k_ref, v_ref, o_ref, *, pairs, blocks, cols, heads_in, fixed, scaling
):
    ql = q_ref.shape[0] // pairs
    kl = k_ref.shape[0] // pairs
    chain = heads_in * ql
    keys = lax.broadcasted_iota(jnp.int32, (chain, kl), 1)
    if fixed is None:
        masks = [keys < lens_ref[p] for p in range(pairs)]
    else:
        masks = [keys < fixed] * pairs

    @pl.loop(0, blocks, unroll=4 if blocks % 4 == 0 else 3)
    def _(j):
        scores = []
        for p in range(pairs):
            q = split_heads(lane_block(q_ref, slice(p * ql, (p + 1) * ql), cols[0] + j), heads_in)
            k = lane_block(k_ref, slice(p * kl, (p + 1) * kl), cols[1] + j)
            scores.append(jnp.where(masks[p], mm_nt(q, k) * scaling, masked_score))
        s = jnp.concatenate(scores, axis=0)
        raised = jnp.exp(s - jnp.max(s, axis=-1, keepdims=True))
        w = (raised * (1.0 / jnp.sum(raised, axis=-1, keepdims=True))).astype(BF16)
        for p in range(pairs):
            v = split_heads(lane_block(v_ref, slice(p * kl, (p + 1) * kl), cols[2] + j), heads_in)
            o = mm(side_by_side(w[p * chain : (p + 1) * chain], heads_in), v)
            put_block(o_ref, slice(p * ql, (p + 1) * ql), j, o.astype(BF16))


def attend(lens, q, k, v, cols, pairs, blocks, heads_in, fixed, scaling):
    rows = q.shape[0]
    krows = k.shape[0]
    same = k is v
    vmem = pl.BlockSpec(memory_space=pltpu.VMEM)
    operands = [lens, q, k] if same else [lens, q, k, v]
    if q is k:
        operands = [lens, q]

    def body(lens_ref, *refs, **kw):
        refs = list(refs)
        o_ref = refs.pop()
        while len(refs) < 3:
            refs.append(refs[-1])
        attend_kernel(lens_ref, *refs, o_ref, **kw)

    return pl.pallas_call(
        functools.partial(
            body,
            pairs=pairs,
            blocks=blocks,
            cols=cols,
            heads_in=heads_in,
            fixed=fixed,
            scaling=scaling,
        ),
        in_specs=[pl.BlockSpec(memory_space=pltpu.SMEM)] + [vmem] * (len(operands) - 1),
        out_specs=vmem,
        out_shape=jax.ShapeDtypeStruct((rows, blocks * LANES), BF16),
        compiler_params=pltpu.CompilerParams(vmem_limit_bytes=10 * 1024 * 1024),
        cost_estimate=cost(5),
        name="attend",
    )(*operands)


def attend_back_kernel(
    lens_ref,
    q_ref,
    k_ref,
    v_ref,
    g_ref,
    dq_ref,
    dk_ref,
    dv_ref,
    *,
    pairs,
    blocks,
    cols,
    out_cols,
    heads_in,
    fixed,
    scaling,
):
    ql = q_ref.shape[0] // pairs
    kl = k_ref.shape[0] // pairs
    keys = lax.broadcasted_iota(jnp.int32, (heads_in * kl, ql), 0)
    if heads_in == 2:
        keys = jnp.where(keys >= kl, keys - kl, keys)
    if fixed is None:
        masks = [keys < lens_ref[p] for p in range(pairs)]
    else:
        masks = [keys < fixed] * pairs

    @pl.loop(0, blocks, unroll=4 if blocks % 4 == 0 else 3)
    def _(j):
        scores, slopes = [], []
        for p in range(pairs):
            qs, ks = slice(p * ql, (p + 1) * ql), slice(p * kl, (p + 1) * kl)
            q, g = lane_block(q_ref, qs, cols[0] + j), lane_block(g_ref, qs, j)
            k = split_heads(lane_block(k_ref, ks, cols[1] + j), heads_in)
            v = split_heads(lane_block(v_ref, ks, cols[2] + j), heads_in)
            scores.append(jnp.where(masks[p], mm_nt(k, q) * scaling, masked_score))
            slopes.append(mm_nt(v, g))
        stacked = (pairs * heads_in, kl, ql)
        s = jnp.concatenate(scores, axis=0).reshape(stacked)
        dp = jnp.concatenate(slopes, axis=0).reshape(stacked)
        raised = jnp.exp(s - jnp.max(s, axis=1, keepdims=True))
        w = raised * (1.0 / jnp.sum(raised, axis=1, keepdims=True))
        inner = jnp.sum(w * dp, axis=1, keepdims=True)
        ds = (w * (dp - inner)).astype(BF16).reshape(-1, ql)
        w = w.astype(BF16).reshape(-1, ql)
        chain = heads_in * kl
        for p in range(pairs):
            qs, ks = slice(p * ql, (p + 1) * ql), slice(p * kl, (p + 1) * kl)
            own = slice(p * chain, (p + 1) * chain)
            q = split_heads(lane_block(q_ref, qs, cols[0] + j), heads_in)
            g = split_heads(lane_block(g_ref, qs, j), heads_in)
            k = split_heads(lane_block(k_ref, ks, cols[1] + j), heads_in)
            dq = mm_tn(ds[own], k) * scaling
            dk = mm(side_by_side(ds[own], heads_in), q) * scaling
            dv = mm(side_by_side(w[own], heads_in), g)
            put_block(dq_ref, qs, out_cols[0] + j, dq.astype(BF16))
            put_block(dk_ref, ks, out_cols[1] + j, dk.astype(BF16))
            put_block(dv_ref, ks, out_cols[2] + j, dv.astype(BF16))


def attend_back(lens, q, k, v, g, cols, pairs, blocks, heads_in, fixed, scaling, packed):
    rows = q.shape[0]
    krows = k.shape[0]
    vmem = pl.BlockSpec(memory_space=pltpu.VMEM)
    width = blocks * LANES
    if packed:
        operands = [lens, q, g]
        out_cols = (0, blocks, 2 * blocks)
        out_shape = jax.ShapeDtypeStruct((rows, 3 * width), BF16)
        out_specs = vmem
    else:
        operands = [lens, q, k, g]
        out_cols = (0, 0, blocks)
        out_shape = [
            jax.ShapeDtypeStruct((rows, width), BF16),
            jax.ShapeDtypeStruct((krows, 2 * width), BF16),
        ]
        out_specs = [vmem, vmem]

    def body(lens_ref, *refs, **kw):
        if packed:
            q_ref, g_ref, out_ref = refs
            ins, outs = (q_ref, q_ref, q_ref, g_ref), (out_ref,) * 3
        else:
            q_ref, k_ref, g_ref, dq_ref, dkv_ref = refs
            ins, outs = (q_ref, k_ref, k_ref, g_ref), (dq_ref, dkv_ref, dkv_ref)
        attend_back_kernel(lens_ref, *ins, *outs, **kw)

    return pl.pallas_call(
        functools.partial(
            body,
            pairs=pairs,
            blocks=blocks,
            cols=cols,
            out_cols=out_cols,
            heads_in=heads_in,
            fixed=fixed,
            scaling=scaling,
        ),
        in_specs=[pl.BlockSpec(memory_space=pltpu.SMEM)] + [vmem] * (len(operands) - 1),
        out_specs=out_specs,
        out_shape=out_shape,
        compiler_params=pltpu.CompilerParams(vmem_limit_bytes=10 * 1024 * 1024),
        cost_estimate=cost(6),
        name="attend_back",
    )(*operands)


class Job:
    def __init__(self, a, b, low, high, place):
        self.a, self.b = a, b
        self.low, self.count = low, high - low
        self.columns = b[3]
        self.place = place


def flat_kernel(side_ref, *refs, plans, found, quarter, resident):
    out_ref, chosen_ref, stage_ref = refs[len(found) : len(found) + 3]
    core = side_ref[0]
    depth = chosen_ref.shape[0] // 2
    if not resident:
        a_buf, b_buf, in_sem = refs[-3:]

    def loads(jobs, k):
        job, slot = jobs[k], k % 2
        copies = []
        for side, buf, start, width in (
            (job.a, a_buf, job.a[2] + job.low, job.count),
            (job.b, b_buf, job.b[2], job.columns),
        ):
            for half in range(2):
                copies.append(
                    pltpu.make_async_copy(
                        refs[found[id(side[half])]].at[:, start : start + width],
                        buf.at[slot, half * depth : (half + 1) * depth, 0:width],
                        in_sem.at[slot, len(copies)],
                    )
                )
        return copies

    def run(jobs):
        if not resident:
            for copy in loads(jobs, 0):
                copy.start()
        for k, job in enumerate(jobs):
            if resident:
                a_refs = [refs[found[id(job.a[half])]] for half in range(2)]
                b_refs = [refs[found[id(job.b[half])]] for half in range(2)]
                a_first, b_first = job.a[2] + job.low, job.b[2]
            else:
                if k + 1 < len(jobs):
                    for copy in loads(jobs, k + 1):
                        copy.start()
                for copy in loads(jobs, k):
                    copy.wait()
                halves = [slice(0, depth), slice(depth, 2 * depth)]
                a_refs = [a_buf.at[k % 2, half] for half in halves]
                b_refs = [b_buf.at[k % 2, half] for half in halves]
                a_first = b_first = 0
            units = job.columns // (2 * UNIT if quarter else UNIT)
            for u in range(units):
                at = 4 * u + 2 * side_ref[1] + core if quarter else 2 * u + core
                block = pl.ds(pl.multiple_of(at * LANES + b_first, LANES), LANES)
                for half in range(2):
                    chosen_ref[half * depth : (half + 1) * depth, u * LANES : (u + 1) * LANES] = (
                        b_refs[half][:, block]
                    )
            bm = best_rows(job.count, units)
            rows = bm * units

            @pl.loop(0, job.count // bm)
            def _(i, job=job, units=units, bm=bm, rows=rows, a_refs=a_refs, a_first=a_first):
                columns = pl.ds(pl.multiple_of(a_first + i * bm, LANES), bm)
                a = jnp.concatenate([a_ref[:, columns] for a_ref in a_refs], axis=0).T
                for u0 in range(0, units, 12):
                    u1 = min(u0 + 12, units)
                    total = mm(a, chosen_ref[:, u0 * LANES : u1 * LANES])
                    for u in range(u0, u1):
                        stage_ref[pl.ds(u, bm, stride=units), :] = total[
                            :, (u - u0) * LANES : (u - u0 + 1) * LANES
                        ]
                first = pl.multiple_of(job.place + i * rows, LANES)
                out_ref[pl.ds(first, rows), :] = stage_ref[:rows].astype(BF16)

    if len(plans) == 1:
        run(plans[0])
    else:
        for side, jobs in enumerate(plans):

            @pl.when(side_ref[1] == side)
            def _(jobs=jobs):
                run(jobs)


def best_rows(count, units):
    most = 512 if units <= 8 else 384
    return max(size for size in range(LANES, most + 1, LANES) if count % size == 0)


def flat_grads(side, total_rows, plans, us, quarter=False, resident=True):
    arrays, found = [], {}
    jobs = [job for plan in plans for job in plan]
    for job in jobs:
        for array in (*job.a[:2], *job.b[:2]):
            if id(array) not in found:
                found[id(array)] = len(arrays)
                arrays.append(array)
    depth = 2 * arrays[0].shape[0]
    widest = max(job.columns for job in jobs)
    tallest = max(job.count for job in jobs)
    factor = 2 * UNIT if quarter else UNIT
    rows = max(best_rows(job.count, job.columns // factor) * job.columns // factor for job in jobs)
    held = 2 * depth * widest * LANES // factor + 4 * rows * LANES
    scratch = [
        pltpu.VMEM((depth, widest * LANES // factor), BF16),
        pltpu.VMEM((rows, LANES), F32),
    ]
    if not resident:
        held += 4 * depth * (tallest + widest)
        scratch += [
            pltpu.VMEM((2, depth, tallest), BF16),
            pltpu.VMEM((2, depth, widest), BF16),
            pltpu.SemaphoreType.DMA((2, 4)),
        ]
    place = pltpu.VMEM if resident else pltpu.HBM
    return pl.pallas_call(
        functools.partial(
            flat_kernel, plans=plans, found=found, quarter=quarter, resident=resident
        ),
        in_specs=[pl.BlockSpec(memory_space=pltpu.SMEM)]
        + [pl.BlockSpec(memory_space=place)] * len(arrays),
        out_specs=pl.BlockSpec(memory_space=pltpu.VMEM),
        out_shape=jax.ShapeDtypeStruct((total_rows, LANES), BF16),
        scratch_shapes=scratch,
        compiler_params=pltpu.CompilerParams(vmem_limit_bytes=held + (8 if resident else 10) * 1024 * 1024),
        cost_estimate=cost(us),
        name="flat_grads",
    )(side, *arrays)


def dp_swap(block, bit):
    count = lax.axis_size("dp")
    return lax.ppermute(block, "dp", [(i, i ^ bit) for i in range(count)])


def stream_swap(block):
    return lax.ppermute(block, "stream", [(0, 1), (1, 0)])


def pick(block, index, axis=0):
    return lax.dynamic_index_in_dim(block, index, axis, keepdims=False)


def plus(a, b):
    return (a.astype(F32) + b.astype(F32)).astype(BF16)


def tied(*values):
    return lax.optimization_barrier(values)


def scatter_parts(flat, cuts):
    count = lax.axis_size("dp")
    top = count.bit_length() - 2
    bits = tuple(range(top, 0, -1))
    rows = flat.shape[0] // (count // 2)
    blocks = flat.reshape((2,) * len(bits) + (rows, LANES))
    natural = tuple(range(1, top + 1))
    turned = natural[1:2] + natural[:1] + natural[2:]
    parts, start = [], 0
    for share, turn in cuts:
        part = lax.slice_in_dim(blocks, start, start + rows * share // 8, axis=len(bits))
        start += rows * share // 8
        parts.append((part, bits, turned if turn else natural))
    return parts


def scatter_step(parts):
    me = lax.axis_index("dp")
    done = []
    for block, left, order in parts:
        bit = order[0]
        axis = left.index(bit)
        mine = (me >> bit) & 1
        keep = pick(block, mine, axis)
        far = dp_swap(pick(block, 1 - mine, axis), 1 << bit)
        block = plus(keep, far) if len(order) > 1 else keep.astype(F32) + far.astype(F32)
        done.append((block, left[:axis] + left[axis + 1 :], order[1:]))
    return done


def scatter_end(parts):
    while parts[0][2]:
        parts = scatter_step(parts)
    blocks = [block for block, _, _ in parts]
    return jnp.concatenate(blocks) if len(blocks) > 1 else blocks[0]


def reduce_scatter(flat, cuts):
    return scatter_end(scatter_parts(flat, cuts))


def share_of(result):
    core = lax.axis_index("dp") & 1
    halves = result.reshape(2, result.shape[0] // 2, LANES)
    mine = pick(halves, core)
    far = dp_swap(pick(halves, 1 - core), 1)
    first = jnp.where(core == 0, mine, far)
    second = jnp.where(core == 0, far, mine)
    return jnp.stack([first, second], axis=1).reshape(-1)


def choices(stream):
    me = lax.axis_index("dp")
    y, odd = (me >> 1) & 1, (me >> 2) & 1
    own = jnp.where(y == 1, odd, 1 - odd)
    values = [me & 1, y, odd, (me >> 3) & 1, 1 - y, own, stream, me >> 1]
    return jnp.stack(values).astype(jnp.int32)


LATE_Y, LATE_OWN, STREAM, CHIP = 4, 5, 6, 7
TEXT_SHARES = (48, 46, 38, 24)


def split_kernel(choice_ref, flat_ref, *refs, chunk, cuts):
    for k, (start, rows, bases, weight, which) in enumerate(cuts):
        mine = choice_ref[which]
        for i, base in enumerate(bases):
            for out_ref, index in ((refs[2 * k], mine), (refs[2 * k + 1], 1 - mine)):
                first = (base + index * weight) * chunk + start
                out_ref[i] = flat_ref[pl.ds(pl.multiple_of(first, 16), rows), :]


def split(choice, flat, chunk, cuts):
    shapes = [
        jax.ShapeDtypeStruct((len(bases), rows, LANES), BF16)
        for _, rows, bases, _, _ in cuts
        for _ in range(2)
    ]
    return pl.pallas_call(
        functools.partial(split_kernel, chunk=chunk, cuts=cuts),
        in_specs=[
            pl.BlockSpec(memory_space=pltpu.SMEM),
            pl.BlockSpec(memory_space=pltpu.VMEM),
        ],
        out_specs=[pl.BlockSpec(memory_space=pltpu.VMEM)] * len(shapes),
        out_shape=shapes,
        compiler_params=pltpu.CompilerParams(vmem_limit_bytes=8 * 1024 * 1024),
        cost_estimate=cost(3),
        name="split",
    )(choice, flat)


def piece_set(choice, flat, firsts, shares):
    chunk = flat.shape[0] // 8
    unit = chunk // sum(shares)
    cuts, start = [], 0
    for first, share in zip(firsts, shares):
        bits = [bit for bit in (3, 2, 1) if bit != first]
        bases = tuple(
            sum(((n >> (1 - at)) & 1) << (b - 1) for at, b in enumerate(bits)) for n in range(4)
        )
        cuts.append((start, unit * share, bases, 1 << (first - 1), first))
        start += unit * share
    arrays = split(choice, flat, chunk, tuple(cuts))
    return [
        Piece(keep, out, first) for keep, out, first in zip(arrays[::2], arrays[1::2], firsts)
    ]


class Piece:
    def __init__(self, keep, out, bit):
        self.keep, self.out, self.bit = keep, out, bit

    def send(self):
        self.far = dp_swap(self.out, 1 << self.bit)


def after(value, pieces, name="far"):
    value, *got = tied(value, *(getattr(piece, name) for piece in pieces))
    for piece, array in zip(pieces, got):
        setattr(piece, name, array)
    return value


def paced(came, leaving, values=()):
    got = tied(*(item.far for item in came), *(item.out for item in leaving), *values)
    for item, array in zip(came, got):
        item.far = array
    for item, array in zip(leaving, got[len(came) :]):
        item.out = array
    return got[len(came) + len(leaving) :]


def added(a_ref, b_ref, index):
    return a_ref[index].astype(F32) + b_ref[index].astype(F32)


def add_split_kernel(choice_ref, *refs, plan, inputs):
    outs = refs[2 * inputs :]
    for k, base, stride, which, out, at in plan:
        keep_ref, far_ref = refs[2 * k : 2 * k + 2]
        mine = choice_ref[which]
        for ref, index in ((outs[2 * out], mine), (outs[2 * out + 1], 1 - mine)):
            ref[at] = added(keep_ref, far_ref, base + index * stride).astype(BF16)


def add_split(choice, groups, which=None):
    operands, plan, shapes = [], [], []
    for out, (bit, pieces) in enumerate(groups):
        at = 0
        for piece in pieces:
            for base in range(0, piece.keep.shape[0], 2):
                plan.append((len(operands) // 2, base, 1, which or bit, out, at))
                at += 1
            operands += [piece.keep, piece.far]
        shape = jax.ShapeDtypeStruct((at,) + pieces[0].keep.shape[1:], BF16)
        shapes += [shape, shape]
    vmem = pl.BlockSpec(memory_space=pltpu.VMEM)
    arrays = pl.pallas_call(
        functools.partial(add_split_kernel, plan=tuple(plan), inputs=len(operands) // 2),
        in_specs=[pl.BlockSpec(memory_space=pltpu.SMEM)] + [vmem] * len(operands),
        out_specs=[vmem] * len(shapes),
        out_shape=shapes,
        compiler_params=pltpu.CompilerParams(vmem_limit_bytes=8 * 1024 * 1024),
        cost_estimate=cost(1),
        name="add_split",
    )(choice, *operands)
    return [
        Piece(arrays[2 * out], arrays[2 * out + 1], bit) for out, (bit, _) in enumerate(groups)
    ]


def finish_kernel(choice_ref, *refs, rows):
    refs = list(refs)
    pairs = [[(refs.pop(0), refs.pop(0)) for _ in group] for group in rows]
    near_ref, far_ref = refs.pop(0), refs.pop(0)
    out_ref, send_ref, *totals, joined_ref = refs
    for total_ref, group, starts in zip(totals, pairs, rows):
        for (keep_ref, came_ref), firsts in zip(group, starts):
            count = keep_ref.shape[1]
            for at, first in enumerate(firsts):
                total_ref[first : first + count] = added(keep_ref, came_ref, at)
    half = near_ref.shape[0]
    joined_ref[pl.ds(0, half, stride=2), :] = near_ref[...].astype(F32)
    joined_ref[pl.ds(1, half, stride=2), :] = far_ref[...].astype(F32)
    image_ref = totals[0]
    total_rows = image_ref.shape[0]
    chip = choice_ref[CHIP]
    first = jnp.where(chip == 1, 1536, 0)
    last = jnp.where(chip == 4, 2048, total_rows)
    here = (chip >= 1) & (chip <= 4) & (choice_ref[STREAM] == 0)
    last = jnp.where(here, last, 0)
    at = lax.broadcasted_iota(jnp.int32, (total_rows, 1), 0)
    image_ref[...] = jnp.where((at >= first) & (at < last), joined_ref[...], image_ref[...])
    core = choice_ref[0]
    row = 0
    for total_ref in totals:
        half = total_ref.shape[0] // 2
        for ref, index in ((out_ref, core), (send_ref, 1 - core)):
            ref[row : row + half, :] = total_ref[pl.ds(pl.multiple_of(index * half, 8), half), :]
        row += half


def join_kernel(choice_ref, near_ref, far_ref, *outs):
    core = choice_ref[0]
    row = 0
    for out_ref in outs:
        half = out_ref.shape[0] // 2
        out_ref[pl.ds(core, half, stride=2), :] = near_ref[row : row + half, :]
        out_ref[pl.ds(1 - core, half, stride=2), :] = far_ref[row : row + half, :]
        row += half


def finished(choice, groups, rows, late):
    sizes = [
        sum(piece.keep.shape[0] * piece.keep.shape[1] for piece in group) for group in groups
    ]
    vmem = pl.BlockSpec(memory_space=pltpu.VMEM)
    smem = pl.BlockSpec(memory_space=pltpu.SMEM)
    operands = [ref for group in groups for piece in group for ref in (piece.keep, piece.far)]
    operands += list(late)
    half = jax.ShapeDtypeStruct((sum(sizes) // 2, LANES), F32)
    near, send = pl.pallas_call(
        functools.partial(finish_kernel, rows=rows),
        in_specs=[smem] + [vmem] * len(operands),
        out_specs=[vmem] * 2,
        out_shape=[half] * 2,
        scratch_shapes=[pltpu.VMEM((rows, LANES), F32) for rows in (*sizes, sizes[0])],
        compiler_params=pltpu.CompilerParams(vmem_limit_bytes=12 * 1024 * 1024),
        cost_estimate=cost(3),
        name="finish",
    )(choice, *operands)
    joined = pl.pallas_call(
        join_kernel,
        in_specs=[smem, vmem, vmem],
        out_specs=[vmem] * 2,
        out_shape=[jax.ShapeDtypeStruct((rows, LANES), F32) for rows in sizes],
        compiler_params=pltpu.CompilerParams(vmem_limit_bytes=12 * 1024 * 1024),
        cost_estimate=cost(2),
        name="join",
    )(choice, near, dp_swap(send, 1))
    return [block.reshape(-1) for block in joined]


CHUNK = 64
ROWS = 128
WIDEST = 1024
WIDEST_GELU = 1024


def tiles(columns, body, widest=None):
    size = max(c for c in range(LANES, (widest or WIDEST) + 1, LANES) if columns % c == 0)
    if size == columns:
        return body(slice(0, columns))

    @pl.loop(0, columns // size)
    def _(j):
        body(pl.ds(pl.multiple_of(j * size, size), size))


def views(pack_ref, *widths):
    found, start = [], 0
    for width in widths:
        found.append(pack_ref.at[:, start : start + width])
        start += width
    return found


def row_chunks(rows, body):
    size = ROWS if rows % ROWS == 0 else CHUNK

    @pl.loop(0, rows // size)
    def _(i):
        body(i * size, pl.ds(pl.multiple_of(i * size, size), size), size)


def normed_chunk(a):
    centred = a - jnp.mean(a, axis=-1, keepdims=True)
    inverse = lax.rsqrt(jnp.mean(centred * centred, axis=-1, keepdims=True) + 1e-05)
    return centred * inverse, inverse


def normed_back_chunk(grad, n, inverse, gain_row):
    scaled = grad * gain_row
    low = jnp.mean(scaled, axis=-1, keepdims=True)
    tilt = jnp.mean(scaled * n, axis=-1, keepdims=True)
    return (scaled - low - n * tilt) * inverse, jnp.sum(grad * n, axis=0, keepdims=True)


def co_kernel(
    lens_ref, x_ref, given_ref, source_ref, g_ref, wmade_ref, wat_ref,
    made_ref, pack_ref, n_ref, inv_ref, a_ref, *, pairs, fixed, scaling, makes_kv,
):
    rows, width = x_ref.shape
    c_ref, h_ref = views(pack_ref, D_C, width)

    def made_tile(cols):
        made_ref[:, cols] = mm(source_ref[...], wmade_ref[:, cols]).astype(BF16)

    def a_tile(cols):
        a_ref[:, cols] = x_ref[:, cols].astype(F32) + mm(c_ref[...], wat_ref[:, cols])

    def norm(i, at, size):
        n, inverse = normed_chunk(a_ref[at, :])
        n_ref[at, :] = n
        inv_ref[at, :] = jnp.broadcast_to(inverse, (size, LANES))
        h_ref[at, :] = (n * g_ref[0:1, :]).astype(BF16)

    tiles(made_ref.shape[1], made_tile)
    q_ref, kv_ref = (given_ref, made_ref) if makes_kv else (made_ref, given_ref)
    blocks = q_ref.shape[1] // LANES
    attend_kernel(
        lens_ref, q_ref, kv_ref, kv_ref, c_ref, pairs=pairs, blocks=blocks,
        cols=(0, 0, blocks), heads_in=1, fixed=fixed, scaling=scaling,
    )
    tiles(width, a_tile)
    row_chunks(rows, norm)


def mlp_kernel(
    pack1_ref, n1_ref, g_ref, wup_ref, wdown_ref, wqkv_ref,
    pack_ref, slope_ref, n_ref, inv_ref, r_ref, a_ref,
):
    rows, width = n1_ref.shape
    _, h1_ref = views(pack1_ref, D_C, width)
    hid_ref, h_ref = views(pack_ref, wup_ref.shape[1], width)

    def up_tile(cols):
        u_all = mm(h1_ref[...], wup_ref[:, cols])
        for at in range(0, rows, CHUNK):
            u = u_all[at : at + CHUNK]
            share = 0.5 + 0.5 * lax.erf(u * 0.7071067811865476)
            hid_ref[at : at + CHUNK, cols] = (u * share).astype(BF16)
            slope = share + u * (0.3989422804014327 * jnp.exp(-0.5 * u * u))
            slope_ref[at : at + CHUNK, cols] = slope.astype(BF16)

    def down_tile(cols):
        a_ref[:, cols] = n1_ref[:, cols] * g_ref[0:1, cols] + mm(hid_ref[...], wdown_ref[:, cols])

    def norm(i, at, size):
        n, inverse = normed_chunk(a_ref[at, :])
        n_ref[at, :] = n
        inv_ref[at, :] = jnp.broadcast_to(inverse, (size, LANES))
        h_ref[at, :] = (n * g_ref[1:2, :]).astype(BF16)

    def qkv_tile(cols):
        r_ref[:, cols] = mm(h_ref[...], wqkv_ref[:, cols]).astype(BF16)

    tiles(wup_ref.shape[1], up_tile, WIDEST_GELU)
    tiles(width, down_tile)
    row_chunks(rows, norm)
    tiles(r_ref.shape[1], qkv_tile)


def self_kernel(
    lens_ref, r_ref, n2_ref, g_ref, wout_ref, cot_ref, far_cot_ref,
    pack_ref, y_ref, de_ref, dg_ref, a_ref, dz_ref,
    *, pairs, heads_in, fixed, scaling,
):
    rows, width = n2_ref.shape
    z_ref, de_low_ref, dr_ref = views(pack_ref, width, width, 3 * width)
    near = cot_ref.shape[0]
    dz_ref[:near, :] = cot_ref[...]
    if near < rows:
        dz_ref[near:, :] = far_cot_ref[...]
    blocks = width // LANES
    cols = (0, blocks, 2 * blocks)
    shared = dict(
        pairs=pairs, blocks=blocks, cols=cols, heads_in=heads_in, fixed=fixed, scaling=scaling
    )

    def out_tile(at):
        a_ref[:, at] = n2_ref[:, at] * g_ref[1:2, at] + mm(z_ref[...], wout_ref[:, at])

    def last(start, at, size):
        n, inverse = normed_chunk(a_ref[at, :])
        y = n * g_ref[2:3, :]
        grad = dz_ref[at, :].astype(F32)
        if fixed is None:
            slots = rows // pairs
            place = lax.broadcasted_iota(jnp.int32, (size, 1), 0) + lax.rem(start, slots)
            valid = (place < lens_ref[lax.div(start, slots)]).astype(F32)
            y, grad = y * valid, grad * valid
        y_ref[at, :] = y.astype(BF16)
        de, dg = normed_back_chunk(grad, n, inverse, g_ref[2:3, :])
        de_ref[at, :] = de
        de_low_ref[at, :] = de.astype(BF16)
        dg_ref[...] += dg

    def dz_tile(at):
        dz_ref[:, at] = mm_nt(de_low_ref[...], wout_ref[at, :]).astype(BF16)

    attend_kernel(lens_ref, r_ref, r_ref, r_ref, z_ref, **shared)
    tiles(width, out_tile)
    dg_ref[...] = jnp.zeros_like(dg_ref)
    row_chunks(rows, last)
    tiles(width, dz_tile)
    attend_back_kernel(
        lens_ref, r_ref, r_ref, r_ref, dz_ref, dr_ref, dr_ref, dr_ref, out_cols=cols, **shared
    )


def mlp_back_kernel(
    pack3_ref, de_ref, n2_ref, inv2_ref, g_ref, slope_ref, wqkv_ref, wdown_ref,
    pack_ref, db_ref, dg_ref, a_ref,
):
    rows, width = n2_ref.shape
    _, _, dr_ref = views(pack3_ref, width, width, 3 * width)
    db_low_ref, du_ref = views(pack_ref, width, slope_ref.shape[1])
    dg_ref[...] = jnp.zeros_like(dg_ref)

    def second_tile(at):
        a_ref[:, at] = de_ref[:, at] + mm_nt(dr_ref[...], wqkv_ref[at, :])

    def second_norm(i, at, size):
        db, dg = normed_back_chunk(a_ref[at, :], n2_ref[at, :], inv2_ref[at, 0:1], g_ref[1:2, :])
        db_ref[at, :] = db
        db_low_ref[at, :] = db.astype(BF16)
        dg_ref[...] += dg

    def du_tile(at):
        grad = mm_nt(db_low_ref[...], wdown_ref[at, :])
        du_ref[:, at] = (grad * slope_ref[:, at].astype(F32)).astype(BF16)

    tiles(width, second_tile)
    row_chunks(rows, second_norm)
    tiles(du_ref.shape[1], du_tile)


def context_back_kernel(
    pack4_ref, db_ref, n1_ref, inv1_ref, g_ref, wup_ref, wat_ref,
    da_low_ref, da_ref, dc_ref, dg_ref, a_ref,
):
    rows, width = n1_ref.shape
    _, du_ref = views(pack4_ref, width, wup_ref.shape[1])
    dg_ref[...] = jnp.zeros_like(dg_ref)

    def first_tile(at):
        a_ref[:, at] = db_ref[:, at] + mm_nt(du_ref[...], wup_ref[at, :])

    def first_norm(i, at, size):
        da, dg = normed_back_chunk(a_ref[at, :], n1_ref[at, :], inv1_ref[at, 0:1], g_ref[0:1, :])
        da_ref[at, :] = da
        da_low_ref[at, :] = da.astype(BF16)
        dg_ref[...] += dg

    def dc_tile(at):
        dc_ref[:, at] = mm_nt(da_low_ref[...], wat_ref[at, :]).astype(BF16)

    tiles(width, first_tile)
    row_chunks(rows, first_norm)
    tiles(dc_ref.shape[1], dc_tile)


def fused(kernel, operands, outs, scratch, name, us, smem_first=False, limit=11):
    vmem = pl.BlockSpec(memory_space=pltpu.VMEM)
    in_specs = [vmem] * len(operands)
    if smem_first:
        in_specs[0] = pl.BlockSpec(memory_space=pltpu.SMEM)
    return pl.pallas_call(
        kernel,
        in_specs=in_specs,
        out_specs=[vmem] * len(outs),
        out_shape=[jax.ShapeDtypeStruct(shape, kind) for shape, kind in outs],
        scratch_shapes=[pltpu.VMEM(shape, kind) for shape, kind in scratch],
        compiler_params=pltpu.CompilerParams(vmem_limit_bytes=limit * 1024 * 1024),
        cost_estimate=cost(us),
        name=name,
    )(*operands)


def co_forward(lens, states, given, source, gains, made_w, attend_w, pairs, fixed):
    rows, width = states.shape
    made, pack1, n1, inv1 = fused(
        functools.partial(
            co_kernel,
            pairs=pairs,
            fixed=fixed,
            scaling=(D_C // H_C) ** (-0.5),
            makes_kv=made_w.shape[1] == 2 * D_C,
        ),
        (lens, states, given, source, gains, made_w, attend_w),
        [
            ((source.shape[0], made_w.shape[1]), BF16),
            ((rows, D_C + width), BF16),
            ((rows, width), F32),
            ((rows, LANES), F32),
        ],
        [((rows, width), F32)],
        "co_forward",
        7,
        True,
    )
    return made, pack1, n1, inv1


def mlp_forward(pack1, n1, gains, up_w, down_w, qkv_w):
    rows, width = n1.shape
    hidden = up_w.shape[1]
    return fused(
        mlp_kernel,
        (pack1, n1, gains, up_w, down_w, qkv_w),
        [
            ((rows, hidden + width), BF16),
            ((rows, hidden), BF16),
            ((rows, width), F32),
            ((rows, LANES), F32),
            ((rows, 3 * width), BF16),
        ],
        [((rows, width), F32)],
        "mlp_forward",
        rows / 40,
    )


def self_turn(lens, r, n2, gains, output_w, cots, pairs, heads, fixed):
    rows, width = n2.shape
    size = width // heads
    return fused(
        functools.partial(
            self_kernel, pairs=pairs, heads_in=LANES // size, fixed=fixed, scaling=size ** (-0.5)
        ),
        (lens, r, n2, gains, output_w, *cots),
        [
            ((rows, 5 * width), BF16),
            ((rows, width), BF16),
            ((rows, width), F32),
            ((1, width), F32),
        ],
        [((rows, width), F32), ((rows, width), BF16)],
        "self_turn",
        rows / 128 + 9,
        True,
    )


def input_kernel(da_ref, dq_ref, dkv_ref, y_ref, trim_ref, wq_ref, wkv_ref, *outs, first):
    grad_ref, result_ref = outs
    rows = pl.ds(first, da_ref.shape[0] // 2)
    grad = da_ref[rows, :] + mm_nt(dq_ref[rows, :], wq_ref[...])
    grad = (grad + mm_nt(dkv_ref[rows, :], wkv_ref[...])).astype(BF16)
    y = y_ref[rows, :]
    if trim_ref.shape[0] < 8:
        grad_ref[...], result_ref[...] = grad, y
    else:
        grad_ref[...] = mm(trim_ref[...], grad).astype(BF16)
        result_ref[...] = mm(trim_ref[...], y).astype(BF16)


def input_grads(da, dq, dkv, y, trim, query_w, keyval_w, first, own):
    vmem = pl.BlockSpec(memory_space=pltpu.VMEM)
    return pl.pallas_call(
        functools.partial(input_kernel, first=first),
        in_specs=[vmem] * 7,
        out_specs=[vmem] * 2,
        out_shape=[jax.ShapeDtypeStruct((own, da.shape[1]), BF16)] * 2,
        compiler_params=pltpu.CompilerParams(vmem_limit_bytes=10 * 1024 * 1024),
        cost_estimate=cost(0.2),
        name="input_grads",
    )(da, dq, dkv, y, trim, query_w, keyval_w)


def mlp_back(pack3, de, n2, inv2, gains, slope, qkv_w, down_w):
    rows, width = n2.shape
    return fused(
        mlp_back_kernel,
        (pack3, de, n2, inv2, gains, slope, qkv_w, down_w),
        [
            ((rows, width + slope.shape[1]), BF16),
            ((rows, width), F32),
            ((1, width), F32),
        ],
        [((rows, width), F32)],
        "mlp_back",
        rows / 70,
    )


def context_back(pack4, db, n1, inv1, gains, up_w, attend_w):
    rows, width = n1.shape
    return fused(
        context_back_kernel,
        (pack4, db, n1, inv1, gains, up_w, attend_w),
        [
            ((rows, width), BF16),
            ((rows, width), F32),
            ((rows, D_C), BF16),
            ((1, width), F32),
        ],
        [((rows, width), F32)],
        "context_back",
        rows / 80,
    )


class Exchange:
    def __init__(self):
        self.far = {}
        self.pending = []
        self.parts = None

    def send(self, **arrays):
        for name, array in arrays.items():
            self.far[name] = dp_swap(array, 1)
            self.pending.append(name)

    def settle(self, value):
        names, self.pending = self.pending, []
        if names:
            value, *got = tied(value, *(self.far[name] for name in names))
            self.far.update(zip(names, got))
        return value

    def pair(self, name, array, start=0, width=None):
        return array, self.far[name], start, width or array.shape[1]


def stream_forward(
    lens, states, given, source, cot, weights, gains, heads, fixed, other_fixed, pairs, moves, hook
):
    made_w, attend_w, up_w, down_w, qkv_w, output_w = weights
    made, pack1, n1, inv1 = co_forward(
        lens, states, given, source, gains, made_w, attend_w, pairs, other_fixed
    )
    pack1 = moves.settle(hook("co", pack1))
    moves.send(pack1=pack1)
    pack2, slope, n2, inv2, r = mlp_forward(pack1, n1, gains, up_w, down_w, qkv_w)
    r, pack2 = tied(moves.settle(hook("mlp", r)), pack2)
    moves.send(pack2=pack2)
    near_cot, far_cot = cot
    cots = (near_cot, far_cot[0] if far_cot else near_cot)
    pack3, result, de, dg2 = self_turn(lens, r, n2, gains, output_w, cots, pairs, heads, fixed)
    pack3 = moves.settle(hook("self", pack3))
    moves.send(pack3=pack3)
    pack4, db, dg1 = mlp_back(pack3, de, n2, inv2, gains, slope, qkv_w, down_w)
    pack4 = moves.settle(hook("mid", pack4))
    moves.send(pack4=pack4)
    da_low, da, dc, dg0 = context_back(pack4, db, n1, inv1, gains, up_w, attend_w)
    dc = moves.settle(hook("back", dc))
    width, hidden = up_w.shape

    def sides(dq, da_low):
        def side(number, start, count):
            pack = (pack1, pack2, pack3, pack4)[number - 1]
            return moves.pair("pack%d" % number, pack, start, count)

        return {
            "query": (moves.pair("states", states), moves.pair("dq", dq)),
            "attend": (side(1, 0, D_C), moves.pair("da", da_low)),
            "up": (side(1, D_C, width), side(4, width, hidden)),
            "down": (side(2, 0, hidden), side(4, 0, width)),
            "qkv": (side(2, hidden, width), side(3, 2 * width, 3 * width)),
            "output": (side(3, 0, width), side(3, width, width)),
        }

    return result, (da, da_low), dc, made, sides, jnp.concatenate([dg0, dg1, dg2])


NAMES = ("query", "keyval", "attend", "up", "down", "qkv", "output")


def half_jobs(both, sizes, total):
    plans, filled = ([], []), 0
    for name in NAMES:
        m, n = sizes[name]
        room = min(max((total // 2 - filled) // n, 0), m)
        for plan, low, high in ((plans[0], 0, room), (plans[1], room, m)):
            if low < high and name in both:
                start = filled + low * n - (0 if plan is plans[0] else total // 2)
                step = min(high - low, 1024)
                for at in range(low, high, step):
                    place = (start + (at - low) * n) // UNIT
                    plan.append(Job(*both[name], at, at + step, place))
        filled += m * n
    return plans


def spread(count, regions, padded, offset, rows):
    target = lax.broadcasted_iota(jnp.int32, (rows, count * regions), 0) - offset
    source = lax.broadcasted_iota(jnp.int32, (rows, count * regions), 1)
    return (target == source // regions * padded + source % regions).astype(BF16)


def local(
    text_states,
    image_states,
    caption_lengths,
    text_query,
    text_keyval,
    text_attend,
    text_up,
    text_down,
    text_qkv,
    text_output,
    text_gains,
    image_query,
    image_keyval,
    image_attend,
    image_up,
    image_down,
    image_qkv,
    image_output,
    image_gains,
    text_cotangent,
    image_cotangent,
):
    own_pairs = caption_lengths.shape[0]
    own_text = text_states.shape[0]
    text_len = own_text // own_pairs
    regions = image_states.shape[0] // own_pairs
    padded = -(-regions // 16) * 16
    own_image = own_pairs * padded
    pairs = 2 * own_pairs
    d_t, d_i = text_states.shape[1], image_states.shape[1]
    stream = lax.axis_index("stream")
    core = lax.axis_index("dp") & 1
    side = jnp.stack([core, stream]).astype(jnp.int32)

    far_put = spread(own_pairs, regions, padded, 0, 2 * own_image)
    near_put = spread(own_pairs, regions, padded, own_image, 2 * own_image)
    trim = near_put[own_image:].T

    def both_images(near):
        return (mm(far_put, stream_swap(near)) + mm(near_put, near)).astype(BF16)

    choice = choices(stream)
    image_all = both_images(image_states)
    image_q = mm(image_all, image_query).astype(BF16)
    image_kv = mm(image_all, image_keyval).astype(BF16)
    far_text, far_lens, image_q, image_kv = tied(
        stream_swap(text_states), stream_swap(caption_lengths), image_q, image_kv
    )
    text_all = jnp.concatenate([text_states, far_text])
    lens = jnp.concatenate([caption_lengths, far_lens])
    image_cotangent, text_cotangent, text_all = tied(image_cotangent, text_cotangent, text_all)
    image_cot = both_images(image_cotangent)
    far_text_cot = stream_swap(text_cotangent)

    co_blocks = D_C // LANES
    co_cols = (0, 0, co_blocks)
    co_scale = (D_C // H_C) ** (-0.5)

    image_moves, text_moves = Exchange(), Exchange()
    image_moves.send(states=image_all)
    cots = [far_text_cot]

    def image_hook(name, value):
        if name == "self":
            value, cots[0] = tied(value, cots[0])
        return value

    image_out, (image_da, image_da_low), image_dc, text_kv, image_sides, image_dg = stream_forward(
        lens,
        image_all,
        image_q,
        text_all,
        (image_cot, None),
        (text_keyval, image_attend, image_up, image_down, image_qkv, image_output),
        image_gains,
        H_I,
        regions,
        None,
        pairs,
        image_moves,
        image_hook,
    )
    image_dq, text_dkv = attend_back(
        lens, image_q, text_kv, text_kv, image_dc, co_cols, pairs, co_blocks, 1, None, co_scale, False,
    )
    image_moves.send(dq=image_dq, da=image_da_low)
    image_sides = image_sides(image_dq, image_da_low)
    text_moves.send(states=text_all, dkv=text_dkv)

    def sizes_of(*weights):
        return {name: weight.shape for name, weight in zip(NAMES, weights)}

    def gather_half(both, sizes):
        total = sum(m * n for m, n in sizes.values())
        total_rows = total // (2 * UNIT)
        plans = half_jobs(both, sizes, total)
        image = both["query"][0][0] is image_all
        return flat_grads(side, total_rows, plans, 6 if image else 14, resident=image)

    image_sizes = sizes_of(
        image_query, image_keyval, image_attend, image_up, image_down, image_qkv, image_output
    )
    text_sizes = sizes_of(
        text_query, text_keyval, text_attend, text_up, text_down, text_qkv, text_output
    )
    early = lax.axis_size("dp") == 16
    if early:
        image_flat = gather_half(image_sides, image_sizes)

    pieces = []

    def hook(name, value):
        if not early:
            return value
        if name == "co":
            value, flat = tied(value, image_flat)
            pieces.extend(piece_set(choice, flat, (1, 2, 1, 2), (1, 1, 1, 1)))
            value = after(value, pieces, "out")
            for piece in pieces[:2]:
                piece.send()
        if name == "mlp":
            (value,) = paced(pieces[:2], pieces[2:], (value,))
            for piece in pieces[2:]:
                piece.send()
        if name == "self":
            (value,) = paced(pieces[2:], (), (value,))
            pieces[:] = add_split(choice, ((2, pieces[0::2]), (1, pieces[1::2])))
            for piece in pieces:
                piece.send()
        return value

    text_out, (text_da, text_da_low), text_dc, text_q, text_sides, text_dg = stream_forward(
        lens,
        text_all,
        image_kv,
        text_all,
        (text_cotangent, cots),
        (text_query, text_attend, text_up, text_down, text_qkv, text_output),
        text_gains,
        H_T,
        None,
        regions,
        pairs,
        text_moves,
        hook,
    )
    gains = pack_gains(text_dg, image_dg)
    bits = [1 << b for b in range(lax.axis_size("dp").bit_length() - 1)]
    text_dq, image_dkv = attend_back(
        lens, text_q, image_kv, image_kv, text_dc, co_cols, pairs, co_blocks, 1, regions, co_scale, False
    )

    if early:
        image_dkv, text_dq, text_da_low = paced(pieces, (), (image_dkv, text_dq, text_da_low))
        pieces[:] = add_split(choice, ((3, pieces[:1]), (3, pieces[1:])))
        pieces[0].send()
    image_moves.send(dkv=image_dkv)
    text_moves.send(dq=text_dq, da=text_da_low)
    text_sides = text_sides(text_dq, text_da_low)
    text_sides["keyval"] = (text_moves.pair("states", text_all), text_moves.pair("dkv", text_dkv))

    def all_input_grads(text_dq, image_dq):
        text = input_grads(
            text_da, text_dq, text_dkv, text_out, trim[:1], text_query, text_keyval, 0, own_text
        )
        image = input_grads(
            image_da,
            image_dq,
            image_dkv,
            image_out,
            trim,
            image_query,
            image_keyval,
            own_image,
            own_pairs * regions,
        )
        return (*text, *image)

    if early:
        late = Late(
            choice,
            side,
            image_moves.pair("states", image_all),
            image_moves.pair("dkv", image_dkv),
        )
        near_dq, *rest = text_sides["query"][1]
        near_dq, late.out = tied(near_dq, late.out)
        text_sides["query"] = (text_sides["query"][0], (near_dq, *rest))
        late.send()
        text_flat = gather_half(text_sides, text_sizes)
        text_flat = after(text_flat, [late, pieces[0]])
        text_pieces = piece_set(choice, text_flat, (1, 1, 1, 1), TEXT_SHARES)
        one, two, three, four = text_pieces
        late.turn()
        one.out, late.out, pieces[1].out, text_dq, image_dq, gains = tied(
            one.out, late.out, pieces[1].out, text_dq, image_dq, gains
        )
        one.send()
        late.send()
        pieces[1].send()
        gains = gain_step(gains, bits.pop())
        grads = all_input_grads(text_dq, image_dq)
        *grads, gains = paced((one, late, pieces[1]), (two,), (*grads, gains))
        (one,) = add_split(choice, ((2, (one,)),))
        late.add(gather=True)
        two.send()
        one.send()
        gains = gain_step(gains, bits.pop())
        (gains,) = paced((one, two, late), (three,), (gains,))
        (one,) = add_split(choice, ((3, (one,)),))
        (two,) = add_split(choice, ((2, (two,)),))
        late.add()
        three.send()
        two.send()
        one.send()
        gains = gain_step(gains, bits.pop())
        (gains,) = paced((one, two, three, late), (four,), (gains,))
        (two,) = add_split(choice, ((3, (two,)),))
        (three,) = add_split(choice, ((2, (three,)),))
        four.send()
        three.send()
        two.send()
        gains = gain_step(gains, bits.pop())
        (gains,) = paced((two, three, four), (), (gains,))
        (three,) = add_split(choice, ((3, (three,)),))
        (four,) = add_split(choice, ((2, (four,)),))
        three.send()
        four.send()
        paced((three, four), ())
        (four,) = add_split(choice, ((3, (four,)),))
        four.send()
        unit = image_flat.shape[0] // 8 // 4
        starts, row = [], 0
        for piece in (one, two, three, four):
            starts.append((row,))
            row += piece.keep.shape[1]
        image_share, text_share = finished(
            choice,
            (pieces, (one, two, three, four)),
            (((0, 2 * unit), (unit, 3 * unit)), tuple(starts)),
            (late.keep[0], late.far[0]),
        )
    else:
        image_sides["keyval"] = (
            image_moves.pair("states", image_all),
            image_moves.pair("dkv", image_dkv),
        )
        image_share = share_of(
            reduce_scatter(gather_half(image_sides, image_sizes), ((8, False),))
        )
        text_share = share_of(reduce_scatter(gather_half(text_sides, text_sizes), ((8, False),)))
        grads = all_input_grads(text_dq, image_dq)
        while bits:
            gains = gain_step(gains, bits.pop())
    text_grad, text_result, image_grad, image_result = grads
    text_gain_sum, image_gain_sum = unpack_gains(gains, text_dg.shape[1])
    return (
        text_result,
        image_result,
        text_grad,
        image_grad,
        text_share,
        image_share,
        text_gain_sum,
        image_gain_sum,
    )


def pack_gains(text_dg, image_dg):
    return jnp.concatenate([text_dg, image_dg], axis=1)


def gain_step(gains, bit):
    return gains + dp_swap(gains, bit)


def unpack_gains(gains, width):
    return gains[:, :width], gains[:, width:]


class Late:
    rows = 1280

    def __init__(self, choice, side, states, grads):
        self.choice = choice
        job = Job(states, grads, 0, states[0].shape[1], 768)
        flat = flat_grads(side, 4 * self.rows, [[job]], 2, True)
        self.keep, self.out = split(choice, flat, self.rows, ((0, self.rows, (0, 2), 1, LATE_Y),))
        self.bit = 2

    def send(self):
        self.far = dp_swap(self.out, self.bit)

    def turn(self):
        (piece,) = add_split(self.choice, ((LATE_OWN, (self,)),))
        self.keep, self.out, self.bit = piece.keep, piece.out, 4

    def add(self, gather=False):
        self.keep = plus(self.keep, self.far)
        if gather:
            route = []
            for i in range(16):
                z, y = i >> 2, (i >> 1) & 1
                goal = 1 if z & 1 else (0 if y else 2)
                if z != goal:
                    route.append((i, goal * 4 + (i & 3)))
            self.far = lax.ppermute(self.keep, "dp", route)
        else:
            self.far = lax.ppermute(self.keep, "stream", [(1, 0)])


def solution(mesh):
    split = P(("stream", "dp"), None)
    flat = P(("stream", "dp"))
    whole = P()
    return jax.shard_map(
        local,
        mesh=mesh,
        in_specs=(split, split, flat) + (whole,) * 16 + (split, split),
        out_specs=(split, split, split, split, flat, flat, whole, whole),
        check_vma=False,
    )
```

```python
import functools

import jax
import jax.numpy as jnp
from jax import lax
from jax.experimental import pallas as pl
from jax.experimental.pallas import tpu as pltpu
from jax.sharding import PartitionSpec as P

H_T = 12
H_I = 8
H_C = 8
D_C = 1024
LANES = 128
UNIT = 256
masked_score = -1e30
F32 = jnp.float32
BF16 = jnp.bfloat16


def mm(a, b):
    return jnp.dot(a, b, preferred_element_type=F32)


def mm_nt(a, b):
    return lax.dot_general(a, b, (((1,), (1,)), ((), ())), preferred_element_type=F32)


def mm_tn(a, b):
    return lax.dot_general(a, b, (((0,), (0,)), ((), ())), preferred_element_type=F32)


def cost(us):
    return pl.CostEstimate(flops=int(us * 10e9), bytes_accessed=1000, transcendentals=0)


def lane_block(ref, rows, block):
    return ref[rows, pl.ds(pl.multiple_of(block * LANES, LANES), LANES)]


def put_block(ref, rows, block, value):
    ref[rows, pl.ds(pl.multiple_of(block * LANES, LANES), LANES)] = value


def split_heads(block, heads_in):
    if heads_in == 1:
        return block
    lanes = lax.broadcasted_iota(jnp.int32, block.shape, 1)
    zero = jnp.zeros_like(block)
    low = lanes < LANES // 2
    return jnp.concatenate([jnp.where(low, block, zero), jnp.where(low, zero, block)], axis=0)


def side_by_side(block, heads_in):
    if heads_in == 1:
        return block
    rows = block.shape[0] // 2
    return jnp.concatenate([block[:rows], block[rows:]], axis=1)


def attend_kernel(
    lens_ref, q_ref, k_ref, v_ref, o_ref, *, pairs, blocks, cols, heads_in, fixed, scaling
):
    ql = q_ref.shape[0] // pairs
    kl = k_ref.shape[0] // pairs
    chain = heads_in * ql
    keys = lax.broadcasted_iota(jnp.int32, (chain, kl), 1)
    if fixed is None:
        masks = [keys < lens_ref[p] for p in range(pairs)]
    else:
        masks = [keys < fixed] * pairs

    @pl.loop(0, blocks, unroll=4 if blocks % 4 == 0 else 3)
    def _(j):
        scores = []
        for p in range(pairs):
            q = split_heads(lane_block(q_ref, slice(p * ql, (p + 1) * ql), cols[0] + j), heads_in)
            k = lane_block(k_ref, slice(p * kl, (p + 1) * kl), cols[1] + j)
            scores.append(jnp.where(masks[p], mm_nt(q, k) * scaling, masked_score))
        s = jnp.concatenate(scores, axis=0)
        raised = jnp.exp(s - jnp.max(s, axis=-1, keepdims=True))
        w = (raised * (1.0 / jnp.sum(raised, axis=-1, keepdims=True))).astype(BF16)
        for p in range(pairs):
            v = split_heads(lane_block(v_ref, slice(p * kl, (p + 1) * kl), cols[2] + j), heads_in)
            o = mm(side_by_side(w[p * chain : (p + 1) * chain], heads_in), v)
            put_block(o_ref, slice(p * ql, (p + 1) * ql), j, o.astype(BF16))


def attend(lens, q, k, v, cols, pairs, blocks, heads_in, fixed, scaling):
    rows = q.shape[0]
    krows = k.shape[0]
    same = k is v
    vmem = pl.BlockSpec(memory_space=pltpu.VMEM)
    operands = [lens, q, k] if same else [lens, q, k, v]
    if q is k:
        operands = [lens, q]

    def body(lens_ref, *refs, **kw):
        refs = list(refs)
        o_ref = refs.pop()
        while len(refs) < 3:
            refs.append(refs[-1])
        attend_kernel(lens_ref, *refs, o_ref, **kw)

    return pl.pallas_call(
        functools.partial(
            body,
            pairs=pairs,
            blocks=blocks,
            cols=cols,
            heads_in=heads_in,
            fixed=fixed,
            scaling=scaling,
        ),
        in_specs=[pl.BlockSpec(memory_space=pltpu.SMEM)] + [vmem] * (len(operands) - 1),
        out_specs=vmem,
        out_shape=jax.ShapeDtypeStruct((rows, blocks * LANES), BF16),
        compiler_params=pltpu.CompilerParams(vmem_limit_bytes=10 * 1024 * 1024),
        cost_estimate=cost(5),
        name="attend",
    )(*operands)


def attend_back_kernel(
    lens_ref,
    q_ref,
    k_ref,
    v_ref,
    g_ref,
    dq_ref,
    dk_ref,
    dv_ref,
    *,
    pairs,
    blocks,
    cols,
    out_cols,
    heads_in,
    fixed,
    scaling,
):
    ql = q_ref.shape[0] // pairs
    kl = k_ref.shape[0] // pairs
    keys = lax.broadcasted_iota(jnp.int32, (heads_in * kl, ql), 0)
    if heads_in == 2:
        keys = jnp.where(keys >= kl, keys - kl, keys)
    if fixed is None:
        masks = [keys < lens_ref[p] for p in range(pairs)]
    else:
        masks = [keys < fixed] * pairs

    @pl.loop(0, blocks, unroll=4 if blocks % 4 == 0 else 3)
    def _(j):
        scores, slopes = [], []
        for p in range(pairs):
            qs, ks = slice(p * ql, (p + 1) * ql), slice(p * kl, (p + 1) * kl)
            q, g = lane_block(q_ref, qs, cols[0] + j), lane_block(g_ref, qs, j)
            k = split_heads(lane_block(k_ref, ks, cols[1] + j), heads_in)
            v = split_heads(lane_block(v_ref, ks, cols[2] + j), heads_in)
            scores.append(jnp.where(masks[p], mm_nt(k, q) * scaling, masked_score))
            slopes.append(mm_nt(v, g))
        stacked = (pairs * heads_in, kl, ql)
        s = jnp.concatenate(scores, axis=0).reshape(stacked)
        dp = jnp.concatenate(slopes, axis=0).reshape(stacked)
        raised = jnp.exp(s - jnp.max(s, axis=1, keepdims=True))
        w = raised * (1.0 / jnp.sum(raised, axis=1, keepdims=True))
        inner = jnp.sum(w * dp, axis=1, keepdims=True)
        ds = (w * (dp - inner)).astype(BF16).reshape(-1, ql)
        w = w.astype(BF16).reshape(-1, ql)
        chain = heads_in * kl
        for p in range(pairs):
            qs, ks = slice(p * ql, (p + 1) * ql), slice(p * kl, (p + 1) * kl)
            own = slice(p * chain, (p + 1) * chain)
            q = split_heads(lane_block(q_ref, qs, cols[0] + j), heads_in)
            g = split_heads(lane_block(g_ref, qs, j), heads_in)
            k = split_heads(lane_block(k_ref, ks, cols[1] + j), heads_in)
            dq = mm_tn(ds[own], k) * scaling
            dk = mm(side_by_side(ds[own], heads_in), q) * scaling
            dv = mm(side_by_side(w[own], heads_in), g)
            put_block(dq_ref, qs, out_cols[0] + j, dq.astype(BF16))
            put_block(dk_ref, ks, out_cols[1] + j, dk.astype(BF16))
            put_block(dv_ref, ks, out_cols[2] + j, dv.astype(BF16))


def attend_back(lens, q, k, v, g, cols, pairs, blocks, heads_in, fixed, scaling, packed):
    rows = q.shape[0]
    krows = k.shape[0]
    vmem = pl.BlockSpec(memory_space=pltpu.VMEM)
    width = blocks * LANES
    if packed:
        operands = [lens, q, g]
        out_cols = (0, blocks, 2 * blocks)
        out_shape = jax.ShapeDtypeStruct((rows, 3 * width), BF16)
        out_specs = vmem
    else:
        operands = [lens, q, k, g]
        out_cols = (0, 0, blocks)
        out_shape = [
            jax.ShapeDtypeStruct((rows, width), BF16),
            jax.ShapeDtypeStruct((krows, 2 * width), BF16),
        ]
        out_specs = [vmem, vmem]

    def body(lens_ref, *refs, **kw):
        if packed:
            q_ref, g_ref, out_ref = refs
            ins, outs = (q_ref, q_ref, q_ref, g_ref), (out_ref,) * 3
        else:
            q_ref, k_ref, g_ref, dq_ref, dkv_ref = refs
            ins, outs = (q_ref, k_ref, k_ref, g_ref), (dq_ref, dkv_ref, dkv_ref)
        attend_back_kernel(lens_ref, *ins, *outs, **kw)

    return pl.pallas_call(
        functools.partial(
            body,
            pairs=pairs,
            blocks=blocks,
            cols=cols,
            out_cols=out_cols,
            heads_in=heads_in,
            fixed=fixed,
            scaling=scaling,
        ),
        in_specs=[pl.BlockSpec(memory_space=pltpu.SMEM)] + [vmem] * (len(operands) - 1),
        out_specs=out_specs,
        out_shape=out_shape,
        compiler_params=pltpu.CompilerParams(vmem_limit_bytes=10 * 1024 * 1024),
        cost_estimate=cost(6),
        name="attend_back",
    )(*operands)


class Job:
    def __init__(self, a, b, low, high, place):
        self.a, self.b = a, b
        self.low, self.count = low, high - low
        self.columns = b[3]
        self.place = place


def flat_kernel(side_ref, *refs, plans, found, quarter, resident):
    out_ref, chosen_ref, stage_ref = refs[len(found) : len(found) + 3]
    core = side_ref[0]
    depth = chosen_ref.shape[0] // 2
    if not resident:
        a_buf, b_buf, in_sem = refs[-3:]

    def loads(jobs, k):
        job, slot = jobs[k], k % 2
        copies = []
        for side, buf, start, width in (
            (job.a, a_buf, job.a[2] + job.low, job.count),
            (job.b, b_buf, job.b[2], job.columns),
        ):
            for half in range(2):
                copies.append(
                    pltpu.make_async_copy(
                        refs[found[id(side[half])]].at[:, start : start + width],
                        buf.at[slot, half * depth : (half + 1) * depth, 0:width],
                        in_sem.at[slot, len(copies)],
                    )
                )
        return copies

    def run(jobs):
        if not resident:
            for copy in loads(jobs, 0):
                copy.start()
        for k, job in enumerate(jobs):
            if resident:
                a_refs = [refs[found[id(job.a[half])]] for half in range(2)]
                b_refs = [refs[found[id(job.b[half])]] for half in range(2)]
                a_first, b_first = job.a[2] + job.low, job.b[2]
            else:
                if k + 1 < len(jobs):
                    for copy in loads(jobs, k + 1):
                        copy.start()
                for copy in loads(jobs, k):
                    copy.wait()
                halves = [slice(0, depth), slice(depth, 2 * depth)]
                a_refs = [a_buf.at[k % 2, half] for half in halves]
                b_refs = [b_buf.at[k % 2, half] for half in halves]
                a_first = b_first = 0
            units = job.columns // (2 * UNIT if quarter else UNIT)
            for u in range(units):
                at = 4 * u + 2 * side_ref[1] + core if quarter else 2 * u + core
                block = pl.ds(pl.multiple_of(at * LANES + b_first, LANES), LANES)
                for half in range(2):
                    chosen_ref[half * depth : (half + 1) * depth, u * LANES : (u + 1) * LANES] = (
                        b_refs[half][:, block]
                    )
            bm = best_rows(job.count, units)
            rows = bm * units

            @pl.loop(0, job.count // bm)
            def _(i, job=job, units=units, bm=bm, rows=rows, a_refs=a_refs, a_first=a_first):
                columns = pl.ds(pl.multiple_of(a_first + i * bm, LANES), bm)
                a = jnp.concatenate([a_ref[:, columns] for a_ref in a_refs], axis=0).T
                for u0 in range(0, units, 12):
                    u1 = min(u0 + 12, units)
                    total = mm(a, chosen_ref[:, u0 * LANES : u1 * LANES])
                    for u in range(u0, u1):
                        stage_ref[pl.ds(u, bm, stride=units), :] = total[
                            :, (u - u0) * LANES : (u - u0 + 1) * LANES
                        ]
                first = pl.multiple_of(job.place + i * rows, LANES)
                out_ref[pl.ds(first, rows), :] = stage_ref[:rows].astype(BF16)

    if len(plans) == 1:
        run(plans[0])
    else:
        for side, jobs in enumerate(plans):

            @pl.when(side_ref[1] == side)
            def _(jobs=jobs):
                run(jobs)


def best_rows(count, units):
    most = 512 if units <= 8 else 384
    return max(size for size in range(LANES, most + 1, LANES) if count % size == 0)


def flat_grads(side, total_rows, plans, us, quarter=False, resident=True):
    arrays, found = [], {}
    jobs = [job for plan in plans for job in plan]
    for job in jobs:
        for array in (*job.a[:2], *job.b[:2]):
            if id(array) not in found:
                found[id(array)] = len(arrays)
                arrays.append(array)
    depth = 2 * arrays[0].shape[0]
    widest = max(job.columns for job in jobs)
    tallest = max(job.count for job in jobs)
    factor = 2 * UNIT if quarter else UNIT
    rows = max(best_rows(job.count, job.columns // factor) * job.columns // factor for job in jobs)
    held = 2 * depth * widest * LANES // factor + 4 * rows * LANES
    scratch = [
        pltpu.VMEM((depth, widest * LANES // factor), BF16),
        pltpu.VMEM((rows, LANES), F32),
    ]
    if not resident:
        held += 4 * depth * (tallest + widest)
        scratch += [
            pltpu.VMEM((2, depth, tallest), BF16),
            pltpu.VMEM((2, depth, widest), BF16),
            pltpu.SemaphoreType.DMA((2, 4)),
        ]
    place = pltpu.VMEM if resident else pltpu.HBM
    return pl.pallas_call(
        functools.partial(
            flat_kernel, plans=plans, found=found, quarter=quarter, resident=resident
        ),
        in_specs=[pl.BlockSpec(memory_space=pltpu.SMEM)]
        + [pl.BlockSpec(memory_space=place)] * len(arrays),
        out_specs=pl.BlockSpec(memory_space=pltpu.VMEM),
        out_shape=jax.ShapeDtypeStruct((total_rows, LANES), BF16),
        scratch_shapes=scratch,
        compiler_params=pltpu.CompilerParams(vmem_limit_bytes=held + (8 if resident else 10) * 1024 * 1024),
        cost_estimate=cost(us),
        name="flat_grads",
    )(side, *arrays)


def dp_swap(block, bit):
    count = lax.axis_size("dp")
    return lax.ppermute(block, "dp", [(i, i ^ bit) for i in range(count)])


def stream_swap(block):
    return lax.ppermute(block, "stream", [(0, 1), (1, 0)])


def pick(block, index, axis=0):
    return lax.dynamic_index_in_dim(block, index, axis, keepdims=False)


def plus(a, b):
    return (a.astype(F32) + b.astype(F32)).astype(BF16)


def tied(*values):
    return lax.optimization_barrier(values)


def scatter_parts(flat, cuts):
    count = lax.axis_size("dp")
    top = count.bit_length() - 2
    bits = tuple(range(top, 0, -1))
    rows = flat.shape[0] // (count // 2)
    blocks = flat.reshape((2,) * len(bits) + (rows, LANES))
    natural = tuple(range(1, top + 1))
    turned = natural[1:2] + natural[:1] + natural[2:]
    parts, start = [], 0
    for share, turn in cuts:
        part = lax.slice_in_dim(blocks, start, start + rows * share // 8, axis=len(bits))
        start += rows * share // 8
        parts.append((part, bits, turned if turn else natural))
    return parts


def scatter_step(parts):
    me = lax.axis_index("dp")
    done = []
    for block, left, order in parts:
        bit = order[0]
        axis = left.index(bit)
        mine = (me >> bit) & 1
        keep = pick(block, mine, axis)
        far = dp_swap(pick(block, 1 - mine, axis), 1 << bit)
        block = plus(keep, far) if len(order) > 1 else keep.astype(F32) + far.astype(F32)
        done.append((block, left[:axis] + left[axis + 1 :], order[1:]))
    return done


def scatter_end(parts):
    while parts[0][2]:
        parts = scatter_step(parts)
    blocks = [block for block, _, _ in parts]
    return jnp.concatenate(blocks) if len(blocks) > 1 else blocks[0]


def reduce_scatter(flat, cuts):
    return scatter_end(scatter_parts(flat, cuts))


def share_of(result):
    core = lax.axis_index("dp") & 1
    halves = result.reshape(2, result.shape[0] // 2, LANES)
    mine = pick(halves, core)
    far = dp_swap(pick(halves, 1 - core), 1)
    first = jnp.where(core == 0, mine, far)
    second = jnp.where(core == 0, far, mine)
    return jnp.stack([first, second], axis=1).reshape(-1)


def choices(stream):
    me = lax.axis_index("dp")
    y, odd = (me >> 1) & 1, (me >> 2) & 1
    own = jnp.where(y == 1, odd, 1 - odd)
    values = [me & 1, y, odd, (me >> 3) & 1, 1 - y, own, stream, me >> 1]
    return jnp.stack(values).astype(jnp.int32)


LATE_Y, LATE_OWN, STREAM, CHIP = 4, 5, 6, 7
TEXT_SHARES = (48, 46, 38, 24)


def split_kernel(choice_ref, flat_ref, *refs, chunk, cuts):
    for k, (start, rows, bases, weight, which) in enumerate(cuts):
        mine = choice_ref[which]
        for i, base in enumerate(bases):
            for out_ref, index in ((refs[2 * k], mine), (refs[2 * k + 1], 1 - mine)):
                first = (base + index * weight) * chunk + start
                out_ref[i] = flat_ref[pl.ds(pl.multiple_of(first, 16), rows), :]


def split(choice, flat, chunk, cuts):
    shapes = [
        jax.ShapeDtypeStruct((len(bases), rows, LANES), BF16)
        for _, rows, bases, _, _ in cuts
        for _ in range(2)
    ]
    return pl.pallas_call(
        functools.partial(split_kernel, chunk=chunk, cuts=cuts),
        in_specs=[
            pl.BlockSpec(memory_space=pltpu.SMEM),
            pl.BlockSpec(memory_space=pltpu.VMEM),
        ],
        out_specs=[pl.BlockSpec(memory_space=pltpu.VMEM)] * len(shapes),
        out_shape=shapes,
        compiler_params=pltpu.CompilerParams(vmem_limit_bytes=8 * 1024 * 1024),
        cost_estimate=cost(3),
        name="split",
    )(choice, flat)


def piece_set(choice, flat, firsts, shares):
    chunk = flat.shape[0] // 8
    unit = chunk // sum(shares)
    cuts, start = [], 0
    for first, share in zip(firsts, shares):
        bits = [bit for bit in (3, 2, 1) if bit != first]
        bases = tuple(
            sum(((n >> (1 - at)) & 1) << (b - 1) for at, b in enumerate(bits)) for n in range(4)
        )
        cuts.append((start, unit * share, bases, 1 << (first - 1), first))
        start += unit * share
    arrays = split(choice, flat, chunk, tuple(cuts))
    return [
        Piece(keep, out, first) for keep, out, first in zip(arrays[::2], arrays[1::2], firsts)
    ]


class Piece:
    def __init__(self, keep, out, bit):
        self.keep, self.out, self.bit = keep, out, bit

    def send(self):
        self.far = dp_swap(self.out, 1 << self.bit)


def after(value, pieces, name="far"):
    value, *got = tied(value, *(getattr(piece, name) for piece in pieces))
    for piece, array in zip(pieces, got):
        setattr(piece, name, array)
    return value


def paced(came, leaving, values=()):
    got = tied(*(item.far for item in came), *(item.out for item in leaving), *values)
    for item, array in zip(came, got):
        item.far = array
    for item, array in zip(leaving, got[len(came) :]):
        item.out = array
    return got[len(came) + len(leaving) :]


def added(a_ref, b_ref, index):
    return a_ref[index].astype(F32) + b_ref[index].astype(F32)


def add_split_kernel(choice_ref, *refs, plan, inputs):
    outs = refs[2 * inputs :]
    for k, base, stride, which, out, at in plan:
        keep_ref, far_ref = refs[2 * k : 2 * k + 2]
        mine = choice_ref[which]
        for ref, index in ((outs[2 * out], mine), (outs[2 * out + 1], 1 - mine)):
            ref[at] = added(keep_ref, far_ref, base + index * stride).astype(BF16)


def add_split(choice, groups, which=None):
    operands, plan, shapes = [], [], []
    for out, (bit, pieces) in enumerate(groups):
        at = 0
        for piece in pieces:
            for base in range(0, piece.keep.shape[0], 2):
                plan.append((len(operands) // 2, base, 1, which or bit, out, at))
                at += 1
            operands += [piece.keep, piece.far]
        shape = jax.ShapeDtypeStruct((at,) + pieces[0].keep.shape[1:], BF16)
        shapes += [shape, shape]
    vmem = pl.BlockSpec(memory_space=pltpu.VMEM)
    arrays = pl.pallas_call(
        functools.partial(add_split_kernel, plan=tuple(plan), inputs=len(operands) // 2),
        in_specs=[pl.BlockSpec(memory_space=pltpu.SMEM)] + [vmem] * len(operands),
        out_specs=[vmem] * len(shapes),
        out_shape=shapes,
        compiler_params=pltpu.CompilerParams(vmem_limit_bytes=8 * 1024 * 1024),
        cost_estimate=cost(1),
        name="add_split",
    )(choice, *operands)
    return [
        Piece(arrays[2 * out], arrays[2 * out + 1], bit) for out, (bit, _) in enumerate(groups)
    ]


def finish_kernel(choice_ref, *refs, rows):
    refs = list(refs)
    pairs = [[(refs.pop(0), refs.pop(0)) for _ in group] for group in rows]
    near_ref, far_ref = refs.pop(0), refs.pop(0)
    out_ref, send_ref, *totals, joined_ref = refs
    for total_ref, group, starts in zip(totals, pairs, rows):
        for (keep_ref, came_ref), firsts in zip(group, starts):
            count = keep_ref.shape[1]
            for at, first in enumerate(firsts):
                total_ref[first : first + count] = added(keep_ref, came_ref, at)
    half = near_ref.shape[0]
    joined_ref[pl.ds(0, half, stride=2), :] = near_ref[...].astype(F32)
    joined_ref[pl.ds(1, half, stride=2), :] = far_ref[...].astype(F32)
    image_ref = totals[0]
    total_rows = image_ref.shape[0]
    chip = choice_ref[CHIP]
    first = jnp.where(chip == 1, 1536, 0)
    last = jnp.where(chip == 4, 2048, total_rows)
    here = (chip >= 1) & (chip <= 4) & (choice_ref[STREAM] == 0)
    last = jnp.where(here, last, 0)
    at = lax.broadcasted_iota(jnp.int32, (total_rows, 1), 0)
    image_ref[...] = jnp.where((at >= first) & (at < last), joined_ref[...], image_ref[...])
    core = choice_ref[0]
    row = 0
    for total_ref in totals:
        half = total_ref.shape[0] // 2
        for ref, index in ((out_ref, core), (send_ref, 1 - core)):
            part = total_ref[pl.ds(pl.multiple_of(index * half, 8), half), :]
            ref[row : row + half, :] = part.astype(ref.dtype)
        row += half


def join_kernel(choice_ref, near_ref, far_ref, *outs):
    core = choice_ref[0]
    row = 0
    for out_ref in outs:
        half = out_ref.shape[0] // 2
        out_ref[pl.ds(core, half, stride=2), :] = near_ref[row : row + half, :]
        out_ref[pl.ds(1 - core, half, stride=2), :] = far_ref[row : row + half, :].astype(F32)
        row += half


def finished(choice, groups, rows, late):
    sizes = [
        sum(piece.keep.shape[0] * piece.keep.shape[1] for piece in group) for group in groups
    ]
    vmem = pl.BlockSpec(memory_space=pltpu.VMEM)
    smem = pl.BlockSpec(memory_space=pltpu.SMEM)
    operands = [ref for group in groups for piece in group for ref in (piece.keep, piece.far)]
    operands += list(late)
    half = jax.ShapeDtypeStruct((sum(sizes) // 2, LANES), F32)
    near, send = pl.pallas_call(
        functools.partial(finish_kernel, rows=rows),
        in_specs=[smem] + [vmem] * len(operands),
        out_specs=[vmem] * 2,
        out_shape=[half, jax.ShapeDtypeStruct(half.shape, BF16)],
        scratch_shapes=[pltpu.VMEM((rows, LANES), F32) for rows in (*sizes, sizes[0])],
        compiler_params=pltpu.CompilerParams(vmem_limit_bytes=12 * 1024 * 1024),
        cost_estimate=cost(3),
        name="finish",
    )(choice, *operands)
    joined = pl.pallas_call(
        join_kernel,
        in_specs=[smem, vmem, vmem],
        out_specs=[vmem] * 2,
        out_shape=[jax.ShapeDtypeStruct((rows, LANES), F32) for rows in sizes],
        compiler_params=pltpu.CompilerParams(vmem_limit_bytes=12 * 1024 * 1024),
        cost_estimate=cost(2),
        name="join",
    )(choice, near, dp_swap(send, 1))
    return [block.reshape(-1) for block in joined]


CHUNK = 64
ROWS = 128
WIDEST = 1024
WIDEST_GELU = 1024


def tiles(columns, body, widest=None):
    size = max(c for c in range(LANES, (widest or WIDEST) + 1, LANES) if columns % c == 0)
    if size == columns:
        return body(slice(0, columns))

    @pl.loop(0, columns // size)
    def _(j):
        body(pl.ds(pl.multiple_of(j * size, size), size))


def views(pack_ref, *widths):
    found, start = [], 0
    for width in widths:
        found.append(pack_ref.at[:, start : start + width])
        start += width
    return found


def row_chunks(rows, body):
    size = ROWS if rows % ROWS == 0 else CHUNK

    @pl.loop(0, rows // size)
    def _(i):
        body(i * size, pl.ds(pl.multiple_of(i * size, size), size), size)


def normed_chunk(a):
    centred = a - jnp.mean(a, axis=-1, keepdims=True)
    inverse = lax.rsqrt(jnp.mean(centred * centred, axis=-1, keepdims=True) + 1e-05)
    return centred * inverse, inverse


def normed_back_chunk(grad, n, inverse, gain_row):
    scaled = grad * gain_row
    low = jnp.mean(scaled, axis=-1, keepdims=True)
    tilt = jnp.mean(scaled * n, axis=-1, keepdims=True)
    return (scaled - low - n * tilt) * inverse, jnp.sum(grad * n, axis=0, keepdims=True)


def co_kernel(
    lens_ref, x_ref, given_ref, source_ref, g_ref, wmade_ref, wat_ref,
    made_ref, pack_ref, n_ref, inv_ref, a_ref, *, pairs, fixed, scaling, makes_kv,
):
    rows, width = x_ref.shape
    c_ref, h_ref = views(pack_ref, D_C, width)

    def made_tile(cols):
        made_ref[:, cols] = mm(source_ref[...], wmade_ref[:, cols]).astype(BF16)

    def a_tile(cols):
        a_ref[:, cols] = x_ref[:, cols].astype(F32) + mm(c_ref[...], wat_ref[:, cols])

    def norm(i, at, size):
        n, inverse = normed_chunk(a_ref[at, :])
        n_ref[at, :] = n
        inv_ref[at, :] = jnp.broadcast_to(inverse, (size, LANES))
        h_ref[at, :] = (n * g_ref[0:1, :]).astype(BF16)

    tiles(made_ref.shape[1], made_tile)
    q_ref, kv_ref = (given_ref, made_ref) if makes_kv else (made_ref, given_ref)
    blocks = q_ref.shape[1] // LANES
    attend_kernel(
        lens_ref, q_ref, kv_ref, kv_ref, c_ref, pairs=pairs, blocks=blocks,
        cols=(0, 0, blocks), heads_in=1, fixed=fixed, scaling=scaling,
    )
    tiles(width, a_tile)
    row_chunks(rows, norm)


def mlp_kernel(
    pack1_ref, n1_ref, g_ref, wup_ref, wdown_ref, wqkv_ref,
    pack_ref, slope_ref, n_ref, inv_ref, r_ref, a_ref,
):
    rows, width = n1_ref.shape
    _, h1_ref = views(pack1_ref, D_C, width)
    hid_ref, h_ref = views(pack_ref, wup_ref.shape[1], width)

    def up_tile(cols):
        u_all = mm(h1_ref[...], wup_ref[:, cols])
        for at in range(0, rows, CHUNK):
            u = u_all[at : at + CHUNK]
            share = 0.5 + 0.5 * lax.erf(u * 0.7071067811865476)
            hid_ref[at : at + CHUNK, cols] = (u * share).astype(BF16)
            slope = share + u * (0.3989422804014327 * jnp.exp(-0.5 * u * u))
            slope_ref[at : at + CHUNK, cols] = slope.astype(BF16)

    def down_tile(cols):
        a_ref[:, cols] = n1_ref[:, cols] * g_ref[0:1, cols] + mm(hid_ref[...], wdown_ref[:, cols])

    def norm(i, at, size):
        n, inverse = normed_chunk(a_ref[at, :])
        n_ref[at, :] = n
        inv_ref[at, :] = jnp.broadcast_to(inverse, (size, LANES))
        h_ref[at, :] = (n * g_ref[1:2, :]).astype(BF16)

    def qkv_tile(cols):
        r_ref[:, cols] = mm(h_ref[...], wqkv_ref[:, cols]).astype(BF16)

    tiles(wup_ref.shape[1], up_tile, WIDEST_GELU)
    tiles(width, down_tile)
    row_chunks(rows, norm)
    tiles(r_ref.shape[1], qkv_tile)


def self_kernel(
    lens_ref, r_ref, n2_ref, g_ref, wout_ref, cot_ref, far_cot_ref,
    pack_ref, y_ref, de_ref, dg_ref, a_ref, dz_ref,
    *, pairs, heads_in, fixed, scaling,
):
    rows, width = n2_ref.shape
    z_ref, de_low_ref, dr_ref = views(pack_ref, width, width, 3 * width)
    near = cot_ref.shape[0]
    dz_ref[:near, :] = cot_ref[...]
    if near < rows:
        dz_ref[near:, :] = far_cot_ref[...]
    blocks = width // LANES
    cols = (0, blocks, 2 * blocks)
    shared = dict(
        pairs=pairs, blocks=blocks, cols=cols, heads_in=heads_in, fixed=fixed, scaling=scaling
    )

    def out_tile(at):
        a_ref[:, at] = n2_ref[:, at] * g_ref[1:2, at] + mm(z_ref[...], wout_ref[:, at])

    def last(start, at, size):
        n, inverse = normed_chunk(a_ref[at, :])
        y = n * g_ref[2:3, :]
        grad = dz_ref[at, :].astype(F32)
        if fixed is None:
            slots = rows // pairs
            place = lax.broadcasted_iota(jnp.int32, (size, 1), 0) + lax.rem(start, slots)
            valid = (place < lens_ref[lax.div(start, slots)]).astype(F32)
            y, grad = y * valid, grad * valid
        y_ref[at, :] = y.astype(BF16)
        de, dg = normed_back_chunk(grad, n, inverse, g_ref[2:3, :])
        de_ref[at, :] = de
        de_low_ref[at, :] = de.astype(BF16)
        dg_ref[...] += dg

    def dz_tile(at):
        dz_ref[:, at] = mm_nt(de_low_ref[...], wout_ref[at, :]).astype(BF16)

    attend_kernel(lens_ref, r_ref, r_ref, r_ref, z_ref, **shared)
    tiles(width, out_tile)
    dg_ref[...] = jnp.zeros_like(dg_ref)
    row_chunks(rows, last)
    tiles(width, dz_tile)
    attend_back_kernel(
        lens_ref, r_ref, r_ref, r_ref, dz_ref, dr_ref, dr_ref, dr_ref, out_cols=cols, **shared
    )


def mlp_back_kernel(
    pack3_ref, de_ref, n2_ref, inv2_ref, g_ref, slope_ref, wqkv_ref, wdown_ref,
    pack_ref, db_ref, dg_ref, a_ref,
):
    rows, width = n2_ref.shape
    _, _, dr_ref = views(pack3_ref, width, width, 3 * width)
    db_low_ref, du_ref = views(pack_ref, width, slope_ref.shape[1])
    dg_ref[...] = jnp.zeros_like(dg_ref)

    def second_tile(at):
        a_ref[:, at] = de_ref[:, at] + mm_nt(dr_ref[...], wqkv_ref[at, :])

    def second_norm(i, at, size):
        db, dg = normed_back_chunk(a_ref[at, :], n2_ref[at, :], inv2_ref[at, 0:1], g_ref[1:2, :])
        db_ref[at, :] = db
        db_low_ref[at, :] = db.astype(BF16)
        dg_ref[...] += dg

    def du_tile(at):
        grad = mm_nt(db_low_ref[...], wdown_ref[at, :])
        du_ref[:, at] = (grad * slope_ref[:, at].astype(F32)).astype(BF16)

    tiles(width, second_tile)
    row_chunks(rows, second_norm)
    tiles(du_ref.shape[1], du_tile)


def context_back_kernel(
    pack4_ref, db_ref, n1_ref, inv1_ref, g_ref, wup_ref, wat_ref,
    da_low_ref, da_ref, dc_ref, dg_ref, a_ref,
):
    rows, width = n1_ref.shape
    _, du_ref = views(pack4_ref, width, wup_ref.shape[1])
    dg_ref[...] = jnp.zeros_like(dg_ref)

    def first_tile(at):
        a_ref[:, at] = db_ref[:, at] + mm_nt(du_ref[...], wup_ref[at, :])

    def first_norm(i, at, size):
        da, dg = normed_back_chunk(a_ref[at, :], n1_ref[at, :], inv1_ref[at, 0:1], g_ref[0:1, :])
        da_ref[at, :] = da
        da_low_ref[at, :] = da.astype(BF16)
        dg_ref[...] += dg

    def dc_tile(at):
        dc_ref[:, at] = mm_nt(da_low_ref[...], wat_ref[at, :]).astype(BF16)

    tiles(width, first_tile)
    row_chunks(rows, first_norm)
    tiles(dc_ref.shape[1], dc_tile)


def fused(kernel, operands, outs, scratch, name, us, smem_first=False, limit=11):
    vmem = pl.BlockSpec(memory_space=pltpu.VMEM)
    in_specs = [vmem] * len(operands)
    if smem_first:
        in_specs[0] = pl.BlockSpec(memory_space=pltpu.SMEM)
    return pl.pallas_call(
        kernel,
        in_specs=in_specs,
        out_specs=[vmem] * len(outs),
        out_shape=[jax.ShapeDtypeStruct(shape, kind) for shape, kind in outs],
        scratch_shapes=[pltpu.VMEM(shape, kind) for shape, kind in scratch],
        compiler_params=pltpu.CompilerParams(vmem_limit_bytes=limit * 1024 * 1024),
        cost_estimate=cost(us),
        name=name,
    )(*operands)


def co_forward(lens, states, given, source, gains, made_w, attend_w, pairs, fixed):
    rows, width = states.shape
    made, pack1, n1, inv1 = fused(
        functools.partial(
            co_kernel,
            pairs=pairs,
            fixed=fixed,
            scaling=(D_C // H_C) ** (-0.5),
            makes_kv=made_w.shape[1] == 2 * D_C,
        ),
        (lens, states, given, source, gains, made_w, attend_w),
        [
            ((source.shape[0], made_w.shape[1]), BF16),
            ((rows, D_C + width), BF16),
            ((rows, width), F32),
            ((rows, LANES), F32),
        ],
        [((rows, width), F32)],
        "co_forward",
        7,
        True,
    )
    return made, pack1, n1, inv1


def mlp_forward(pack1, n1, gains, up_w, down_w, qkv_w):
    rows, width = n1.shape
    hidden = up_w.shape[1]
    return fused(
        mlp_kernel,
        (pack1, n1, gains, up_w, down_w, qkv_w),
        [
            ((rows, hidden + width), BF16),
            ((rows, hidden), BF16),
            ((rows, width), F32),
            ((rows, LANES), F32),
            ((rows, 3 * width), BF16),
        ],
        [((rows, width), F32)],
        "mlp_forward",
        rows / 40,
    )


def self_turn(lens, r, n2, gains, output_w, cots, pairs, heads, fixed):
    rows, width = n2.shape
    size = width // heads
    return fused(
        functools.partial(
            self_kernel, pairs=pairs, heads_in=LANES // size, fixed=fixed, scaling=size ** (-0.5)
        ),
        (lens, r, n2, gains, output_w, *cots),
        [
            ((rows, 5 * width), BF16),
            ((rows, width), BF16),
            ((rows, width), F32),
            ((1, width), F32),
        ],
        [((rows, width), F32), ((rows, width), BF16)],
        "self_turn",
        rows / 128 + 9,
        True,
    )


def input_kernel(da_ref, dq_ref, dkv_ref, y_ref, trim_ref, wq_ref, wkv_ref, *outs, first):
    grad_ref, result_ref = outs
    rows = pl.ds(first, da_ref.shape[0] // 2)
    grad = da_ref[rows, :] + mm_nt(dq_ref[rows, :], wq_ref[...])
    grad = (grad + mm_nt(dkv_ref[rows, :], wkv_ref[...])).astype(BF16)
    y = y_ref[rows, :]
    if trim_ref.shape[0] < 8:
        grad_ref[...], result_ref[...] = grad, y
    else:
        grad_ref[...] = mm(trim_ref[...], grad).astype(BF16)
        result_ref[...] = mm(trim_ref[...], y).astype(BF16)


def input_grads(da, dq, dkv, y, trim, query_w, keyval_w, first, own):
    vmem = pl.BlockSpec(memory_space=pltpu.VMEM)
    return pl.pallas_call(
        functools.partial(input_kernel, first=first),
        in_specs=[vmem] * 7,
        out_specs=[vmem] * 2,
        out_shape=[jax.ShapeDtypeStruct((own, da.shape[1]), BF16)] * 2,
        compiler_params=pltpu.CompilerParams(vmem_limit_bytes=10 * 1024 * 1024),
        cost_estimate=cost(0.2),
        name="input_grads",
    )(da, dq, dkv, y, trim, query_w, keyval_w)


def mlp_back(pack3, de, n2, inv2, gains, slope, qkv_w, down_w):
    rows, width = n2.shape
    return fused(
        mlp_back_kernel,
        (pack3, de, n2, inv2, gains, slope, qkv_w, down_w),
        [
            ((rows, width + slope.shape[1]), BF16),
            ((rows, width), F32),
            ((1, width), F32),
        ],
        [((rows, width), F32)],
        "mlp_back",
        rows / 70,
    )


def context_back(pack4, db, n1, inv1, gains, up_w, attend_w):
    rows, width = n1.shape
    return fused(
        context_back_kernel,
        (pack4, db, n1, inv1, gains, up_w, attend_w),
        [
            ((rows, width), BF16),
            ((rows, width), F32),
            ((rows, D_C), BF16),
            ((1, width), F32),
        ],
        [((rows, width), F32)],
        "context_back",
        rows / 80,
    )


class Exchange:
    def __init__(self):
        self.far = {}
        self.pending = []
        self.parts = None

    def send(self, **arrays):
        for name, array in arrays.items():
            self.far[name] = dp_swap(array, 1)
            self.pending.append(name)

    def settle(self, value):
        names, self.pending = self.pending, []
        if names:
            value, *got = tied(value, *(self.far[name] for name in names))
            self.far.update(zip(names, got))
        return value

    def pair(self, name, array, start=0, width=None):
        return array, self.far[name], start, width or array.shape[1]


def stream_forward(
    lens, states, given, source, cot, weights, gains, heads, fixed, other_fixed, pairs, moves, hook
):
    made_w, attend_w, up_w, down_w, qkv_w, output_w = weights
    made, pack1, n1, inv1 = co_forward(
        lens, states, given, source, gains, made_w, attend_w, pairs, other_fixed
    )
    pack1 = moves.settle(hook("co", pack1))
    moves.send(pack1=pack1)
    pack2, slope, n2, inv2, r = mlp_forward(pack1, n1, gains, up_w, down_w, qkv_w)
    r, pack2 = tied(moves.settle(hook("mlp", r)), pack2)
    moves.send(pack2=pack2)
    near_cot, far_cot = cot
    cots = (near_cot, far_cot[0] if far_cot else near_cot)
    pack3, result, de, dg2 = self_turn(lens, r, n2, gains, output_w, cots, pairs, heads, fixed)
    pack3 = moves.settle(hook("self", pack3))
    moves.send(pack3=pack3)
    pack4, db, dg1 = mlp_back(pack3, de, n2, inv2, gains, slope, qkv_w, down_w)
    pack4 = moves.settle(hook("mid", pack4))
    moves.send(pack4=pack4)
    da_low, da, dc, dg0 = context_back(pack4, db, n1, inv1, gains, up_w, attend_w)
    dc = moves.settle(hook("back", dc))
    width, hidden = up_w.shape

    def sides(dq, da_low):
        def side(number, start, count):
            pack = (pack1, pack2, pack3, pack4)[number - 1]
            return moves.pair("pack%d" % number, pack, start, count)

        return {
            "query": (moves.pair("states", states), moves.pair("dq", dq)),
            "attend": (side(1, 0, D_C), moves.pair("da", da_low)),
            "up": (side(1, D_C, width), side(4, width, hidden)),
            "down": (side(2, 0, hidden), side(4, 0, width)),
            "qkv": (side(2, hidden, width), side(3, 2 * width, 3 * width)),
            "output": (side(3, 0, width), side(3, width, width)),
        }

    return result, (da, da_low), dc, made, sides, jnp.concatenate([dg0, dg1, dg2])


NAMES = ("query", "keyval", "attend", "up", "down", "qkv", "output")


def half_jobs(both, sizes, total):
    plans, filled = ([], []), 0
    for name in NAMES:
        m, n = sizes[name]
        room = min(max((total // 2 - filled) // n, 0), m)
        for plan, low, high in ((plans[0], 0, room), (plans[1], room, m)):
            if low < high and name in both:
                start = filled + low * n - (0 if plan is plans[0] else total // 2)
                step = min(high - low, 1024)
                for at in range(low, high, step):
                    place = (start + (at - low) * n) // UNIT
                    plan.append(Job(*both[name], at, at + step, place))
        filled += m * n
    return plans


def spread(count, regions, padded, offset, rows):
    target = lax.broadcasted_iota(jnp.int32, (rows, count * regions), 0) - offset
    source = lax.broadcasted_iota(jnp.int32, (rows, count * regions), 1)
    return (target == source // regions * padded + source % regions).astype(BF16)


def local(
    text_states,
    image_states,
    caption_lengths,
    text_query,
    text_keyval,
    text_attend,
    text_up,
    text_down,
    text_qkv,
    text_output,
    text_gains,
    image_query,
    image_keyval,
    image_attend,
    image_up,
    image_down,
    image_qkv,
    image_output,
    image_gains,
    text_cotangent,
    image_cotangent,
):
    own_pairs = caption_lengths.shape[0]
    own_text = text_states.shape[0]
    text_len = own_text // own_pairs
    regions = image_states.shape[0] // own_pairs
    padded = -(-regions // 16) * 16
    own_image = own_pairs * padded
    pairs = 2 * own_pairs
    d_t, d_i = text_states.shape[1], image_states.shape[1]
    stream = lax.axis_index("stream")
    core = lax.axis_index("dp") & 1
    side = jnp.stack([core, stream]).astype(jnp.int32)

    far_put = spread(own_pairs, regions, padded, 0, 2 * own_image)
    near_put = spread(own_pairs, regions, padded, own_image, 2 * own_image)
    trim = near_put[own_image:].T

    def both_images(near):
        return (mm(far_put, stream_swap(near)) + mm(near_put, near)).astype(BF16)

    choice = choices(stream)
    image_all = both_images(image_states)
    image_q = mm(image_all, image_query).astype(BF16)
    image_kv = mm(image_all, image_keyval).astype(BF16)
    far_text, far_lens, image_q, image_kv = tied(
        stream_swap(text_states), stream_swap(caption_lengths), image_q, image_kv
    )
    text_all = jnp.concatenate([text_states, far_text])
    lens = jnp.concatenate([caption_lengths, far_lens])
    image_cotangent, text_cotangent, text_all = tied(image_cotangent, text_cotangent, text_all)
    image_cot = both_images(image_cotangent)
    far_text_cot = stream_swap(text_cotangent)

    co_blocks = D_C // LANES
    co_cols = (0, 0, co_blocks)
    co_scale = (D_C // H_C) ** (-0.5)

    image_moves, text_moves = Exchange(), Exchange()
    image_moves.send(states=image_all)
    cots = [far_text_cot]

    def image_hook(name, value):
        if name == "self":
            value, cots[0] = tied(value, cots[0])
        return value

    image_out, (image_da, image_da_low), image_dc, text_kv, image_sides, image_dg = stream_forward(
        lens,
        image_all,
        image_q,
        text_all,
        (image_cot, None),
        (text_keyval, image_attend, image_up, image_down, image_qkv, image_output),
        image_gains,
        H_I,
        regions,
        None,
        pairs,
        image_moves,
        image_hook,
    )
    image_dq, text_dkv = attend_back(
        lens, image_q, text_kv, text_kv, image_dc, co_cols, pairs, co_blocks, 1, None, co_scale, False,
    )
    image_moves.send(dq=image_dq, da=image_da_low)
    image_sides = image_sides(image_dq, image_da_low)
    text_moves.send(states=text_all, dkv=text_dkv)

    def sizes_of(*weights):
        return {name: weight.shape for name, weight in zip(NAMES, weights)}

    def gather_half(both, sizes):
        total = sum(m * n for m, n in sizes.values())
        total_rows = total // (2 * UNIT)
        plans = half_jobs(both, sizes, total)
        image = both["query"][0][0] is image_all
        return flat_grads(side, total_rows, plans, 6 if image else 14, resident=image)

    image_sizes = sizes_of(
        image_query, image_keyval, image_attend, image_up, image_down, image_qkv, image_output
    )
    text_sizes = sizes_of(
        text_query, text_keyval, text_attend, text_up, text_down, text_qkv, text_output
    )
    early = lax.axis_size("dp") == 16
    if early:
        image_flat = gather_half(image_sides, image_sizes)

    pieces = []

    def hook(name, value):
        if not early:
            return value
        if name == "co":
            value, flat = tied(value, image_flat)
            pieces.extend(piece_set(choice, flat, (1, 2, 1, 2), (1, 1, 1, 1)))
            value = after(value, pieces, "out")
            for piece in pieces[:2]:
                piece.send()
        if name == "mlp":
            (value,) = paced(pieces[:2], pieces[2:], (value,))
            for piece in pieces[2:]:
                piece.send()
        if name == "self":
            (value,) = paced(pieces[2:], (), (value,))
            pieces[:] = add_split(choice, ((2, pieces[0::2]), (1, pieces[1::2])))
            for piece in pieces:
                piece.send()
        return value

    text_out, (text_da, text_da_low), text_dc, text_q, text_sides, text_dg = stream_forward(
        lens,
        text_all,
        image_kv,
        text_all,
        (text_cotangent, cots),
        (text_query, text_attend, text_up, text_down, text_qkv, text_output),
        text_gains,
        H_T,
        None,
        regions,
        pairs,
        text_moves,
        hook,
    )
    gains = pack_gains(text_dg, image_dg)
    bits = [1 << b for b in range(lax.axis_size("dp").bit_length() - 1)]
    text_dq, image_dkv = attend_back(
        lens, text_q, image_kv, image_kv, text_dc, co_cols, pairs, co_blocks, 1, regions, co_scale, False
    )

    if early:
        image_dkv, text_dq, text_da_low = paced(pieces, (), (image_dkv, text_dq, text_da_low))
        pieces[:] = add_split(choice, ((3, pieces[:1]), (3, pieces[1:])))
        pieces[0].send()
    image_moves.send(dkv=image_dkv)
    text_moves.send(dq=text_dq, da=text_da_low)
    text_sides = text_sides(text_dq, text_da_low)
    text_sides["keyval"] = (text_moves.pair("states", text_all), text_moves.pair("dkv", text_dkv))

    def all_input_grads(text_dq, image_dq):
        text = input_grads(
            text_da, text_dq, text_dkv, text_out, trim[:1], text_query, text_keyval, 0, own_text
        )
        image = input_grads(
            image_da,
            image_dq,
            image_dkv,
            image_out,
            trim,
            image_query,
            image_keyval,
            own_image,
            own_pairs * regions,
        )
        return (*text, *image)

    if early:
        late = Late(
            choice,
            side,
            image_moves.pair("states", image_all),
            image_moves.pair("dkv", image_dkv),
        )
        near_dq, *rest = text_sides["query"][1]
        near_dq, late.out = tied(near_dq, late.out)
        text_sides["query"] = (text_sides["query"][0], (near_dq, *rest))
        late.send()
        text_flat = gather_half(text_sides, text_sizes)
        text_flat = after(text_flat, [late, pieces[0]])
        text_pieces = piece_set(choice, text_flat, (1, 1, 1, 1), TEXT_SHARES)
        one, two, three, four = text_pieces
        late.turn()
        one.out, late.out, pieces[1].out, text_dq, image_dq, gains = tied(
            one.out, late.out, pieces[1].out, text_dq, image_dq, gains
        )
        one.send()
        late.send()
        pieces[1].send()
        gains = gain_step(gains, bits.pop())
        grads = all_input_grads(text_dq, image_dq)
        *grads, gains = paced((one, late, pieces[1]), (two,), (*grads, gains))
        (one,) = add_split(choice, ((2, (one,)),))
        late.add(gather=True)
        two.send()
        one.send()
        gains = gain_step(gains, bits.pop())
        (gains,) = paced((one, two, late), (three,), (gains,))
        (one,) = add_split(choice, ((3, (one,)),))
        (two,) = add_split(choice, ((2, (two,)),))
        late.add()
        three.send()
        two.send()
        one.send()
        gains = gain_step(gains, bits.pop())
        (gains,) = paced((one, two, three, late), (four,), (gains,))
        (two,) = add_split(choice, ((3, (two,)),))
        (three,) = add_split(choice, ((2, (three,)),))
        four.send()
        three.send()
        two.send()
        gains = gain_step(gains, bits.pop())
        (gains,) = paced((two, three, four), (), (gains,))
        (three,) = add_split(choice, ((3, (three,)),))
        (four,) = add_split(choice, ((2, (four,)),))
        three.send()
        four.send()
        paced((three, four), ())
        (four,) = add_split(choice, ((3, (four,)),))
        four.send()
        unit = image_flat.shape[0] // 8 // 4
        starts, row = [], 0
        for piece in (one, two, three, four):
            starts.append((row,))
            row += piece.keep.shape[1]
        image_share, text_share = finished(
            choice,
            (pieces, (one, two, three, four)),
            (((0, 2 * unit), (unit, 3 * unit)), tuple(starts)),
            (late.keep[0], late.far[0]),
        )
    else:
        image_sides["keyval"] = (
            image_moves.pair("states", image_all),
            image_moves.pair("dkv", image_dkv),
        )
        image_share = share_of(
            reduce_scatter(gather_half(image_sides, image_sizes), ((8, False),))
        )
        text_share = share_of(reduce_scatter(gather_half(text_sides, text_sizes), ((8, False),)))
        grads = all_input_grads(text_dq, image_dq)
        while bits:
            gains = gain_step(gains, bits.pop())
    text_grad, text_result, image_grad, image_result = grads
    text_gain_sum, image_gain_sum = unpack_gains(gains, text_dg.shape[1])
    return (
        text_result,
        image_result,
        text_grad,
        image_grad,
        text_share,
        image_share,
        text_gain_sum,
        image_gain_sum,
    )


def pack_gains(text_dg, image_dg):
    return jnp.concatenate([text_dg, image_dg], axis=1)


def gain_step(gains, bit):
    return gains + dp_swap(gains, bit)


def unpack_gains(gains, width):
    return gains[:, :width], gains[:, width:]


class Late:
    rows = 1280

    def __init__(self, choice, side, states, grads):
        self.choice = choice
        job = Job(states, grads, 0, states[0].shape[1], 768)
        flat = flat_grads(side, 4 * self.rows, [[job]], 2, True)
        self.keep, self.out = split(choice, flat, self.rows, ((0, self.rows, (0, 2), 1, LATE_Y),))
        self.bit = 2

    def send(self):
        self.far = dp_swap(self.out, self.bit)

    def turn(self):
        (piece,) = add_split(self.choice, ((LATE_OWN, (self,)),))
        self.keep, self.out, self.bit = piece.keep, piece.out, 4

    def add(self, gather=False):
        self.keep = plus(self.keep, self.far)
        if gather:
            route = []
            for i in range(16):
                z, y = i >> 2, (i >> 1) & 1
                goal = 1 if z & 1 else (0 if y else 2)
                if z != goal:
                    route.append((i, goal * 4 + (i & 3)))
            self.far = lax.ppermute(self.keep, "dp", route)
        else:
            self.far = lax.ppermute(self.keep, "stream", [(1, 0)])


def solution(mesh):
    split = P(("stream", "dp"), None)
    flat = P(("stream", "dp"))
    whole = P()
    return jax.shard_map(
        local,
        mesh=mesh,
        in_specs=(split, split, flat) + (whole,) * 16 + (split, split),
        out_specs=(split, split, split, split, flat, flat, whole, whole),
        check_vma=False,
    )
```

```python
import functools

import jax
import jax.numpy as jnp
from jax import lax
from jax.experimental import pallas as pl
from jax.experimental.pallas import tpu as pltpu
from jax.sharding import PartitionSpec as P

H_T = 12
H_I = 8
H_C = 8
D_C = 1024
LANES = 128
UNIT = 256
masked_score = -1e30
F32 = jnp.float32
BF16 = jnp.bfloat16


def mm(a, b):
    return jnp.dot(a, b, preferred_element_type=F32)


def mm_nt(a, b):
    return lax.dot_general(a, b, (((1,), (1,)), ((), ())), preferred_element_type=F32)


def mm_tn(a, b):
    return lax.dot_general(a, b, (((0,), (0,)), ((), ())), preferred_element_type=F32)


def cost(us):
    return pl.CostEstimate(flops=int(us * 10e9), bytes_accessed=1000, transcendentals=0)


def lane_block(ref, rows, block):
    return ref[rows, pl.ds(pl.multiple_of(block * LANES, LANES), LANES)]


def put_block(ref, rows, block, value):
    ref[rows, pl.ds(pl.multiple_of(block * LANES, LANES), LANES)] = value


def split_heads(block, heads_in):
    if heads_in == 1:
        return block
    lanes = lax.broadcasted_iota(jnp.int32, block.shape, 1)
    zero = jnp.zeros_like(block)
    low = lanes < LANES // 2
    return jnp.concatenate([jnp.where(low, block, zero), jnp.where(low, zero, block)], axis=0)


def side_by_side(block, heads_in):
    if heads_in == 1:
        return block
    rows = block.shape[0] // 2
    return jnp.concatenate([block[:rows], block[rows:]], axis=1)


def attend_kernel(
    lens_ref, q_ref, k_ref, v_ref, o_ref, *, pairs, blocks, cols, heads_in, fixed, scaling
):
    ql = q_ref.shape[0] // pairs
    kl = k_ref.shape[0] // pairs
    chain = heads_in * ql
    keys = lax.broadcasted_iota(jnp.int32, (chain, kl), 1)
    if fixed is None:
        masks = [keys < lens_ref[p] for p in range(pairs)]
    else:
        masks = [keys < fixed] * pairs

    @pl.loop(0, blocks, unroll=blocks)
    def _(j):
        scores = []
        for p in range(pairs):
            q = split_heads(lane_block(q_ref, slice(p * ql, (p + 1) * ql), cols[0] + j), heads_in)
            k = lane_block(k_ref, slice(p * kl, (p + 1) * kl), cols[1] + j)
            scores.append(jnp.where(masks[p], mm_nt(q, k) * scaling, masked_score))
        s = jnp.concatenate(scores, axis=0)
        raised = jnp.exp(s - jnp.max(s, axis=-1, keepdims=True))
        w = (raised * (1.0 / jnp.sum(raised, axis=-1, keepdims=True))).astype(BF16)
        for p in range(pairs):
            v = split_heads(lane_block(v_ref, slice(p * kl, (p + 1) * kl), cols[2] + j), heads_in)
            o = mm(side_by_side(w[p * chain : (p + 1) * chain], heads_in), v)
            put_block(o_ref, slice(p * ql, (p + 1) * ql), j, o.astype(BF16))


def attend(lens, q, k, v, cols, pairs, blocks, heads_in, fixed, scaling):
    rows = q.shape[0]
    krows = k.shape[0]
    same = k is v
    vmem = pl.BlockSpec(memory_space=pltpu.VMEM)
    operands = [lens, q, k] if same else [lens, q, k, v]
    if q is k:
        operands = [lens, q]

    def body(lens_ref, *refs, **kw):
        refs = list(refs)
        o_ref = refs.pop()
        while len(refs) < 3:
            refs.append(refs[-1])
        attend_kernel(lens_ref, *refs, o_ref, **kw)

    return pl.pallas_call(
        functools.partial(
            body,
            pairs=pairs,
            blocks=blocks,
            cols=cols,
            heads_in=heads_in,
            fixed=fixed,
            scaling=scaling,
        ),
        in_specs=[pl.BlockSpec(memory_space=pltpu.SMEM)] + [vmem] * (len(operands) - 1),
        out_specs=vmem,
        out_shape=jax.ShapeDtypeStruct((rows, blocks * LANES), BF16),
        compiler_params=pltpu.CompilerParams(vmem_limit_bytes=10 * 1024 * 1024),
        cost_estimate=cost(5),
        name="attend",
    )(*operands)


def attend_back_kernel(
    lens_ref,
    q_ref,
    k_ref,
    v_ref,
    g_ref,
    dq_ref,
    dk_ref,
    dv_ref,
    *,
    pairs,
    blocks,
    cols,
    out_cols,
    heads_in,
    fixed,
    scaling,
):
    ql = q_ref.shape[0] // pairs
    kl = k_ref.shape[0] // pairs
    keys = lax.broadcasted_iota(jnp.int32, (heads_in * kl, ql), 0)
    if heads_in == 2:
        keys = jnp.where(keys >= kl, keys - kl, keys)
    if fixed is None:
        masks = [keys < lens_ref[p] for p in range(pairs)]
    else:
        masks = [keys < fixed] * pairs

    @pl.loop(0, blocks, unroll=blocks)
    def _(j):
        scores, slopes = [], []
        for p in range(pairs):
            qs, ks = slice(p * ql, (p + 1) * ql), slice(p * kl, (p + 1) * kl)
            q, g = lane_block(q_ref, qs, cols[0] + j), lane_block(g_ref, qs, j)
            k = split_heads(lane_block(k_ref, ks, cols[1] + j), heads_in)
            v = split_heads(lane_block(v_ref, ks, cols[2] + j), heads_in)
            scores.append(jnp.where(masks[p], mm_nt(k, q) * scaling, masked_score))
            slopes.append(mm_nt(v, g))
        stacked = (pairs * heads_in, kl, ql)
        s = jnp.concatenate(scores, axis=0).reshape(stacked)
        dp = jnp.concatenate(slopes, axis=0).reshape(stacked)
        raised = jnp.exp(s - jnp.max(s, axis=1, keepdims=True))
        w = raised * (1.0 / jnp.sum(raised, axis=1, keepdims=True))
        inner = jnp.sum(w * dp, axis=1, keepdims=True)
        ds = (w * (dp - inner)).astype(BF16).reshape(-1, ql)
        w = w.astype(BF16).reshape(-1, ql)
        chain = heads_in * kl
        for p in range(pairs):
            qs, ks = slice(p * ql, (p + 1) * ql), slice(p * kl, (p + 1) * kl)
            own = slice(p * chain, (p + 1) * chain)
            q = split_heads(lane_block(q_ref, qs, cols[0] + j), heads_in)
            g = split_heads(lane_block(g_ref, qs, j), heads_in)
            k = split_heads(lane_block(k_ref, ks, cols[1] + j), heads_in)
            dq = mm_tn(ds[own], k) * scaling
            dk = mm(side_by_side(ds[own], heads_in), q) * scaling
            dv = mm(side_by_side(w[own], heads_in), g)
            put_block(dq_ref, qs, out_cols[0] + j, dq.astype(BF16))
            put_block(dk_ref, ks, out_cols[1] + j, dk.astype(BF16))
            put_block(dv_ref, ks, out_cols[2] + j, dv.astype(BF16))


def attend_back(lens, q, k, v, g, cols, pairs, blocks, heads_in, fixed, scaling, packed):
    rows = q.shape[0]
    krows = k.shape[0]
    vmem = pl.BlockSpec(memory_space=pltpu.VMEM)
    width = blocks * LANES
    if packed:
        operands = [lens, q, g]
        out_cols = (0, blocks, 2 * blocks)
        out_shape = jax.ShapeDtypeStruct((rows, 3 * width), BF16)
        out_specs = vmem
    else:
        operands = [lens, q, k, g]
        out_cols = (0, 0, blocks)
        out_shape = [
            jax.ShapeDtypeStruct((rows, width), BF16),
            jax.ShapeDtypeStruct((krows, 2 * width), BF16),
        ]
        out_specs = [vmem, vmem]

    def body(lens_ref, *refs, **kw):
        if packed:
            q_ref, g_ref, out_ref = refs
            ins, outs = (q_ref, q_ref, q_ref, g_ref), (out_ref,) * 3
        else:
            q_ref, k_ref, g_ref, dq_ref, dkv_ref = refs
            ins, outs = (q_ref, k_ref, k_ref, g_ref), (dq_ref, dkv_ref, dkv_ref)
        attend_back_kernel(lens_ref, *ins, *outs, **kw)

    return pl.pallas_call(
        functools.partial(
            body,
            pairs=pairs,
            blocks=blocks,
            cols=cols,
            out_cols=out_cols,
            heads_in=heads_in,
            fixed=fixed,
            scaling=scaling,
        ),
        in_specs=[pl.BlockSpec(memory_space=pltpu.SMEM)] + [vmem] * (len(operands) - 1),
        out_specs=out_specs,
        out_shape=out_shape,
        compiler_params=pltpu.CompilerParams(vmem_limit_bytes=10 * 1024 * 1024),
        cost_estimate=cost(6),
        name="attend_back",
    )(*operands)


class Job:
    def __init__(self, a, b, low, high, place):
        self.a, self.b = a, b
        self.low, self.count = low, high - low
        self.columns = b[3]
        self.place = place


def flat_kernel(side_ref, *refs, plans, found, quarter, resident):
    out_ref, chosen_ref, stage_ref = refs[len(found) : len(found) + 3]
    core = side_ref[0]
    depth = chosen_ref.shape[0] // 2
    if not resident:
        a_buf, b_buf, in_sem = refs[-3:]

    def loads(jobs, k):
        job, slot = jobs[k], k % 2
        copies = []
        for side, buf, start, width in (
            (job.a, a_buf, job.a[2] + job.low, job.count),
            (job.b, b_buf, job.b[2], job.columns),
        ):
            for half in range(2):
                copies.append(
                    pltpu.make_async_copy(
                        refs[found[id(side[half])]].at[:, start : start + width],
                        buf.at[slot, half * depth : (half + 1) * depth, 0:width],
                        in_sem.at[slot, len(copies)],
                    )
                )
        return copies

    def run(jobs):
        if not resident:
            for copy in loads(jobs, 0):
                copy.start()
        for k, job in enumerate(jobs):
            if resident:
                a_refs = [refs[found[id(job.a[half])]] for half in range(2)]
                b_refs = [refs[found[id(job.b[half])]] for half in range(2)]
                a_first, b_first = job.a[2] + job.low, job.b[2]
            else:
                if k + 1 < len(jobs):
                    for copy in loads(jobs, k + 1):
                        copy.start()
                for copy in loads(jobs, k):
                    copy.wait()
                halves = [slice(0, depth), slice(depth, 2 * depth)]
                a_refs = [a_buf.at[k % 2, half] for half in halves]
                b_refs = [b_buf.at[k % 2, half] for half in halves]
                a_first = b_first = 0
            units = job.columns // (2 * UNIT if quarter else UNIT)
            for u in range(units):
                at = 4 * u + 2 * side_ref[1] + core if quarter else 2 * u + core
                block = pl.ds(pl.multiple_of(at * LANES + b_first, LANES), LANES)
                for half in range(2):
                    chosen_ref[half * depth : (half + 1) * depth, u * LANES : (u + 1) * LANES] = (
                        b_refs[half][:, block]
                    )
            bm = best_rows(job.count, units)
            rows = bm * units

            @pl.loop(0, job.count // bm)
            def _(i, job=job, units=units, bm=bm, rows=rows, a_refs=a_refs, a_first=a_first):
                columns = pl.ds(pl.multiple_of(a_first + i * bm, LANES), bm)
                a = jnp.concatenate([a_ref[:, columns] for a_ref in a_refs], axis=0).T
                for u0 in range(0, units, 12):
                    u1 = min(u0 + 12, units)
                    total = mm(a, chosen_ref[:, u0 * LANES : u1 * LANES])
                    for u in range(u0, u1):
                        stage_ref[pl.ds(u, bm, stride=units), :] = total[
                            :, (u - u0) * LANES : (u - u0 + 1) * LANES
                        ]
                first = pl.multiple_of(job.place + i * rows, LANES)
                out_ref[pl.ds(first, rows), :] = stage_ref[:rows].astype(BF16)

    if len(plans) == 1:
        run(plans[0])
    else:
        for side, jobs in enumerate(plans):

            @pl.when(side_ref[1] == side)
            def _(jobs=jobs):
                run(jobs)


def best_rows(count, units):
    most = 512 if units <= 8 else 384
    return max(size for size in range(LANES, most + 1, LANES) if count % size == 0)


def flat_grads(side, total_rows, plans, us, quarter=False, resident=True):
    arrays, found = [], {}
    jobs = [job for plan in plans for job in plan]
    for job in jobs:
        for array in (*job.a[:2], *job.b[:2]):
            if id(array) not in found:
                found[id(array)] = len(arrays)
                arrays.append(array)
    depth = 2 * arrays[0].shape[0]
    widest = max(job.columns for job in jobs)
    tallest = max(job.count for job in jobs)
    factor = 2 * UNIT if quarter else UNIT
    rows = max(best_rows(job.count, job.columns // factor) * job.columns // factor for job in jobs)
    held = 2 * depth * widest * LANES // factor + 4 * rows * LANES
    scratch = [
        pltpu.VMEM((depth, widest * LANES // factor), BF16),
        pltpu.VMEM((rows, LANES), F32),
    ]
    if not resident:
        held += 4 * depth * (tallest + widest)
        scratch += [
            pltpu.VMEM((2, depth, tallest), BF16),
            pltpu.VMEM((2, depth, widest), BF16),
            pltpu.SemaphoreType.DMA((2, 4)),
        ]
    place = pltpu.VMEM if resident else pltpu.HBM
    return pl.pallas_call(
        functools.partial(
            flat_kernel, plans=plans, found=found, quarter=quarter, resident=resident
        ),
        in_specs=[pl.BlockSpec(memory_space=pltpu.SMEM)]
        + [pl.BlockSpec(memory_space=place)] * len(arrays),
        out_specs=pl.BlockSpec(memory_space=pltpu.VMEM),
        out_shape=jax.ShapeDtypeStruct((total_rows, LANES), BF16),
        scratch_shapes=scratch,
        compiler_params=pltpu.CompilerParams(vmem_limit_bytes=held + (8 if resident else 10) * 1024 * 1024),
        cost_estimate=cost(us),
        name="flat_grads",
    )(side, *arrays)


def dp_swap(block, bit):
    count = lax.axis_size("dp")
    return lax.ppermute(block, "dp", [(i, i ^ bit) for i in range(count)])


def stream_swap(block):
    return lax.ppermute(block, "stream", [(0, 1), (1, 0)])


def pick(block, index, axis=0):
    return lax.dynamic_index_in_dim(block, index, axis, keepdims=False)


def plus(a, b):
    return (a.astype(F32) + b.astype(F32)).astype(BF16)


def tied(*values):
    return lax.optimization_barrier(values)


def scatter_parts(flat, cuts):
    count = lax.axis_size("dp")
    top = count.bit_length() - 2
    bits = tuple(range(top, 0, -1))
    rows = flat.shape[0] // (count // 2)
    blocks = flat.reshape((2,) * len(bits) + (rows, LANES))
    natural = tuple(range(1, top + 1))
    turned = natural[1:2] + natural[:1] + natural[2:]
    parts, start = [], 0
    for share, turn in cuts:
        part = lax.slice_in_dim(blocks, start, start + rows * share // 8, axis=len(bits))
        start += rows * share // 8
        parts.append((part, bits, turned if turn else natural))
    return parts


def scatter_step(parts):
    me = lax.axis_index("dp")
    done = []
    for block, left, order in parts:
        bit = order[0]
        axis = left.index(bit)
        mine = (me >> bit) & 1
        keep = pick(block, mine, axis)
        far = dp_swap(pick(block, 1 - mine, axis), 1 << bit)
        block = plus(keep, far) if len(order) > 1 else keep.astype(F32) + far.astype(F32)
        done.append((block, left[:axis] + left[axis + 1 :], order[1:]))
    return done


def scatter_end(parts):
    while parts[0][2]:
        parts = scatter_step(parts)
    blocks = [block for block, _, _ in parts]
    return jnp.concatenate(blocks) if len(blocks) > 1 else blocks[0]


def reduce_scatter(flat, cuts):
    return scatter_end(scatter_parts(flat, cuts))


def share_of(result):
    core = lax.axis_index("dp") & 1
    halves = result.reshape(2, result.shape[0] // 2, LANES)
    mine = pick(halves, core)
    far = dp_swap(pick(halves, 1 - core), 1)
    first = jnp.where(core == 0, mine, far)
    second = jnp.where(core == 0, far, mine)
    return jnp.stack([first, second], axis=1).reshape(-1)


def choices(stream):
    me = lax.axis_index("dp")
    y, odd = (me >> 1) & 1, (me >> 2) & 1
    own = jnp.where(y == 1, odd, 1 - odd)
    values = [me & 1, y, odd, (me >> 3) & 1, 1 - y, own, stream, me >> 1]
    return jnp.stack(values).astype(jnp.int32)


LATE_Y, LATE_OWN, STREAM, CHIP = 4, 5, 6, 7
TEXT_SHARES = (48, 46, 38, 24)


def split_kernel(choice_ref, flat_ref, *refs, chunk, cuts):
    for k, (start, rows, bases, weight, which) in enumerate(cuts):
        mine = choice_ref[which]
        for i, base in enumerate(bases):
            for out_ref, index in ((refs[2 * k], mine), (refs[2 * k + 1], 1 - mine)):
                first = (base + index * weight) * chunk + start
                out_ref[i] = flat_ref[pl.ds(pl.multiple_of(first, 16), rows), :]


def split(choice, flat, chunk, cuts):
    shapes = [
        jax.ShapeDtypeStruct((len(bases), rows, LANES), BF16)
        for _, rows, bases, _, _ in cuts
        for _ in range(2)
    ]
    return pl.pallas_call(
        functools.partial(split_kernel, chunk=chunk, cuts=cuts),
        in_specs=[
            pl.BlockSpec(memory_space=pltpu.SMEM),
            pl.BlockSpec(memory_space=pltpu.VMEM),
        ],
        out_specs=[pl.BlockSpec(memory_space=pltpu.VMEM)] * len(shapes),
        out_shape=shapes,
        compiler_params=pltpu.CompilerParams(vmem_limit_bytes=8 * 1024 * 1024),
        cost_estimate=cost(3),
        name="split",
    )(choice, flat)


def piece_set(choice, flat, firsts, shares):
    chunk = flat.shape[0] // 8
    unit = chunk // sum(shares)
    cuts, start = [], 0
    for first, share in zip(firsts, shares):
        bits = [bit for bit in (3, 2, 1) if bit != first]
        bases = tuple(
            sum(((n >> (1 - at)) & 1) << (b - 1) for at, b in enumerate(bits)) for n in range(4)
        )
        cuts.append((start, unit * share, bases, 1 << (first - 1), first))
        start += unit * share
    arrays = split(choice, flat, chunk, tuple(cuts))
    return [
        Piece(keep, out, first) for keep, out, first in zip(arrays[::2], arrays[1::2], firsts)
    ]


class Piece:
    def __init__(self, keep, out, bit):
        self.keep, self.out, self.bit = keep, out, bit

    def send(self):
        self.far = dp_swap(self.out, 1 << self.bit)


def after(value, pieces, name="far"):
    value, *got = tied(value, *(getattr(piece, name) for piece in pieces))
    for piece, array in zip(pieces, got):
        setattr(piece, name, array)
    return value


def paced(came, leaving, values=()):
    got = tied(*(item.far for item in came), *(item.out for item in leaving), *values)
    for item, array in zip(came, got):
        item.far = array
    for item, array in zip(leaving, got[len(came) :]):
        item.out = array
    return got[len(came) + len(leaving) :]


def added(a_ref, b_ref, index):
    return a_ref[index].astype(F32) + b_ref[index].astype(F32)


def add_split_kernel(choice_ref, *refs, plan, inputs):
    outs = refs[2 * inputs :]
    for k, base, stride, which, out, at in plan:
        keep_ref, far_ref = refs[2 * k : 2 * k + 2]
        mine = choice_ref[which]
        for ref, index in ((outs[2 * out], mine), (outs[2 * out + 1], 1 - mine)):
            ref[at] = added(keep_ref, far_ref, base + index * stride).astype(BF16)


def add_split(choice, groups, which=None):
    operands, plan, shapes = [], [], []
    for out, (bit, pieces) in enumerate(groups):
        at = 0
        for piece in pieces:
            for base in range(0, piece.keep.shape[0], 2):
                plan.append((len(operands) // 2, base, 1, which or bit, out, at))
                at += 1
            operands += [piece.keep, piece.far]
        shape = jax.ShapeDtypeStruct((at,) + pieces[0].keep.shape[1:], BF16)
        shapes += [shape, shape]
    vmem = pl.BlockSpec(memory_space=pltpu.VMEM)
    arrays = pl.pallas_call(
        functools.partial(add_split_kernel, plan=tuple(plan), inputs=len(operands) // 2),
        in_specs=[pl.BlockSpec(memory_space=pltpu.SMEM)] + [vmem] * len(operands),
        out_specs=[vmem] * len(shapes),
        out_shape=shapes,
        compiler_params=pltpu.CompilerParams(vmem_limit_bytes=8 * 1024 * 1024),
        cost_estimate=cost(1),
        name="add_split",
    )(choice, *operands)
    return [
        Piece(arrays[2 * out], arrays[2 * out + 1], bit) for out, (bit, _) in enumerate(groups)
    ]


def finish_kernel(choice_ref, *refs, rows):
    refs = list(refs)
    pairs = [[(refs.pop(0), refs.pop(0)) for _ in group] for group in rows]
    near_ref, far_ref = refs.pop(0), refs.pop(0)
    out_ref, send_ref, *totals, joined_ref = refs
    for total_ref, group, starts in zip(totals, pairs, rows):
        for (keep_ref, came_ref), firsts in zip(group, starts):
            count = keep_ref.shape[1]
            for at, first in enumerate(firsts):
                total_ref[first : first + count] = added(keep_ref, came_ref, at)
    half = near_ref.shape[0]
    joined_ref[pl.ds(0, half, stride=2), :] = near_ref[...].astype(F32)
    joined_ref[pl.ds(1, half, stride=2), :] = far_ref[...].astype(F32)
    image_ref = totals[0]
    total_rows = image_ref.shape[0]
    chip = choice_ref[CHIP]
    first = jnp.where(chip == 1, 1536, 0)
    last = jnp.where(chip == 4, 2048, total_rows)
    here = (chip >= 1) & (chip <= 4) & (choice_ref[STREAM] == 0)
    last = jnp.where(here, last, 0)
    at = lax.broadcasted_iota(jnp.int32, (total_rows, 1), 0)
    image_ref[...] = jnp.where((at >= first) & (at < last), joined_ref[...], image_ref[...])
    core = choice_ref[0]
    row = 0
    for total_ref in totals:
        half = total_ref.shape[0] // 2
        for ref, index in ((out_ref, core), (send_ref, 1 - core)):
            part = total_ref[pl.ds(pl.multiple_of(index * half, 8), half), :]
            ref[row : row + half, :] = part.astype(ref.dtype)
        row += half


def join_kernel(choice_ref, near_ref, far_ref, *outs):
    core = choice_ref[0]
    row = 0
    for out_ref in outs:
        half = out_ref.shape[0] // 2
        out_ref[pl.ds(core, half, stride=2), :] = near_ref[row : row + half, :]
        out_ref[pl.ds(1 - core, half, stride=2), :] = far_ref[row : row + half, :].astype(F32)
        row += half


def finished(choice, groups, rows, late):
    sizes = [
        sum(piece.keep.shape[0] * piece.keep.shape[1] for piece in group) for group in groups
    ]
    vmem = pl.BlockSpec(memory_space=pltpu.VMEM)
    smem = pl.BlockSpec(memory_space=pltpu.SMEM)
    operands = [ref for group in groups for piece in group for ref in (piece.keep, piece.far)]
    operands += list(late)
    half = jax.ShapeDtypeStruct((sum(sizes) // 2, LANES), F32)
    near, send = pl.pallas_call(
        functools.partial(finish_kernel, rows=rows),
        in_specs=[smem] + [vmem] * len(operands),
        out_specs=[vmem] * 2,
        out_shape=[half, jax.ShapeDtypeStruct(half.shape, BF16)],
        scratch_shapes=[pltpu.VMEM((rows, LANES), F32) for rows in (*sizes, sizes[0])],
        compiler_params=pltpu.CompilerParams(vmem_limit_bytes=12 * 1024 * 1024),
        cost_estimate=cost(3),
        name="finish",
    )(choice, *operands)
    joined = pl.pallas_call(
        join_kernel,
        in_specs=[smem, vmem, vmem],
        out_specs=[vmem] * 2,
        out_shape=[jax.ShapeDtypeStruct((rows, LANES), F32) for rows in sizes],
        compiler_params=pltpu.CompilerParams(vmem_limit_bytes=12 * 1024 * 1024),
        cost_estimate=cost(2),
        name="join",
    )(choice, near, dp_swap(send, 1))
    return [block.reshape(-1) for block in joined]


CHUNK = 64
ROWS = 128
WIDEST = 1024
WIDEST_GELU = 1024


def tiles(columns, body, widest=None):
    size = max(c for c in range(LANES, (widest or WIDEST) + 1, LANES) if columns % c == 0)
    if size == columns:
        return body(slice(0, columns))

    @pl.loop(0, columns // size)
    def _(j):
        body(pl.ds(pl.multiple_of(j * size, size), size))


def views(pack_ref, *widths):
    found, start = [], 0
    for width in widths:
        found.append(pack_ref.at[:, start : start + width])
        start += width
    return found


def row_chunks(rows, body):
    size = ROWS if rows % ROWS == 0 else CHUNK

    @pl.loop(0, rows // size)
    def _(i):
        body(i * size, pl.ds(pl.multiple_of(i * size, size), size), size)


def normed_chunk(a):
    centred = a - jnp.mean(a, axis=-1, keepdims=True)
    inverse = lax.rsqrt(jnp.mean(centred * centred, axis=-1, keepdims=True) + 1e-05)
    return centred * inverse, inverse


def normed_back_chunk(grad, n, inverse, gain_row):
    scaled = grad * gain_row
    low = jnp.mean(scaled, axis=-1, keepdims=True)
    tilt = jnp.mean(scaled * n, axis=-1, keepdims=True)
    return (scaled - low - n * tilt) * inverse, jnp.sum(grad * n, axis=0, keepdims=True)


def co_kernel(
    lens_ref, x_ref, given_ref, source_ref, g_ref, wmade_ref, wat_ref,
    made_ref, pack_ref, n_ref, inv_ref, a_ref, *, pairs, fixed, scaling, makes_kv,
):
    rows, width = x_ref.shape
    c_ref, h_ref = views(pack_ref, D_C, width)

    def made_tile(cols):
        made_ref[:, cols] = mm(source_ref[...], wmade_ref[:, cols]).astype(BF16)

    def a_tile(cols):
        a_ref[:, cols] = x_ref[:, cols].astype(F32) + mm(c_ref[...], wat_ref[:, cols])

    def norm(i, at, size):
        n, inverse = normed_chunk(a_ref[at, :])
        n_ref[at, :] = n
        inv_ref[at, :] = jnp.broadcast_to(inverse, (size, LANES))
        h_ref[at, :] = (n * g_ref[0:1, :]).astype(BF16)

    tiles(made_ref.shape[1], made_tile)
    q_ref, kv_ref = (given_ref, made_ref) if makes_kv else (made_ref, given_ref)
    blocks = q_ref.shape[1] // LANES
    attend_kernel(
        lens_ref, q_ref, kv_ref, kv_ref, c_ref, pairs=pairs, blocks=blocks,
        cols=(0, 0, blocks), heads_in=1, fixed=fixed, scaling=scaling,
    )
    tiles(width, a_tile)
    row_chunks(rows, norm)


def mlp_kernel(
    pack1_ref, n1_ref, g_ref, wup_ref, wdown_ref, wqkv_ref,
    pack_ref, slope_ref, n_ref, inv_ref, r_ref, a_ref,
):
    rows, width = n1_ref.shape
    _, h1_ref = views(pack1_ref, D_C, width)
    hid_ref, h_ref = views(pack_ref, wup_ref.shape[1], width)

    def up_tile(cols):
        u_all = mm(h1_ref[...], wup_ref[:, cols])
        for at in range(0, rows, CHUNK):
            u = u_all[at : at + CHUNK]
            share = 0.5 + 0.5 * lax.erf(u * 0.7071067811865476)
            hid_ref[at : at + CHUNK, cols] = (u * share).astype(BF16)
            slope = share + u * (0.3989422804014327 * jnp.exp(-0.5 * u * u))
            slope_ref[at : at + CHUNK, cols] = slope.astype(BF16)

    def down_tile(cols):
        a_ref[:, cols] = n1_ref[:, cols] * g_ref[0:1, cols] + mm(hid_ref[...], wdown_ref[:, cols])

    def norm(i, at, size):
        n, inverse = normed_chunk(a_ref[at, :])
        n_ref[at, :] = n
        inv_ref[at, :] = jnp.broadcast_to(inverse, (size, LANES))
        h_ref[at, :] = (n * g_ref[1:2, :]).astype(BF16)

    def qkv_tile(cols):
        r_ref[:, cols] = mm(h_ref[...], wqkv_ref[:, cols]).astype(BF16)

    tiles(wup_ref.shape[1], up_tile, WIDEST_GELU)
    tiles(width, down_tile)
    row_chunks(rows, norm)
    tiles(r_ref.shape[1], qkv_tile)


def self_kernel(
    lens_ref, r_ref, n2_ref, g_ref, wout_ref, cot_ref, far_cot_ref,
    pack_ref, y_ref, de_ref, dg_ref, a_ref, dz_ref,
    *, pairs, heads_in, fixed, scaling,
):
    rows, width = n2_ref.shape
    z_ref, de_low_ref, dr_ref = views(pack_ref, width, width, 3 * width)
    near = cot_ref.shape[0]
    dz_ref[:near, :] = cot_ref[...]
    if near < rows:
        dz_ref[near:, :] = far_cot_ref[...]
    blocks = width // LANES
    cols = (0, blocks, 2 * blocks)
    shared = dict(
        pairs=pairs, blocks=blocks, cols=cols, heads_in=heads_in, fixed=fixed, scaling=scaling
    )

    def out_tile(at):
        a_ref[:, at] = n2_ref[:, at] * g_ref[1:2, at] + mm(z_ref[...], wout_ref[:, at])

    def last(start, at, size):
        n, inverse = normed_chunk(a_ref[at, :])
        y = n * g_ref[2:3, :]
        grad = dz_ref[at, :].astype(F32)
        if fixed is None:
            slots = rows // pairs
            place = lax.broadcasted_iota(jnp.int32, (size, 1), 0) + lax.rem(start, slots)
            valid = (place < lens_ref[lax.div(start, slots)]).astype(F32)
            y, grad = y * valid, grad * valid
        y_ref[at, :] = y.astype(BF16)
        de, dg = normed_back_chunk(grad, n, inverse, g_ref[2:3, :])
        de_ref[at, :] = de
        de_low_ref[at, :] = de.astype(BF16)
        dg_ref[...] += dg

    def dz_tile(at):
        dz_ref[:, at] = mm_nt(de_low_ref[...], wout_ref[at, :]).astype(BF16)

    attend_kernel(lens_ref, r_ref, r_ref, r_ref, z_ref, **shared)
    tiles(width, out_tile)
    dg_ref[...] = jnp.zeros_like(dg_ref)
    row_chunks(rows, last)
    tiles(width, dz_tile)
    attend_back_kernel(
        lens_ref, r_ref, r_ref, r_ref, dz_ref, dr_ref, dr_ref, dr_ref, out_cols=cols, **shared
    )


def mlp_back_kernel(
    pack3_ref, de_ref, n2_ref, inv2_ref, g_ref, slope_ref, wqkv_ref, wdown_ref,
    pack_ref, db_ref, dg_ref, a_ref,
):
    rows, width = n2_ref.shape
    _, _, dr_ref = views(pack3_ref, width, width, 3 * width)
    db_low_ref, du_ref = views(pack_ref, width, slope_ref.shape[1])
    dg_ref[...] = jnp.zeros_like(dg_ref)

    def second_tile(at):
        a_ref[:, at] = de_ref[:, at] + mm_nt(dr_ref[...], wqkv_ref[at, :])

    def second_norm(i, at, size):
        db, dg = normed_back_chunk(a_ref[at, :], n2_ref[at, :], inv2_ref[at, 0:1], g_ref[1:2, :])
        db_ref[at, :] = db
        db_low_ref[at, :] = db.astype(BF16)
        dg_ref[...] += dg

    def du_tile(at):
        grad = mm_nt(db_low_ref[...], wdown_ref[at, :])
        du_ref[:, at] = (grad * slope_ref[:, at].astype(F32)).astype(BF16)

    tiles(width, second_tile)
    row_chunks(rows, second_norm)
    tiles(du_ref.shape[1], du_tile)


def context_back_kernel(
    pack4_ref, db_ref, n1_ref, inv1_ref, g_ref, wup_ref, wat_ref,
    da_low_ref, da_ref, dc_ref, dg_ref, a_ref,
):
    rows, width = n1_ref.shape
    _, du_ref = views(pack4_ref, width, wup_ref.shape[1])
    dg_ref[...] = jnp.zeros_like(dg_ref)

    def first_tile(at):
        a_ref[:, at] = db_ref[:, at] + mm_nt(du_ref[...], wup_ref[at, :])

    def first_norm(i, at, size):
        da, dg = normed_back_chunk(a_ref[at, :], n1_ref[at, :], inv1_ref[at, 0:1], g_ref[0:1, :])
        da_ref[at, :] = da
        da_low_ref[at, :] = da.astype(BF16)
        dg_ref[...] += dg

    def dc_tile(at):
        dc_ref[:, at] = mm_nt(da_low_ref[...], wat_ref[at, :]).astype(BF16)

    tiles(width, first_tile)
    row_chunks(rows, first_norm)
    tiles(dc_ref.shape[1], dc_tile)


def fused(kernel, operands, outs, scratch, name, us, smem_first=False, limit=11):
    vmem = pl.BlockSpec(memory_space=pltpu.VMEM)
    in_specs = [vmem] * len(operands)
    if smem_first:
        in_specs[0] = pl.BlockSpec(memory_space=pltpu.SMEM)
    return pl.pallas_call(
        kernel,
        in_specs=in_specs,
        out_specs=[vmem] * len(outs),
        out_shape=[jax.ShapeDtypeStruct(shape, kind) for shape, kind in outs],
        scratch_shapes=[pltpu.VMEM(shape, kind) for shape, kind in scratch],
        compiler_params=pltpu.CompilerParams(vmem_limit_bytes=limit * 1024 * 1024),
        cost_estimate=cost(us),
        name=name,
    )(*operands)


def co_forward(lens, states, given, source, gains, made_w, attend_w, pairs, fixed):
    rows, width = states.shape
    made, pack1, n1, inv1 = fused(
        functools.partial(
            co_kernel,
            pairs=pairs,
            fixed=fixed,
            scaling=(D_C // H_C) ** (-0.5),
            makes_kv=made_w.shape[1] == 2 * D_C,
        ),
        (lens, states, given, source, gains, made_w, attend_w),
        [
            ((source.shape[0], made_w.shape[1]), BF16),
            ((rows, D_C + width), BF16),
            ((rows, width), F32),
            ((rows, LANES), F32),
        ],
        [((rows, width), F32)],
        "co_forward",
        7,
        True,
    )
    return made, pack1, n1, inv1


def mlp_forward(pack1, n1, gains, up_w, down_w, qkv_w):
    rows, width = n1.shape
    hidden = up_w.shape[1]
    return fused(
        mlp_kernel,
        (pack1, n1, gains, up_w, down_w, qkv_w),
        [
            ((rows, hidden + width), BF16),
            ((rows, hidden), BF16),
            ((rows, width), F32),
            ((rows, LANES), F32),
            ((rows, 3 * width), BF16),
        ],
        [((rows, width), F32)],
        "mlp_forward",
        rows / 40,
    )


def self_turn(lens, r, n2, gains, output_w, cots, pairs, heads, fixed):
    rows, width = n2.shape
    size = width // heads
    return fused(
        functools.partial(
            self_kernel, pairs=pairs, heads_in=LANES // size, fixed=fixed, scaling=size ** (-0.5)
        ),
        (lens, r, n2, gains, output_w, *cots),
        [
            ((rows, 5 * width), BF16),
            ((rows, width), BF16),
            ((rows, width), F32),
            ((1, width), F32),
        ],
        [((rows, width), F32), ((rows, width), BF16)],
        "self_turn",
        rows / 128 + 9,
        True,
    )


def input_kernel(da_ref, dq_ref, dkv_ref, y_ref, trim_ref, wq_ref, wkv_ref, *outs, first):
    grad_ref, result_ref = outs
    rows = pl.ds(first, da_ref.shape[0] // 2)
    grad = da_ref[rows, :] + mm_nt(dq_ref[rows, :], wq_ref[...])
    grad = (grad + mm_nt(dkv_ref[rows, :], wkv_ref[...])).astype(BF16)
    y = y_ref[rows, :]
    if trim_ref.shape[0] < 8:
        grad_ref[...], result_ref[...] = grad, y
    else:
        grad_ref[...] = mm(trim_ref[...], grad).astype(BF16)
        result_ref[...] = mm(trim_ref[...], y).astype(BF16)


def input_grads(da, dq, dkv, y, trim, query_w, keyval_w, first, own):
    vmem = pl.BlockSpec(memory_space=pltpu.VMEM)
    return pl.pallas_call(
        functools.partial(input_kernel, first=first),
        in_specs=[vmem] * 7,
        out_specs=[vmem] * 2,
        out_shape=[jax.ShapeDtypeStruct((own, da.shape[1]), BF16)] * 2,
        compiler_params=pltpu.CompilerParams(vmem_limit_bytes=10 * 1024 * 1024),
        cost_estimate=cost(0.2),
        name="input_grads",
    )(da, dq, dkv, y, trim, query_w, keyval_w)


def mlp_back(pack3, de, n2, inv2, gains, slope, qkv_w, down_w):
    rows, width = n2.shape
    return fused(
        mlp_back_kernel,
        (pack3, de, n2, inv2, gains, slope, qkv_w, down_w),
        [
            ((rows, width + slope.shape[1]), BF16),
            ((rows, width), F32),
            ((1, width), F32),
        ],
        [((rows, width), F32)],
        "mlp_back",
        rows / 70,
    )


def context_back(pack4, db, n1, inv1, gains, up_w, attend_w):
    rows, width = n1.shape
    return fused(
        context_back_kernel,
        (pack4, db, n1, inv1, gains, up_w, attend_w),
        [
            ((rows, width), BF16),
            ((rows, width), F32),
            ((rows, D_C), BF16),
            ((1, width), F32),
        ],
        [((rows, width), F32)],
        "context_back",
        rows / 80,
    )


class Exchange:
    def __init__(self):
        self.far = {}
        self.pending = []
        self.parts = None

    def send(self, **arrays):
        for name, array in arrays.items():
            self.far[name] = dp_swap(array, 1)
            self.pending.append(name)

    def settle(self, value):
        names, self.pending = self.pending, []
        if names:
            value, *got = tied(value, *(self.far[name] for name in names))
            self.far.update(zip(names, got))
        return value

    def pair(self, name, array, start=0, width=None):
        return array, self.far[name], start, width or array.shape[1]


def stream_forward(
    lens, states, given, source, cot, weights, gains, heads, fixed, other_fixed, pairs, moves, hook
):
    made_w, attend_w, up_w, down_w, qkv_w, output_w = weights
    made, pack1, n1, inv1 = co_forward(
        lens, states, given, source, gains, made_w, attend_w, pairs, other_fixed
    )
    pack1 = moves.settle(hook("co", pack1))
    moves.send(pack1=pack1)
    pack2, slope, n2, inv2, r = mlp_forward(pack1, n1, gains, up_w, down_w, qkv_w)
    r, pack2 = tied(moves.settle(hook("mlp", r)), pack2)
    moves.send(pack2=pack2)
    near_cot, far_cot = cot
    cots = (near_cot, far_cot[0] if far_cot else near_cot)
    pack3, result, de, dg2 = self_turn(lens, r, n2, gains, output_w, cots, pairs, heads, fixed)
    pack3 = moves.settle(hook("self", pack3))
    moves.send(pack3=pack3)
    pack4, db, dg1 = mlp_back(pack3, de, n2, inv2, gains, slope, qkv_w, down_w)
    pack4 = moves.settle(hook("mid", pack4))
    moves.send(pack4=pack4)
    da_low, da, dc, dg0 = context_back(pack4, db, n1, inv1, gains, up_w, attend_w)
    dc = moves.settle(hook("back", dc))
    width, hidden = up_w.shape

    def sides(dq, da_low):
        def side(number, start, count):
            pack = (pack1, pack2, pack3, pack4)[number - 1]
            return moves.pair("pack%d" % number, pack, start, count)

        return {
            "query": (moves.pair("states", states), moves.pair("dq", dq)),
            "attend": (side(1, 0, D_C), moves.pair("da", da_low)),
            "up": (side(1, D_C, width), side(4, width, hidden)),
            "down": (side(2, 0, hidden), side(4, 0, width)),
            "qkv": (side(2, hidden, width), side(3, 2 * width, 3 * width)),
            "output": (side(3, 0, width), side(3, width, width)),
        }

    return result, (da, da_low), dc, made, sides, jnp.concatenate([dg0, dg1, dg2])


NAMES = ("query", "keyval", "attend", "up", "down", "qkv", "output")


def half_jobs(both, sizes, total):
    plans, filled = ([], []), 0
    for name in NAMES:
        m, n = sizes[name]
        room = min(max((total // 2 - filled) // n, 0), m)
        for plan, low, high in ((plans[0], 0, room), (plans[1], room, m)):
            if low < high and name in both:
                start = filled + low * n - (0 if plan is plans[0] else total // 2)
                step = min(high - low, 1024)
                for at in range(low, high, step):
                    place = (start + (at - low) * n) // UNIT
                    plan.append(Job(*both[name], at, at + step, place))
        filled += m * n
    return plans


def spread(count, regions, padded, offset, rows):
    target = lax.broadcasted_iota(jnp.int32, (rows, count * regions), 0) - offset
    source = lax.broadcasted_iota(jnp.int32, (rows, count * regions), 1)
    return (target == source // regions * padded + source % regions).astype(BF16)


def local(
    text_states,
    image_states,
    caption_lengths,
    text_query,
    text_keyval,
    text_attend,
    text_up,
    text_down,
    text_qkv,
    text_output,
    text_gains,
    image_query,
    image_keyval,
    image_attend,
    image_up,
    image_down,
    image_qkv,
    image_output,
    image_gains,
    text_cotangent,
    image_cotangent,
):
    own_pairs = caption_lengths.shape[0]
    own_text = text_states.shape[0]
    text_len = own_text // own_pairs
    regions = image_states.shape[0] // own_pairs
    padded = -(-regions // 16) * 16
    own_image = own_pairs * padded
    pairs = 2 * own_pairs
    d_t, d_i = text_states.shape[1], image_states.shape[1]
    stream = lax.axis_index("stream")
    core = lax.axis_index("dp") & 1
    side = jnp.stack([core, stream]).astype(jnp.int32)

    far_put = spread(own_pairs, regions, padded, 0, 2 * own_image)
    near_put = spread(own_pairs, regions, padded, own_image, 2 * own_image)
    trim = near_put[own_image:].T

    def both_images(near):
        return (mm(far_put, stream_swap(near)) + mm(near_put, near)).astype(BF16)

    choice = choices(stream)
    image_all = both_images(image_states)
    image_q = mm(image_all, image_query).astype(BF16)
    image_kv = mm(image_all, image_keyval).astype(BF16)
    far_text, far_lens, image_q, image_kv = tied(
        stream_swap(text_states), stream_swap(caption_lengths), image_q, image_kv
    )
    text_all = jnp.concatenate([text_states, far_text])
    lens = jnp.concatenate([caption_lengths, far_lens])
    image_cotangent, text_cotangent, text_all = tied(image_cotangent, text_cotangent, text_all)
    image_cot = both_images(image_cotangent)
    far_text_cot = stream_swap(text_cotangent)

    co_blocks = D_C // LANES
    co_cols = (0, 0, co_blocks)
    co_scale = (D_C // H_C) ** (-0.5)

    image_moves, text_moves = Exchange(), Exchange()
    image_moves.send(states=image_all)
    cots = [far_text_cot]

    def image_hook(name, value):
        if name == "self":
            value, cots[0] = tied(value, cots[0])
        return value

    image_out, (image_da, image_da_low), image_dc, text_kv, image_sides, image_dg = stream_forward(
        lens,
        image_all,
        image_q,
        text_all,
        (image_cot, None),
        (text_keyval, image_attend, image_up, image_down, image_qkv, image_output),
        image_gains,
        H_I,
        regions,
        None,
        pairs,
        image_moves,
        image_hook,
    )
    image_dq, text_dkv = attend_back(
        lens, image_q, text_kv, text_kv, image_dc, co_cols, pairs, co_blocks, 1, None, co_scale, False,
    )
    image_moves.send(dq=image_dq, da=image_da_low)
    image_sides = image_sides(image_dq, image_da_low)
    text_moves.send(states=text_all, dkv=text_dkv)

    def sizes_of(*weights):
        return {name: weight.shape for name, weight in zip(NAMES, weights)}

    def gather_half(both, sizes):
        total = sum(m * n for m, n in sizes.values())
        total_rows = total // (2 * UNIT)
        plans = half_jobs(both, sizes, total)
        image = both["query"][0][0] is image_all
        return flat_grads(side, total_rows, plans, 6 if image else 14, resident=image)

    image_sizes = sizes_of(
        image_query, image_keyval, image_attend, image_up, image_down, image_qkv, image_output
    )
    text_sizes = sizes_of(
        text_query, text_keyval, text_attend, text_up, text_down, text_qkv, text_output
    )
    early = lax.axis_size("dp") == 16
    if early:
        image_flat = gather_half(image_sides, image_sizes)

    pieces = []

    def hook(name, value):
        if not early:
            return value
        if name == "co":
            value, flat = tied(value, image_flat)
            pieces.extend(piece_set(choice, flat, (1, 2, 1, 2), (1, 1, 1, 1)))
            value = after(value, pieces, "out")
            for piece in pieces[:2]:
                piece.send()
        if name == "mlp":
            (value,) = paced(pieces[:2], pieces[2:], (value,))
            for piece in pieces[2:]:
                piece.send()
        if name == "self":
            (value,) = paced(pieces[2:], (), (value,))
            pieces[:] = add_split(choice, ((2, pieces[0::2]), (1, pieces[1::2])))
            for piece in pieces:
                piece.send()
        return value

    text_out, (text_da, text_da_low), text_dc, text_q, text_sides, text_dg = stream_forward(
        lens,
        text_all,
        image_kv,
        text_all,
        (text_cotangent, cots),
        (text_query, text_attend, text_up, text_down, text_qkv, text_output),
        text_gains,
        H_T,
        None,
        regions,
        pairs,
        text_moves,
        hook,
    )
    gains = pack_gains(text_dg, image_dg)
    bits = [1 << b for b in range(lax.axis_size("dp").bit_length() - 1)]
    text_dq, image_dkv = attend_back(
        lens, text_q, image_kv, image_kv, text_dc, co_cols, pairs, co_blocks, 1, regions, co_scale, False
    )

    if early:
        image_dkv, text_dq, text_da_low = paced(pieces, (), (image_dkv, text_dq, text_da_low))
        pieces[:] = add_split(choice, ((3, pieces[:1]), (3, pieces[1:])))
        pieces[0].send()
    image_moves.send(dkv=image_dkv)
    text_moves.send(dq=text_dq, da=text_da_low)
    text_sides = text_sides(text_dq, text_da_low)
    text_sides["keyval"] = (text_moves.pair("states", text_all), text_moves.pair("dkv", text_dkv))

    def all_input_grads(text_dq, image_dq):
        text = input_grads(
            text_da, text_dq, text_dkv, text_out, trim[:1], text_query, text_keyval, 0, own_text
        )
        image = input_grads(
            image_da,
            image_dq,
            image_dkv,
            image_out,
            trim,
            image_query,
            image_keyval,
            own_image,
            own_pairs * regions,
        )
        return (*text, *image)

    if early:
        late = Late(
            choice,
            side,
            image_moves.pair("states", image_all),
            image_moves.pair("dkv", image_dkv),
        )
        near_dq, *rest = text_sides["query"][1]
        near_dq, late.out = tied(near_dq, late.out)
        text_sides["query"] = (text_sides["query"][0], (near_dq, *rest))
        late.send()
        text_flat = gather_half(text_sides, text_sizes)
        text_flat = after(text_flat, [late, pieces[0]])
        text_pieces = piece_set(choice, text_flat, (1, 1, 1, 1), TEXT_SHARES)
        one, two, three, four = text_pieces
        late.turn()
        one.out, late.out, pieces[1].out, text_dq, image_dq, gains = tied(
            one.out, late.out, pieces[1].out, text_dq, image_dq, gains
        )
        one.send()
        late.send()
        pieces[1].send()
        gains = gain_step(gains, bits.pop())
        grads = all_input_grads(text_dq, image_dq)
        *grads, gains = paced((one, late, pieces[1]), (two,), (*grads, gains))
        (one,) = add_split(choice, ((2, (one,)),))
        late.add(gather=True)
        two.send()
        one.send()
        gains = gain_step(gains, bits.pop())
        (gains,) = paced((one, two, late), (three,), (gains,))
        (one,) = add_split(choice, ((3, (one,)),))
        (two,) = add_split(choice, ((2, (two,)),))
        late.add()
        three.send()
        two.send()
        one.send()
        gains = gain_step(gains, bits.pop())
        (gains,) = paced((one, two, three, late), (four,), (gains,))
        (two,) = add_split(choice, ((3, (two,)),))
        (three,) = add_split(choice, ((2, (three,)),))
        four.send()
        three.send()
        two.send()
        gains = gain_step(gains, bits.pop())
        (gains,) = paced((two, three, four), (), (gains,))
        (three,) = add_split(choice, ((3, (three,)),))
        (four,) = add_split(choice, ((2, (four,)),))
        three.send()
        four.send()
        paced((three, four), ())
        (four,) = add_split(choice, ((3, (four,)),))
        four.send()
        unit = image_flat.shape[0] // 8 // 4
        starts, row = [], 0
        for piece in (one, two, three, four):
            starts.append((row,))
            row += piece.keep.shape[1]
        image_share, text_share = finished(
            choice,
            (pieces, (one, two, three, four)),
            (((0, 2 * unit), (unit, 3 * unit)), tuple(starts)),
            (late.keep[0], late.far[0]),
        )
    else:
        image_sides["keyval"] = (
            image_moves.pair("states", image_all),
            image_moves.pair("dkv", image_dkv),
        )
        image_share = share_of(
            reduce_scatter(gather_half(image_sides, image_sizes), ((8, False),))
        )
        text_share = share_of(reduce_scatter(gather_half(text_sides, text_sizes), ((8, False),)))
        grads = all_input_grads(text_dq, image_dq)
        while bits:
            gains = gain_step(gains, bits.pop())
    text_grad, text_result, image_grad, image_result = grads
    text_gain_sum, image_gain_sum = unpack_gains(gains, text_dg.shape[1])
    return (
        text_result,
        image_result,
        text_grad,
        image_grad,
        text_share,
        image_share,
        text_gain_sum,
        image_gain_sum,
    )


def pack_gains(text_dg, image_dg):
    return jnp.concatenate([text_dg, image_dg], axis=1)


def gain_step(gains, bit):
    return gains + dp_swap(gains, bit)


def unpack_gains(gains, width):
    return gains[:, :width], gains[:, width:]


class Late:
    rows = 1280

    def __init__(self, choice, side, states, grads):
        self.choice = choice
        job = Job(states, grads, 0, states[0].shape[1], 768)
        flat = flat_grads(side, 4 * self.rows, [[job]], 2, True)
        self.keep, self.out = split(choice, flat, self.rows, ((0, self.rows, (0, 2), 1, LATE_Y),))
        self.bit = 2

    def send(self):
        self.far = dp_swap(self.out, self.bit)

    def turn(self):
        (piece,) = add_split(self.choice, ((LATE_OWN, (self,)),))
        self.keep, self.out, self.bit = piece.keep, piece.out, 4

    def add(self, gather=False):
        self.keep = plus(self.keep, self.far)
        if gather:
            route = []
            for i in range(16):
                z, y = i >> 2, (i >> 1) & 1
                goal = 1 if z & 1 else (0 if y else 2)
                if z != goal:
                    route.append((i, goal * 4 + (i & 3)))
            self.far = lax.ppermute(self.keep, "dp", route)
        else:
            self.far = lax.ppermute(self.keep, "stream", [(1, 0)])


def solution(mesh):
    split = P(("stream", "dp"), None)
    flat = P(("stream", "dp"))
    whole = P()
    return jax.shard_map(
        local,
        mesh=mesh,
        in_specs=(split, split, flat) + (whole,) * 16 + (split, split),
        out_specs=(split, split, split, split, flat, flat, whole, whole),
        check_vma=False,
    )
```
